32 devices in a mesh: dp: 2 (over y), seq: 16 (over z, x, core).
Axes of the slice: x: 2, y: 2, z: 4, core: 2. Of those that a mesh axis runs over, the one named last changes fastest.
Arguments:
- tokens: bfloat16 [4, 2048, 768], P('dp', 'seq'), may hold values from -6 to 6
- segments: int32 [4, 2048], P('dp', 'seq'), may hold values from -1 to 3, as said below
- query_route: int32 [4, 256], P('dp'), may hold values from 0 to 2047, as said below
- kv_route: int32 [4, 256], P('dp'), may hold values from 0 to 2047, as said below
- ffn_route: int32 [4, 256], P('dp', 'seq'), may hold values from 0 to 2047, as said below
- grad_out: bfloat16 [4, 2048, 768], P('dp', 'seq'), may hold values from -6 to 6
- attn_gain: float32 [768], replicated, may hold values from 0.5 to 1.5
- light_qkv: bfloat16 [768, 2304], replicated, may hold values from -0.21875 to 0.21875
- light_out: bfloat16 [768, 768], replicated, may hold values from -2.5 to 2.5
- heavy_q: bfloat16 [768, 768], replicated, may hold values from -0.21875 to 0.21875
- heavy_kv: bfloat16 [768, 1536], replicated, may hold values from -0.21875 to 0.21875
- heavy_out: bfloat16 [768, 768], replicated, may hold values from -6 to 6
- route_query: bfloat16 [768], replicated, may hold values from -0.21875 to 0.21875
- ffn_gain: float32 [768], replicated, may hold values from 0.5 to 1.5
- light_gate_up: bfloat16 [768, 2048], replicated, may hold values from -0.21875 to 0.21875
- light_down: bfloat16 [1024, 768], replicated, may hold values from -0.1875 to 0.1875
- heavy_gate_up: bfloat16 [768, 8192], replicated, may hold values from -0.21875 to 0.21875
- heavy_down: bfloat16 [4096, 768], replicated, may hold values from -0.09375 to 0.09375
- route_ffn: bfloat16 [768], replicated, may hold values from -0.21875 to 0.21875
Outputs:
- outputs: bfloat16 [4, 2048, 768], P('dp', 'seq')
- grad_tokens: bfloat16 [4, 2048, 768], P('dp', 'seq')
- grad_attn_gain: float32 [768], P('seq')
- grad_light_qkv: float32 [768, 2304], P('seq', 'dp')
- grad_light_out: float32 [768, 768], P('seq', 'dp')
- grad_heavy_q: float32 [768, 768], P('seq', 'dp')
- grad_heavy_kv: float32 [768, 1536], P('seq', 'dp')
- grad_heavy_out: float32 [768, 768], P('seq', 'dp')
- grad_route_query: float32 [768], P('seq')
- grad_ffn_gain: float32 [768], P('seq')
- grad_light_gate_up: float32 [768, 2048], P('seq', 'dp')
- grad_light_down: float32 [1024, 768], P('seq', 'dp')
- grad_heavy_gate_up: float32 [768, 8192], P('seq', 'dp')
- grad_heavy_down: float32 [4096, 768], P('seq', 'dp')
- grad_route_ffn: float32 [768], P('seq')
- rms_stats: float32 [5], replicated
The draws below stay inside these ranges and needn't reach their ends.
Inputs may be any that keep to these rules, and one draw needn't show every extreme that they name: `segments`: never falls along a row; -1 only fills the end of the last row, from a quarter to a half of it; in each group of 2 rows the first row is a single document. `query_route`: entries k * 16 to (k + 1) * 16 - 1 of a row are distinct positions from k * 128 to (k + 1) * 128 - 1. `kv_route`: entries k * 16 to (k + 1) * 16 - 1 of a row are distinct positions from k * 128 to (k + 1) * 128 - 1. `ffn_route`: entries k * 16 to (k + 1) * 16 - 1 of a row are distinct positions from k * 128 to (k + 1) * 128 - 1.
All inputs are finite; a program needn't handle non-finite values.
Results may differ from the reference program's by a relative error of at most 0.015.
Values may be sent and summed in bfloat16 or wider, within the bound.
No kernel may reach another device: no remote copies, remote signals or barrier semaphores. Data moves between devices by JAX's collectives and lax.ppermute only.
A program may use at most 256 MiB of HBM per device.

```python
import math
import jax
import jax.numpy as jnp
from jax import lax

D = 768
HL = 8
DL = 96
HH = 12
DH = 64
FL = 1024
FH = 4096
RADIUS = 64
CUTS = 3
ROWS_DP = 2
SEG_DEV = 128
ROWS = 4
LENGTH = 2048
RQ = 16
HW = 768
N_DP = 2
N_SEQ = 16


def route_blocks(key):
    block_keys = jax.random.split(key, ROWS * N_SEQ)
    chosen = jax.vmap(lambda sub_key: jax.random.permutation(sub_key, SEG_DEV)[:RQ])(block_keys)
    chosen = chosen.reshape(ROWS, N_SEQ, RQ).astype(jnp.int32)
    first = chosen[:, :, 0:1]
    block_place = jnp.arange(N_SEQ).astype(jnp.int32)[None, :, None]
    turn = jnp.where(block_place == 0, -first, jnp.where(block_place == N_SEQ - 1, SEG_DEV - 1 - first, 0))
    chosen = ((chosen + turn + SEG_DEV) % SEG_DEV).astype(jnp.int32)
    offsets = (jnp.arange(N_SEQ) * SEG_DEV).astype(jnp.int32)[None, :, None]
    return (chosen + offsets).reshape(ROWS, N_SEQ * RQ).astype(jnp.int32)


def draw_segments(key, part):
    key = jax.random.fold_in(key, 7)
    cut_key, pick_key, pad_key = jax.random.split(key, 3)
    row_len = SEG_DEV * N_SEQ
    cuts = jax.random.randint(cut_key, (ROWS, CUTS), 1, row_len)
    whole_rows = jax.random.randint(pick_key, (N_DP,), 0, ROWS_DP - 1) + jnp.arange(N_DP) * ROWS_DP
    is_whole = jnp.any(jnp.arange(ROWS)[:, None] == whole_rows[None, :], axis=1)
    cuts = jnp.where(is_whole[:, None], row_len, cuts)
    spots = jnp.arange(row_len)
    numbers = jnp.sum((cuts[:, None, :] <= spots[None, :, None]).astype(jnp.int32), axis=2)
    padding = jax.random.randint(pad_key, (), row_len // 4, row_len // 2 + 1)
    padded = (jnp.arange(ROWS)[:, None] == ROWS - 1) & (spots[None, :] >= row_len - padding)
    return jnp.where(padded, -1, numbers).astype(jnp.int32)


def draw_query_route(key, part):
    key = jax.random.fold_in(key, 11)
    return route_blocks(key)


def draw_kv_route(key, part):
    key = jax.random.fold_in(key, 13)
    return route_blocks(key)


def draw_ffn_route(key, part):
    key = jax.random.fold_in(key, 17)
    return route_blocks(key)


def shard_levels(rng, shape, cuts, smallest, high):
    def one(position, blocks):
        draws = jax.random.uniform(jax.random.fold_in(jax.random.fold_in(rng, 6), position), (blocks,), jnp.float32, smallest / len(cuts), high / len(cuts))
        return jnp.repeat(jnp.exp(draws), shape[position] // blocks).reshape((-1,) + (1,) * (len(shape) - position - 1))

    factor_of = one(*cuts[0])
    for cut in cuts[1:]:
        factor_of = factor_of * one(*cut)
    return factor_of


def scatter_about(key, shape, width, most, cuts=(), held_as=jnp.bfloat16):
    factor_of = shard_levels(key, shape, cuts, -0.22, 0.18) if cuts else 1.0
    entries = jax.random.normal(key, shape, jnp.float32) * width * factor_of
    return jnp.minimum(jnp.maximum(entries, -most), most).astype(held_as)


def setup_inputs(seed: int = 0) -> dict:
    key_of = jax.random.split(jax.random.key(seed), 20)
    tokens = scatter_about(key_of[0], (ROWS, LENGTH, D), 1.0, 6.0, ((0, 2), (1, 16)))
    segments = draw_segments(jax.random.fold_in(key_of[19], 71), 0)
    query_route = draw_query_route(jax.random.fold_in(key_of[19], 71), 0)
    kv_route = draw_kv_route(jax.random.fold_in(key_of[19], 71), 0)
    ffn_route = draw_ffn_route(jax.random.fold_in(key_of[19], 71), 0)
    grad_out = scatter_about(key_of[5], (ROWS, LENGTH, D), 1.0, 6.0, ((0, 2), (1, 16)))
    attn_gain = jnp.clip(1.0 + 0.1 * jax.random.normal(key_of[6], (D,), jnp.float32), 0.5, 1.5)
    light_qkv = scatter_about(key_of[7], (D, 3 * D), D ** -0.5, 0.21875)
    light_out = scatter_about(key_of[8], (D, D), (max(1, D // 128)) ** -0.5, 2.5)
    heavy_q = scatter_about(key_of[9], (D, HW), D ** -0.5, 0.21875)
    heavy_kv = scatter_about(key_of[10], (D, 2 * HW), D ** -0.5, 0.21875)
    heavy_out = scatter_about(key_of[11], (HW, D), (max(1, HW // 512)) ** -0.5, 6.0)
    route_query = scatter_about(key_of[12], (D,), D ** -0.5, 0.21875)
    ffn_gain = jnp.clip(1.0 + 0.1 * jax.random.normal(key_of[13], (D,), jnp.float32), 0.5, 1.5)
    light_gate_up = scatter_about(key_of[14], (D, 2 * FL), D ** -0.5, 0.21875)
    light_down = scatter_about(key_of[15], (FL, D), FL ** -0.5, 0.1875)
    heavy_gate_up = scatter_about(key_of[16], (D, 2 * FH), D ** -0.5, 0.21875)
    heavy_down = scatter_about(key_of[17], (FH, D), FH ** -0.5, 0.09375)
    route_ffn = scatter_about(key_of[18], (D,), D ** -0.5, 0.21875)
    return {"tokens": tokens, "segments": segments, "query_route": query_route, "kv_route": kv_route, "ffn_route": ffn_route, "grad_out": grad_out, "attn_gain": attn_gain, "light_qkv": light_qkv, "light_out": light_out, "heavy_q": heavy_q, "heavy_kv": heavy_kv, "heavy_out": heavy_out, "route_query": route_query, "ffn_gain": ffn_gain, "light_gate_up": light_gate_up, "light_down": light_down, "heavy_gate_up": heavy_gate_up, "heavy_down": heavy_down, "route_ffn": route_ffn}


@jax.custom_vjp
def low(v):
    return lax.optimization_barrier(v.astype(jnp.bfloat16)).astype(jnp.float32)

@jax.custom_vjp
def low_back(v):
    return v

def low_keep(v):
    return (low(v), None)

def low_pass(kept, grad):
    return (grad,)

def back_keep(v):
    return (v, None)

def back_low(kept, grad):
    return (low(grad),)
low.defvjp(low_keep, low_pass)
low_back.defvjp(back_keep, back_low)
PRECISE = lax.Precision.HIGHEST
EPSILON = 1e-06
NEG_FILL = -1e+30

def matmul(left, right):
    return jnp.dot(left, right, precision=PRECISE)

def rms_scaled(hidden, gain_vec):
    factor = lax.rsqrt(lax.optimization_barrier(jnp.mean(hidden * hidden, axis=-1, keepdims=True)) + EPSILON)
    return hidden * factor * gain_vec

def geglu_hidden(inputs, weight, inner_width):
    both_parts = matmul(inputs, weight)
    gate_part = low_back(both_parts[:, :inner_width])
    up_part = low_back(both_parts[:, inner_width:])
    return low(jax.nn.gelu(gate_part, approximate=True) * up_part)

def window_block(queries, key_pad, val_pad, query_seg, seg_pad, start_at):
    block_len = queries.shape[0]
    extent = block_len + 2 * RADIUS
    near_keys = lax.dynamic_slice_in_dim(key_pad, start_at, extent, 0)
    near_vals = lax.dynamic_slice_in_dim(val_pad, start_at, extent, 0)
    near_seg = lax.dynamic_slice_in_dim(seg_pad, start_at, extent, 0)
    raw_scores = jnp.einsum('qhd,khd->hqk', queries, near_keys, precision=PRECISE) / math.sqrt(DL)
    scores = low_back(raw_scores)
    offset = jnp.arange(block_len)[:, None] - jnp.arange(extent)[None, :] + RADIUS
    allowed = (jnp.abs(offset) <= RADIUS) & (query_seg[:, None] == near_seg[None, :])
    scores = jnp.where(allowed[None], scores, NEG_FILL)
    probabilities = low(jax.nn.softmax(scores, axis=-1))
    return jnp.einsum('hqk,khd->qhd', probabilities, near_vals, precision=PRECISE)

def routed_block(queries, query_seg, keys_all, vals_all, key_seg):
    raw_scores = jnp.einsum('qhd,khd->hqk', queries, keys_all, precision=PRECISE) / math.sqrt(DH)
    scores = low_back(raw_scores)
    allowed = query_seg[:, None] == key_seg[None, :]
    scores = jnp.where(allowed[None], scores, NEG_FILL)
    sink_col = jnp.zeros(scores.shape[:2] + (1,), scores.dtype)
    probabilities = jax.nn.softmax(jnp.concatenate([scores, sink_col], axis=-1), axis=-1)[..., :-1]
    return jnp.einsum('hqk,khd->qhd', low(probabilities), vals_all, precision=PRECISE)

def row_forward(weights, hidden, seg_row, query_pos, key_pos, ffn_pos):
    attn_gain, light_qkv, light_out, heavy_q, heavy_kv, heavy_out, route_query, ffn_gain, light_gate_up, light_down, heavy_gate_up, heavy_down, route_ffn = weights
    length = hidden.shape[0]
    normed = rms_scaled(hidden, attn_gain)
    normed_low = low(normed)
    qkv_all = low(low_back(matmul(normed_low, light_qkv)))
    queries = qkv_all[:, :D].reshape(length, HL, DL)
    key_pad = jnp.pad(qkv_all[:, D:2 * D].reshape(length, HL, DL), ((RADIUS, RADIUS), (0, 0), (0, 0)))
    val_pad = jnp.pad(qkv_all[:, 2 * D:].reshape(length, HL, DL), ((RADIUS, RADIUS), (0, 0), (0, 0)))
    seg_pad = jnp.pad(seg_row, (RADIUS, RADIUS), constant_values=-2)
    block_len = math.gcd(length, 512)
    starts = (jnp.arange(length // block_len) * block_len).astype(jnp.int32)

    def window_part(start_at):
        part_queries = lax.dynamic_slice_in_dim(queries, start_at, block_len, 0)
        part_seg = lax.dynamic_slice_in_dim(seg_row, start_at, block_len, 0)
        return window_block(part_queries, key_pad, val_pad, part_seg, seg_pad, start_at)
    light_mix = lax.map(jax.checkpoint(window_part), starts).reshape(length, D)
    light_mix = low(low_back(light_mix))
    light_attn = low_back(matmul(light_mix, light_out))
    routed_count = query_pos.shape[0]
    heavy_query = low(low_back(matmul(normed_low[query_pos], heavy_q)))
    heavy_keyval = low(low_back(matmul(normed_low[key_pos], heavy_kv)))
    heavy_keys = heavy_keyval[:, :HH * DH].reshape(routed_count, HH, DH)
    heavy_vals = heavy_keyval[:, HH * DH:].reshape(routed_count, HH, DH)
    query_seg = seg_row[query_pos]
    key_seg = seg_row[key_pos]
    routed_len = math.gcd(routed_count, 512)
    query_blocks = heavy_query.reshape(routed_count // routed_len, routed_len, HH, DH)
    seg_blocks = query_seg.reshape(routed_count // routed_len, routed_len)

    def routed_part(pieces):
        return routed_block(pieces[0], pieces[1], heavy_keys, heavy_vals, key_seg)
    heavy_mix = lax.map(jax.checkpoint(routed_part), (query_blocks, seg_blocks)).reshape(routed_count, HH * DH)
    heavy_mix = low(low_back(heavy_mix))
    query_gate = jax.nn.sigmoid(matmul(normed[query_pos], route_query))
    heavy_rows = query_gate[:, None] * low_back(matmul(heavy_mix, heavy_out))
    heavy_attn = jnp.zeros_like(hidden).at[query_pos].add(heavy_rows)
    middle = hidden + light_attn + heavy_attn
    normed_two = rms_scaled(middle, ffn_gain)
    low_two = low(normed_two)
    light_ff = low_back(matmul(geglu_hidden(low_two, light_gate_up, FL), light_down))
    ffn_gate = jax.nn.sigmoid(matmul(normed_two[ffn_pos], route_ffn))
    heavy_ffn_rows = ffn_gate[:, None] * low_back(matmul(geglu_hidden(low_two[ffn_pos], heavy_gate_up, FH), heavy_down))
    heavy_ff = jnp.zeros_like(hidden).at[ffn_pos].add(heavy_ffn_rows)
    return (middle + light_ff + heavy_ff, (light_attn, heavy_attn, light_ff, heavy_ff))

def reference(tokens, segments, query_route, kv_route, ffn_route, grad_out, attn_gain, light_qkv, light_out, heavy_q, heavy_kv, heavy_out, route_query, ffn_gain, light_gate_up, light_down, heavy_gate_up, heavy_down, route_ffn):
    weights = tuple((param.astype(jnp.float32) for param in (attn_gain, light_qkv, light_out, heavy_q, heavy_kv, heavy_out, route_query, ffn_gain, light_gate_up, light_down, heavy_gate_up, heavy_down, route_ffn)))

    def per_row(carried, inputs):
        token_row, seg_row, query_row, key_row, ffn_row, cotangent_row = inputs
        start_hidden = token_row.astype(jnp.float32)
        output_row, pull_back, branches = jax.vjp(lambda params, hidden: row_forward(params, hidden, seg_row, query_row, key_row, ffn_row), weights, start_hidden, has_aux=True)
        weight_grads, input_grad = pull_back(cotangent_row.astype(jnp.float32))
        valid_rows = (seg_row >= 0).astype(jnp.float32)[:, None]
        squares = jnp.stack([jnp.sum(valid_rows * branch * branch) for branch in (start_hidden,) + tuple(branches)])
        grads_sum, squares_sum, valid_sum = carried
        carried = (jax.tree.map(jnp.add, grads_sum, weight_grads), squares_sum + squares, valid_sum + jnp.sum(valid_rows))
        return (carried, (output_row.astype(jnp.bfloat16), input_grad.astype(jnp.bfloat16)))
    initial = (tuple((jnp.zeros_like(param) for param in weights)), jnp.zeros((5,), jnp.float32), jnp.zeros((), jnp.float32))
    (grads_sum, squares_sum, valid_sum), (outputs, grad_tokens) = lax.scan(per_row, initial, (tokens, segments, query_route, kv_route, ffn_route, grad_out))
    rms_stats = jnp.sqrt(squares_sum / (valid_sum * D))
    return (outputs, grad_tokens, grads_sum[0], grads_sum[1], grads_sum[2], grads_sum[3], grads_sum[4], grads_sum[5], grads_sum[6], grads_sum[7], grads_sum[8], grads_sum[9], grads_sum[10], grads_sum[11], grads_sum[12], rms_stats)
```

```python
import math

import jax
import jax.numpy as jnp
from jax import lax
from jax.sharding import PartitionSpec as P

DL = 96
DH = 64
RADIUS = 64
LANES = 128


PRECISE = lax.Precision.HIGHEST
EPSILON = 1e-06
NEG_FILL = -1e30
F32 = jnp.float32
BF16 = jnp.bfloat16


def swap(value, axis, bit):
    return lax.ppermute(value, axis, [(i, i ^ bit) for i in range(lax.axis_size(axis))])


def shifted(block, axis, distance):
    devices = range(lax.axis_size(axis))
    route = [(i - distance, i) for i in devices if i - distance in devices]
    return lax.ppermute(block, axis, route)


def gather_blocks(block):
    held = block[None]
    bit = lax.axis_size("seq") // 2
    while bit:
        held = jnp.concatenate([held, swap(held, "seq", bit)], axis=0)
        bit //= 2
    return held


def add_halves(value, dim, axis, bit, out_type=BF16):
    half = value.shape[dim] // 2
    keep = lax.slice_in_dim(value, 0, half, axis=dim)
    sent = lax.slice_in_dim(value, half, 2 * half, axis=dim)
    return (keep.astype(F32) + swap(sent, axis, bit).astype(F32)).astype(out_type)


def scatter_sum(slots):
    devices = lax.axis_size("seq")
    rows = slots.shape[2]
    slots = add_halves(slots, 0, "seq", 1)
    left, right = slots[:, :, : rows // 2], slots[:, :, rows // 2 :]
    left = add_halves(left, 0, "seq", 2)
    right = add_halves(right, 1, "dp", 1)
    left = add_halves(left, 1, "dp", 1)
    right = add_halves(right, 0, "seq", 2)
    both = jnp.concatenate([left, right], axis=2)
    bit = 4
    while bit < devices:
        both = add_halves(both, 0, "seq", bit, BF16 if 2 * bit < devices else F32)
        bit *= 2
    return both[0, 0]


def slot_places(me, devices):
    bits = devices.bit_length() - 1
    places = [int(format(p, f"0{bits}b")[::-1], 2) for p in range(devices)]
    return jnp.array(places, jnp.int32) ^ me


def slot_columns(value, me, devices):
    width = value.shape[-1]
    block = width // devices
    order = (slot_places(me, devices)[:, None] * block + jnp.arange(block)[None, :]).reshape(-1)
    onehot = (jnp.arange(width)[:, None] == order[None, :]).astype(BF16)
    return jnp.dot(value, onehot, preferred_element_type=F32).astype(BF16)


def own_half_first(value, place):
    half = value.shape[-1] // 2
    first, second = value[..., :half], value[..., half:]
    return (jnp.where(place == 0, first, second), jnp.where(place == 0, second, first))


def slot_block(grad_halves, devices):
    stacked = jnp.stack(grad_halves)
    _, total, cols = stacked.shape
    parts = stacked.reshape(2, devices, total // devices, cols // LANES, LANES)
    return parts.transpose(1, 0, 3, 2, 4).reshape(devices, 2, -1, LANES).astype(BF16)


def unslot(rows, cols):
    return rows.reshape(cols // LANES, -1, LANES).transpose(1, 0, 2).reshape(-1, cols)


def slot_vectors(vectors, me, devices):
    block = vectors[0].shape[0] // devices
    table = jnp.stack(vectors, axis=-1).reshape(devices, block, len(vectors))
    table = jnp.take(table, slot_places(me, devices), axis=0)
    table = jnp.pad(table, ((0, 0), (0, 0), (0, LANES - len(vectors))))
    return jnp.broadcast_to(table[:, None], (devices, 2, block, LANES)).astype(BF16)


def split_parts(value):
    high = lax.reduce_precision(value, 8, 7)
    middle = lax.reduce_precision(value - high, 8, 7)
    return (high, middle, value - high - middle)


def rms_factor(hidden):
    return lax.rsqrt(jnp.mean(hidden * hidden, axis=-1, keepdims=True) + EPSILON)


def norm_back(hidden, factor, gain_vec, upstream):
    weighted = upstream * gain_vec
    inner_mean = jnp.mean(weighted * hidden, axis=-1, keepdims=True)
    return factor * weighted - hidden * (factor * factor * factor) * inner_mean


def pick_rows(source, positions):
    return jnp.take_along_axis(source, positions[..., None], axis=1)


def place_rows(values, positions, extent):
    onehot = (positions[..., None] == jnp.arange(extent)[None, None, :]).astype(F32)
    return jnp.einsum("rqs,rqd->rsd", onehot, values, precision=PRECISE)


def matmul(left, right):
    return jnp.einsum("...d,de->...e", left, right, preferred_element_type=F32)


def matmul_t(left, right):
    return jnp.einsum("...e,de->...d", left, right, preferred_element_type=F32)


def outer(left, right):
    return jnp.einsum("rsd,rse->de", left, right, preferred_element_type=F32)


def glu_value(gate_part, up_part):
    return jax.nn.gelu(gate_part, approximate=True) * up_part


def geglu(inputs, gate_up, down, upstream_low):
    width = down.shape[0]
    both = matmul(inputs, gate_up)
    gate_part, up_part = both[..., :width], both[..., width:]
    hidden, pull_back = jax.vjp(glu_value, gate_part, up_part)
    gate_grad, up_grad = pull_back(matmul_t(upstream_low, down))
    return (hidden.astype(BF16), gate_grad.astype(BF16), up_grad.astype(BF16))


def routed_probs(query_heads, key_heads, query_seg, key_seg):
    scores = jnp.einsum("rqd,rkd->rqk", query_heads, key_heads, preferred_element_type=F32)
    scores = scores / math.sqrt(DH)
    allowed = query_seg[:, :, None] == key_seg[:, None, :]
    scores = jnp.where(allowed, scores, NEG_FILL)
    peak = jnp.maximum(jnp.max(scores, axis=-1, keepdims=True), 0.0)
    numer = jnp.exp(scores - peak)
    return numer / (jnp.exp(-peak) + jnp.sum(numer, axis=-1, keepdims=True))


def heavy_forward(query, keys, vals, query_seg, key_seg):
    def head(parts):
        query_h, key_h, val_h = parts
        probs = routed_probs(query_h, key_h, query_seg, key_seg).astype(BF16)
        return jnp.einsum("rqk,rkd->rqd", probs, val_h, preferred_element_type=F32).astype(BF16)

    return join_heads(jax.vmap(head)((split_heads(query), split_heads(keys), split_heads(vals))))


def heavy_both(query, keys, vals, query_seg, key_seg, mix_grad):
    def head(parts, query_seg=query_seg, key_seg=key_seg):
        query_h, key_h, val_h, grad_h = parts
        probs = routed_probs(query_h, key_h, query_seg, key_seg)
        probs_low = probs.astype(BF16)
        mix = jnp.einsum("rqk,rkd->rqd", probs_low, val_h, preferred_element_type=F32)
        prob_grad = jnp.einsum("rqd,rkd->rqk", grad_h, val_h, preferred_element_type=F32)
        delta = jnp.sum(probs * prob_grad, axis=-1, keepdims=True)
        score_grad = (probs * (prob_grad - delta)).astype(BF16)
        dquery = jnp.einsum("rqk,rkd->rqd", score_grad, key_h, preferred_element_type=F32)
        dkey = jnp.einsum("rqk,rqd->rkd", score_grad, query_h, preferred_element_type=F32)
        dval = jnp.einsum("rqk,rqd->rkd", probs_low, grad_h, preferred_element_type=F32)
        scale = 1.0 / math.sqrt(DH)
        return (mix.astype(BF16), (dquery * scale).astype(BF16), (dkey * scale).astype(BF16), dval.astype(BF16))

    heads = tuple(split_heads(v) for v in (query, keys, vals, mix_grad))
    if query.shape[1] <= 512:
        return tuple(join_heads(v) for v in jax.vmap(head)(heads))
    count, rows = heads[0].shape[:2]
    place = jnp.tile(jnp.arange(rows), count)
    parts = tuple(v.reshape(count * rows, 1, *v.shape[2:]) for v in heads)
    done = lax.map(lambda p: head(p[0], query_seg[p[1]][None], key_seg[p[1]][None]), (parts, place))
    return tuple(join_heads(v.reshape(count, rows, *v.shape[2:])) for v in done)


def split_heads(value):
    rows, tokens, width = value.shape
    return value.reshape(rows, tokens, width // DH, DH).transpose(2, 0, 1, 3)


def join_heads(value):
    heads, rows, tokens, width = value.shape
    return value.transpose(1, 2, 0, 3).reshape(rows, tokens, heads * width)


def tokens_of(blocks):
    devices, rows, count, width = blocks.shape
    return blocks.transpose(1, 0, 2, 3).reshape(rows, devices * count, width)


def with_segment(rows, segs):
    marks = jnp.broadcast_to((segs + 2).astype(BF16)[..., None], segs.shape + (LANES,))
    return jnp.concatenate([rows, marks], axis=-1)


def local(
    tokens,
    segments,
    query_route,
    kv_route,
    ffn_route,
    grad_out,
    attn_gain,
    light_qkv,
    light_out,
    heavy_q,
    heavy_kv,
    heavy_out,
    route_query,
    ffn_gain,
    light_gate_up,
    light_down,
    heavy_gate_up,
    heavy_down,
    route_ffn,
):
    row_count, seg_span, width = tokens.shape
    light_heads = width // DL
    ffn_heavy = heavy_down.shape[0]
    devices = lax.axis_size("seq")
    me = lax.axis_index("seq")
    half_place = lax.axis_index("dp")
    anchor = me * seg_span
    routed_own = query_route.shape[1] // devices
    own_query = lax.dynamic_slice_in_dim(query_route, me * routed_own, routed_own, 1) - anchor
    own_key = lax.dynamic_slice_in_dim(kv_route, me * routed_own, routed_own, 1) - anchor
    own_ffn = ffn_route - anchor

    marked = with_segment(tokens, segments)
    before = shifted(marked[:, seg_span - RADIUS :], "seq", 1)
    after = shifted(marked[:, :RADIUS], "seq", -1)
    hidden = tokens.astype(F32)
    factor_one = rms_factor(hidden)
    normed = hidden * factor_one * attn_gain
    normed_low = normed.astype(BF16)
    key_rows = pick_rows(normed_low, own_key)
    key_payload = with_segment(key_rows, jnp.take_along_axis(segments, own_key, axis=1))
    key_blocks = tokens_of(gather_blocks(key_payload))
    key_all, key_seg = key_blocks[..., :width], key_blocks[..., width]

    extended = jnp.concatenate([before, marked, after], axis=1)
    seg_ext = extended[..., width]
    hidden_ext = extended[..., :width].astype(F32)
    factor_ext = rms_factor(hidden_ext)
    normed_ext_low = (hidden_ext * factor_ext * attn_gain).astype(BF16)
    extent = seg_span + 2 * RADIUS
    query_low = matmul(normed_low, light_qkv[:, :width]).astype(BF16)
    query_low = query_low.reshape(row_count, seg_span, light_heads, DL)
    kv_ext = matmul(normed_ext_low, light_qkv[:, width:]).astype(BF16)
    key_ext = kv_ext[..., :width].reshape(row_count, extent, light_heads, DL)
    val_ext = kv_ext[..., width:].reshape(row_count, extent, light_heads, DL)
    offset = jnp.arange(seg_span)[:, None] - jnp.arange(extent)[None, :] + RADIUS
    seg_own = seg_ext[:, RADIUS : RADIUS + seg_span]
    allowed = (jnp.abs(offset) <= RADIUS)[None] & (seg_own[:, :, None] == seg_ext[:, None, :])
    light_scale = 1.0 / math.sqrt(DL)
    scores = jnp.einsum("rqhd,rkhd->rhqk", query_low, key_ext, preferred_element_type=F32)
    scores = jnp.where(allowed[:, None], scores * light_scale, NEG_FILL)
    numerators = jnp.exp(scores - jnp.max(scores, axis=-1, keepdims=True))
    probs_light = numerators / jnp.sum(numerators, axis=-1, keepdims=True)
    probs_low = probs_light.astype(BF16)
    light_mix = jnp.einsum("rhqk,rkhd->rqhd", probs_low, val_ext, preferred_element_type=F32)
    light_mix = light_mix.reshape(row_count, seg_span, width).astype(BF16)
    light_attn = matmul(light_mix, light_out)

    query_rows = pick_rows(normed_low, own_query)
    query_seg_own = (jnp.take_along_axis(segments, own_query, axis=1) + 2).astype(BF16)
    heavy_query = matmul(query_rows, heavy_q).astype(BF16)
    keyval_all = matmul(key_all, heavy_kv).astype(BF16)
    heavy_width = heavy_q.shape[1]
    keys_all, vals_all = keyval_all[..., :heavy_width], keyval_all[..., heavy_width:]
    heavy_mix = heavy_forward(heavy_query, keys_all, vals_all, query_seg_own, key_seg)
    heavy_proj = matmul(heavy_mix, heavy_out)
    query_normed = pick_rows(normed, own_query)
    route_query_full = route_query.astype(F32)
    query_gate = jax.nn.sigmoid(jnp.sum(query_normed * route_query_full, axis=-1))
    heavy_attn = place_rows(query_gate[..., None] * heavy_proj, own_query, seg_span)

    middle = hidden + light_attn + heavy_attn
    factor_two = rms_factor(middle)
    normed_two = middle * factor_two * ffn_gain
    low_two = normed_two.astype(BF16)
    upstream = grad_out.astype(F32)
    ffn_normed = pick_rows(normed_two, own_ffn)
    ffn_rows = ffn_normed.astype(BF16)
    route_ffn_full = route_ffn.astype(F32)
    ffn_gate = jax.nn.sigmoid(jnp.sum(ffn_normed * route_ffn_full, axis=-1))
    ffn_upstream = pick_rows(upstream, own_ffn)
    ffn_low = (ffn_upstream * ffn_gate[..., None]).astype(BF16)
    routed_payload = with_segment(
        jnp.concatenate([ffn_rows, ffn_low, query_rows], axis=-1),
        jnp.take_along_axis(segments, own_query, axis=1),
    )
    routed_blocks = tokens_of(gather_blocks(routed_payload))
    ffn_all = routed_blocks[..., :width]
    ffn_low_all = routed_blocks[..., width : 2 * width]
    query_all = routed_blocks[..., 2 * width : 3 * width]
    query_seg = routed_blocks[..., 3 * width]

    hidden_light, gate_grad, up_grad = geglu(low_two, light_gate_up, light_down, grad_out)
    light_ff = matmul(hidden_light, light_down)
    light_both = jnp.concatenate([gate_grad, up_grad], axis=-1)
    normed_two_grad = matmul_t(light_both, light_gate_up)
    hidden_heavy, gate_grad_h, up_grad_h = geglu(ffn_rows, heavy_gate_up, heavy_down, ffn_low)
    heavy_ffn_proj = matmul(hidden_heavy, heavy_down)
    heavy_ff = place_rows(ffn_gate[..., None] * heavy_ffn_proj, own_ffn, seg_span)
    outputs = (middle + light_ff + heavy_ff).astype(BF16)
    ffn_gate_grad = jnp.sum(ffn_upstream * heavy_ffn_proj, axis=-1)
    ffn_logit_grad = ffn_gate_grad * ffn_gate * (1.0 - ffn_gate)
    route_ffn_grad = jnp.sum(ffn_logit_grad[..., None] * ffn_normed, axis=(0, 1))
    ffn_rows_grad = matmul_t(jnp.concatenate([gate_grad_h, up_grad_h], axis=-1), heavy_gate_up)
    ffn_rows_grad = ffn_rows_grad + ffn_logit_grad[..., None] * route_ffn_full
    normed_two_grad = normed_two_grad + place_rows(ffn_rows_grad, own_ffn, seg_span)
    ffn_gain_grad = jnp.sum(normed_two_grad * middle * factor_two, axis=(0, 1))
    middle_grad = upstream + norm_back(middle, factor_two, ffn_gain, normed_two_grad)
    middle_low = middle_grad.astype(BF16)

    valid_rows = (segments >= 0).astype(F32)[..., None]
    sums = jnp.stack(
        [
            jnp.sum(valid_rows * branch * branch)
            for branch in (hidden, light_attn, heavy_attn, light_ff, heavy_ff)
        ]
        + [jnp.sum(valid_rows)]
    )
    heavy_upstream = pick_rows(middle_grad, own_query)
    query_gate_grad = jnp.sum(heavy_upstream * heavy_proj, axis=-1)
    proj_low = (heavy_upstream * query_gate[..., None]).astype(BF16)
    sum_lanes = jnp.pad(jnp.concatenate(split_parts(sums)), (0, LANES - 18)).astype(BF16)
    sum_lanes = jnp.broadcast_to(sum_lanes, proj_low.shape[:2] + (LANES,))
    proj_blocks = gather_blocks(jnp.concatenate([proj_low, sum_lanes], axis=-1))
    sums_all = jnp.sum(proj_blocks[:, 0, 0, width : width + 18].astype(F32), axis=0)
    sums_all = jnp.sum(sums_all.reshape(3, 6), axis=0)
    sums_all = sums_all + swap(sums_all, "dp", 1)
    rms_stats = jnp.sqrt(sums_all[:5] / (sums_all[5] * width))
    proj_all = tokens_of(proj_blocks)[..., :width]

    flat = lambda v: v.reshape(-1, v.shape[-1])
    gate_up_grad = [
        jnp.dot(slot_columns(flat(low_two), me, devices).T, flat(part), preferred_element_type=F32)
        for part in own_half_first(light_both, half_place)
    ]
    hidden_slots = slot_columns(flat(hidden_light), me, devices).T
    down_grad = [
        jnp.dot(hidden_slots, flat(part), preferred_element_type=F32)
        for part in own_half_first(grad_out, half_place)
    ]
    mix_slots = slot_columns(flat(light_mix), me, devices).T
    out_grad = [
        jnp.dot(mix_slots, flat(part), preferred_element_type=F32)
        for part in own_half_first(middle_low, half_place)
    ]
    first_sum = scatter_sum(
        jnp.concatenate(
            [
                slot_block(gate_up_grad, devices),
                slot_block(down_grad, devices),
                slot_block(out_grad, devices),
                slot_vectors((ffn_gain_grad, route_ffn_grad), me, devices),
            ],
            axis=2,
        )
    )
    block = width // devices
    block_ff = light_down.shape[0] // devices
    cuts = [0]
    for rows in (
        block * light_gate_up.shape[1] // 2 // LANES,
        block_ff * width // 2 // LANES,
        block * width // 2 // LANES,
        block,
    ):
        cuts.append(cuts[-1] + rows)
    light_gate_up_grad = unslot(first_sum[cuts[0] : cuts[1]], light_gate_up.shape[1] // 2)
    light_down_grad = unslot(first_sum[cuts[1] : cuts[2]], width // 2)
    light_out_grad = unslot(first_sum[cuts[2] : cuts[3]], width // 2)
    ffn_gain_grad = first_sum[cuts[3] : cuts[4], 0]
    route_ffn_grad = first_sum[cuts[3] : cuts[4], 1]

    group = min(4, devices)
    low_place, high_place = me % group, me // group
    groups = devices // group
    unit = ffn_heavy // devices
    gate_up_parts = heavy_gate_up.reshape(width, 2, groups, group, unit)
    gate_up_mine = lax.dynamic_index_in_dim(gate_up_parts, low_place, 3, False)
    down_mine = lax.dynamic_index_in_dim(
        heavy_down.reshape(groups, group, unit, width), low_place, 1, False
    )
    x_all = flat(ffn_all)
    up_all = flat(ffn_low_all)
    hidden_mine, gate_mine, up_mine = geglu(
        x_all,
        gate_up_mine.reshape(width, -1),
        down_mine.reshape(-1, width),
        up_all,
    )
    hidden_block = lax.dynamic_slice_in_dim(hidden_mine, high_place * unit, unit, 1)
    heavy_down_half = [
        jnp.dot(hidden_block.T, part, preferred_element_type=F32)
        for part in own_half_first(up_all, half_place)
    ]
    heavy_down_grad = heavy_down_half[0] + swap(heavy_down_half[1].astype(BF16), "dp", 1).astype(F32)
    x_group = lax.dynamic_slice_in_dim(x_all, high_place * group * block, group * block, 1)
    x_group = x_group.reshape(-1, group, block)
    x_group = jnp.take(x_group, jnp.arange(group) ^ low_place, axis=1).reshape(-1, group * block)
    gate_half, up_half = (
        jnp.dot(x_group.T, part, preferred_element_type=F32) for part in (gate_mine, up_mine)
    )
    kept = jnp.where(half_place == 0, gate_half, up_half)
    sent = jnp.where(half_place == 0, up_half, gate_half)
    kept = (kept + swap(sent.astype(BF16), "dp", 1).astype(F32)).reshape(group, block, groups, unit)
    pieces = [kept[0]]
    for place in range(1, group):
        pieces.append(swap(kept[place].astype(BF16), "seq", place).astype(F32))
    pieces = jnp.take(jnp.stack(pieces, axis=2), jnp.arange(group) ^ low_place, axis=2)
    heavy_gate_up_grad = pieces.reshape(block, ffn_heavy)

    mix_grad = matmul_t(middle_low, light_out).astype(BF16)
    mix_grad = mix_grad.reshape(row_count, seg_span, light_heads, DL)
    val_grad = jnp.einsum("rhqk,rqhd->rkhd", probs_low, mix_grad, preferred_element_type=F32)
    prob_grad = jnp.einsum("rqhd,rkhd->rhqk", mix_grad, val_ext, preferred_element_type=F32)
    delta = jnp.sum(probs_light * prob_grad, axis=-1, keepdims=True)
    score_grad = (probs_light * (prob_grad - delta)).astype(BF16)
    query_grad = jnp.einsum("rhqk,rkhd->rqhd", score_grad, key_ext, preferred_element_type=F32)
    key_grad = jnp.einsum("rhqk,rqhd->rkhd", score_grad, query_low, preferred_element_type=F32)
    query_grad = (query_grad * light_scale).reshape(row_count, seg_span, width).astype(BF16)
    kv_grad = jnp.concatenate(
        [
            (key_grad * light_scale).reshape(row_count, extent, width),
            val_grad.reshape(row_count, extent, width),
        ],
        axis=-1,
    ).astype(BF16)
    normed_grad_ext = matmul_t(kv_grad, light_qkv[:, width:])
    normed_grad = matmul_t(query_grad, light_qkv[:, :width])
    normed_grad = normed_grad + normed_grad_ext[:, RADIUS : RADIUS + seg_span]
    from_right = shifted(normed_grad_ext[:, :RADIUS].astype(BF16), "seq", -1)
    from_left = shifted(normed_grad_ext[:, seg_span + RADIUS :].astype(BF16), "seq", 1)
    normed_grad = normed_grad.at[:, :RADIUS].add(from_left.astype(F32))
    normed_grad = normed_grad.at[:, seg_span - RADIUS :].add(from_right.astype(F32))

    hq_all = matmul(query_all, heavy_q).astype(BF16)
    do2_all = matmul_t(proj_all, heavy_out).astype(BF16)
    mix_all, dhq_all, dhk_all, dhv_all = heavy_both(
        hq_all, keys_all, vals_all, query_seg, key_seg, do2_all
    )
    dhkv_all = jnp.concatenate([dhk_all, dhv_all], axis=-1)
    mine = lambda v: lax.dynamic_slice_in_dim(flat(v), me * block, block, 1).T
    heavy_grads = [
        own_half_first(jnp.dot(mine(left), flat(right), preferred_element_type=F32), half_place)
        for left, right in ((query_all, dhq_all), (key_all, dhkv_all), (mix_all, proj_all))
    ]
    heavy_kept = jnp.concatenate([pair[0] for pair in heavy_grads], axis=-1)
    heavy_sent = jnp.concatenate([pair[1] for pair in heavy_grads], axis=-1)
    heavy_sum = heavy_kept + swap(heavy_sent.astype(BF16), "dp", 1).astype(F32)
    heavy_half = heavy_width // 2
    heavy_q_grad = heavy_sum[:, :heavy_half]
    heavy_kv_grad = heavy_sum[:, heavy_half : 3 * heavy_half]
    heavy_out_grad = heavy_sum[:, 3 * heavy_half :]
    query_logit_grad = query_gate_grad * query_gate * (1.0 - query_gate)
    route_query_grad = jnp.sum(query_logit_grad[..., None] * query_normed, axis=(0, 1))
    query_rows_grad = (
        matmul_t(dhq_all[:, :routed_own], heavy_q) + query_logit_grad[..., None] * route_query_full
    )
    key_rows_grad = matmul_t(dhkv_all[:, :routed_own], heavy_kv)
    normed_grad = (
        normed_grad
        + place_rows(query_rows_grad, own_query, seg_span)
        + place_rows(key_rows_grad, own_key, seg_span)
    )
    attn_gain_grad = jnp.sum(normed_grad * hidden * factor_one, axis=(0, 1))
    hidden_norm_grad = norm_back(hidden, factor_one, attn_gain, normed_grad)
    grad_tokens = (middle_grad + hidden_norm_grad).astype(BF16)

    own_slots = slot_columns(flat(normed_low), me, devices).T
    ext_slots = slot_columns(flat(normed_ext_low), me, devices).T
    qkv_grad = jnp.concatenate(
        [
            jnp.dot(own_slots, flat(query_grad), preferred_element_type=F32),
            jnp.dot(ext_slots, flat(kv_grad), preferred_element_type=F32),
        ],
        axis=-1,
    )
    second_sum = scatter_sum(
        jnp.concatenate(
            [
                slot_block(own_half_first(qkv_grad, half_place), devices),
                slot_vectors((attn_gain_grad, route_query_grad), me, devices),
            ],
            axis=2,
        )
    )
    qkv_cols = light_qkv.shape[1] // 2
    qkv_rows = block * qkv_cols // LANES
    light_qkv_grad = unslot(second_sum[:qkv_rows], qkv_cols)
    attn_gain_grad = second_sum[qkv_rows:, 0]
    route_query_grad = second_sum[qkv_rows:, 1]
    return (
        outputs,
        grad_tokens,
        attn_gain_grad,
        light_qkv_grad,
        light_out_grad,
        heavy_q_grad,
        heavy_kv_grad,
        heavy_out_grad,
        route_query_grad,
        ffn_gain_grad,
        light_gate_up_grad,
        light_down_grad,
        heavy_gate_up_grad,
        heavy_down_grad,
        route_ffn_grad,
        rms_stats,
    )


def solution(mesh):
    placed = (
        P("dp", "seq", None),
        P("dp", "seq"),
        P("dp", None),
        P("dp", None),
        P("dp", "seq"),
        P("dp", "seq", None),
    ) + (P(),) * 13
    matrix = P("seq", "dp")
    vector = P("seq")
    return jax.shard_map(
        local,
        mesh=mesh,
        in_specs=placed,
        out_specs=(
            P("dp", "seq", None),
            P("dp", "seq", None),
            vector,
            matrix,
            matrix,
            matrix,
            matrix,
            matrix,
            vector,
            vector,
            matrix,
            matrix,
            matrix,
            matrix,
            vector,
            P(),
        ),
        check_vma=False,
    )
```

```python
import functools
import math

import jax
import jax.numpy as jnp
from jax import lax
from jax.experimental import pallas as pl
from jax.experimental.pallas import tpu as pltpu
from jax.sharding import PartitionSpec as P

DL = 96
DH = 64
RADIUS = 64
LANES = 128


PRECISE = lax.Precision.HIGHEST
EPSILON = 1e-06
NEG_FILL = -1e30
F32 = jnp.float32
BF16 = jnp.bfloat16


def swap(value, axis, bit):
    return lax.ppermute(value, axis, [(i, i ^ bit) for i in range(lax.axis_size(axis))])


def shifted(block, axis, distance):
    devices = range(lax.axis_size(axis))
    route = [(i - distance, i) for i in devices if i - distance in devices]
    return lax.ppermute(block, axis, route)


def gather_blocks(block):
    held = block[None]
    bit = lax.axis_size("seq") // 2
    while bit:
        held = jnp.concatenate([held, swap(held, "seq", bit)], axis=0)
        bit //= 2
    return held


def add_halves(value, dim, axis, bit, out_type=BF16):
    half = value.shape[dim] // 2
    keep = lax.slice_in_dim(value, 0, half, axis=dim)
    sent = lax.slice_in_dim(value, half, 2 * half, axis=dim)
    return (keep.astype(F32) + swap(sent, axis, bit).astype(F32)).astype(out_type)


def scatter_sum(slots):
    devices = lax.axis_size("seq")
    rows = slots.shape[2]
    slots = add_halves(slots, 0, "seq", 1)
    left, right = slots[:, :, : rows // 2], slots[:, :, rows // 2 :]
    left = add_halves(left, 0, "seq", 2)
    right = add_halves(right, 1, "dp", 1)
    left = add_halves(left, 1, "dp", 1)
    right = add_halves(right, 0, "seq", 2)
    both = jnp.concatenate([left, right], axis=2)
    bit = 4
    while bit < devices:
        both = add_halves(both, 0, "seq", bit, BF16 if 2 * bit < devices else F32)
        bit *= 2
    return both[0, 0]


def slot_places(me, devices):
    bits = devices.bit_length() - 1
    places = [int(format(p, f"0{bits}b")[::-1], 2) for p in range(devices)]
    return jnp.array(places, jnp.int32) ^ me


def slot_columns(value, me, devices):
    width = value.shape[-1]
    block = width // devices
    order = (slot_places(me, devices)[:, None] * block + jnp.arange(block)[None, :]).reshape(-1)
    onehot = (jnp.arange(width)[:, None] == order[None, :]).astype(BF16)
    return jnp.dot(value, onehot, preferred_element_type=F32).astype(BF16)


def own_half_first(value, place):
    half = value.shape[-1] // 2
    first, second = value[..., :half], value[..., half:]
    return (jnp.where(place == 0, first, second), jnp.where(place == 0, second, first))


def slot_block(grad_halves, devices):
    stacked = jnp.stack(grad_halves)
    _, total, cols = stacked.shape
    parts = stacked.reshape(2, devices, total // devices, cols // LANES, LANES)
    return parts.transpose(1, 0, 3, 2, 4).reshape(devices, 2, -1, LANES).astype(BF16)


def unslot(rows, cols):
    return rows.reshape(cols // LANES, -1, LANES).transpose(1, 0, 2).reshape(-1, cols)


def slot_vectors(vectors, me, devices):
    block = vectors[0].shape[0] // devices
    table = jnp.stack(vectors, axis=-1).reshape(devices, block, len(vectors))
    table = jnp.take(table, slot_places(me, devices), axis=0)
    table = jnp.pad(table, ((0, 0), (0, 0), (0, LANES - len(vectors))))
    return jnp.broadcast_to(table[:, None], (devices, 2, block, LANES)).astype(BF16)


def split_parts(value):
    high = lax.reduce_precision(value, 8, 7)
    middle = lax.reduce_precision(value - high, 8, 7)
    return (high, middle, value - high - middle)


def rms_factor(hidden):
    return lax.rsqrt(jnp.mean(hidden * hidden, axis=-1, keepdims=True) + EPSILON)


def norm_back(hidden, factor, gain_vec, upstream):
    weighted = upstream * gain_vec
    inner_mean = jnp.mean(weighted * hidden, axis=-1, keepdims=True)
    return factor * weighted - hidden * (factor * factor * factor) * inner_mean


def pick_rows(source, positions):
    return jnp.take_along_axis(source, positions[..., None], axis=1)


def place_rows(values, positions, extent):
    onehot = (positions[..., None] == jnp.arange(extent)[None, None, :]).astype(F32)
    return jnp.einsum("rqs,rqd->rsd", onehot, values, precision=PRECISE)


def matmul(left, right):
    return jnp.einsum("...d,de->...e", left, right, preferred_element_type=F32)


def matmul_t(left, right):
    return jnp.einsum("...e,de->...d", left, right, preferred_element_type=F32)


def outer(left, right):
    return jnp.einsum("rsd,rse->de", left, right, preferred_element_type=F32)


def glu_value(gate_part, up_part):
    return jax.nn.gelu(gate_part, approximate=True) * up_part


def geglu(inputs, gate_up, down, upstream_low):
    width = down.shape[0]
    both = matmul(inputs, gate_up)
    gate_part, up_part = both[..., :width], both[..., width:]
    hidden, pull_back = jax.vjp(glu_value, gate_part, up_part)
    gate_grad, up_grad = pull_back(matmul_t(upstream_low, down))
    return (hidden.astype(BF16), gate_grad.astype(BF16), up_grad.astype(BF16))


def routed_probs(query_heads, key_heads, query_seg, key_seg):
    scores = jnp.einsum("rqd,rkd->rqk", query_heads, key_heads, preferred_element_type=F32)
    scores = scores / math.sqrt(DH)
    allowed = query_seg[:, :, None] == key_seg[:, None, :]
    scores = jnp.where(allowed, scores, NEG_FILL)
    peak = jnp.maximum(jnp.max(scores, axis=-1, keepdims=True), 0.0)
    numer = jnp.exp(scores - peak)
    return numer / (jnp.exp(-peak) + jnp.sum(numer, axis=-1, keepdims=True))


def heavy_forward(query, keys, vals, query_seg, key_seg):
    def head(parts):
        query_h, key_h, val_h = parts
        probs = routed_probs(query_h, key_h, query_seg, key_seg).astype(BF16)
        return jnp.einsum("rqk,rkd->rqd", probs, val_h, preferred_element_type=F32).astype(BF16)

    return join_heads(jax.vmap(head)((split_heads(query), split_heads(keys), split_heads(vals))))


def heavy_both(query, keys, vals, query_seg, key_seg, mix_grad):
    def head(parts, query_seg=query_seg, key_seg=key_seg):
        query_h, key_h, val_h, grad_h = parts
        probs = routed_probs(query_h, key_h, query_seg, key_seg)
        probs_low = probs.astype(BF16)
        mix = jnp.einsum("rqk,rkd->rqd", probs_low, val_h, preferred_element_type=F32)
        prob_grad = jnp.einsum("rqd,rkd->rqk", grad_h, val_h, preferred_element_type=F32)
        delta = jnp.sum(probs * prob_grad, axis=-1, keepdims=True)
        score_grad = (probs * (prob_grad - delta)).astype(BF16)
        dquery = jnp.einsum("rqk,rkd->rqd", score_grad, key_h, preferred_element_type=F32)
        dkey = jnp.einsum("rqk,rqd->rkd", score_grad, query_h, preferred_element_type=F32)
        dval = jnp.einsum("rqk,rqd->rkd", probs_low, grad_h, preferred_element_type=F32)
        scale = 1.0 / math.sqrt(DH)
        return (mix.astype(BF16), (dquery * scale).astype(BF16), (dkey * scale).astype(BF16), dval.astype(BF16))

    heads = tuple(split_heads(v) for v in (query, keys, vals, mix_grad))
    if query.shape[1] <= 512:
        return tuple(join_heads(v) for v in jax.vmap(head)(heads))
    count, rows = heads[0].shape[:2]
    place = jnp.tile(jnp.arange(rows), count)
    parts = tuple(v.reshape(count * rows, 1, *v.shape[2:]) for v in heads)
    done = lax.map(lambda p: head(p[0], query_seg[p[1]][None], key_seg[p[1]][None]), (parts, place))
    return tuple(join_heads(v.reshape(count, rows, *v.shape[2:])) for v in done)


def split_heads(value):
    rows, tokens, width = value.shape
    return value.reshape(rows, tokens, width // DH, DH).transpose(2, 0, 1, 3)


def join_heads(value):
    heads, rows, tokens, width = value.shape
    return value.transpose(1, 2, 0, 3).reshape(rows, tokens, heads * width)


def tokens_of(blocks):
    devices, rows, count, width = blocks.shape
    return blocks.transpose(1, 0, 2, 3).reshape(rows, devices * count, width)


def with_segment(rows, segs):
    marks = jnp.broadcast_to((segs + 2).astype(BF16)[..., None], segs.shape + (LANES,))
    return jnp.concatenate([rows, marks], axis=-1)


def local_wide(
    tokens,
    segments,
    query_route,
    kv_route,
    ffn_route,
    grad_out,
    attn_gain,
    light_qkv,
    light_out,
    heavy_q,
    heavy_kv,
    heavy_out,
    route_query,
    ffn_gain,
    light_gate_up,
    light_down,
    heavy_gate_up,
    heavy_down,
    route_ffn,
):
    row_count, seg_span, width = tokens.shape
    light_heads = width // DL
    ffn_heavy = heavy_down.shape[0]
    devices = lax.axis_size("seq")
    me = lax.axis_index("seq")
    half_place = lax.axis_index("dp")
    anchor = me * seg_span
    routed_own = query_route.shape[1] // devices
    own_query = lax.dynamic_slice_in_dim(query_route, me * routed_own, routed_own, 1) - anchor
    own_key = lax.dynamic_slice_in_dim(kv_route, me * routed_own, routed_own, 1) - anchor
    own_ffn = ffn_route - anchor

    marked = with_segment(tokens, segments)
    before = shifted(marked[:, seg_span - RADIUS :], "seq", 1)
    after = shifted(marked[:, :RADIUS], "seq", -1)
    hidden = tokens.astype(F32)
    factor_one = rms_factor(hidden)
    normed = hidden * factor_one * attn_gain
    normed_low = normed.astype(BF16)
    key_rows = pick_rows(normed_low, own_key)
    key_payload = with_segment(key_rows, jnp.take_along_axis(segments, own_key, axis=1))
    key_blocks = tokens_of(gather_blocks(key_payload))
    key_all, key_seg = key_blocks[..., :width], key_blocks[..., width]

    extended = jnp.concatenate([before, marked, after], axis=1)
    seg_ext = extended[..., width]
    hidden_ext = extended[..., :width].astype(F32)
    factor_ext = rms_factor(hidden_ext)
    normed_ext_low = (hidden_ext * factor_ext * attn_gain).astype(BF16)
    extent = seg_span + 2 * RADIUS
    query_low = matmul(normed_low, light_qkv[:, :width]).astype(BF16)
    query_low = query_low.reshape(row_count, seg_span, light_heads, DL)
    kv_ext = matmul(normed_ext_low, light_qkv[:, width:]).astype(BF16)
    key_ext = kv_ext[..., :width].reshape(row_count, extent, light_heads, DL)
    val_ext = kv_ext[..., width:].reshape(row_count, extent, light_heads, DL)
    offset = jnp.arange(seg_span)[:, None] - jnp.arange(extent)[None, :] + RADIUS
    seg_own = seg_ext[:, RADIUS : RADIUS + seg_span]
    allowed = (jnp.abs(offset) <= RADIUS)[None] & (seg_own[:, :, None] == seg_ext[:, None, :])
    light_scale = 1.0 / math.sqrt(DL)
    scores = jnp.einsum("rqhd,rkhd->rhqk", query_low, key_ext, preferred_element_type=F32)
    scores = jnp.where(allowed[:, None], scores * light_scale, NEG_FILL)
    numerators = jnp.exp(scores - jnp.max(scores, axis=-1, keepdims=True))
    probs_light = numerators / jnp.sum(numerators, axis=-1, keepdims=True)
    probs_low = probs_light.astype(BF16)
    light_mix = jnp.einsum("rhqk,rkhd->rqhd", probs_low, val_ext, preferred_element_type=F32)
    light_mix = light_mix.reshape(row_count, seg_span, width).astype(BF16)
    light_attn = matmul(light_mix, light_out)

    query_rows = pick_rows(normed_low, own_query)
    query_seg_own = (jnp.take_along_axis(segments, own_query, axis=1) + 2).astype(BF16)
    heavy_query = matmul(query_rows, heavy_q).astype(BF16)
    keyval_all = matmul(key_all, heavy_kv).astype(BF16)
    heavy_width = heavy_q.shape[1]
    keys_all, vals_all = keyval_all[..., :heavy_width], keyval_all[..., heavy_width:]
    heavy_mix = heavy_forward(heavy_query, keys_all, vals_all, query_seg_own, key_seg)
    heavy_proj = matmul(heavy_mix, heavy_out)
    query_normed = pick_rows(normed, own_query)
    route_query_full = route_query.astype(F32)
    query_gate = jax.nn.sigmoid(jnp.sum(query_normed * route_query_full, axis=-1))
    heavy_attn = place_rows(query_gate[..., None] * heavy_proj, own_query, seg_span)

    middle = hidden + light_attn + heavy_attn
    factor_two = rms_factor(middle)
    normed_two = middle * factor_two * ffn_gain
    low_two = normed_two.astype(BF16)
    upstream = grad_out.astype(F32)
    ffn_normed = pick_rows(normed_two, own_ffn)
    ffn_rows = ffn_normed.astype(BF16)
    route_ffn_full = route_ffn.astype(F32)
    ffn_gate = jax.nn.sigmoid(jnp.sum(ffn_normed * route_ffn_full, axis=-1))
    ffn_upstream = pick_rows(upstream, own_ffn)
    ffn_low = (ffn_upstream * ffn_gate[..., None]).astype(BF16)
    routed_payload = with_segment(
        jnp.concatenate([ffn_rows, ffn_low, query_rows], axis=-1),
        jnp.take_along_axis(segments, own_query, axis=1),
    )
    routed_blocks = tokens_of(gather_blocks(routed_payload))
    ffn_all = routed_blocks[..., :width]
    ffn_low_all = routed_blocks[..., width : 2 * width]
    query_all = routed_blocks[..., 2 * width : 3 * width]
    query_seg = routed_blocks[..., 3 * width]

    hidden_light, gate_grad, up_grad = geglu(low_two, light_gate_up, light_down, grad_out)
    light_ff = matmul(hidden_light, light_down)
    light_both = jnp.concatenate([gate_grad, up_grad], axis=-1)
    normed_two_grad = matmul_t(light_both, light_gate_up)
    hidden_heavy, gate_grad_h, up_grad_h = geglu(ffn_rows, heavy_gate_up, heavy_down, ffn_low)
    heavy_ffn_proj = matmul(hidden_heavy, heavy_down)
    heavy_ff = place_rows(ffn_gate[..., None] * heavy_ffn_proj, own_ffn, seg_span)
    outputs = (middle + light_ff + heavy_ff).astype(BF16)
    ffn_gate_grad = jnp.sum(ffn_upstream * heavy_ffn_proj, axis=-1)
    ffn_logit_grad = ffn_gate_grad * ffn_gate * (1.0 - ffn_gate)
    route_ffn_grad = jnp.sum(ffn_logit_grad[..., None] * ffn_normed, axis=(0, 1))
    ffn_rows_grad = matmul_t(jnp.concatenate([gate_grad_h, up_grad_h], axis=-1), heavy_gate_up)
    ffn_rows_grad = ffn_rows_grad + ffn_logit_grad[..., None] * route_ffn_full
    normed_two_grad = normed_two_grad + place_rows(ffn_rows_grad, own_ffn, seg_span)
    ffn_gain_grad = jnp.sum(normed_two_grad * middle * factor_two, axis=(0, 1))
    middle_grad = upstream + norm_back(middle, factor_two, ffn_gain, normed_two_grad)
    middle_low = middle_grad.astype(BF16)

    valid_rows = (segments >= 0).astype(F32)[..., None]
    sums = jnp.stack(
        [
            jnp.sum(valid_rows * branch * branch)
            for branch in (hidden, light_attn, heavy_attn, light_ff, heavy_ff)
        ]
        + [jnp.sum(valid_rows)]
    )
    heavy_upstream = pick_rows(middle_grad, own_query)
    query_gate_grad = jnp.sum(heavy_upstream * heavy_proj, axis=-1)
    proj_low = (heavy_upstream * query_gate[..., None]).astype(BF16)
    sum_lanes = jnp.pad(jnp.concatenate(split_parts(sums)), (0, LANES - 18)).astype(BF16)
    sum_lanes = jnp.broadcast_to(sum_lanes, proj_low.shape[:2] + (LANES,))
    proj_blocks = gather_blocks(jnp.concatenate([proj_low, sum_lanes], axis=-1))
    sums_all = jnp.sum(proj_blocks[:, 0, 0, width : width + 18].astype(F32), axis=0)
    sums_all = jnp.sum(sums_all.reshape(3, 6), axis=0)
    sums_all = sums_all + swap(sums_all, "dp", 1)
    rms_stats = jnp.sqrt(sums_all[:5] / (sums_all[5] * width))
    proj_all = tokens_of(proj_blocks)[..., :width]

    flat = lambda v: v.reshape(-1, v.shape[-1])
    gate_up_grad = [
        jnp.dot(slot_columns(flat(low_two), me, devices).T, flat(part), preferred_element_type=F32)
        for part in own_half_first(light_both, half_place)
    ]
    hidden_slots = slot_columns(flat(hidden_light), me, devices).T
    down_grad = [
        jnp.dot(hidden_slots, flat(part), preferred_element_type=F32)
        for part in own_half_first(grad_out, half_place)
    ]
    mix_slots = slot_columns(flat(light_mix), me, devices).T
    out_grad = [
        jnp.dot(mix_slots, flat(part), preferred_element_type=F32)
        for part in own_half_first(middle_low, half_place)
    ]
    first_sum = scatter_sum(
        jnp.concatenate(
            [
                slot_block(gate_up_grad, devices),
                slot_block(down_grad, devices),
                slot_block(out_grad, devices),
                slot_vectors((ffn_gain_grad, route_ffn_grad), me, devices),
            ],
            axis=2,
        )
    )
    block = width // devices
    block_ff = light_down.shape[0] // devices
    cuts = [0]
    for rows in (
        block * light_gate_up.shape[1] // 2 // LANES,
        block_ff * width // 2 // LANES,
        block * width // 2 // LANES,
        block,
    ):
        cuts.append(cuts[-1] + rows)
    light_gate_up_grad = unslot(first_sum[cuts[0] : cuts[1]], light_gate_up.shape[1] // 2)
    light_down_grad = unslot(first_sum[cuts[1] : cuts[2]], width // 2)
    light_out_grad = unslot(first_sum[cuts[2] : cuts[3]], width // 2)
    ffn_gain_grad = first_sum[cuts[3] : cuts[4], 0]
    route_ffn_grad = first_sum[cuts[3] : cuts[4], 1]

    group = min(4, devices)
    low_place, high_place = me % group, me // group
    groups = devices // group
    unit = ffn_heavy // devices
    gate_up_parts = heavy_gate_up.reshape(width, 2, groups, group, unit)
    gate_up_mine = lax.dynamic_index_in_dim(gate_up_parts, low_place, 3, False)
    down_mine = lax.dynamic_index_in_dim(
        heavy_down.reshape(groups, group, unit, width), low_place, 1, False
    )
    x_all = flat(ffn_all)
    up_all = flat(ffn_low_all)
    hidden_mine, gate_mine, up_mine = geglu(
        x_all,
        gate_up_mine.reshape(width, -1),
        down_mine.reshape(-1, width),
        up_all,
    )
    hidden_block = lax.dynamic_slice_in_dim(hidden_mine, high_place * unit, unit, 1)
    heavy_down_half = [
        jnp.dot(hidden_block.T, part, preferred_element_type=F32)
        for part in own_half_first(up_all, half_place)
    ]
    heavy_down_grad = heavy_down_half[0] + swap(heavy_down_half[1].astype(BF16), "dp", 1).astype(F32)
    x_group = lax.dynamic_slice_in_dim(x_all, high_place * group * block, group * block, 1)
    x_group = x_group.reshape(-1, group, block)
    x_group = jnp.take(x_group, jnp.arange(group) ^ low_place, axis=1).reshape(-1, group * block)
    gate_half, up_half = (
        jnp.dot(x_group.T, part, preferred_element_type=F32) for part in (gate_mine, up_mine)
    )
    kept = jnp.where(half_place == 0, gate_half, up_half)
    sent = jnp.where(half_place == 0, up_half, gate_half)
    kept = (kept + swap(sent.astype(BF16), "dp", 1).astype(F32)).reshape(group, block, groups, unit)
    pieces = [kept[0]]
    for place in range(1, group):
        pieces.append(swap(kept[place].astype(BF16), "seq", place).astype(F32))
    pieces = jnp.take(jnp.stack(pieces, axis=2), jnp.arange(group) ^ low_place, axis=2)
    heavy_gate_up_grad = pieces.reshape(block, ffn_heavy)

    mix_grad = matmul_t(middle_low, light_out).astype(BF16)
    mix_grad = mix_grad.reshape(row_count, seg_span, light_heads, DL)
    val_grad = jnp.einsum("rhqk,rqhd->rkhd", probs_low, mix_grad, preferred_element_type=F32)
    prob_grad = jnp.einsum("rqhd,rkhd->rhqk", mix_grad, val_ext, preferred_element_type=F32)
    delta = jnp.sum(probs_light * prob_grad, axis=-1, keepdims=True)
    score_grad = (probs_light * (prob_grad - delta)).astype(BF16)
    query_grad = jnp.einsum("rhqk,rkhd->rqhd", score_grad, key_ext, preferred_element_type=F32)
    key_grad = jnp.einsum("rhqk,rqhd->rkhd", score_grad, query_low, preferred_element_type=F32)
    query_grad = (query_grad * light_scale).reshape(row_count, seg_span, width).astype(BF16)
    kv_grad = jnp.concatenate(
        [
            (key_grad * light_scale).reshape(row_count, extent, width),
            val_grad.reshape(row_count, extent, width),
        ],
        axis=-1,
    ).astype(BF16)
    normed_grad_ext = matmul_t(kv_grad, light_qkv[:, width:])
    normed_grad = matmul_t(query_grad, light_qkv[:, :width])
    normed_grad = normed_grad + normed_grad_ext[:, RADIUS : RADIUS + seg_span]
    from_right = shifted(normed_grad_ext[:, :RADIUS].astype(BF16), "seq", -1)
    from_left = shifted(normed_grad_ext[:, seg_span + RADIUS :].astype(BF16), "seq", 1)
    normed_grad = normed_grad.at[:, :RADIUS].add(from_left.astype(F32))
    normed_grad = normed_grad.at[:, seg_span - RADIUS :].add(from_right.astype(F32))

    hq_all = matmul(query_all, heavy_q).astype(BF16)
    do2_all = matmul_t(proj_all, heavy_out).astype(BF16)
    mix_all, dhq_all, dhk_all, dhv_all = heavy_both(
        hq_all, keys_all, vals_all, query_seg, key_seg, do2_all
    )
    dhkv_all = jnp.concatenate([dhk_all, dhv_all], axis=-1)
    mine = lambda v: lax.dynamic_slice_in_dim(flat(v), me * block, block, 1).T
    heavy_grads = [
        own_half_first(jnp.dot(mine(left), flat(right), preferred_element_type=F32), half_place)
        for left, right in ((query_all, dhq_all), (key_all, dhkv_all), (mix_all, proj_all))
    ]
    heavy_kept = jnp.concatenate([pair[0] for pair in heavy_grads], axis=-1)
    heavy_sent = jnp.concatenate([pair[1] for pair in heavy_grads], axis=-1)
    heavy_sum = heavy_kept + swap(heavy_sent.astype(BF16), "dp", 1).astype(F32)
    heavy_half = heavy_width // 2
    heavy_q_grad = heavy_sum[:, :heavy_half]
    heavy_kv_grad = heavy_sum[:, heavy_half : 3 * heavy_half]
    heavy_out_grad = heavy_sum[:, 3 * heavy_half :]
    query_logit_grad = query_gate_grad * query_gate * (1.0 - query_gate)
    route_query_grad = jnp.sum(query_logit_grad[..., None] * query_normed, axis=(0, 1))
    query_rows_grad = (
        matmul_t(dhq_all[:, :routed_own], heavy_q) + query_logit_grad[..., None] * route_query_full
    )
    key_rows_grad = matmul_t(dhkv_all[:, :routed_own], heavy_kv)
    normed_grad = (
        normed_grad
        + place_rows(query_rows_grad, own_query, seg_span)
        + place_rows(key_rows_grad, own_key, seg_span)
    )
    attn_gain_grad = jnp.sum(normed_grad * hidden * factor_one, axis=(0, 1))
    hidden_norm_grad = norm_back(hidden, factor_one, attn_gain, normed_grad)
    grad_tokens = (middle_grad + hidden_norm_grad).astype(BF16)

    own_slots = slot_columns(flat(normed_low), me, devices).T
    ext_slots = slot_columns(flat(normed_ext_low), me, devices).T
    qkv_grad = jnp.concatenate(
        [
            jnp.dot(own_slots, flat(query_grad), preferred_element_type=F32),
            jnp.dot(ext_slots, flat(kv_grad), preferred_element_type=F32),
        ],
        axis=-1,
    )
    second_sum = scatter_sum(
        jnp.concatenate(
            [
                slot_block(own_half_first(qkv_grad, half_place), devices),
                slot_vectors((attn_gain_grad, route_query_grad), me, devices),
            ],
            axis=2,
        )
    )
    qkv_cols = light_qkv.shape[1] // 2
    qkv_rows = block * qkv_cols // LANES
    light_qkv_grad = unslot(second_sum[:qkv_rows], qkv_cols)
    attn_gain_grad = second_sum[qkv_rows:, 0]
    route_query_grad = second_sum[qkv_rows:, 1]
    return (
        outputs,
        grad_tokens,
        attn_gain_grad,
        light_qkv_grad,
        light_out_grad,
        heavy_q_grad,
        heavy_kv_grad,
        heavy_out_grad,
        route_query_grad,
        ffn_gain_grad,
        light_gate_up_grad,
        light_down_grad,
        heavy_gate_up_grad,
        heavy_down_grad,
        route_ffn_grad,
        rms_stats,
    )


VMEM = pl.BlockSpec(memory_space=pltpu.VMEM)
SMEM = pl.BlockSpec(memory_space=pltpu.SMEM)
GELU_RATE = math.sqrt(2.0 / math.pi)
GELU_CUBE = 0.044715
VMEM_BYTES = 52 * 1024 * 1024


def shape(dims, dtype):
    return jax.ShapeDtypeStruct(dims, dtype)


def call(kernel, outs, ins, smem=0, scratch=(), flops=0, moved=0):
    return pl.pallas_call(
        kernel,
        out_shape=outs,
        in_specs=[SMEM] * smem + [VMEM] * (len(ins) - smem),
        out_specs=[VMEM] * len(outs),
        scratch_shapes=list(scratch),
        compiler_params=pltpu.CompilerParams(vmem_limit_bytes=VMEM_BYTES),
        cost_estimate=pl.CostEstimate(flops=flops, bytes_accessed=moved, transcendentals=0),
    )(*ins)


def dot(left, right):
    return jnp.dot(left, right, preferred_element_type=F32)


def dot_t(left, right):
    return lax.dot_general(left, right, (((1,), (1,)), ((), ())), preferred_element_type=F32)


def t_dot(left, right):
    return lax.dot_general(left, right, (((0,), (0,)), ((), ())), preferred_element_type=F32)


def row_factor(value):
    return lax.rsqrt(jnp.mean(value * value, axis=-1, keepdims=True) + EPSILON)


def as_column(row):
    count = row.shape[1]
    down = lax.broadcasted_iota(jnp.int32, (count, count), 0)
    along = lax.broadcasted_iota(jnp.int32, (count, count), 1)
    return jnp.sum(jnp.where(down == along, row, 0.0), axis=1, keepdims=True)


def head_window(head, size):
    first = head * size // LANES * LANES
    lanes = (head * size + size - 1) // LANES * LANES + LANES - first
    place = lax.broadcasted_iota(jnp.int32, (1, lanes), 1) + first
    return first, lanes, (place >= head * size) & (place < head * size + size)


def slot_select(width, devices, me):
    block = width // devices
    bits = devices.bit_length() - 1
    along = lax.broadcasted_iota(jnp.int32, (block, width), 1)
    inside = lax.broadcasted_iota(jnp.int32, (block, width), 0)
    rows = []
    for p in range(devices):
        owner = int(format(p, f"0{bits}b")[::-1], 2) ^ me
        rows.append((along == inside + owner * block).astype(F32))
    return jnp.concatenate(rows, axis=0).astype(BF16)


def two_gelu(value):
    square = value * value
    bend = jnp.tanh(GELU_RATE * value * (1.0 + GELU_CUBE * square))
    half = 0.5 * (1.0 + bend)
    slope = half + 0.5 * value * (1.0 - bend * bend) * GELU_RATE * (1.0 + 3.0 * GELU_CUBE * square)
    return value * half, slope


def first_kernel(routed, route, seg_at, tokens, segs, gain, keys, upper, lower, normed, picked):
    rows, span, width = tokens.shape
    me = lax.axis_index("seq")
    hidden = tokens[...].reshape(rows * span, width).astype(F32)
    normed[...] = hidden * row_factor(hidden) * gain[...]
    for r in range(rows):
        for k in range(routed):
            place = route[r, me * routed + k] - me * span
            at = pl.ds(r * routed + k, 1)
            picked[at, :width] = normed[pl.ds(r * span + place, 1), :]
            picked[at, width:] = jnp.full((1, LANES), (seg_at[r, place] + 2).astype(F32))
    keys[...] = picked[...].astype(BF16).reshape(keys.shape)
    marks = (segs[...] + 2).astype(F32)
    for out, start in ((upper, span - RADIUS), (lower, 0)):
        out[:, :RADIUS, :] = tokens[:, start : start + RADIUS, :]
        out[:, RADIUS:, :] = jnp.zeros((rows, 16, width), BF16)
        for r in range(rows):
            out[r, RADIUS:, :span] = jnp.broadcast_to(marks[r : r + 1], (16, span)).astype(BF16)


def light_kernel(
    before, tokens, after, segs, gain, w_qkv, w_out,
    normed, query, keyval, probs, mix, attn, seg_row, mix_t,
):
    rows, span, width = tokens.shape
    extent = span + 2 * RADIUS
    heads = width // DL
    for r in range(rows):
        for part, at in ((before, 0), (tokens, RADIUS), (after, RADIUS + span)):
            size = span if part is tokens else RADIUS
            value = part[r, :size, :].astype(F32)
            value = value * row_factor(value) * gain[...]
            normed[r * extent + at : r * extent + at + size, :] = value.astype(BF16)
    keyval[...] = dot(normed[...], w_qkv[:, width:]).astype(BF16)
    own = [normed[r * extent + RADIUS : r * extent + RADIUS + span, :] for r in range(rows)]
    query[...] = dot(jnp.concatenate(own, axis=0), w_qkv[:, :width]).astype(BF16)
    down = lax.broadcasted_iota(jnp.int32, (extent, span), 0)
    along = lax.broadcasted_iota(jnp.int32, (extent, span), 1)
    near = jnp.abs(along - down + RADIUS) <= RADIUS
    for r in range(rows):
        marks = (segs[r : r + 1, :] + 2).astype(F32)
        seg_row[:, :span] = before[r, RADIUS : RADIUS + 8, :span].astype(F32)
        seg_row[:, span : 2 * span] = jnp.broadcast_to(marks, (8, span))
        seg_row[:, 2 * span :] = after[r, RADIUS : RADIUS + 8, :span].astype(F32)
        columns = [as_column(seg_row[0:1, c * span : (c + 1) * span]) for c in range(3)]
        key_marks = jnp.concatenate([columns[0][span - RADIUS :], columns[1], columns[2][:RADIUS]], axis=0)
        allowed = near & (key_marks == marks)
        key_rows = slice(r * extent, (r + 1) * extent)
        val_t = keyval[key_rows, width:].T
        for h in range(heads):
            first, lanes, mask = head_window(h, DL)
            window = slice(first, first + lanes)
            q_head = jnp.where(mask, query[r * span : (r + 1) * span, window], 0)
            scores = dot_t(keyval[key_rows, window], q_head)
            scores = jnp.where(allowed, scores * (1.0 / math.sqrt(DL)), NEG_FILL)
            numer = jnp.exp(scores - jnp.max(scores, axis=0, keepdims=True))
            share = (numer / jnp.sum(numer, axis=0, keepdims=True)).astype(BF16)
            probs[r * heads + h] = share
            mix_t[h * DL : (h + 1) * DL, :] = dot(val_t[h * DL : (h + 1) * DL, :], share)
        mix[r * span : (r + 1) * span, :] = mix_t[...].T.astype(BF16)
    attn[...] = dot(mix[...], w_out[...])


def stat_row(value):
    total = jnp.sum(jnp.sum(value, axis=0, keepdims=True), axis=1, keepdims=True)
    return jnp.broadcast_to(total, (1, LANES))


def valid_column(segs):
    rows = segs.shape[0]
    parts = [as_column((segs[r : r + 1, :] >= 0).astype(F32)) for r in range(rows)]
    return jnp.concatenate(parts, axis=0)


def router(rows, weights):
    return jax.nn.sigmoid(jnp.sum(rows[...] * weights[...].astype(F32), axis=-1, keepdims=True))


def middle_kernel(
    routed, q_route, f_route, seg_at, tokens, segs, keys, attn, upstream, gain, ffn_gain,
    w_q, w_kv, w_out, route_q, route_f,
    middle, normed_two, keyval, payload, q_rows, f_rows, f_up, proj, f_marks, stats,
    full, marks, placed,
):
    rows, span, width = tokens.shape
    devices = keys.shape[0]
    me = lax.axis_index("seq")
    count = rows * routed
    hidden = tokens[...].reshape(rows * span, width).astype(F32)
    full[...] = hidden * row_factor(hidden) * gain[...]
    for r in range(rows):
        for k in range(routed):
            at = pl.ds(r * routed + k, 1)
            place = q_route[r, me * routed + k] - me * span
            q_rows[at, :] = full[pl.ds(r * span + place, 1), :]
            marks[at, :] = jnp.full((1, LANES), (seg_at[r, place] + 2).astype(F32))
            place = f_route[r, k] - me * span
            f_marks[at, :] = jnp.full((1, LANES), (seg_at[r, place] + 2).astype(F32))
    q_low = q_rows[...].astype(BF16)
    payload[:, :, 2 * width : 3 * width] = q_low.reshape(rows, routed, width)
    payload[:, :, 3 * width :] = marks[...].astype(BF16).reshape(rows, routed, LANES)
    key_low = keys[:, :, :, :width].reshape(devices * count, width)
    keyval[...] = dot(key_low, w_kv[...]).astype(BF16).reshape(keyval.shape)
    query = dot(q_low, w_q[...]).astype(BF16)
    heads = width // DH
    lane = lax.broadcasted_iota(jnp.int32, (1, width), 1)
    masks = [(lane >= h * DH) & (lane < (h + 1) * DH) for h in range(heads)]
    mixed = []
    for r in range(rows):
        mine = query[r * routed : (r + 1) * routed]
        wide = jnp.concatenate([jnp.where(m, mine, 0) for m in masks], axis=0)
        key_r = keyval[:, r, :, :width].reshape(devices * routed, width)
        val_r = keyval[:, r, :, width:].reshape(devices * routed, width)
        scores = dot_t(wide, key_r) * (1.0 / math.sqrt(DH))
        key_marks = keys[:, r, :, width:].reshape(devices * routed, LANES).astype(F32).T[0:1, :]
        query_marks = jnp.concatenate([marks[r * routed : (r + 1) * routed, 0:1]] * heads, axis=0)
        scores = jnp.where(query_marks == key_marks, scores, NEG_FILL)
        peak = jnp.maximum(jnp.max(scores, axis=-1, keepdims=True), 0.0)
        numer = jnp.exp(scores - peak)
        share = numer / (jnp.exp(-peak) + jnp.sum(numer, axis=-1, keepdims=True))
        part = dot(share.astype(BF16), val_r)
        total = jnp.zeros((routed, width), F32)
        for h in range(heads):
            total = total + jnp.where(masks[h], part[h * routed : (h + 1) * routed], 0.0)
        mixed.append(total)
    mixed = jnp.concatenate(mixed, axis=0).astype(BF16)
    proj[...] = dot(mixed, w_out[...])
    placed[...] = router(q_rows, route_q) * proj[...]
    light = attn[...]
    middle[...] = hidden + light
    for r in range(rows):
        for k in range(routed):
            place = q_route[r, me * routed + k] - me * span
            at = pl.ds(r * span + place, 1)
            middle[at, :] = middle[at, :] + placed[pl.ds(r * routed + k, 1), :]
    valid = valid_column(segs)
    stats[...] = jnp.zeros(stats.shape, F32)
    stats[0:1, :] = stat_row(valid * hidden * hidden)
    stats[1:2, :] = stat_row(valid * light * light)
    stats[2:3, :] = stat_row(jnp.where(marks[:, 0:1] >= 2.0, placed[...] * placed[...], 0.0))
    stats[5:6, :] = stat_row(valid)
    mid = middle[...]
    full[...] = mid * row_factor(mid) * ffn_gain[...]
    normed_two[...] = full[...].astype(BF16)
    for r in range(rows):
        for k in range(routed):
            place = f_route[r, k] - me * span
            f_rows[pl.ds(r * routed + k, 1), :] = full[pl.ds(r * span + place, 1), :]
    full[...] = upstream[...].reshape(rows * span, width).astype(F32)
    for r in range(rows):
        for k in range(routed):
            place = f_route[r, k] - me * span
            f_up[pl.ds(r * routed + k, 1), :] = full[pl.ds(r * span + place, 1), :]
    f_low = (router(f_rows, route_f) * f_up[...]).astype(BF16)
    payload[:, :, :width] = f_rows[...].astype(BF16).reshape(rows, routed, width)
    payload[:, :, width : 2 * width] = f_low.reshape(rows, routed, width)


def glu_parts(inputs, back_in, gate_w, up_w, down_w):
    act, slope = two_gelu(dot(inputs, gate_w))
    lift = dot(inputs, up_w)
    back = dot_t(back_in, down_w)
    hidden = (act * lift).astype(BF16)
    return hidden, (back * lift * slope).astype(BF16), (back * act).astype(BF16)


def three_parts(value):
    high = value.astype(BF16).astype(F32)
    middle = (value - high).astype(BF16).astype(F32)
    return high, middle, value - high - middle


def ffn_kernel(
    routed, q_route, f_route, normed_two, upstream, middle, w_gate, w_up, w_down,
    h_gate, h_up, h_down, q_rows, f_rows, f_up, proj, f_marks, ffn_gain, route_q, route_f, stats, segs,
    outputs, dmid, dmid_low, hidden_out, grad_gate, grad_up, payload, vectors,
    z_light, d_light, z_heavy, d_heavy, placed, full,
):
    step = pl.program_id(0)
    width = middle.shape[1]
    rows, span = segs.shape
    me = lax.axis_index("seq")

    @pl.when(step == 0)
    def _():
        for total in (z_light, d_light, z_heavy, d_heavy):
            total[...] = jnp.zeros(total.shape, F32)

    grad = upstream[...].reshape(rows * span, width)
    hidden, d_gate, d_up = glu_parts(normed_two[...], grad, w_gate[...], w_up[...], w_down[...])
    hidden_out[...] = hidden
    grad_gate[...] = d_gate
    grad_up[...] = d_up
    z_light[...] += dot(hidden, w_down[...])
    d_light[...] += dot_t(d_gate, w_gate[...]) + dot_t(d_up, w_up[...])
    f_gate = router(f_rows, route_f)
    f_low = (f_gate * f_up[...]).astype(BF16)
    f_in = f_rows[...].astype(BF16)
    hidden, d_gate, d_up = glu_parts(f_in, f_low, h_gate[...], h_up[...], h_down[...])
    z_heavy[...] += dot(hidden, h_down[...])
    d_heavy[...] += dot_t(d_gate, h_gate[...]) + dot_t(d_up, h_up[...])

    @pl.when(step == pl.num_programs(0) - 1)
    def _():
        mid = middle[...]
        placed[...] = f_gate * z_heavy[...]
        full[...] = mid + z_light[...]
        logit = jnp.sum(f_up[...] * z_heavy[...], axis=-1, keepdims=True) * f_gate * (1.0 - f_gate)
        d_heavy[...] += logit * route_f[...].astype(F32)
        for r in range(rows):
            for k in range(routed):
                place = f_route[r, k] - me * span
                at, source = pl.ds(r * span + place, 1), pl.ds(r * routed + k, 1)
                full[at, :] = full[at, :] + placed[source, :]
                d_light[at, :] = d_light[at, :] + d_heavy[source, :]
        outputs[...] = full[...].astype(BF16).reshape(outputs.shape)
        factor = row_factor(mid)
        d_norm = d_light[...]
        vectors[...] = jnp.zeros(vectors.shape, F32)
        vectors[0:1, :] = jnp.sum(d_norm * mid * factor, axis=0, keepdims=True)
        vectors[1:2, :] = jnp.sum(logit * f_rows[...], axis=0, keepdims=True)
        weighted = d_norm * ffn_gain[...]
        inner = jnp.mean(weighted * mid, axis=-1, keepdims=True)
        total = grad.astype(F32) + factor * weighted - mid * (factor * factor * factor) * inner
        dmid[...] = total
        dmid_low[...] = total.astype(BF16)
        sums = stats[...]
        place = lax.broadcasted_iota(jnp.int32, sums.shape, 0)
        lane = lax.broadcasted_iota(jnp.int32, sums.shape, 1)
        light_sum = stat_row(valid_column(segs) * z_light[...] * z_light[...])
        heavy_sum = stat_row(jnp.where(f_marks[:, 0:1] >= 2.0, placed[...] * placed[...], 0.0))
        sums = jnp.where(place == 3, light_sum, jnp.where(place == 4, heavy_sum, sums))
        lanes = jnp.zeros(sums.shape, F32)
        for k, part in enumerate(three_parts(sums)):
            lanes = lanes + jnp.where(lane == place + 8 * k, part, 0.0)
        lanes = jnp.sum(lanes, axis=0, keepdims=True)
        full[...] = total
        for r in range(rows):
            for k in range(routed):
                place = q_route[r, me * routed + k] - me * span
                placed[pl.ds(r * routed + k, 1), :] = full[pl.ds(r * span + place, 1), :]
        q_gate = router(q_rows, route_q)
        logit = jnp.sum(placed[...] * proj[...], axis=-1, keepdims=True) * q_gate * (1.0 - q_gate)
        payload[:, :, :width] = (q_gate * placed[...]).astype(BF16).reshape(rows, routed, width)
        lane = lax.broadcasted_iota(jnp.int32, (rows * routed, LANES), 1)
        extra = jnp.broadcast_to(lanes, (rows * routed, LANES))
        for k, part in enumerate(three_parts(logit)):
            extra = jnp.where(lane == 24 + k, part, extra)
        payload[:, :, width:] = extra.astype(BF16).reshape(rows, routed, LANES)


def halves_of(value, place):
    half = value.shape[-1] // 2
    first, second = value[..., :half], value[..., half:]
    return jnp.where(place == 0, first, second), jnp.where(place == 0, second, first)


def store_slots(outs, place, base, grads):
    kept, sent = outs
    slots = kept.shape[0]
    block = grads.shape[0] // (2 * slots)
    low = grads.astype(BF16)
    for c in range(grads.shape[1] // LANES):
        for p in range(2 * slots):
            part = low[p * block : (p + 1) * block, c * LANES : (c + 1) * LANES]
            out = kept if p < slots else sent
            out[p % slots, place, base + c * block : base + (c + 1) * block, :] = part
    return base + grads.shape[1] // LANES * block


def slot_vector_block(select, vectors):
    table = jnp.concatenate([vectors, jnp.zeros((LANES - vectors.shape[0], vectors.shape[1]), F32)], axis=0)
    return dot_t(select, table.astype(BF16))


def first_grads_kernel(
    normed_two, grad_gate, grad_up, hidden, upstream, mix, dmid_low, vectors, kept, sent
):
    devices = 2 * kept.shape[0]
    width = normed_two.shape[1]
    me = lax.axis_index("seq")
    place = lax.axis_index("dp")
    select = slot_select(width, devices, me)
    inputs_t = dot_t(select, normed_two[...]).astype(BF16)
    gate, up = grad_gate[...], grad_up[...]
    ways = (jnp.where(place == 0, gate, up), jnp.where(place == 0, up, gate))
    for half in range(2):
        base = store_slots((kept, sent), half, 0, dot(inputs_t, ways[half]))
    hidden_t = dot_t(slot_select(hidden.shape[1], devices, me), hidden[...]).astype(BF16)
    ways = halves_of(upstream[...].reshape(-1, width), place)
    for half in range(2):
        base_two = store_slots((kept, sent), half, base, dot(hidden_t, ways[half]))
    mix_t = dot_t(select, mix[...]).astype(BF16)
    ways = halves_of(dmid_low[...], place)
    for half in range(2):
        base_three = store_slots((kept, sent), half, base_two, dot(mix_t, ways[half]))
    table = slot_vector_block(select, vectors[...])
    for half in range(2):
        store_slots((kept, sent), half, base_three, table)


def light_back_kernel(
    dmid_low, query, keyval, probs, normed, gain, w_qkv, w_out,
    dnorm, to_right, to_left, kept, sent, d_all, dkv, dq_t,
):
    rows, rim, width = to_right.shape
    span = dmid_low.shape[0] // rows
    extent = span + 2 * rim
    heads = width // DL
    scale = 1.0 / math.sqrt(DL)
    me = lax.axis_index("seq")
    place = lax.axis_index("dp")
    mix_grad = dot_t(dmid_low[...], w_out[...]).astype(BF16)
    for r in range(rows):
        key_rows = slice(r * extent, (r + 1) * extent)
        own_rows = slice(r * span, (r + 1) * span)
        key_t = keyval[key_rows, :width].T
        dkv[...] = jnp.zeros(dkv.shape, F32)
        for h in range(heads):
            first, lanes, mask = head_window(h, DL)
            window = slice(first, first + lanes)
            v_window = slice(width + first, width + first + lanes)
            q_head = jnp.where(mask, query[own_rows, window], 0)
            g_head = jnp.where(mask, mix_grad[own_rows, window], 0)
            share = probs[r * heads + h]
            full_share = share.astype(F32)
            prob_grad = dot_t(keyval[key_rows, v_window], g_head)
            delta = jnp.sum(full_share * prob_grad, axis=0, keepdims=True)
            score_grad = (full_share * (prob_grad - delta)).astype(BF16)
            dkv[:, window] += dot(score_grad, q_head)
            dkv[:, v_window] += dot(share, g_head)
            dq_t[h * DL : (h + 1) * DL, :] = dot(key_t[h * DL : (h + 1) * DL, :], score_grad)
        d_all[key_rows, :width] = jnp.zeros((extent, width), BF16)
        d_all[r * extent + rim : r * extent + rim + span, :width] = (dq_t[...].T * scale).astype(BF16)
        d_all[key_rows, width : 2 * width] = (dkv[:, :width] * scale).astype(BF16)
        d_all[key_rows, 2 * width :] = dkv[:, width:].astype(BF16)
    d_norm = dot_t(d_all[...], w_qkv[...])
    gain_grad = jnp.sum(d_norm * normed[...].astype(F32), axis=0, keepdims=True) / gain[...]
    for r in range(rows):
        to_left[r] = d_norm[r * extent : r * extent + rim].astype(BF16)
        dnorm[r * span : (r + 1) * span, :] = d_norm[r * extent + rim : r * extent + rim + span]
        to_right[r] = d_norm[r * extent + rim + span : (r + 1) * extent].astype(BF16)
    select = slot_select(width, 2 * kept.shape[0], me)
    inputs_t = dot_t(select, normed[...]).astype(BF16)
    ways = halves_of(d_all[...], place)
    table = slot_vector_block(select, jnp.broadcast_to(gain_grad, (8, width)))
    for half in range(2):
        base = store_slots((kept, sent), half, 0, dot(inputs_t, ways[half]))
        store_slots((kept, sent), half, base, table)


def heavy_ffn_kernel(
    me_at, routed_all, h_gate, h_up, h_down, kept, sent, down_kept, down_sent, picked,
):
    step = pl.program_id(0)
    devices, rows, routed, _ = routed_all.shape
    width = h_gate.shape[0]
    count = devices * rows * routed
    me = me_at[0]
    place = lax.axis_index("dp")
    group = picked.shape[0] * devices // width
    low_place = lax.rem(me, group)
    high_place = lax.div(me, group)
    block = width // devices
    inputs = routed_all[:, :, :, :width].reshape(count, width)
    back_in = routed_all[:, :, :, width : 2 * width].reshape(count, width)

    @pl.when(step == 0)
    def _():
        along = lax.broadcasted_iota(jnp.int32, (block, width), 1)
        inside = lax.broadcasted_iota(jnp.int32, (block, width), 0)
        picks = []
        for j in range(group):
            owner = high_place * group + (low_place ^ j)
            picks.append((along == inside + owner * block).astype(F32))
        picked[...] = dot_t(jnp.concatenate(picks, axis=0).astype(BF16), inputs).astype(BF16)

    hidden, d_gate, d_up = glu_parts(inputs, back_in, h_gate[...], h_up[...], h_down[...])
    kept[...] = dot(picked[...], jnp.where(place == 0, d_gate, d_up))
    sent[...] = dot(picked[...], jnp.where(place == 0, d_up, d_gate)).astype(BF16)

    @pl.when(step == high_place)
    def _():
        hidden_t = hidden.T
        mine, other = halves_of(back_in, place)
        down_kept[...] = dot(hidden_t, mine)
        down_sent[...] = dot(hidden_t, other).astype(BF16)


def heavy_back_kernel(
    routed, q_route, k_route, routed_all, proj_all, keyval, keys, dnorm, from_left, from_right, dmid, tokens,
    gain, w_q, w_kv, w_out, route_q,
    grad_tokens, kept, sent,
    total, q_rows, k_rows, mix_t, dq_t, dkv,
):
    rows, span, width = tokens.shape
    devices = keys.shape[0]
    per_row = devices * routed
    heads = width // DH
    scale = 1.0 / math.sqrt(DH)
    me = lax.axis_index("seq")
    place = lax.axis_index("dp")
    block = width // devices
    along = lax.broadcasted_iota(jnp.int32, (block, width), 1)
    inside = lax.broadcasted_iota(jnp.int32, (block, width), 0)
    own_full = (along == inside + me * block).astype(F32)
    own = own_full.astype(BF16)
    q_grad = jnp.zeros((block, width), F32)
    kv_grad = jnp.zeros((block, 2 * width), F32)
    out_grad = jnp.zeros((block, width), F32)
    route_grad = jnp.zeros((block, 1), F32)
    for r in range(rows):
        in_q = routed_all[:, r, :, 2 * width : 3 * width].reshape(per_row, width)
        in_k = keys[:, r, :, :width].reshape(per_row, width)
        q_marks = routed_all[:, r, :, 3 * width :].reshape(per_row, LANES).astype(F32).T[0:1, :]
        k_marks = keys[:, r, :, width:].reshape(per_row, LANES).astype(F32)[:, 0:1]
        allowed = k_marks == q_marks
        grad_in = proj_all[:, r, :, :width].reshape(per_row, width)
        extra = proj_all[:, r, :, width:].reshape(per_row, LANES).astype(F32)
        extra_t = extra.T
        query = dot(in_q, w_q[...]).astype(BF16)
        mix_grad = dot_t(grad_in, w_out[...]).astype(BF16)
        key_t = keyval[:, r, :, :width].reshape(per_row, width).T
        val_t = keyval[:, r, :, width:].reshape(per_row, width).T
        for first in range(0, width, LANES):
            window = slice(first, first + LANES)
            v_window = slice(width + first, width + first + LANES)
            keys_w = keyval[:, r, :, window].reshape(per_row, LANES)
            vals_w = keyval[:, r, :, v_window].reshape(per_row, LANES)
            dk, dv = None, None
            for h in range(first // DH, (first + LANES) // DH):
                lane = lax.broadcasted_iota(jnp.int32, (1, LANES), 1) + first
                mask = (lane >= h * DH) & (lane < (h + 1) * DH)
                q_head = jnp.where(mask, query[:, window], 0)
                g_head = jnp.where(mask, mix_grad[:, window], 0)
                scores = jnp.where(allowed, dot_t(keys_w, q_head) * scale, NEG_FILL)
                peak = jnp.maximum(jnp.max(scores, axis=0, keepdims=True), 0.0)
                numer = jnp.exp(scores - peak)
                share = numer / (jnp.exp(-peak) + jnp.sum(numer, axis=0, keepdims=True))
                share_low = share.astype(BF16)
                prob_grad = dot_t(vals_w, g_head)
                delta = jnp.sum(share * prob_grad, axis=0, keepdims=True)
                score_grad = (share * (prob_grad - delta)).astype(BF16)
                at = slice(h * DH, (h + 1) * DH)
                mix_t[at, :] = dot(val_t[at, :], share_low).astype(BF16)
                dq_t[at, :] = dot(key_t[at, :], score_grad)
                part_k, part_v = dot(score_grad, q_head), dot(share_low, g_head)
                dk, dv = (part_k, part_v) if dk is None else (dk + part_k, dv + part_v)
            dkv[:, window] = (dk * scale).astype(BF16)
            dkv[:, v_window] = dv.astype(BF16)
        dq = (dq_t[...].T * scale).astype(BF16)
        in_q_t = dot_t(own, in_q)
        q_grad = q_grad + dot(in_q_t.astype(BF16), dq)
        kv_grad = kv_grad + dot(dot_t(own, in_k).astype(BF16), dkv[...])
        out_grad = out_grad + dot(dot(own, mix_t[...]).astype(BF16), grad_in)
        logit_row = extra_t[24:25, :] + extra_t[25:26, :] + extra_t[26:27, :]
        route_grad = route_grad + jnp.sum(in_q_t * logit_row, axis=1, keepdims=True)
        logit = extra[:routed, 24:25] + extra[:routed, 25:26] + extra[:routed, 26:27]
        own_at = slice(r * routed, (r + 1) * routed)
        q_rows[own_at, :] = dot_t(dq[:routed], w_q[...]) + logit * route_q[...].astype(F32)
        k_rows[own_at, :] = dot_t(dkv[:routed, :], w_kv[...])
        at = r * span
        total[at : at + span, :] = dnorm[at : at + span, :]
        total[at : at + RADIUS, :] += from_left[r].astype(F32)
        total[at + span - RADIUS : at + span, :] += from_right[r].astype(F32)
        for k in range(routed):
            for route, part in ((q_route, q_rows), (k_route, k_rows)):
                spot = route[r, me * routed + k] - me * span
                row = pl.ds(at + spot, 1)
                total[row, :] = total[row, :] + part[pl.ds(r * routed + k, 1), :]
    hidden = tokens[...].reshape(rows * span, width).astype(F32)
    factor = row_factor(hidden)
    weighted = total[...] * gain[...]
    inner = jnp.mean(weighted * hidden, axis=-1, keepdims=True)
    d_hidden = dmid[...] + factor * weighted - hidden * (factor * factor * factor) * inner
    grad_tokens[...] = d_hidden.astype(BF16).reshape(grad_tokens.shape)
    own_gain = jnp.sum(own_full * gain[...], axis=1, keepdims=True)
    own_route = jnp.sum(own_full * route_q[...].astype(F32), axis=1, keepdims=True)
    gain_grad = jnp.sum(dot(own, w_q[...]) * q_grad, axis=1, keepdims=True)
    gain_grad = gain_grad + jnp.sum(dot(own, w_kv[...]) * kv_grad, axis=1, keepdims=True)
    gain_grad = (gain_grad + own_route * route_grad) / own_gain
    lane = lax.broadcasted_iota(jnp.int32, (block, LANES), 1)
    sums = jnp.sum(proj_all[:, 0, 0:1, width:].astype(F32), axis=0)
    sums = jnp.broadcast_to(sums, (8, LANES))
    sums = sums + pltpu.roll(sums, LANES - 8, 1) + pltpu.roll(sums, LANES - 16, 1)
    sums = jnp.where(lane[:8] < 8, sums, 0.0)
    vectors = jnp.where(lane == 0, gain_grad, jnp.where(lane == 1, route_grad, 0.0))
    own_sums = pltpu.roll(sums, 8, 1)[0:1, :]
    sent_sums = jnp.zeros((1, LANES), F32)
    for k, part in enumerate(three_parts(sums)):
        sent_sums = sent_sums + pltpu.roll(part, 8 + 8 * k, 1)[0:1, :]
    at = 0
    for grad in (q_grad, kv_grad, out_grad):
        mine, other = halves_of(grad, place)
        size = mine.shape[1]
        kept[:, at : at + size] = mine
        sent[:, at : at + size] = other.astype(BF16)
        at += size
    kept[:, at:] = vectors + own_sums
    sent[:, at:] = (vectors + sent_sums).astype(BF16)


def fold_kernel(pieces, count, *refs):
    ins, outs = refs[: 2 * count], refs[2 * count :]
    for out, parts in zip(outs, pieces):
        for target, pair, index in parts:
            value = ins[2 * pair][index].astype(F32) + ins[2 * pair + 1][index].astype(F32)
            out[target] = value.astype(out.dtype)


def finish_light_kernel(kept, received, *outs):
    total = kept[0, 0].astype(F32) + received[0, 0].astype(F32)
    base = 0
    for ref in outs:
        block = ref.shape[0]
        for c in range(ref.shape[1] // LANES):
            ref[:, c * LANES : (c + 1) * LANES] = total[base : base + block]
            base += block


def finish_heavy_kernel(
    groups, heavy_kept, heavy_got, down_kept, down_got, own_piece, piece_one, piece_two, piece_three,
    q_out, kv_out, out_out, vectors, stats, down_out, gate_up_out,
):
    me = lax.axis_index("seq")
    total = heavy_kept[...] + heavy_got[...].astype(F32)
    at = 0
    for ref in (q_out, kv_out, out_out, vectors):
        ref[...] = total[:, at : at + ref.shape[1]]
        at += ref.shape[1]
    sums = total[:8, at - LANES :]
    stats[...] = sums + pltpu.roll(sums, LANES - 8, 1) + pltpu.roll(sums, LANES - 16, 1)
    down_out[...] = down_kept[...] + down_got[...].astype(F32)
    pieces = (own_piece, piece_one, piece_two, piece_three)
    group = len(pieces)
    low_place = lax.rem(me, group)
    unit = own_piece.shape[1] // groups
    for j, piece in enumerate(pieces):
        for z in range(groups):
            at = pl.multiple_of((z * group + (low_place ^ j)) * unit, unit)
            gate_up_out[:, pl.ds(at, unit)] = piece[:, z * unit : (z + 1) * unit].astype(F32)


def fold(pairs, outs):
    flat = [ref for pair in pairs for ref in pair]
    kernel = functools.partial(fold_kernel, [parts for _, _, parts in outs], len(pairs))
    moved = sum(v.size * v.dtype.itemsize for v in flat)
    return call(kernel, [shape(dims, dtype) for dims, dtype, _ in outs], flat, moved=2 * moved)


def scatter_folds(kept, sent):
    devices = lax.axis_size("seq")
    slots, _, rows, _ = kept.shape
    part, quarter = rows // 2, slots // 2
    every = slice(None)
    low, high = slice(0, part), slice(part, rows)
    one, two = slice(0, 1), slice(1, 2)
    near, far = slice(0, quarter), slice(quarter, slots)
    left_keep, left_sent, right_keep, right_sent = fold(
        [(kept, swap(sent, "seq", 1))],
        [
            ((quarter, 2, part, LANES), BF16, [(every, 0, (near, every, low))]),
            ((quarter, 2, part, LANES), BF16, [(every, 0, (far, every, low))]),
            ((slots, 1, part, LANES), BF16, [(every, 0, (every, one, high))]),
            ((slots, 1, part, LANES), BF16, [(every, 0, (every, two, high))]),
        ],
    )
    left_got, right_got = swap(left_sent, "seq", 2), swap(right_sent, "dp", 1)
    left_keep, left_sent, right_keep, right_sent = fold(
        [(left_keep, left_got), (right_keep, right_got)],
        [
            ((quarter, 1, part, LANES), BF16, [(every, 0, (every, one))]),
            ((quarter, 1, part, LANES), BF16, [(every, 0, (every, two))]),
            ((quarter, 1, part, LANES), BF16, [(every, 1, near)]),
            ((quarter, 1, part, LANES), BF16, [(every, 1, far)]),
        ],
    )
    left_got, right_got = swap(left_sent, "dp", 1), swap(right_sent, "seq", 2)
    pairs = [(left_keep, left_got), (right_keep, right_got)]
    count, bit = quarter, 4
    while bit < devices:
        half = count // 2
        halves = (slice(0, half), slice(half, count))
        if len(pairs) == 2:
            wants = [
                [((every, every, low), 0, side), ((every, every, high), 1, side)] for side in halves
            ]
        else:
            wants = [[(every, 0, side)] for side in halves]
        kept, sent = fold(pairs, [((half, 1, rows, LANES), BF16, want) for want in wants])
        pairs = [(kept, swap(sent, "seq", bit))]
        count, bit = half, 2 * bit
    return pairs[0]


def local_kernels(
    tokens,
    segments,
    query_route,
    kv_route,
    ffn_route,
    grad_out,
    attn_gain,
    light_qkv,
    light_out,
    heavy_q,
    heavy_kv,
    heavy_out,
    route_query,
    ffn_gain,
    light_gate_up,
    light_down,
    heavy_gate_up,
    heavy_down,
    route_ffn,
):
    rows, span, width = tokens.shape
    devices = lax.axis_size("seq")
    routed = query_route.shape[1] // devices
    own, count = rows * span, rows * routed
    extent = span + 2 * RADIUS
    block = width // devices
    light_heads = width // DL
    ffn_light, ffn_heavy = light_down.shape[0], heavy_down.shape[0]
    attn_gain, ffn_gain, route_query, route_ffn = (
        v.reshape(1, width) for v in (attn_gain, ffn_gain, route_query, route_ffn)
    )
    marked = width + LANES

    rim = shape((rows, RADIUS + 16, width), BF16)
    keys, upper, lower = call(
        functools.partial(first_kernel, routed),
        [shape((rows, routed, marked), BF16), rim, rim],
        [kv_route, segments, tokens, segments, attn_gain],
        smem=2,
        scratch=[pltpu.VMEM((own, width), F32), pltpu.VMEM((count, marked), F32)],
    )
    before = shifted(upper, "seq", 1)
    after = shifted(lower, "seq", -1)
    keys_all = gather_blocks(keys)

    normed, query, keyval, probs, mix, attn = call(
        light_kernel,
        [
            shape((rows * extent, width), BF16),
            shape((own, width), BF16),
            shape((rows * extent, 2 * width), BF16),
            shape((rows * light_heads, extent, span), BF16),
            shape((own, width), BF16),
            shape((own, width), F32),
        ],
        [before, tokens, after, segments, attn_gain, light_qkv, light_out],
        scratch=[pltpu.VMEM((8, 3 * span), F32), pltpu.VMEM((width, span), F32)],
        flops=4 * 10**9,
        moved=8 * 10**6,
    )

    small = shape((count, width), F32)
    middle, normed_two, keyval_all, payload, q_rows, f_rows, f_up, proj, f_marks, stats = call(
        functools.partial(middle_kernel, routed),
        [
            shape((own, width), F32),
            shape((own, width), BF16),
            shape((devices, rows, routed, 2 * width), BF16),
            shape((rows, routed, 3 * width + LANES), BF16),
            small,
            small,
            small,
            small,
            shape((count, LANES), F32),
            shape((8, LANES), F32),
        ],
        [
            query_route, ffn_route, segments, tokens, segments, keys_all, attn, grad_out,
            attn_gain, ffn_gain, heavy_q, heavy_kv, heavy_out, route_query, route_ffn,
        ],
        smem=3,
        scratch=[
            pltpu.VMEM((own, width), F32),
            pltpu.VMEM((count, LANES), F32),
            pltpu.VMEM((count, width), F32),
        ],
        flops=2 * 10**9,
        moved=10**7,
    )
    routed_all = gather_blocks(payload)

    steps = 4
    whole = lambda *dims: pl.BlockSpec(dims, lambda j: (0,) * len(dims))
    light_unit, heavy_unit = ffn_light // steps, ffn_heavy // steps
    columns = lambda unit, at: pl.BlockSpec((width, unit), lambda j: (0, at + j))
    downs = lambda unit: pl.BlockSpec((unit, width), lambda j: (j, 0))
    share = pl.BlockSpec((own, light_unit), lambda j: (0, j))
    outputs, dmid, dmid_low, hidden, grad_gate, grad_up, proj_payload, vectors = pl.pallas_call(
        functools.partial(ffn_kernel, routed),
        grid=(steps,),
        out_shape=[
            shape((rows, span, width), BF16),
            shape((own, width), F32),
            shape((own, width), BF16),
            shape((own, ffn_light), BF16),
            shape((own, ffn_light), BF16),
            shape((own, ffn_light), BF16),
            shape((rows, routed, marked), BF16),
            shape((8, width), F32),
        ],
        in_specs=[
            SMEM,
            SMEM,
            whole(own, width),
            whole(rows, span, width),
            whole(own, width),
            columns(light_unit, 0),
            columns(light_unit, steps),
            downs(light_unit),
            columns(heavy_unit, 0),
            columns(heavy_unit, steps),
            downs(heavy_unit),
        ]
        + [whole(count, width)] * 4
        + [whole(count, LANES)]
        + [whole(1, width)] * 3
        + [whole(8, LANES), whole(rows, span)],
        out_specs=[
            whole(rows, span, width),
            whole(own, width),
            whole(own, width),
            share,
            share,
            share,
            whole(rows, routed, marked),
            whole(8, width),
        ],
        scratch_shapes=[pltpu.VMEM((own, width), F32)] * 2
        + [pltpu.VMEM((count, width), F32)] * 3
        + [pltpu.VMEM((own, width), F32)],
        compiler_params=pltpu.CompilerParams(vmem_limit_bytes=VMEM_BYTES),
        cost_estimate=pl.CostEstimate(flops=10**10, bytes_accessed=3 * 10**7, transcendentals=0),
    )(
        query_route, ffn_route, normed_two, grad_out, middle, light_gate_up, light_gate_up, light_down,
        heavy_gate_up, heavy_gate_up, heavy_down, q_rows, f_rows, f_up, proj, f_marks,
        ffn_gain, route_query, route_ffn, stats, segments,
    )
    proj_all = gather_blocks(proj_payload)

    slot_rows = (
        block * ffn_light // LANES
        + ffn_light // devices * (width // 2) // LANES
        + block * (width // 2) // LANES
        + block
    )
    slots = shape((devices // 2, 2, slot_rows, LANES), BF16)
    kept, sent = call(
        first_grads_kernel,
        [slots, slots],
        [normed_two, grad_gate, grad_up, hidden, grad_out, mix, dmid_low, vectors],
        flops=3 * 10**9,
        moved=8 * 10**6,
    )
    first_pair = scatter_folds(kept, sent)

    slot_rows = block * (3 * width // 2) // LANES + block
    slots = shape((devices // 2, 2, slot_rows, LANES), BF16)
    rim = shape((rows, RADIUS, width), BF16)
    dnorm, to_right, to_left, kept, sent = call(
        light_back_kernel,
        [shape((own, width), F32), rim, rim, slots, slots],
        [dmid_low, query, keyval, probs, normed, attn_gain, light_qkv, light_out],
        scratch=[
            pltpu.VMEM((rows * extent, 3 * width), BF16),
            pltpu.VMEM((extent, 2 * width), F32),
            pltpu.VMEM((width, span), F32),
        ],
        flops=6 * 10**9,
        moved=10**7,
    )
    from_left = shifted(to_right, "seq", 1)
    from_right = shifted(to_left, "seq", -1)
    second_pair = scatter_folds(kept, sent)

    group = min(4, devices)
    groups = devices // group
    unit = ffn_heavy // devices
    me = lax.axis_index("seq").astype(jnp.int32).reshape(1)
    at_whole = lambda *dims: pl.BlockSpec(dims, lambda z, at: (0,) * len(dims))
    hidden_block = lambda start: pl.BlockSpec(
        (width, unit), lambda z, at: (0, start + z * group + lax.rem(at[0], group))
    )
    gate_kept, gate_sent, down_kept, down_sent = pl.pallas_call(
        heavy_ffn_kernel,
        grid_spec=pltpu.PrefetchScalarGridSpec(
            num_scalar_prefetch=1,
            grid=(groups,),
            in_specs=[
                at_whole(*routed_all.shape),
                hidden_block(0),
                hidden_block(devices),
                pl.BlockSpec((unit, width), lambda z, at: (z * group + lax.rem(at[0], group), 0)),
            ],
            out_specs=[pl.BlockSpec((group * block, unit), lambda z, at: (0, z))] * 2
            + [at_whole(unit, width // 2)] * 2,
            scratch_shapes=[pltpu.VMEM((group * block, devices * count), BF16)],
        ),
        out_shape=[
            shape((group * block, groups * unit), F32),
            shape((group * block, groups * unit), BF16),
            shape((unit, width // 2), F32),
            shape((unit, width // 2), BF16),
        ],
        compiler_params=pltpu.CompilerParams(vmem_limit_bytes=VMEM_BYTES),
        cost_estimate=pl.CostEstimate(flops=4 * 10**9, bytes_accessed=10**7, transcendentals=0),
    )(me, routed_all, heavy_gate_up, heavy_gate_up, heavy_down)
    down_got = swap(down_sent, "dp", 1)
    rows_of = lambda j: slice(j * block, (j + 1) * block)
    pieces = fold(
        [(gate_kept, swap(gate_sent, "dp", 1))],
        [
            ((block, groups * unit), F32 if j == 0 else BF16, [(slice(None), 0, rows_of(j))])
            for j in range(group)
        ],
    )
    pieces = [pieces[0]] + [swap(pieces[j], "seq", j) for j in range(1, group)]

    grad_tokens, heavy_kept, heavy_sent = call(
        functools.partial(heavy_back_kernel, routed),
        [
            shape((rows, span, width), BF16),
            shape((block, 2 * width + LANES), F32),
            shape((block, 2 * width + LANES), BF16),
        ],
        [
            query_route, kv_route, routed_all, proj_all, keyval_all, keys_all, dnorm, from_left, from_right,
            dmid, tokens, attn_gain, heavy_q, heavy_kv, heavy_out, route_query,
        ],
        smem=2,
        scratch=[
            pltpu.VMEM((own, width), F32),
            pltpu.VMEM((count, width), F32),
            pltpu.VMEM((count, width), F32),
            pltpu.VMEM((width, devices * routed), BF16),
            pltpu.VMEM((width, devices * routed), F32),
            pltpu.VMEM((devices * routed, 2 * width), BF16),
        ],
        flops=8 * 10**9,
        moved=2 * 10**7,
    )
    heavy_got = swap(heavy_sent, "dp", 1)
    heavy_q_grad, heavy_kv_grad, heavy_out_grad, heavy_vectors, stats, heavy_down_grad, heavy_gate_up_grad = call(
        functools.partial(finish_heavy_kernel, groups),
        [
            shape((block, width // 2), F32),
            shape((block, width), F32),
            shape((block, width // 2), F32),
            shape((block, LANES), F32),
            shape((8, LANES), F32),
            shape((unit, width // 2), F32),
            shape((block, ffn_heavy), F32),
        ],
        [heavy_kept, heavy_got, down_kept, down_got, *pieces],
    )
    light_gate_up_grad, light_down_grad, light_out_grad, first_vectors = call(
        finish_light_kernel,
        [
            shape((block, ffn_light), F32),
            shape((ffn_light // devices, width // 2), F32),
            shape((block, width // 2), F32),
            shape((block, LANES), F32),
        ],
        first_pair,
    )
    light_qkv_grad, second_vectors = call(
        finish_light_kernel,
        [shape((block, 3 * width // 2), F32), shape((block, LANES), F32)],
        second_pair,
    )
    sums = stats[0, 8:14]
    return (
        outputs,
        grad_tokens,
        second_vectors[:, 0] + heavy_vectors[:, 0],
        light_qkv_grad,
        light_out_grad,
        heavy_q_grad,
        heavy_kv_grad,
        heavy_out_grad,
        heavy_vectors[:, 1],
        first_vectors[:, 0],
        light_gate_up_grad,
        light_down_grad,
        heavy_gate_up_grad,
        heavy_down_grad,
        first_vectors[:, 1],
        jnp.sqrt(sums[:5] / (sums[5] * width)),
    )


def local(tokens, segments, query_route, *others):
    block = tokens.shape[2] // lax.axis_size("seq")
    fits = query_route.shape[1] <= 256 and block % 16 == 0
    return (local_kernels if fits else local_wide)(tokens, segments, query_route, *others)


def solution(mesh):
    placed = (
        P("dp", "seq", None),
        P("dp", "seq"),
        P("dp", None),
        P("dp", None),
        P("dp", "seq"),
        P("dp", "seq", None),
    ) + (P(),) * 13
    matrix = P("seq", "dp")
    vector = P("seq")
    return jax.shard_map(
        local,
        mesh=mesh,
        in_specs=placed,
        out_specs=(
            P("dp", "seq", None),
            P("dp", "seq", None),
            vector,
            matrix,
            matrix,
            matrix,
            matrix,
            matrix,
            vector,
            vector,
            matrix,
            matrix,
            matrix,
            matrix,
            vector,
            P(),
        ),
        check_vma=False,
    )
```

```python
import functools
import math

import jax
import jax.numpy as jnp
from jax import lax
from jax.experimental import pallas as pl
from jax.experimental.pallas import tpu as pltpu
from jax.sharding import PartitionSpec as P

DL = 96
DH = 64
RADIUS = 64
LANES = 128


PRECISE = lax.Precision.HIGHEST
EPSILON = 1e-06
NEG_FILL = -1e30
F32 = jnp.float32
BF16 = jnp.bfloat16


def swap(value, axis, bit):
    return lax.ppermute(value, axis, [(i, i ^ bit) for i in range(lax.axis_size(axis))])


def shifted(block, axis, distance):
    devices = range(lax.axis_size(axis))
    route = [(i - distance, i) for i in devices if i - distance in devices]
    return lax.ppermute(block, axis, route)


def gather_blocks(block):
    held = block[None]
    bit = lax.axis_size("seq") // 2
    while bit:
        held = jnp.concatenate([held, swap(held, "seq", bit)], axis=0)
        bit //= 2
    return held


def add_halves(value, dim, axis, bit, out_type=BF16):
    half = value.shape[dim] // 2
    keep = lax.slice_in_dim(value, 0, half, axis=dim)
    sent = lax.slice_in_dim(value, half, 2 * half, axis=dim)
    return (keep.astype(F32) + swap(sent, axis, bit).astype(F32)).astype(out_type)


def scatter_sum(slots):
    devices = lax.axis_size("seq")
    rows = slots.shape[2]
    slots = add_halves(slots, 0, "seq", 1)
    left, right = slots[:, :, : rows // 2], slots[:, :, rows // 2 :]
    left = add_halves(left, 0, "seq", 2)
    right = add_halves(right, 1, "dp", 1)
    left = add_halves(left, 1, "dp", 1)
    right = add_halves(right, 0, "seq", 2)
    both = jnp.concatenate([left, right], axis=2)
    bit = 4
    while bit < devices:
        both = add_halves(both, 0, "seq", bit, BF16 if 2 * bit < devices else F32)
        bit *= 2
    return both[0, 0]


def slot_places(me, devices):
    bits = devices.bit_length() - 1
    places = [int(format(p, f"0{bits}b")[::-1], 2) for p in range(devices)]
    return jnp.array(places, jnp.int32) ^ me


def slot_columns(value, me, devices):
    width = value.shape[-1]
    block = width // devices
    order = (slot_places(me, devices)[:, None] * block + jnp.arange(block)[None, :]).reshape(-1)
    onehot = (jnp.arange(width)[:, None] == order[None, :]).astype(BF16)
    return jnp.dot(value, onehot, preferred_element_type=F32).astype(BF16)


def own_half_first(value, place):
    half = value.shape[-1] // 2
    first, second = value[..., :half], value[..., half:]
    return (jnp.where(place == 0, first, second), jnp.where(place == 0, second, first))


def slot_block(grad_halves, devices):
    stacked = jnp.stack(grad_halves)
    _, total, cols = stacked.shape
    parts = stacked.reshape(2, devices, total // devices, cols // LANES, LANES)
    return parts.transpose(1, 0, 3, 2, 4).reshape(devices, 2, -1, LANES).astype(BF16)


def unslot(rows, cols):
    return rows.reshape(cols // LANES, -1, LANES).transpose(1, 0, 2).reshape(-1, cols)


def slot_vectors(vectors, me, devices):
    block = vectors[0].shape[0] // devices
    table = jnp.stack(vectors, axis=-1).reshape(devices, block, len(vectors))
    table = jnp.take(table, slot_places(me, devices), axis=0)
    table = jnp.pad(table, ((0, 0), (0, 0), (0, LANES - len(vectors))))
    return jnp.broadcast_to(table[:, None], (devices, 2, block, LANES)).astype(BF16)


def split_parts(value):
    high = lax.reduce_precision(value, 8, 7)
    middle = lax.reduce_precision(value - high, 8, 7)
    return (high, middle, value - high - middle)


def rms_factor(hidden):
    return lax.rsqrt(jnp.mean(hidden * hidden, axis=-1, keepdims=True) + EPSILON)


def norm_back(hidden, factor, gain_vec, upstream):
    weighted = upstream * gain_vec
    inner_mean = jnp.mean(weighted * hidden, axis=-1, keepdims=True)
    return factor * weighted - hidden * (factor * factor * factor) * inner_mean


def pick_rows(source, positions):
    return jnp.take_along_axis(source, positions[..., None], axis=1)


def place_rows(values, positions, extent):
    onehot = (positions[..., None] == jnp.arange(extent)[None, None, :]).astype(F32)
    return jnp.einsum("rqs,rqd->rsd", onehot, values, precision=PRECISE)


def matmul(left, right):
    return jnp.einsum("...d,de->...e", left, right, preferred_element_type=F32)


def matmul_t(left, right):
    return jnp.einsum("...e,de->...d", left, right, preferred_element_type=F32)


def outer(left, right):
    return jnp.einsum("rsd,rse->de", left, right, preferred_element_type=F32)


def glu_value(gate_part, up_part):
    return jax.nn.gelu(gate_part, approximate=True) * up_part


def geglu(inputs, gate_up, down, upstream_low):
    width = down.shape[0]
    both = matmul(inputs, gate_up)
    gate_part, up_part = both[..., :width], both[..., width:]
    hidden, pull_back = jax.vjp(glu_value, gate_part, up_part)
    gate_grad, up_grad = pull_back(matmul_t(upstream_low, down))
    return (hidden.astype(BF16), gate_grad.astype(BF16), up_grad.astype(BF16))


def routed_probs(query_heads, key_heads, query_seg, key_seg):
    scores = jnp.einsum("rqd,rkd->rqk", query_heads, key_heads, preferred_element_type=F32)
    scores = scores / math.sqrt(DH)
    allowed = query_seg[:, :, None] == key_seg[:, None, :]
    scores = jnp.where(allowed, scores, NEG_FILL)
    peak = jnp.maximum(jnp.max(scores, axis=-1, keepdims=True), 0.0)
    numer = jnp.exp(scores - peak)
    return numer / (jnp.exp(-peak) + jnp.sum(numer, axis=-1, keepdims=True))


def heavy_forward(query, keys, vals, query_seg, key_seg):
    def head(parts):
        query_h, key_h, val_h = parts
        probs = routed_probs(query_h, key_h, query_seg, key_seg).astype(BF16)
        return jnp.einsum("rqk,rkd->rqd", probs, val_h, preferred_element_type=F32).astype(BF16)

    return join_heads(jax.vmap(head)((split_heads(query), split_heads(keys), split_heads(vals))))


def heavy_both(query, keys, vals, query_seg, key_seg, mix_grad):
    def head(parts, query_seg=query_seg, key_seg=key_seg):
        query_h, key_h, val_h, grad_h = parts
        probs = routed_probs(query_h, key_h, query_seg, key_seg)
        probs_low = probs.astype(BF16)
        mix = jnp.einsum("rqk,rkd->rqd", probs_low, val_h, preferred_element_type=F32)
        prob_grad = jnp.einsum("rqd,rkd->rqk", grad_h, val_h, preferred_element_type=F32)
        delta = jnp.sum(probs * prob_grad, axis=-1, keepdims=True)
        score_grad = (probs * (prob_grad - delta)).astype(BF16)
        dquery = jnp.einsum("rqk,rkd->rqd", score_grad, key_h, preferred_element_type=F32)
        dkey = jnp.einsum("rqk,rqd->rkd", score_grad, query_h, preferred_element_type=F32)
        dval = jnp.einsum("rqk,rqd->rkd", probs_low, grad_h, preferred_element_type=F32)
        scale = 1.0 / math.sqrt(DH)
        return (mix.astype(BF16), (dquery * scale).astype(BF16), (dkey * scale).astype(BF16), dval.astype(BF16))

    heads = tuple(split_heads(v) for v in (query, keys, vals, mix_grad))
    if query.shape[1] <= 512:
        return tuple(join_heads(v) for v in jax.vmap(head)(heads))
    count, rows = heads[0].shape[:2]
    place = jnp.tile(jnp.arange(rows), count)
    parts = tuple(v.reshape(count * rows, 1, *v.shape[2:]) for v in heads)
    done = lax.map(lambda p: head(p[0], query_seg[p[1]][None], key_seg[p[1]][None]), (parts, place))
    return tuple(join_heads(v.reshape(count, rows, *v.shape[2:])) for v in done)


def split_heads(value):
    rows, tokens, width = value.shape
    return value.reshape(rows, tokens, width // DH, DH).transpose(2, 0, 1, 3)


def join_heads(value):
    heads, rows, tokens, width = value.shape
    return value.transpose(1, 2, 0, 3).reshape(rows, tokens, heads * width)


def tokens_of(blocks):
    devices, rows, count, width = blocks.shape
    return blocks.transpose(1, 0, 2, 3).reshape(rows, devices * count, width)


def with_segment(rows, segs):
    marks = jnp.broadcast_to((segs + 2).astype(BF16)[..., None], segs.shape + (LANES,))
    return jnp.concatenate([rows, marks], axis=-1)


def local_wide(
    tokens,
    segments,
    query_route,
    kv_route,
    ffn_route,
    grad_out,
    attn_gain,
    light_qkv,
    light_out,
    heavy_q,
    heavy_kv,
    heavy_out,
    route_query,
    ffn_gain,
    light_gate_up,
    light_down,
    heavy_gate_up,
    heavy_down,
    route_ffn,
):
    row_count, seg_span, width = tokens.shape
    light_heads = width // DL
    ffn_heavy = heavy_down.shape[0]
    devices = lax.axis_size("seq")
    me = lax.axis_index("seq")
    half_place = lax.axis_index("dp")
    anchor = me * seg_span
    routed_own = query_route.shape[1] // devices
    own_query = lax.dynamic_slice_in_dim(query_route, me * routed_own, routed_own, 1) - anchor
    own_key = lax.dynamic_slice_in_dim(kv_route, me * routed_own, routed_own, 1) - anchor
    own_ffn = ffn_route - anchor

    marked = with_segment(tokens, segments)
    before = shifted(marked[:, seg_span - RADIUS :], "seq", 1)
    after = shifted(marked[:, :RADIUS], "seq", -1)
    hidden = tokens.astype(F32)
    factor_one = rms_factor(hidden)
    normed = hidden * factor_one * attn_gain
    normed_low = normed.astype(BF16)
    key_rows = pick_rows(normed_low, own_key)
    key_payload = with_segment(key_rows, jnp.take_along_axis(segments, own_key, axis=1))
    key_blocks = tokens_of(gather_blocks(key_payload))
    key_all, key_seg = key_blocks[..., :width], key_blocks[..., width]

    extended = jnp.concatenate([before, marked, after], axis=1)
    seg_ext = extended[..., width]
    hidden_ext = extended[..., :width].astype(F32)
    factor_ext = rms_factor(hidden_ext)
    normed_ext_low = (hidden_ext * factor_ext * attn_gain).astype(BF16)
    extent = seg_span + 2 * RADIUS
    query_low = matmul(normed_low, light_qkv[:, :width]).astype(BF16)
    query_low = query_low.reshape(row_count, seg_span, light_heads, DL)
    kv_ext = matmul(normed_ext_low, light_qkv[:, width:]).astype(BF16)
    key_ext = kv_ext[..., :width].reshape(row_count, extent, light_heads, DL)
    val_ext = kv_ext[..., width:].reshape(row_count, extent, light_heads, DL)
    offset = jnp.arange(seg_span)[:, None] - jnp.arange(extent)[None, :] + RADIUS
    seg_own = seg_ext[:, RADIUS : RADIUS + seg_span]
    allowed = (jnp.abs(offset) <= RADIUS)[None] & (seg_own[:, :, None] == seg_ext[:, None, :])
    light_scale = 1.0 / math.sqrt(DL)
    scores = jnp.einsum("rqhd,rkhd->rhqk", query_low, key_ext, preferred_element_type=F32)
    scores = jnp.where(allowed[:, None], scores * light_scale, NEG_FILL)
    numerators = jnp.exp(scores - jnp.max(scores, axis=-1, keepdims=True))
    probs_light = numerators / jnp.sum(numerators, axis=-1, keepdims=True)
    probs_low = probs_light.astype(BF16)
    light_mix = jnp.einsum("rhqk,rkhd->rqhd", probs_low, val_ext, preferred_element_type=F32)
    light_mix = light_mix.reshape(row_count, seg_span, width).astype(BF16)
    light_attn = matmul(light_mix, light_out)

    query_rows = pick_rows(normed_low, own_query)
    query_seg_own = (jnp.take_along_axis(segments, own_query, axis=1) + 2).astype(BF16)
    heavy_query = matmul(query_rows, heavy_q).astype(BF16)
    keyval_all = matmul(key_all, heavy_kv).astype(BF16)
    heavy_width = heavy_q.shape[1]
    keys_all, vals_all = keyval_all[..., :heavy_width], keyval_all[..., heavy_width:]
    heavy_mix = heavy_forward(heavy_query, keys_all, vals_all, query_seg_own, key_seg)
    heavy_proj = matmul(heavy_mix, heavy_out)
    query_normed = pick_rows(normed, own_query)
    route_query_full = route_query.astype(F32)
    query_gate = jax.nn.sigmoid(jnp.sum(query_normed * route_query_full, axis=-1))
    heavy_attn = place_rows(query_gate[..., None] * heavy_proj, own_query, seg_span)

    middle = hidden + light_attn + heavy_attn
    factor_two = rms_factor(middle)
    normed_two = middle * factor_two * ffn_gain
    low_two = normed_two.astype(BF16)
    upstream = grad_out.astype(F32)
    ffn_normed = pick_rows(normed_two, own_ffn)
    ffn_rows = ffn_normed.astype(BF16)
    route_ffn_full = route_ffn.astype(F32)
    ffn_gate = jax.nn.sigmoid(jnp.sum(ffn_normed * route_ffn_full, axis=-1))
    ffn_upstream = pick_rows(upstream, own_ffn)
    ffn_low = (ffn_upstream * ffn_gate[..., None]).astype(BF16)
    routed_payload = with_segment(
        jnp.concatenate([ffn_rows, ffn_low, query_rows], axis=-1),
        jnp.take_along_axis(segments, own_query, axis=1),
    )
    routed_blocks = tokens_of(gather_blocks(routed_payload))
    ffn_all = routed_blocks[..., :width]
    ffn_low_all = routed_blocks[..., width : 2 * width]
    query_all = routed_blocks[..., 2 * width : 3 * width]
    query_seg = routed_blocks[..., 3 * width]

    hidden_light, gate_grad, up_grad = geglu(low_two, light_gate_up, light_down, grad_out)
    light_ff = matmul(hidden_light, light_down)
    light_both = jnp.concatenate([gate_grad, up_grad], axis=-1)
    normed_two_grad = matmul_t(light_both, light_gate_up)
    hidden_heavy, gate_grad_h, up_grad_h = geglu(ffn_rows, heavy_gate_up, heavy_down, ffn_low)
    heavy_ffn_proj = matmul(hidden_heavy, heavy_down)
    heavy_ff = place_rows(ffn_gate[..., None] * heavy_ffn_proj, own_ffn, seg_span)
    outputs = (middle + light_ff + heavy_ff).astype(BF16)
    ffn_gate_grad = jnp.sum(ffn_upstream * heavy_ffn_proj, axis=-1)
    ffn_logit_grad = ffn_gate_grad * ffn_gate * (1.0 - ffn_gate)
    route_ffn_grad = jnp.sum(ffn_logit_grad[..., None] * ffn_normed, axis=(0, 1))
    ffn_rows_grad = matmul_t(jnp.concatenate([gate_grad_h, up_grad_h], axis=-1), heavy_gate_up)
    ffn_rows_grad = ffn_rows_grad + ffn_logit_grad[..., None] * route_ffn_full
    normed_two_grad = normed_two_grad + place_rows(ffn_rows_grad, own_ffn, seg_span)
    ffn_gain_grad = jnp.sum(normed_two_grad * middle * factor_two, axis=(0, 1))
    middle_grad = upstream + norm_back(middle, factor_two, ffn_gain, normed_two_grad)
    middle_low = middle_grad.astype(BF16)

    valid_rows = (segments >= 0).astype(F32)[..., None]
    sums = jnp.stack(
        [
            jnp.sum(valid_rows * branch * branch)
            for branch in (hidden, light_attn, heavy_attn, light_ff, heavy_ff)
        ]
        + [jnp.sum(valid_rows)]
    )
    heavy_upstream = pick_rows(middle_grad, own_query)
    query_gate_grad = jnp.sum(heavy_upstream * heavy_proj, axis=-1)
    proj_low = (heavy_upstream * query_gate[..., None]).astype(BF16)
    sum_lanes = jnp.pad(jnp.concatenate(split_parts(sums)), (0, LANES - 18)).astype(BF16)
    sum_lanes = jnp.broadcast_to(sum_lanes, proj_low.shape[:2] + (LANES,))
    proj_blocks = gather_blocks(jnp.concatenate([proj_low, sum_lanes], axis=-1))
    sums_all = jnp.sum(proj_blocks[:, 0, 0, width : width + 18].astype(F32), axis=0)
    sums_all = jnp.sum(sums_all.reshape(3, 6), axis=0)
    sums_all = sums_all + swap(sums_all, "dp", 1)
    rms_stats = jnp.sqrt(sums_all[:5] / (sums_all[5] * width))
    proj_all = tokens_of(proj_blocks)[..., :width]

    flat = lambda v: v.reshape(-1, v.shape[-1])
    gate_up_grad = [
        jnp.dot(slot_columns(flat(low_two), me, devices).T, flat(part), preferred_element_type=F32)
        for part in own_half_first(light_both, half_place)
    ]
    hidden_slots = slot_columns(flat(hidden_light), me, devices).T
    down_grad = [
        jnp.dot(hidden_slots, flat(part), preferred_element_type=F32)
        for part in own_half_first(grad_out, half_place)
    ]
    mix_slots = slot_columns(flat(light_mix), me, devices).T
    out_grad = [
        jnp.dot(mix_slots, flat(part), preferred_element_type=F32)
        for part in own_half_first(middle_low, half_place)
    ]
    first_sum = scatter_sum(
        jnp.concatenate(
            [
                slot_block(gate_up_grad, devices),
                slot_block(down_grad, devices),
                slot_block(out_grad, devices),
                slot_vectors((ffn_gain_grad, route_ffn_grad), me, devices),
            ],
            axis=2,
        )
    )
    block = width // devices
    block_ff = light_down.shape[0] // devices
    cuts = [0]
    for rows in (
        block * light_gate_up.shape[1] // 2 // LANES,
        block_ff * width // 2 // LANES,
        block * width // 2 // LANES,
        block,
    ):
        cuts.append(cuts[-1] + rows)
    light_gate_up_grad = unslot(first_sum[cuts[0] : cuts[1]], light_gate_up.shape[1] // 2)
    light_down_grad = unslot(first_sum[cuts[1] : cuts[2]], width // 2)
    light_out_grad = unslot(first_sum[cuts[2] : cuts[3]], width // 2)
    ffn_gain_grad = first_sum[cuts[3] : cuts[4], 0]
    route_ffn_grad = first_sum[cuts[3] : cuts[4], 1]

    group = min(4, devices)
    low_place, high_place = me % group, me // group
    groups = devices // group
    unit = ffn_heavy // devices
    gate_up_parts = heavy_gate_up.reshape(width, 2, groups, group, unit)
    gate_up_mine = lax.dynamic_index_in_dim(gate_up_parts, low_place, 3, False)
    down_mine = lax.dynamic_index_in_dim(
        heavy_down.reshape(groups, group, unit, width), low_place, 1, False
    )
    x_all = flat(ffn_all)
    up_all = flat(ffn_low_all)
    hidden_mine, gate_mine, up_mine = geglu(
        x_all,
        gate_up_mine.reshape(width, -1),
        down_mine.reshape(-1, width),
        up_all,
    )
    hidden_block = lax.dynamic_slice_in_dim(hidden_mine, high_place * unit, unit, 1)
    heavy_down_half = [
        jnp.dot(hidden_block.T, part, preferred_element_type=F32)
        for part in own_half_first(up_all, half_place)
    ]
    heavy_down_grad = heavy_down_half[0] + swap(heavy_down_half[1].astype(BF16), "dp", 1).astype(F32)
    x_group = lax.dynamic_slice_in_dim(x_all, high_place * group * block, group * block, 1)
    x_group = x_group.reshape(-1, group, block)
    x_group = jnp.take(x_group, jnp.arange(group) ^ low_place, axis=1).reshape(-1, group * block)
    gate_half, up_half = (
        jnp.dot(x_group.T, part, preferred_element_type=F32) for part in (gate_mine, up_mine)
    )
    kept = jnp.where(half_place == 0, gate_half, up_half)
    sent = jnp.where(half_place == 0, up_half, gate_half)
    kept = (kept + swap(sent.astype(BF16), "dp", 1).astype(F32)).reshape(group, block, groups, unit)
    pieces = [kept[0]]
    for place in range(1, group):
        pieces.append(swap(kept[place].astype(BF16), "seq", place).astype(F32))
    pieces = jnp.take(jnp.stack(pieces, axis=2), jnp.arange(group) ^ low_place, axis=2)
    heavy_gate_up_grad = pieces.reshape(block, ffn_heavy)

    mix_grad = matmul_t(middle_low, light_out).astype(BF16)
    mix_grad = mix_grad.reshape(row_count, seg_span, light_heads, DL)
    val_grad = jnp.einsum("rhqk,rqhd->rkhd", probs_low, mix_grad, preferred_element_type=F32)
    prob_grad = jnp.einsum("rqhd,rkhd->rhqk", mix_grad, val_ext, preferred_element_type=F32)
    delta = jnp.sum(probs_light * prob_grad, axis=-1, keepdims=True)
    score_grad = (probs_light * (prob_grad - delta)).astype(BF16)
    query_grad = jnp.einsum("rhqk,rkhd->rqhd", score_grad, key_ext, preferred_element_type=F32)
    key_grad = jnp.einsum("rhqk,rqhd->rkhd", score_grad, query_low, preferred_element_type=F32)
    query_grad = (query_grad * light_scale).reshape(row_count, seg_span, width).astype(BF16)
    kv_grad = jnp.concatenate(
        [
            (key_grad * light_scale).reshape(row_count, extent, width),
            val_grad.reshape(row_count, extent, width),
        ],
        axis=-1,
    ).astype(BF16)
    normed_grad_ext = matmul_t(kv_grad, light_qkv[:, width:])
    normed_grad = matmul_t(query_grad, light_qkv[:, :width])
    normed_grad = normed_grad + normed_grad_ext[:, RADIUS : RADIUS + seg_span]
    from_right = shifted(normed_grad_ext[:, :RADIUS].astype(BF16), "seq", -1)
    from_left = shifted(normed_grad_ext[:, seg_span + RADIUS :].astype(BF16), "seq", 1)
    normed_grad = normed_grad.at[:, :RADIUS].add(from_left.astype(F32))
    normed_grad = normed_grad.at[:, seg_span - RADIUS :].add(from_right.astype(F32))

    hq_all = matmul(query_all, heavy_q).astype(BF16)
    do2_all = matmul_t(proj_all, heavy_out).astype(BF16)
    mix_all, dhq_all, dhk_all, dhv_all = heavy_both(
        hq_all, keys_all, vals_all, query_seg, key_seg, do2_all
    )
    dhkv_all = jnp.concatenate([dhk_all, dhv_all], axis=-1)
    mine = lambda v: lax.dynamic_slice_in_dim(flat(v), me * block, block, 1).T
    heavy_grads = [
        own_half_first(jnp.dot(mine(left), flat(right), preferred_element_type=F32), half_place)
        for left, right in ((query_all, dhq_all), (key_all, dhkv_all), (mix_all, proj_all))
    ]
    heavy_kept = jnp.concatenate([pair[0] for pair in heavy_grads], axis=-1)
    heavy_sent = jnp.concatenate([pair[1] for pair in heavy_grads], axis=-1)
    heavy_sum = heavy_kept + swap(heavy_sent.astype(BF16), "dp", 1).astype(F32)
    heavy_half = heavy_width // 2
    heavy_q_grad = heavy_sum[:, :heavy_half]
    heavy_kv_grad = heavy_sum[:, heavy_half : 3 * heavy_half]
    heavy_out_grad = heavy_sum[:, 3 * heavy_half :]
    query_logit_grad = query_gate_grad * query_gate * (1.0 - query_gate)
    route_query_grad = jnp.sum(query_logit_grad[..., None] * query_normed, axis=(0, 1))
    query_rows_grad = (
        matmul_t(dhq_all[:, :routed_own], heavy_q) + query_logit_grad[..., None] * route_query_full
    )
    key_rows_grad = matmul_t(dhkv_all[:, :routed_own], heavy_kv)
    normed_grad = (
        normed_grad
        + place_rows(query_rows_grad, own_query, seg_span)
        + place_rows(key_rows_grad, own_key, seg_span)
    )
    attn_gain_grad = jnp.sum(normed_grad * hidden * factor_one, axis=(0, 1))
    hidden_norm_grad = norm_back(hidden, factor_one, attn_gain, normed_grad)
    grad_tokens = (middle_grad + hidden_norm_grad).astype(BF16)

    own_slots = slot_columns(flat(normed_low), me, devices).T
    ext_slots = slot_columns(flat(normed_ext_low), me, devices).T
    qkv_grad = jnp.concatenate(
        [
            jnp.dot(own_slots, flat(query_grad), preferred_element_type=F32),
            jnp.dot(ext_slots, flat(kv_grad), preferred_element_type=F32),
        ],
        axis=-1,
    )
    second_sum = scatter_sum(
        jnp.concatenate(
            [
                slot_block(own_half_first(qkv_grad, half_place), devices),
                slot_vectors((attn_gain_grad, route_query_grad), me, devices),
            ],
            axis=2,
        )
    )
    qkv_cols = light_qkv.shape[1] // 2
    qkv_rows = block * qkv_cols // LANES
    light_qkv_grad = unslot(second_sum[:qkv_rows], qkv_cols)
    attn_gain_grad = second_sum[qkv_rows:, 0]
    route_query_grad = second_sum[qkv_rows:, 1]
    return (
        outputs,
        grad_tokens,
        attn_gain_grad,
        light_qkv_grad,
        light_out_grad,
        heavy_q_grad,
        heavy_kv_grad,
        heavy_out_grad,
        route_query_grad,
        ffn_gain_grad,
        light_gate_up_grad,
        light_down_grad,
        heavy_gate_up_grad,
        heavy_down_grad,
        route_ffn_grad,
        rms_stats,
    )


VMEM = pl.BlockSpec(memory_space=pltpu.VMEM)
SMEM = pl.BlockSpec(memory_space=pltpu.SMEM)
ANY = pl.BlockSpec(memory_space=pl.ANY)
GELU_RATE = math.sqrt(2.0 / math.pi)
GELU_CUBE = 0.044715
MIB = 1024 * 1024
CUTS = 4


def shape(dims, dtype):
    return jax.ShapeDtypeStruct(dims, dtype)


def call(kernel, outs, ins, smem=0, scratch=(), micros=1, mib=16, after=()):
    used = len(ins)

    def body(*refs):
        kernel(*refs[:used], *refs[used + len(after) :])

    return pl.pallas_call(
        body,
        out_shape=outs,
        in_specs=[SMEM] * smem + [VMEM] * (used - smem) + [ANY] * len(after),
        out_specs=[VMEM] * len(outs),
        scratch_shapes=list(scratch),
        compiler_params=pltpu.CompilerParams(vmem_limit_bytes=mib * MIB),
        cost_estimate=cost(micros),
    )(*ins, *after)


def cost(micros):
    return pl.CostEstimate(flops=int(micros * 10**9), bytes_accessed=10**6, transcendentals=0)


def dot(left, right):
    return jnp.dot(left, right, preferred_element_type=F32)


def dot_t(left, right):
    return lax.dot_general(left, right, (((1,), (1,)), ((), ())), preferred_element_type=F32)


def t_dot(left, right):
    return lax.dot_general(left, right, (((0,), (0,)), ((), ())), preferred_element_type=F32)


def row_factor(value):
    return lax.rsqrt(jnp.mean(value * value, axis=-1, keepdims=True) + EPSILON)


def as_column(row):
    count = row.shape[1]
    down = lax.broadcasted_iota(jnp.int32, (count, count), 0)
    along = lax.broadcasted_iota(jnp.int32, (count, count), 1)
    return jnp.sum(jnp.where(down == along, row, 0.0), axis=1, keepdims=True)


def head_window(head, size):
    first = head * size // LANES * LANES
    lanes = (head * size + size - 1) // LANES * LANES + LANES - first
    place = lax.broadcasted_iota(jnp.int32, (1, lanes), 1) + first
    return first, lanes, (place >= head * size) & (place < head * size + size)


def slot_owners(me, bits):
    owners = []
    for p in range(1 << len(bits)):
        flips = sum(bit for k, bit in enumerate(bits) if p >> (len(bits) - 1 - k) & 1)
        owners.append(flips ^ me)
    return owners


def slot_select(width, bits, me):
    block = width >> len(bits)
    along = lax.broadcasted_iota(jnp.int32, (block, width), 1)
    inside = lax.broadcasted_iota(jnp.int32, (block, width), 0)
    rows = [(along == inside + owner * block).astype(F32) for owner in slot_owners(me, bits)]
    return jnp.concatenate(rows, axis=0).astype(BF16)


def two_gelu(value):
    square = value * value
    bend = jnp.tanh(GELU_RATE * value * (1.0 + GELU_CUBE * square))
    half = 0.5 * (1.0 + bend)
    slope = half + 0.5 * value * (1.0 - bend * bend) * GELU_RATE * (1.0 + 3.0 * GELU_CUBE * square)
    return value * half, slope


def first_kernel(routed, route, seg_at, tokens, segs, table, keys, upper, lower, normed, picked):
    rows, span, width = tokens.shape
    me = lax.axis_index("seq")
    hidden = tokens[...].reshape(rows * span, width).astype(F32)
    normed[...] = hidden * row_factor(hidden) * table[0:1, :]
    for r in range(rows):
        for k in range(routed):
            place = route[r, me * routed + k] - me * span
            at = pl.ds(r * routed + k, 1)
            picked[at, :width] = normed[pl.ds(r * span + place, 1), :]
            picked[at, width:] = jnp.full((1, LANES), (seg_at[r, place] + 2).astype(F32))
    keys[...] = picked[...].astype(BF16).reshape(keys.shape)
    marks = (segs[...] + 2).astype(F32)
    for out, start in ((upper, span - RADIUS), (lower, 0)):
        out[:, :RADIUS, :] = tokens[:, start : start + RADIUS, :]
        out[:, RADIUS:, :] = jnp.zeros((rows, 16, width), BF16)
        for r in range(rows):
            out[r, RADIUS:, :span] = jnp.broadcast_to(marks[r : r + 1], (16, span)).astype(BF16)


def light_kernel(
    before, tokens, after, segs, table, w_qkv, w_out,
    normed, query, keyval, probs, mix, attn, seg_row, mix_t,
):
    rows, span, width = tokens.shape
    extent = span + 2 * RADIUS
    heads = width // DL
    for r in range(rows):
        for part, at in ((before, 0), (tokens, RADIUS), (after, RADIUS + span)):
            size = span if part is tokens else RADIUS
            value = part[r, :size, :].astype(F32)
            value = value * row_factor(value) * table[0:1, :]
            normed[r * extent + at : r * extent + at + size, :] = value.astype(BF16)
    keyval[...] = dot(normed[...], w_qkv[:, width:]).astype(BF16)
    own = [normed[r * extent + RADIUS : r * extent + RADIUS + span, :] for r in range(rows)]
    query[...] = dot(jnp.concatenate(own, axis=0), w_qkv[:, :width]).astype(BF16)
    down = lax.broadcasted_iota(jnp.int32, (extent, span), 0)
    along = lax.broadcasted_iota(jnp.int32, (extent, span), 1)
    near = jnp.abs(along - down + RADIUS) <= RADIUS
    for r in range(rows):
        marks = (segs[r : r + 1, :] + 2).astype(F32)
        seg_row[:, :span] = before[r, RADIUS : RADIUS + 8, :span].astype(F32)
        seg_row[:, span : 2 * span] = jnp.broadcast_to(marks, (8, span))
        seg_row[:, 2 * span :] = after[r, RADIUS : RADIUS + 8, :span].astype(F32)
        columns = [as_column(seg_row[0:1, c * span : (c + 1) * span]) for c in range(3)]
        key_marks = jnp.concatenate([columns[0][span - RADIUS :], columns[1], columns[2][:RADIUS]], axis=0)
        allowed = near & (key_marks == marks)
        key_rows = slice(r * extent, (r + 1) * extent)
        val_t = keyval[key_rows, width:].T
        for h in range(heads):
            first, lanes, mask = head_window(h, DL)
            window = slice(first, first + lanes)
            q_head = jnp.where(mask, query[r * span : (r + 1) * span, window], 0)
            scores = dot_t(keyval[key_rows, window], q_head)
            scores = jnp.where(allowed, scores * (1.0 / math.sqrt(DL)), NEG_FILL)
            numer = jnp.exp(scores - jnp.max(scores, axis=0, keepdims=True))
            share = (numer / jnp.sum(numer, axis=0, keepdims=True)).astype(BF16)
            probs[r * heads + h] = share
            mix_t[h * DL : (h + 1) * DL, :] = dot(val_t[h * DL : (h + 1) * DL, :], share)
        mix[r * span : (r + 1) * span, :] = mix_t[...].T.astype(BF16)
    attn[...] = dot(mix[...], w_out[...])


def stat_row(value):
    total = jnp.sum(jnp.sum(value, axis=0, keepdims=True), axis=1, keepdims=True)
    return jnp.broadcast_to(total, (1, LANES))


def valid_column(segs):
    rows = segs.shape[0]
    parts = [as_column((segs[r : r + 1, :] >= 0).astype(F32)) for r in range(rows)]
    return jnp.concatenate(parts, axis=0)


def router(rows, weights):
    return jax.nn.sigmoid(jnp.sum(rows[...] * weights, axis=-1, keepdims=True))


def gathered(refs, row, lanes):
    value = jnp.concatenate([ref[:, row, :, lanes] for ref in refs], axis=0)
    return value.reshape(-1, value.shape[-1])


def middle_kernel(routed, parts, q_route, f_route, seg_at, tokens, segs, *refs):
    keys, refs = refs[:parts], refs[parts:]
    attn, upstream, table, w_q, w_kv, w_out = refs[:6]
    middle, normed_two, keyval, payload, q_rows, f_rows, f_up, proj, f_marks, stats = refs[6:16]
    full, marks, placed = refs[16:]
    rows, span, width = tokens.shape
    me = lax.axis_index("seq")
    hidden = tokens[...].reshape(rows * span, width).astype(F32)
    full[...] = hidden * row_factor(hidden) * table[0:1, :]
    for r in range(rows):
        for k in range(routed):
            at = pl.ds(r * routed + k, 1)
            place = q_route[r, me * routed + k] - me * span
            q_rows[at, :] = full[pl.ds(r * span + place, 1), :]
            marks[at, :] = jnp.full((1, LANES), (seg_at[r, place] + 2).astype(F32))
            place = f_route[r, k] - me * span
            f_marks[at, :] = jnp.full((1, LANES), (seg_at[r, place] + 2).astype(F32))
    q_low = q_rows[...].astype(BF16)
    payload[:, :, 2 * width : 3 * width] = q_low.reshape(rows, routed, width)
    payload[:, :, 3 * width :] = marks[...].astype(BF16).reshape(rows, routed, LANES)
    key_low = jnp.concatenate([gathered(keys, r, slice(0, width)) for r in range(rows)], axis=0)
    keyval[...] = dot(key_low, w_kv[...]).astype(BF16).reshape(keyval.shape)
    query = dot(q_low, w_q[...]).astype(BF16)
    heads = width // DH
    lane = lax.broadcasted_iota(jnp.int32, (1, width), 1)
    masks = [(lane >= h * DH) & (lane < (h + 1) * DH) for h in range(heads)]
    mixed = []
    for r in range(rows):
        mine = query[r * routed : (r + 1) * routed]
        wide = jnp.concatenate([jnp.where(m, mine, 0) for m in masks], axis=0)
        scores = dot_t(wide, keyval[r, :, :width]) * (1.0 / math.sqrt(DH))
        key_marks = gathered(keys, r, slice(width, width + LANES)).astype(F32).T[0:1, :]
        query_marks = jnp.concatenate([marks[r * routed : (r + 1) * routed, 0:1]] * heads, axis=0)
        scores = jnp.where(query_marks == key_marks, scores, NEG_FILL)
        peak = jnp.maximum(jnp.max(scores, axis=-1, keepdims=True), 0.0)
        numer = jnp.exp(scores - peak)
        share = numer / (jnp.exp(-peak) + jnp.sum(numer, axis=-1, keepdims=True))
        part = dot(share.astype(BF16), keyval[r, :, width:])
        total = jnp.zeros((routed, width), F32)
        for h in range(heads):
            total = total + jnp.where(masks[h], part[h * routed : (h + 1) * routed], 0.0)
        mixed.append(total)
    mixed = jnp.concatenate(mixed, axis=0).astype(BF16)
    proj[...] = dot(mixed, w_out[...])
    placed[...] = router(q_rows, table[2:3, :]) * proj[...]
    light = attn[...]
    middle[...] = hidden + light
    for r in range(rows):
        for k in range(routed):
            place = q_route[r, me * routed + k] - me * span
            at = pl.ds(r * span + place, 1)
            middle[at, :] = middle[at, :] + placed[pl.ds(r * routed + k, 1), :]
    valid = valid_column(segs)
    stats[...] = jnp.zeros(stats.shape, F32)
    stats[0:1, :] = stat_row(valid * hidden * hidden)
    stats[1:2, :] = stat_row(valid * light * light)
    stats[2:3, :] = stat_row(jnp.where(marks[:, 0:1] >= 2.0, placed[...] * placed[...], 0.0))
    stats[5:6, :] = stat_row(valid)
    mid = middle[...]
    full[...] = mid * row_factor(mid) * table[1:2, :]
    normed_two[...] = full[...].astype(BF16)
    for r in range(rows):
        for k in range(routed):
            place = f_route[r, k] - me * span
            f_rows[pl.ds(r * routed + k, 1), :] = full[pl.ds(r * span + place, 1), :]
    full[...] = upstream[...].reshape(rows * span, width).astype(F32)
    for r in range(rows):
        for k in range(routed):
            place = f_route[r, k] - me * span
            f_up[pl.ds(r * routed + k, 1), :] = full[pl.ds(r * span + place, 1), :]
    f_low = (router(f_rows, table[3:4, :]) * f_up[...]).astype(BF16)
    payload[:, :, :width] = f_rows[...].astype(BF16).reshape(rows, routed, width)
    payload[:, :, width : 2 * width] = f_low.reshape(rows, routed, width)


def glu_parts(inputs, back_in, gate_w, up_w, down_w):
    act, slope = two_gelu(dot(inputs, gate_w))
    lift = dot(inputs, up_w)
    back = dot_t(back_in, down_w)
    hidden = (act * lift).astype(BF16)
    return hidden, (back * lift * slope).astype(BF16), (back * act).astype(BF16)


def three_parts(value):
    high = value.astype(BF16).astype(F32)
    middle = (value - high).astype(BF16).astype(F32)
    return high, middle, value - high - middle


def light_ffn_kernel(normed_two, upstream, w_gate_up, w_down, z_light, d_light, hidden_out, grad_gate, grad_up):
    width = normed_two.shape[1]
    inner = w_down.shape[0]
    back_in = upstream[...].reshape(-1, width)
    unit = 256
    for at in range(0, inner, unit):
        part = slice(at, at + unit)
        gate_w, up_w = w_gate_up[:, part], w_gate_up[:, inner + at : inner + at + unit]
        hidden, d_gate, d_up = glu_parts(normed_two[...], back_in, gate_w, up_w, w_down[part, :])
        hidden_out[:, part] = hidden
        grad_gate[:, part] = d_gate
        grad_up[:, part] = d_up
    z_light[...] = dot(hidden_out[...], w_down[...])
    d_light[...] = dot_t(grad_gate[...], w_gate_up[:, :inner]) + dot_t(grad_up[...], w_gate_up[:, inner:])


def ffn_kernel(
    routed, q_route, f_route, upstream, middle, z_light, d_light_in,
    h_gate, h_up, h_down, q_rows, f_rows, f_up, proj, f_marks, table, stats, segs,
    outputs, dmid, dmid_low, payload, vectors,
    z_heavy, d_heavy, placed, full, d_light,
):
    step = pl.program_id(0)
    width = middle.shape[1]
    rows, span = segs.shape
    me = lax.axis_index("seq")

    @pl.when(step == 0)
    def _():
        for total in (z_heavy, d_heavy):
            total[...] = jnp.zeros(total.shape, F32)

    f_gate = router(f_rows, table[3:4, :])
    f_low = (f_gate * f_up[...]).astype(BF16)
    f_in = f_rows[...].astype(BF16)
    hidden, d_gate, d_up = glu_parts(f_in, f_low, h_gate[...], h_up[...], h_down[...])
    z_heavy[...] += dot(hidden, h_down[...])
    d_heavy[...] += dot_t(d_gate, h_gate[...]) + dot_t(d_up, h_up[...])

    @pl.when(step == pl.num_programs(0) - 1)
    def _():
        mid = middle[...]
        d_light[...] = d_light_in[...]
        placed[...] = f_gate * z_heavy[...]
        full[...] = mid + z_light[...]
        logit = jnp.sum(f_up[...] * z_heavy[...], axis=-1, keepdims=True) * f_gate * (1.0 - f_gate)
        d_heavy[...] += logit * table[3:4, :]
        for r in range(rows):
            for k in range(routed):
                place = f_route[r, k] - me * span
                at, source = pl.ds(r * span + place, 1), pl.ds(r * routed + k, 1)
                full[at, :] = full[at, :] + placed[source, :]
                d_light[at, :] = d_light[at, :] + d_heavy[source, :]
        outputs[...] = full[...].astype(BF16).reshape(outputs.shape)
        factor = row_factor(mid)
        d_norm = d_light[...]
        vectors[...] = jnp.zeros(vectors.shape, F32)
        vectors[0:1, :] = jnp.sum(d_norm * mid * factor, axis=0, keepdims=True)
        vectors[1:2, :] = jnp.sum(logit * f_rows[...], axis=0, keepdims=True)
        weighted = d_norm * table[1:2, :]
        inner = jnp.mean(weighted * mid, axis=-1, keepdims=True)
        total = upstream[...].reshape(rows * span, width).astype(F32) + factor * weighted - mid * (factor * factor * factor) * inner
        dmid[...] = total
        dmid_low[...] = total.astype(BF16)
        sums = stats[...]
        place = lax.broadcasted_iota(jnp.int32, sums.shape, 0)
        lane = lax.broadcasted_iota(jnp.int32, sums.shape, 1)
        light_sum = stat_row(valid_column(segs) * z_light[...] * z_light[...])
        heavy_sum = stat_row(jnp.where(f_marks[:, 0:1] >= 2.0, placed[...] * placed[...], 0.0))
        sums = jnp.where(place == 3, light_sum, jnp.where(place == 4, heavy_sum, sums))
        lanes = jnp.zeros(sums.shape, F32)
        for k, part in enumerate(three_parts(sums)):
            lanes = lanes + jnp.where(lane == place + 8 * k, part, 0.0)
        lanes = jnp.sum(lanes, axis=0, keepdims=True)
        full[...] = total
        for r in range(rows):
            for k in range(routed):
                place = q_route[r, me * routed + k] - me * span
                placed[pl.ds(r * routed + k, 1), :] = full[pl.ds(r * span + place, 1), :]
        q_gate = router(q_rows, table[2:3, :])
        logit = jnp.sum(placed[...] * proj[...], axis=-1, keepdims=True) * q_gate * (1.0 - q_gate)
        payload[:, :, :width] = (q_gate * placed[...]).astype(BF16).reshape(rows, routed, width)
        lane = lax.broadcasted_iota(jnp.int32, (rows * routed, LANES), 1)
        extra = jnp.broadcast_to(lanes, (rows * routed, LANES))
        for k, part in enumerate(three_parts(logit)):
            extra = jnp.where(lane == 24 + k, part, extra)
        payload[:, :, width:] = extra.astype(BF16).reshape(rows, routed, LANES)


def halves_of(value, place):
    half = value.shape[-1] // 2
    first, second = value[..., :half], value[..., half:]
    return jnp.where(place == 0, first, second), jnp.where(place == 0, second, first)


def store_slots(outs, place, base, grads):
    each = outs[0].shape[0]
    block = grads.shape[0] // (each * len(outs))
    low = grads.astype(BF16)
    for c in range(grads.shape[1] // LANES):
        for p in range(each * len(outs)):
            part = low[p * block : (p + 1) * block, c * LANES : (c + 1) * LANES]
            outs[p // each][p % each, place, base + c * block : base + (c + 1) * block, :] = part
    return base + grads.shape[1] // LANES * block


def slot_vector_block(select, vectors):
    table = jnp.concatenate([vectors, jnp.zeros((LANES - vectors.shape[0], vectors.shape[1]), F32)], axis=0)
    return dot_t(select, table.astype(BF16))


def first_grads_kernel(bits, normed_two, grad_gate, grad_up, hidden, upstream, *outs):
    width = normed_two.shape[1]
    me = lax.axis_index("seq")
    place = lax.axis_index("dp")
    inputs_t = dot_t(slot_select(width, bits, me), normed_two[...]).astype(BF16)
    gate, up = grad_gate[...], grad_up[...]
    ways = (jnp.where(place == 0, gate, up), jnp.where(place == 0, up, gate))
    for half in range(2):
        base = store_slots(outs, half, 0, dot(inputs_t, ways[half]))
    hidden_t = dot_t(slot_select(hidden.shape[1], bits, me), hidden[...]).astype(BF16)
    ways = halves_of(upstream[...].reshape(-1, width), place)
    for half in range(2):
        store_slots(outs, half, base, dot(hidden_t, ways[half]))


def light_back_kernel(
    bits, dmid_low, query, keyval, probs, normed, mix, vectors, table, w_qkv, w_out,
    dnorm, to_right, to_left, *refs,
):
    outs, (d_all, dkv, dq_t) = refs[:-3], refs[-3:]
    rows, rim, width = to_right.shape
    span = dmid_low.shape[0] // rows
    extent = span + 2 * rim
    heads = width // DL
    scale = 1.0 / math.sqrt(DL)
    me = lax.axis_index("seq")
    place = lax.axis_index("dp")
    mix_grad = dot_t(dmid_low[...], w_out[...]).astype(BF16)
    for r in range(rows):
        key_rows = slice(r * extent, (r + 1) * extent)
        own_rows = slice(r * span, (r + 1) * span)
        key_t = keyval[key_rows, :width].T
        dkv[...] = jnp.zeros(dkv.shape, F32)
        for h in range(heads):
            first, lanes, mask = head_window(h, DL)
            window = slice(first, first + lanes)
            v_window = slice(width + first, width + first + lanes)
            q_head = jnp.where(mask, query[own_rows, window], 0)
            g_head = jnp.where(mask, mix_grad[own_rows, window], 0)
            share = probs[r * heads + h]
            full_share = share.astype(F32)
            prob_grad = dot_t(keyval[key_rows, v_window], g_head)
            delta = jnp.sum(full_share * prob_grad, axis=0, keepdims=True)
            score_grad = (full_share * (prob_grad - delta)).astype(BF16)
            dkv[:, window] += dot(score_grad, q_head)
            dkv[:, v_window] += dot(share, g_head)
            dq_t[h * DL : (h + 1) * DL, :] = dot(key_t[h * DL : (h + 1) * DL, :], score_grad)
        d_all[key_rows, :width] = jnp.zeros((extent, width), BF16)
        d_all[r * extent + rim : r * extent + rim + span, :width] = (dq_t[...].T * scale).astype(BF16)
        d_all[key_rows, width : 2 * width] = (dkv[:, :width] * scale).astype(BF16)
        d_all[key_rows, 2 * width :] = dkv[:, width:].astype(BF16)
    d_norm = dot_t(d_all[...], w_qkv[...])
    gain_grad = jnp.sum(d_norm * normed[...].astype(F32), axis=0, keepdims=True) / table[0:1, :]
    for r in range(rows):
        to_left[r] = d_norm[r * extent : r * extent + rim].astype(BF16)
        dnorm[r * span : (r + 1) * span, :] = d_norm[r * extent + rim : r * extent + rim + span]
        to_right[r] = d_norm[r * extent + rim + span : (r + 1) * extent].astype(BF16)
    select = slot_select(width, bits, me)
    inputs_t = dot_t(select, normed[...]).astype(BF16)
    ways = halves_of(d_all[...], place)
    for half in range(2):
        base = store_slots(outs, half, 0, dot(inputs_t, ways[half]))
    mix_t = dot_t(select, mix[...]).astype(BF16)
    ways = halves_of(dmid_low[...], place)
    for half in range(2):
        base_two = store_slots(outs, half, base, dot(mix_t, ways[half]))
    line = lax.broadcasted_iota(jnp.int32, (8, width), 0)
    block = slot_vector_block(select, jnp.where(line == 2, gain_grad, vectors[...]))
    for half in range(2):
        store_slots(outs, half, base_two, block)


def heavy_ffn_kernel(parts, me_at, *refs):
    blocks, (h_gate, h_up, h_down) = refs[:parts], refs[parts : parts + 3]
    kept, sent, picked = refs[-3:]
    step = pl.program_id(0)
    devices = lax.axis_size("seq")
    width = h_gate.shape[0]
    me = me_at[0]
    place = lax.axis_index("dp")
    group = picked.shape[0] * devices // width
    low_place = lax.rem(me, group)
    high_place = lax.div(me, group)
    block = width // devices
    rows = range(blocks[0].shape[1])
    inputs = jnp.concatenate([gathered(blocks, r, slice(0, width)) for r in rows], axis=0)
    back_in = jnp.concatenate([gathered(blocks, r, slice(width, 2 * width)) for r in rows], axis=0)

    @pl.when(step == 0)
    def _():
        along = lax.broadcasted_iota(jnp.int32, (block, width), 1)
        inside = lax.broadcasted_iota(jnp.int32, (block, width), 0)
        picks = []
        for j in range(group):
            owner = high_place * group + (low_place ^ j)
            picks.append((along == inside + owner * block).astype(F32))
        picked[...] = dot_t(jnp.concatenate(picks, axis=0).astype(BF16), inputs).astype(BF16)

    hidden, d_gate, d_up = glu_parts(inputs, back_in, h_gate[...], h_up[...], h_down[...])
    unit = hidden.shape[1]
    count = picked.shape[0]
    lanes = pl.ds(pl.multiple_of(step * unit, unit), unit)
    kept[:count, lanes] = dot(picked[...], jnp.where(place == 0, d_gate, d_up))
    sent[:count, lanes] = dot(picked[...], jnp.where(place == 0, d_up, d_gate)).astype(BF16)

    @pl.when(step == high_place)
    def _():
        hidden_t = hidden.T
        for out, part in zip((kept, sent), halves_of(back_in, place)):
            grad = dot(hidden_t, part).astype(out.dtype)
            size = grad.shape[1]
            out[count:, :size] = grad[: unit // 2]
            out[count:, size : 2 * size] = grad[unit // 2 :]
            out[count:, 2 * size :] = jnp.zeros((unit // 2, out.shape[1] - 2 * size), out.dtype)


def pieces_kernel(kept, received, *outs):
    pieces, down = outs[:-1], outs[-1]
    total = kept[...] + received[...].astype(F32)
    block = pieces[0].shape[0]
    for j, piece in enumerate(pieces):
        piece[...] = total[j * block : (j + 1) * block].astype(piece.dtype)
    below = total[len(pieces) * block :]
    half, size = below.shape[0], down.shape[1]
    down[:half, :] = below[:, :size]
    down[half:, :] = below[:, size : 2 * size]


def join_kernel(held, got, *outs):
    count, each = held.shape[0], outs[0].shape[0]
    for k, out in enumerate(outs):
        for b in range(each):
            at = k * each + b
            out[b] = held[at] if at < count else got[at - count]


def heavy_row(
    r, routed, routed_parts, proj_parts, key_parts, keyval, table, w_q, w_kv, w_out, mix_t, dq_t, dkv,
):
    width = w_q.shape[0]
    scale = 1.0 / math.sqrt(DH)
    me = lax.axis_index("seq")
    block = width // lax.axis_size("seq")
    along = lax.broadcasted_iota(jnp.int32, (block, width), 1)
    inside = lax.broadcasted_iota(jnp.int32, (block, width), 0)
    own = (along == inside + me * block).astype(F32).astype(BF16)
    in_q = gathered(routed_parts, r, slice(2 * width, 3 * width))
    in_k = gathered(key_parts, r, slice(0, width))
    q_marks = gathered(routed_parts, r, slice(3 * width, 3 * width + LANES)).astype(F32).T[0:1, :]
    k_marks = gathered(key_parts, r, slice(width, width + LANES)).astype(F32)[:, 0:1]
    allowed = k_marks == q_marks
    grad_in = gathered(proj_parts, r, slice(0, width))
    extra = gathered(proj_parts, r, slice(width, width + LANES)).astype(F32)
    query = dot(in_q, w_q[...]).astype(BF16)
    mix_grad = dot_t(grad_in, w_out[...]).astype(BF16)
    key_t = keyval[r, :, :width].T
    val_t = keyval[r, :, width:].T
    lane = lax.broadcasted_iota(jnp.int32, (1, LANES), 1)
    for first in range(0, width, LANES):
        window = slice(first, first + LANES)
        v_window = slice(width + first, width + first + LANES)
        keys_w, vals_w = keyval[r, :, window], keyval[r, :, v_window]
        dk, dv = None, None
        for h in range(first // DH, (first + LANES) // DH):
            mask = (lane + first >= h * DH) & (lane + first < (h + 1) * DH)
            q_head = jnp.where(mask, query[:, window], 0)
            g_head = jnp.where(mask, mix_grad[:, window], 0)
            scores = jnp.where(allowed, dot_t(keys_w, q_head) * scale, NEG_FILL)
            peak = jnp.maximum(jnp.max(scores, axis=0, keepdims=True), 0.0)
            numer = jnp.exp(scores - peak)
            share = numer / (jnp.exp(-peak) + jnp.sum(numer, axis=0, keepdims=True))
            share_low = share.astype(BF16)
            prob_grad = dot_t(vals_w, g_head)
            delta = jnp.sum(share * prob_grad, axis=0, keepdims=True)
            score_grad = (share * (prob_grad - delta)).astype(BF16)
            at = slice(h * DH, (h + 1) * DH)
            mix_t[at, :] = dot(val_t[at, :], share_low).astype(BF16)
            dq_t[at, :] = dot(key_t[at, :], score_grad)
            part_k, part_v = dot(score_grad, q_head), dot(share_low, g_head)
            dk, dv = (part_k, part_v) if dk is None else (dk + part_k, dv + part_v)
        dkv[:, window] = (dk * scale).astype(BF16)
        dkv[:, v_window] = dv.astype(BF16)
    dq = (dq_t[...].T * scale).astype(BF16)
    in_q_t = dot_t(own, in_q)
    logits = jnp.sum(jnp.where((lane >= 24) & (lane < 27), extra, 0.0), axis=1, keepdims=True)
    logit_row = jnp.sum(extra.T[24:27, :], axis=0, keepdims=True)
    grads = jnp.concatenate(
        [
            dot(in_q_t.astype(BF16), dq),
            dot(dot_t(own, in_k).astype(BF16), dkv[...]),
            dot(dot(own, mix_t[...]).astype(BF16), grad_in),
            jnp.broadcast_to(jnp.sum(in_q_t * logit_row, axis=1, keepdims=True), (block, LANES)),
        ],
        axis=1,
    )
    q_part = dot_t(dq[:routed], w_q[...]) + logits[:routed] * table[2:3, :]
    return grads, q_part, dot_t(dkv[:routed, :], w_kv[...])


def heavy_inputs(counts, refs):
    ins = []
    for count in counts:
        ins.append(refs[:count])
        refs = refs[count:]
    return ins + list(refs[:5]), refs[5:]


def heavy_first_kernel(routed, counts, *refs):
    ins, refs = heavy_inputs(counts, refs)
    (grads, parts), scratch = refs[:2], refs[2:]
    grads[...], parts[0], parts[1] = heavy_row(0, routed, *ins, *scratch)


def heavy_last_kernel(routed, counts, q_route, k_route, *refs):
    ins, refs = heavy_inputs(counts, refs)
    grads_in, parts_in, dnorm, from_left, from_right, dmid, tokens, grad_tokens, kept, sent, total, parts = refs[:12]
    scratch = refs[12:]
    rows, span, width = tokens.shape
    proj_parts, table, w_q, w_kv = ins[1], ins[4], ins[5], ins[6]
    me = lax.axis_index("seq")
    place = lax.axis_index("dp")
    block = width // lax.axis_size("seq")
    grads, q_part, k_part = heavy_row(rows - 1, routed, *ins, *scratch)
    grads = grads + grads_in[...]
    parts[0, 0], parts[0, 1] = parts_in[0], parts_in[1]
    parts[1, 0], parts[1, 1] = q_part, k_part
    for r in range(rows):
        at = r * span
        total[at : at + span, :] = dnorm[at : at + span, :]
        total[at : at + RADIUS, :] += from_left[r].astype(F32)
        total[at + span - RADIUS : at + span, :] += from_right[r].astype(F32)
        for k in range(routed):
            for which, route in enumerate((q_route, k_route)):
                spot = route[r, me * routed + k] - me * span
                row = pl.ds(at + spot, 1)
                total[row, :] = total[row, :] + parts[r, which, k : k + 1, :]
    hidden = tokens[...].reshape(rows * span, width).astype(F32)
    factor = row_factor(hidden)
    weighted = total[...] * table[0:1, :]
    inner = jnp.mean(weighted * hidden, axis=-1, keepdims=True)
    d_hidden = dmid[...] + factor * weighted - hidden * (factor * factor * factor) * inner
    grad_tokens[...] = d_hidden.astype(BF16).reshape(grad_tokens.shape)
    along = lax.broadcasted_iota(jnp.int32, (block, width), 1)
    inside = lax.broadcasted_iota(jnp.int32, (block, width), 0)
    own_full = (along == inside + me * block).astype(F32)
    own = own_full.astype(BF16)
    own_gain = jnp.sum(own_full * table[0:1, :], axis=1, keepdims=True)
    own_route = jnp.sum(own_full * table[2:3, :], axis=1, keepdims=True)
    route_grad = grads[:, 4 * width : 4 * width + 1]
    gain_grad = jnp.sum(dot(own, w_q[...]) * grads[:, :width], axis=1, keepdims=True)
    gain_grad = gain_grad + jnp.sum(dot(own, w_kv[...]) * grads[:, width : 3 * width], axis=1, keepdims=True)
    gain_grad = (gain_grad + own_route * route_grad) / own_gain
    lane = lax.broadcasted_iota(jnp.int32, (block, LANES), 1)
    sums = sum(jnp.sum(ref[:, 0, 0:1, width:].astype(F32), axis=0) for ref in proj_parts)
    sums = jnp.broadcast_to(sums, (8, LANES))
    sums = sums + pltpu.roll(sums, LANES - 8, 1) + pltpu.roll(sums, LANES - 16, 1)
    sums = jnp.where(lane[:8] < 8, sums, 0.0)
    vectors = jnp.where(lane == 0, gain_grad, jnp.where(lane == 1, route_grad, 0.0))
    own_sums = pltpu.roll(sums, 8, 1)[0:1, :]
    sent_sums = jnp.zeros((1, LANES), F32)
    for k, part in enumerate(three_parts(sums)):
        sent_sums = sent_sums + pltpu.roll(part, 8 + 8 * k, 1)[0:1, :]
    at = 0
    for grad in (grads[:, :width], grads[:, width : 3 * width], grads[:, 3 * width : 4 * width]):
        mine, other = halves_of(grad, place)
        size = mine.shape[1]
        kept[:, at : at + size] = mine
        sent[:, at : at + size] = other.astype(BF16)
        at += size
    kept[:, at:] = vectors + own_sums
    sent[:, at:] = (vectors + sent_sums).astype(BF16)


def fold_kernel(pieces, count, *refs):
    ins, outs = refs[: 2 * count], refs[2 * count :]
    for out, parts in zip(outs, pieces):
        for target, pair, index in parts:
            value = ins[2 * pair][index].astype(F32) + ins[2 * pair + 1][index].astype(F32)
            out[target] = value.astype(out.dtype)


def finish_light_kernel(kept, received, *outs):
    total = kept[0, 0].astype(F32) + received[0, 0].astype(F32)
    base = 0
    for ref in outs:
        block = ref.shape[0]
        for c in range(ref.shape[1] // LANES):
            ref[:, c * LANES : (c + 1) * LANES] = total[base : base + block]
            base += block


def finish_heavy_kernel(
    groups, heavy_kept, heavy_got, own_piece, piece_one, piece_two, piece_three,
    q_out, kv_out, out_out, vectors, stats, gate_up_out,
):
    me = lax.axis_index("seq")
    total = heavy_kept[...] + heavy_got[...].astype(F32)
    at = 0
    for ref in (q_out, kv_out, out_out, vectors):
        ref[...] = total[:, at : at + ref.shape[1]]
        at += ref.shape[1]
    sums = total[:8, at - LANES :]
    stats[...] = sums + pltpu.roll(sums, LANES - 8, 1) + pltpu.roll(sums, LANES - 16, 1)
    pieces = (own_piece, piece_one, piece_two, piece_three)
    group = len(pieces)
    low_place = lax.rem(me, group)
    unit = own_piece.shape[1] // groups
    for j, piece in enumerate(pieces):
        for z in range(groups):
            at = pl.multiple_of((z * group + (low_place ^ j)) * unit, unit)
            gate_up_out[:, pl.ds(at, unit)] = piece[:, z * unit : (z + 1) * unit].astype(F32)


def fold(pairs, outs, after=()):
    flat = [ref for pair in pairs for ref in pair]
    kernel = functools.partial(fold_kernel, [parts for _, _, parts in outs], len(pairs))
    return call(kernel, [shape(dims, dtype) for dims, dtype, _ in outs], flat, mib=14, after=after)


def skip_operand(kernel, place):
    return lambda *refs: kernel(*refs[:place], *refs[place + 1 :])


class ScatterFolds:
    def __init__(self, parts, bits):
        half = len(parts) // 2
        each, _, self.rows, _ = parts[0].shape
        self.slots = half * each
        self.bits = bits
        self.pairs = [(kept, swap(sent, "seq", bits[0])) for kept, sent in zip(parts[:half], parts[half:])]
        self.stage, self.count = 0, self.slots // 2

    def step(self, after=()):
        slots, rows, quarter = self.slots, self.rows, self.slots // 2
        part = rows // 2
        every = slice(None)
        low, high = slice(0, part), slice(part, rows)
        one, two = slice(0, 1), slice(1, 2)
        near, far = slice(0, quarter), slice(quarter, slots)
        self.stage += 1
        if self.stage == 1:
            cuts = len(self.pairs)
            each = slots // cuts
            span = lambda k: slice(k * each, (k + 1) * each)
            lower = [(span(k), k, (every, every, low)) for k in range(cuts // 2)]
            upper = [(span(k), k + cuts // 2, (every, every, low)) for k in range(cuts // 2)]
            ways = [[(span(k), k, (every, side, high)) for k in range(cuts)] for side in (one, two)]
            left_keep, left_sent, right_keep, right_sent = fold(
                self.pairs,
                [
                    ((quarter, 2, part, LANES), BF16, lower),
                    ((quarter, 2, part, LANES), BF16, upper),
                    ((slots, 1, part, LANES), BF16, ways[0]),
                    ((slots, 1, part, LANES), BF16, ways[1]),
                ],
                after,
            )
            self.pairs = [
                (left_keep, swap(left_sent, "seq", self.bits[1])),
                (right_keep, swap(right_sent, "dp", 1)),
            ]
            return left_keep
        if self.stage == 2:
            left_keep, left_sent, right_keep, right_sent = fold(
                self.pairs,
                [
                    ((quarter, 1, part, LANES), BF16, [(every, 0, (every, one))]),
                    ((quarter, 1, part, LANES), BF16, [(every, 0, (every, two))]),
                    ((quarter, 1, part, LANES), BF16, [(every, 1, near)]),
                    ((quarter, 1, part, LANES), BF16, [(every, 1, far)]),
                ],
                after,
            )
            self.pairs = [
                (left_keep, swap(left_sent, "dp", 1)),
                (right_keep, swap(right_sent, "seq", self.bits[1])),
            ]
            return left_keep
        half = self.count // 2
        halves = (slice(0, half), slice(half, self.count))
        if len(self.pairs) == 2:
            wants = [[((every, every, low), 0, side), ((every, every, high), 1, side)] for side in halves]
        else:
            wants = [[(every, 0, side)] for side in halves]
        kept, sent = fold(self.pairs, [((half, 1, rows, LANES), BF16, want) for want in wants], after)
        self.pairs = [(kept, swap(sent, "seq", self.bits[self.stage - 1]))]
        self.count = half
        return kept

    def pair(self):
        return self.pairs[0]


class Gather:
    def __init__(self, block, bits):
        self.held = [block[None]]
        self.bits = list(bits)
        self.got = [swap(self.held[0], "seq", self.bits.pop(0))]

    def step(self, after=()):
        (held,), (got,) = self.held, self.got
        cuts = 1 if len(self.bits) > 1 else CUTS
        piece = shape((2 * held.shape[0] // cuts, *held.shape[1:]), held.dtype)
        self.held = call(join_kernel, [piece] * cuts, [held, got], micros=0.5, mib=8, after=after)
        bit = self.bits.pop(0)
        self.got = [swap(part, "seq", bit) for part in self.held]
        return self.held[0]

    def parts(self):
        return [*self.held, *self.got]


def local_kernels(
    tokens,
    segments,
    query_route,
    kv_route,
    ffn_route,
    grad_out,
    attn_gain,
    light_qkv,
    light_out,
    heavy_q,
    heavy_kv,
    heavy_out,
    route_query,
    ffn_gain,
    light_gate_up,
    light_down,
    heavy_gate_up,
    heavy_down,
    route_ffn,
):
    rows, span, width = tokens.shape
    devices = lax.axis_size("seq")
    routed = query_route.shape[1] // devices
    own, count = rows * span, rows * routed
    per_row = devices * routed
    extent = span + 2 * RADIUS
    block = width // devices
    light_heads = width // DL
    ffn_light, ffn_heavy = light_down.shape[0], heavy_down.shape[0]
    table = jnp.stack([attn_gain, ffn_gain, route_query.astype(F32), route_ffn.astype(F32)])
    marked = width + LANES

    rim = shape((rows, RADIUS + 16, width), BF16)
    keys, upper, lower = call(
        functools.partial(first_kernel, routed),
        [shape((rows, routed, marked), BF16), rim, rim],
        [kv_route, segments, tokens, segments, table],
        smem=2,
        scratch=[pltpu.VMEM((own, width), F32), pltpu.VMEM((count, marked), F32)],
        mib=6,
    )
    key_gather = Gather(keys, (8, 4, 2, 1))
    before = shifted(upper, "seq", 1)
    after = shifted(lower, "seq", -1)
    key_gather.step()
    last = key_gather.step()

    normed, query, keyval, probs, mix, attn = call(
        light_kernel,
        [
            shape((rows * extent, width), BF16),
            shape((own, width), BF16),
            shape((rows * extent, 2 * width), BF16),
            shape((rows * light_heads, extent, span), BF16),
            shape((own, width), BF16),
            shape((own, width), F32),
        ],
        [before, tokens, after, segments, table, light_qkv, light_out],
        scratch=[pltpu.VMEM((8, 3 * span), F32), pltpu.VMEM((width, span), F32)],
        micros=6,
        mib=20,
        after=[last],
    )
    key_gather.step([attn])
    key_parts = key_gather.parts()

    small = shape((count, width), F32)
    middle, normed_two, keyval_all, payload, q_rows, f_rows, f_up, proj, f_marks, stats = call(
        functools.partial(middle_kernel, routed, len(key_parts)),
        [
            shape((own, width), F32),
            shape((own, width), BF16),
            shape((rows, per_row, 2 * width), BF16),
            shape((rows, routed, 3 * width + LANES), BF16),
            small,
            small,
            small,
            small,
            shape((count, LANES), F32),
            shape((8, LANES), F32),
        ],
        [
            query_route, ffn_route, segments, tokens, segments, *key_parts, attn, grad_out,
            table, heavy_q, heavy_kv, heavy_out,
        ],
        smem=3,
        scratch=[
            pltpu.VMEM((own, width), F32),
            pltpu.VMEM((count, LANES), F32),
            pltpu.VMEM((count, width), F32),
        ],
        micros=4,
        mib=20,
    )
    routed_gather = Gather(payload, (8, 4, 2, 1))

    share = shape((own, ffn_light), BF16)
    z_light, d_light, hidden, grad_gate, grad_up = call(
        light_ffn_kernel,
        [shape((own, width), F32), shape((own, width), F32), share, share, share],
        [normed_two, grad_out, light_gate_up, light_down],
        micros=6,
        mib=16,
    )
    half_rows = (width // 2) // LANES
    slot_rows = block * ffn_light // LANES + ffn_light // devices * half_rows
    slots = [shape((devices // (2 * CUTS), 2, slot_rows, LANES), BF16)] * (2 * CUTS)
    first_bits, second_bits = (1, 4, 2, 8), (1, 2, 4, 8)
    slots = call(
        functools.partial(first_grads_kernel, first_bits),
        slots,
        [normed_two, grad_gate, grad_up, hidden, grad_out],
        micros=4,
        mib=20,
    )
    first = ScatterFolds(slots, first_bits)
    last = routed_gather.step([slots[0]])

    steps = 4
    whole = lambda *dims: pl.BlockSpec(dims, lambda j: (0,) * len(dims))
    heavy_unit = ffn_heavy // steps
    columns = lambda at: pl.BlockSpec((width, heavy_unit), lambda j: (0, at + j))
    outputs, dmid, dmid_low, proj_payload, vectors = pl.pallas_call(
        skip_operand(functools.partial(ffn_kernel, routed), 17),
        grid=(steps,),
        out_shape=[
            shape((rows, span, width), BF16),
            shape((own, width), F32),
            shape((own, width), BF16),
            shape((rows, routed, marked), BF16),
            shape((8, width), F32),
        ],
        in_specs=[SMEM, SMEM, whole(rows, span, width)]
        + [whole(own, width)] * 3
        + [columns(0), columns(steps), pl.BlockSpec((heavy_unit, width), lambda j: (j, 0))]
        + [whole(count, width)] * 4
        + [whole(count, LANES), whole(4, width), whole(8, LANES), whole(rows, span), ANY],
        out_specs=[
            whole(rows, span, width),
            whole(own, width),
            whole(own, width),
            whole(rows, routed, marked),
            whole(8, width),
        ],
        scratch_shapes=[pltpu.VMEM((count, width), F32)] * 3 + [pltpu.VMEM((own, width), F32)] * 2,
        compiler_params=pltpu.CompilerParams(vmem_limit_bytes=24 * MIB),
        cost_estimate=cost(12),
    )(
        query_route, ffn_route, grad_out, middle, z_light, d_light, heavy_gate_up, heavy_gate_up, heavy_down,
        q_rows, f_rows, f_up, proj, f_marks, table, stats, segments, last,
    )
    proj_gather = Gather(proj_payload, (8, 4, 2, 1))
    last = routed_gather.step([vectors])
    last = first.step([last])
    last = proj_gather.step([last])

    slot_rows = block * 3 * half_rows + block * half_rows + block
    slots = [shape((devices // (2 * CUTS), 2, slot_rows, LANES), BF16)] * (2 * CUTS)
    rim = shape((rows, RADIUS, width), BF16)
    dnorm, to_right, to_left, *slots = call(
        functools.partial(light_back_kernel, second_bits),
        [shape((own, width), F32), rim, rim, *slots],
        [dmid_low, query, keyval, probs, normed, mix, vectors, table, light_qkv, light_out],
        scratch=[
            pltpu.VMEM((rows * extent, 3 * width), BF16),
            pltpu.VMEM((extent, 2 * width), F32),
            pltpu.VMEM((width, span), F32),
        ],
        micros=10,
        mib=28,
        after=[last],
    )
    from_left = shifted(to_right, "seq", 1)
    from_right = shifted(to_left, "seq", -1)
    second = ScatterFolds(slots, second_bits)
    last = first.step([dnorm])
    last = proj_gather.step([last])
    last = routed_gather.step([last])
    routed_parts = routed_gather.parts()
    last = second.step([last])

    group = min(4, devices)
    groups = devices // group
    unit = ffn_heavy // devices
    me = lax.axis_index("seq").astype(jnp.int32).reshape(1)
    at_whole = lambda *dims: pl.BlockSpec(dims, lambda z, at: (0,) * len(dims))
    hidden_block = lambda start: pl.BlockSpec(
        (width, unit), lambda z, at: (0, start + z * group + lax.rem(at[0], group))
    )
    heavy_rows = group * block + unit // 2
    ffn_kept, ffn_sent = pl.pallas_call(
        functools.partial(heavy_ffn_kernel, len(routed_parts)),
        grid_spec=pltpu.PrefetchScalarGridSpec(
            num_scalar_prefetch=1,
            grid=(groups,),
            in_specs=[
                *(at_whole(*part.shape) for part in routed_parts),
                hidden_block(0),
                hidden_block(devices),
                pl.BlockSpec((unit, width), lambda z, at: (z * group + lax.rem(at[0], group), 0)),
                ANY,
            ],
            out_specs=[at_whole(heavy_rows, groups * unit)] * 2,
            scratch_shapes=[pltpu.VMEM((group * block, rows * per_row), BF16)],
        ),
        out_shape=[shape((heavy_rows, groups * unit), F32), shape((heavy_rows, groups * unit), BF16)],
        compiler_params=pltpu.CompilerParams(vmem_limit_bytes=40 * MIB),
        cost_estimate=cost(7),
    )(me, *routed_parts, heavy_gate_up, heavy_gate_up, heavy_down, last)
    ffn_got = swap(ffn_sent, "dp", 1)
    last = first.step([ffn_kept])
    last = proj_gather.step([last])
    proj_parts = proj_gather.parts()

    gathers = (routed_parts, proj_parts, key_parts)
    counts = [len(parts) for parts in gathers]
    shared = [*sum(gathers, []), keyval_all, table, heavy_q, heavy_kv, heavy_out]
    scratch = [
        pltpu.VMEM((width, per_row), BF16),
        pltpu.VMEM((width, per_row), F32),
        pltpu.VMEM((per_row, 2 * width), BF16),
    ]
    heavy_grads, heavy_parts = call(
        functools.partial(heavy_first_kernel, routed, counts),
        [shape((block, 4 * width + LANES), F32), shape((2, routed, width), F32)],
        shared,
        scratch=scratch,
        micros=8,
        mib=20,
        after=[last],
    )
    last = second.step([heavy_grads])
    last = first.step([last])
    piece = shape((block, groups * unit), BF16)
    *pieces, heavy_down_grad = call(
        pieces_kernel,
        [shape(piece.shape, F32)] + [piece] * (group - 1) + [shape((unit, width // 2), F32)],
        [ffn_kept, ffn_got],
        micros=0.5,
        mib=8,
        after=[last],
    )
    pieces = [pieces[0]] + [swap(pieces[j], "seq", j) for j in range(1, group)]
    grad_tokens, heavy_kept, heavy_sent = call(
        functools.partial(heavy_last_kernel, routed, counts),
        [
            shape((rows, span, width), BF16),
            shape((block, 2 * width + LANES), F32),
            shape((block, 2 * width + LANES), BF16),
        ],
        [query_route, kv_route, *shared, heavy_grads, heavy_parts, dnorm, from_left, from_right, dmid, tokens],
        smem=2,
        scratch=[pltpu.VMEM((own, width), F32), pltpu.VMEM((rows, 2, routed, width), F32)] + scratch,
        micros=9,
        mib=22,
        after=[pieces[0]],
    )
    heavy_got = swap(heavy_sent, "dp", 1)
    last = second.step([heavy_kept])
    light_gate_up_grad, light_down_grad = call(
        finish_light_kernel,
        [shape((block, ffn_light), F32), shape((ffn_light // devices, width // 2), F32)],
        first.pair(),
        after=[last],
    )
    heavy_q_grad, heavy_kv_grad, heavy_out_grad, heavy_vectors, stats, heavy_gate_up_grad = call(
        functools.partial(finish_heavy_kernel, groups),
        [
            shape((block, width // 2), F32),
            shape((block, width), F32),
            shape((block, width // 2), F32),
            shape((block, LANES), F32),
            shape((8, LANES), F32),
            shape((block, ffn_heavy), F32),
        ],
        [heavy_kept, heavy_got, *pieces],
        after=[light_down_grad],
    )
    last = second.step([heavy_vectors])
    light_qkv_grad, light_out_grad, light_vectors = call(
        finish_light_kernel,
        [
            shape((block, 3 * width // 2), F32),
            shape((block, width // 2), F32),
            shape((block, LANES), F32),
        ],
        second.pair(),
        after=[last],
    )
    sums = stats[0, 8:14]
    return (
        outputs,
        grad_tokens,
        light_vectors[:, 2] + heavy_vectors[:, 0],
        light_qkv_grad,
        light_out_grad,
        heavy_q_grad,
        heavy_kv_grad,
        heavy_out_grad,
        heavy_vectors[:, 1],
        light_vectors[:, 0],
        light_gate_up_grad,
        light_down_grad,
        heavy_gate_up_grad,
        heavy_down_grad,
        light_vectors[:, 1],
        jnp.sqrt(sums[:5] / (sums[5] * width)),
    )


def local(tokens, segments, query_route, *others):
    block = tokens.shape[2] // lax.axis_size("seq")
    fits = query_route.shape[1] <= 256 and block % 16 == 0
    return (local_kernels if fits else local_wide)(tokens, segments, query_route, *others)


def solution(mesh):
    placed = (
        P("dp", "seq", None),
        P("dp", "seq"),
        P("dp", None),
        P("dp", None),
        P("dp", "seq"),
        P("dp", "seq", None),
    ) + (P(),) * 13
    matrix = P("seq", "dp")
    vector = P("seq")
    return jax.shard_map(
        local,
        mesh=mesh,
        in_specs=placed,
        out_specs=(
            P("dp", "seq", None),
            P("dp", "seq", None),
            vector,
            matrix,
            matrix,
            matrix,
            matrix,
            matrix,
            vector,
            vector,
            matrix,
            matrix,
            matrix,
            matrix,
            vector,
            P(),
        ),
        check_vma=False,
    )
```

```python
import functools
import math

import jax
import jax.numpy as jnp
from jax import lax
from jax.experimental import pallas as pl
from jax.experimental.pallas import tpu as pltpu
from jax.sharding import PartitionSpec as P

DL = 96
DH = 64
RADIUS = 64
LANES = 128


PRECISE = lax.Precision.HIGHEST
EPSILON = 1e-06
NEG_FILL = -1e30
F32 = jnp.float32
BF16 = jnp.bfloat16


def swap(value, axis, bit):
    return lax.ppermute(value, axis, [(i, i ^ bit) for i in range(lax.axis_size(axis))])


def shifted(block, axis, distance):
    devices = range(lax.axis_size(axis))
    route = [(i - distance, i) for i in devices if i - distance in devices]
    return lax.ppermute(block, axis, route)


def gather_blocks(block):
    held = block[None]
    bit = lax.axis_size("seq") // 2
    while bit:
        held = jnp.concatenate([held, swap(held, "seq", bit)], axis=0)
        bit //= 2
    return held


def add_halves(value, dim, axis, bit, out_type=BF16):
    half = value.shape[dim] // 2
    keep = lax.slice_in_dim(value, 0, half, axis=dim)
    sent = lax.slice_in_dim(value, half, 2 * half, axis=dim)
    return (keep.astype(F32) + swap(sent, axis, bit).astype(F32)).astype(out_type)


def scatter_sum(slots):
    devices = lax.axis_size("seq")
    rows = slots.shape[2]
    slots = add_halves(slots, 0, "seq", 1)
    left, right = slots[:, :, : rows // 2], slots[:, :, rows // 2 :]
    left = add_halves(left, 0, "seq", 2)
    right = add_halves(right, 1, "dp", 1)
    left = add_halves(left, 1, "dp", 1)
    right = add_halves(right, 0, "seq", 2)
    both = jnp.concatenate([left, right], axis=2)
    bit = 4
    while bit < devices:
        both = add_halves(both, 0, "seq", bit, BF16 if 2 * bit < devices else F32)
        bit *= 2
    return both[0, 0]


def slot_places(me, devices):
    bits = devices.bit_length() - 1
    places = [int(format(p, f"0{bits}b")[::-1], 2) for p in range(devices)]
    return jnp.array(places, jnp.int32) ^ me


def slot_columns(value, me, devices):
    width = value.shape[-1]
    block = width // devices
    order = (slot_places(me, devices)[:, None] * block + jnp.arange(block)[None, :]).reshape(-1)
    onehot = (jnp.arange(width)[:, None] == order[None, :]).astype(BF16)
    return jnp.dot(value, onehot, preferred_element_type=F32).astype(BF16)


def own_half_first(value, place):
    half = value.shape[-1] // 2
    first, second = value[..., :half], value[..., half:]
    return (jnp.where(place == 0, first, second), jnp.where(place == 0, second, first))


def slot_block(grad_halves, devices):
    stacked = jnp.stack(grad_halves)
    _, total, cols = stacked.shape
    parts = stacked.reshape(2, devices, total // devices, cols // LANES, LANES)
    return parts.transpose(1, 0, 3, 2, 4).reshape(devices, 2, -1, LANES).astype(BF16)


def unslot(rows, cols):
    return rows.reshape(cols // LANES, -1, LANES).transpose(1, 0, 2).reshape(-1, cols)


def slot_vectors(vectors, me, devices):
    block = vectors[0].shape[0] // devices
    table = jnp.stack(vectors, axis=-1).reshape(devices, block, len(vectors))
    table = jnp.take(table, slot_places(me, devices), axis=0)
    table = jnp.pad(table, ((0, 0), (0, 0), (0, LANES - len(vectors))))
    return jnp.broadcast_to(table[:, None], (devices, 2, block, LANES)).astype(BF16)


def split_parts(value):
    high = lax.reduce_precision(value, 8, 7)
    middle = lax.reduce_precision(value - high, 8, 7)
    return (high, middle, value - high - middle)


def rms_factor(hidden):
    return lax.rsqrt(jnp.mean(hidden * hidden, axis=-1, keepdims=True) + EPSILON)


def norm_back(hidden, factor, gain_vec, upstream):
    weighted = upstream * gain_vec
    inner_mean = jnp.mean(weighted * hidden, axis=-1, keepdims=True)
    return factor * weighted - hidden * (factor * factor * factor) * inner_mean


def pick_rows(source, positions):
    return jnp.take_along_axis(source, positions[..., None], axis=1)


def place_rows(values, positions, extent):
    onehot = (positions[..., None] == jnp.arange(extent)[None, None, :]).astype(F32)
    return jnp.einsum("rqs,rqd->rsd", onehot, values, precision=PRECISE)


def matmul(left, right):
    return jnp.einsum("...d,de->...e", left, right, preferred_element_type=F32)


def matmul_t(left, right):
    return jnp.einsum("...e,de->...d", left, right, preferred_element_type=F32)


def outer(left, right):
    return jnp.einsum("rsd,rse->de", left, right, preferred_element_type=F32)


def glu_value(gate_part, up_part):
    return jax.nn.gelu(gate_part, approximate=True) * up_part


def geglu(inputs, gate_up, down, upstream_low):
    width = down.shape[0]
    both = matmul(inputs, gate_up)
    gate_part, up_part = both[..., :width], both[..., width:]
    hidden, pull_back = jax.vjp(glu_value, gate_part, up_part)
    gate_grad, up_grad = pull_back(matmul_t(upstream_low, down))
    return (hidden.astype(BF16), gate_grad.astype(BF16), up_grad.astype(BF16))


def routed_probs(query_heads, key_heads, query_seg, key_seg):
    scores = jnp.einsum("rqd,rkd->rqk", query_heads, key_heads, preferred_element_type=F32)
    scores = scores / math.sqrt(DH)
    allowed = query_seg[:, :, None] == key_seg[:, None, :]
    scores = jnp.where(allowed, scores, NEG_FILL)
    peak = jnp.maximum(jnp.max(scores, axis=-1, keepdims=True), 0.0)
    numer = jnp.exp(scores - peak)
    return numer / (jnp.exp(-peak) + jnp.sum(numer, axis=-1, keepdims=True))


def heavy_forward(query, keys, vals, query_seg, key_seg):
    def head(parts):
        query_h, key_h, val_h = parts
        probs = routed_probs(query_h, key_h, query_seg, key_seg).astype(BF16)
        return jnp.einsum("rqk,rkd->rqd", probs, val_h, preferred_element_type=F32).astype(BF16)

    return join_heads(jax.vmap(head)((split_heads(query), split_heads(keys), split_heads(vals))))


def heavy_both(query, keys, vals, query_seg, key_seg, mix_grad):
    def head(parts, query_seg=query_seg, key_seg=key_seg):
        query_h, key_h, val_h, grad_h = parts
        probs = routed_probs(query_h, key_h, query_seg, key_seg)
        probs_low = probs.astype(BF16)
        mix = jnp.einsum("rqk,rkd->rqd", probs_low, val_h, preferred_element_type=F32)
        prob_grad = jnp.einsum("rqd,rkd->rqk", grad_h, val_h, preferred_element_type=F32)
        delta = jnp.sum(probs * prob_grad, axis=-1, keepdims=True)
        score_grad = (probs * (prob_grad - delta)).astype(BF16)
        dquery = jnp.einsum("rqk,rkd->rqd", score_grad, key_h, preferred_element_type=F32)
        dkey = jnp.einsum("rqk,rqd->rkd", score_grad, query_h, preferred_element_type=F32)
        dval = jnp.einsum("rqk,rqd->rkd", probs_low, grad_h, preferred_element_type=F32)
        scale = 1.0 / math.sqrt(DH)
        return (mix.astype(BF16), (dquery * scale).astype(BF16), (dkey * scale).astype(BF16), dval.astype(BF16))

    heads = tuple(split_heads(v) for v in (query, keys, vals, mix_grad))
    if query.shape[1] <= 512:
        return tuple(join_heads(v) for v in jax.vmap(head)(heads))
    count, rows = heads[0].shape[:2]
    place = jnp.tile(jnp.arange(rows), count)
    parts = tuple(v.reshape(count * rows, 1, *v.shape[2:]) for v in heads)
    done = lax.map(lambda p: head(p[0], query_seg[p[1]][None], key_seg[p[1]][None]), (parts, place))
    return tuple(join_heads(v.reshape(count, rows, *v.shape[2:])) for v in done)


def split_heads(value):
    rows, tokens, width = value.shape
    return value.reshape(rows, tokens, width // DH, DH).transpose(2, 0, 1, 3)


def join_heads(value):
    heads, rows, tokens, width = value.shape
    return value.transpose(1, 2, 0, 3).reshape(rows, tokens, heads * width)


def tokens_of(blocks):
    devices, rows, count, width = blocks.shape
    return blocks.transpose(1, 0, 2, 3).reshape(rows, devices * count, width)


def with_segment(rows, segs):
    marks = jnp.broadcast_to((segs + 2).astype(BF16)[..., None], segs.shape + (LANES,))
    return jnp.concatenate([rows, marks], axis=-1)


def local_wide(
    tokens,
    segments,
    query_route,
    kv_route,
    ffn_route,
    grad_out,
    attn_gain,
    light_qkv,
    light_out,
    heavy_q,
    heavy_kv,
    heavy_out,
    route_query,
    ffn_gain,
    light_gate_up,
    light_down,
    heavy_gate_up,
    heavy_down,
    route_ffn,
):
    row_count, seg_span, width = tokens.shape
    light_heads = width // DL
    ffn_heavy = heavy_down.shape[0]
    devices = lax.axis_size("seq")
    me = lax.axis_index("seq")
    half_place = lax.axis_index("dp")
    anchor = me * seg_span
    routed_own = query_route.shape[1] // devices
    own_query = lax.dynamic_slice_in_dim(query_route, me * routed_own, routed_own, 1) - anchor
    own_key = lax.dynamic_slice_in_dim(kv_route, me * routed_own, routed_own, 1) - anchor
    own_ffn = ffn_route - anchor

    marked = with_segment(tokens, segments)
    before = shifted(marked[:, seg_span - RADIUS :], "seq", 1)
    after = shifted(marked[:, :RADIUS], "seq", -1)
    hidden = tokens.astype(F32)
    factor_one = rms_factor(hidden)
    normed = hidden * factor_one * attn_gain
    normed_low = normed.astype(BF16)
    key_rows = pick_rows(normed_low, own_key)
    key_payload = with_segment(key_rows, jnp.take_along_axis(segments, own_key, axis=1))
    key_blocks = tokens_of(gather_blocks(key_payload))
    key_all, key_seg = key_blocks[..., :width], key_blocks[..., width]

    extended = jnp.concatenate([before, marked, after], axis=1)
    seg_ext = extended[..., width]
    hidden_ext = extended[..., :width].astype(F32)
    factor_ext = rms_factor(hidden_ext)
    normed_ext_low = (hidden_ext * factor_ext * attn_gain).astype(BF16)
    extent = seg_span + 2 * RADIUS
    query_low = matmul(normed_low, light_qkv[:, :width]).astype(BF16)
    query_low = query_low.reshape(row_count, seg_span, light_heads, DL)
    kv_ext = matmul(normed_ext_low, light_qkv[:, width:]).astype(BF16)
    key_ext = kv_ext[..., :width].reshape(row_count, extent, light_heads, DL)
    val_ext = kv_ext[..., width:].reshape(row_count, extent, light_heads, DL)
    offset = jnp.arange(seg_span)[:, None] - jnp.arange(extent)[None, :] + RADIUS
    seg_own = seg_ext[:, RADIUS : RADIUS + seg_span]
    allowed = (jnp.abs(offset) <= RADIUS)[None] & (seg_own[:, :, None] == seg_ext[:, None, :])
    light_scale = 1.0 / math.sqrt(DL)
    scores = jnp.einsum("rqhd,rkhd->rhqk", query_low, key_ext, preferred_element_type=F32)
    scores = jnp.where(allowed[:, None], scores * light_scale, NEG_FILL)
    numerators = jnp.exp(scores - jnp.max(scores, axis=-1, keepdims=True))
    probs_light = numerators / jnp.sum(numerators, axis=-1, keepdims=True)
    probs_low = probs_light.astype(BF16)
    light_mix = jnp.einsum("rhqk,rkhd->rqhd", probs_low, val_ext, preferred_element_type=F32)
    light_mix = light_mix.reshape(row_count, seg_span, width).astype(BF16)
    light_attn = matmul(light_mix, light_out)

    query_rows = pick_rows(normed_low, own_query)
    query_seg_own = (jnp.take_along_axis(segments, own_query, axis=1) + 2).astype(BF16)
    heavy_query = matmul(query_rows, heavy_q).astype(BF16)
    keyval_all = matmul(key_all, heavy_kv).astype(BF16)
    heavy_width = heavy_q.shape[1]
    keys_all, vals_all = keyval_all[..., :heavy_width], keyval_all[..., heavy_width:]
    heavy_mix = heavy_forward(heavy_query, keys_all, vals_all, query_seg_own, key_seg)
    heavy_proj = matmul(heavy_mix, heavy_out)
    query_normed = pick_rows(normed, own_query)
    route_query_full = route_query.astype(F32)
    query_gate = jax.nn.sigmoid(jnp.sum(query_normed * route_query_full, axis=-1))
    heavy_attn = place_rows(query_gate[..., None] * heavy_proj, own_query, seg_span)

    middle = hidden + light_attn + heavy_attn
    factor_two = rms_factor(middle)
    normed_two = middle * factor_two * ffn_gain
    low_two = normed_two.astype(BF16)
    upstream = grad_out.astype(F32)
    ffn_normed = pick_rows(normed_two, own_ffn)
    ffn_rows = ffn_normed.astype(BF16)
    route_ffn_full = route_ffn.astype(F32)
    ffn_gate = jax.nn.sigmoid(jnp.sum(ffn_normed * route_ffn_full, axis=-1))
    ffn_upstream = pick_rows(upstream, own_ffn)
    ffn_low = (ffn_upstream * ffn_gate[..., None]).astype(BF16)
    routed_payload = with_segment(
        jnp.concatenate([ffn_rows, ffn_low, query_rows], axis=-1),
        jnp.take_along_axis(segments, own_query, axis=1),
    )
    routed_blocks = tokens_of(gather_blocks(routed_payload))
    ffn_all = routed_blocks[..., :width]
    ffn_low_all = routed_blocks[..., width : 2 * width]
    query_all = routed_blocks[..., 2 * width : 3 * width]
    query_seg = routed_blocks[..., 3 * width]

    hidden_light, gate_grad, up_grad = geglu(low_two, light_gate_up, light_down, grad_out)
    light_ff = matmul(hidden_light, light_down)
    light_both = jnp.concatenate([gate_grad, up_grad], axis=-1)
    normed_two_grad = matmul_t(light_both, light_gate_up)
    hidden_heavy, gate_grad_h, up_grad_h = geglu(ffn_rows, heavy_gate_up, heavy_down, ffn_low)
    heavy_ffn_proj = matmul(hidden_heavy, heavy_down)
    heavy_ff = place_rows(ffn_gate[..., None] * heavy_ffn_proj, own_ffn, seg_span)
    outputs = (middle + light_ff + heavy_ff).astype(BF16)
    ffn_gate_grad = jnp.sum(ffn_upstream * heavy_ffn_proj, axis=-1)
    ffn_logit_grad = ffn_gate_grad * ffn_gate * (1.0 - ffn_gate)
    route_ffn_grad = jnp.sum(ffn_logit_grad[..., None] * ffn_normed, axis=(0, 1))
    ffn_rows_grad = matmul_t(jnp.concatenate([gate_grad_h, up_grad_h], axis=-1), heavy_gate_up)
    ffn_rows_grad = ffn_rows_grad + ffn_logit_grad[..., None] * route_ffn_full
    normed_two_grad = normed_two_grad + place_rows(ffn_rows_grad, own_ffn, seg_span)
    ffn_gain_grad = jnp.sum(normed_two_grad * middle * factor_two, axis=(0, 1))
    middle_grad = upstream + norm_back(middle, factor_two, ffn_gain, normed_two_grad)
    middle_low = middle_grad.astype(BF16)

    valid_rows = (segments >= 0).astype(F32)[..., None]
    sums = jnp.stack(
        [
            jnp.sum(valid_rows * branch * branch)
            for branch in (hidden, light_attn, heavy_attn, light_ff, heavy_ff)
        ]
        + [jnp.sum(valid_rows)]
    )
    heavy_upstream = pick_rows(middle_grad, own_query)
    query_gate_grad = jnp.sum(heavy_upstream * heavy_proj, axis=-1)
    proj_low = (heavy_upstream * query_gate[..., None]).astype(BF16)
    sum_lanes = jnp.pad(jnp.concatenate(split_parts(sums)), (0, LANES - 18)).astype(BF16)
    sum_lanes = jnp.broadcast_to(sum_lanes, proj_low.shape[:2] + (LANES,))
    proj_blocks = gather_blocks(jnp.concatenate([proj_low, sum_lanes], axis=-1))
    sums_all = jnp.sum(proj_blocks[:, 0, 0, width : width + 18].astype(F32), axis=0)
    sums_all = jnp.sum(sums_all.reshape(3, 6), axis=0)
    sums_all = sums_all + swap(sums_all, "dp", 1)
    rms_stats = jnp.sqrt(sums_all[:5] / (sums_all[5] * width))
    proj_all = tokens_of(proj_blocks)[..., :width]

    flat = lambda v: v.reshape(-1, v.shape[-1])
    gate_up_grad = [
        jnp.dot(slot_columns(flat(low_two), me, devices).T, flat(part), preferred_element_type=F32)
        for part in own_half_first(light_both, half_place)
    ]
    hidden_slots = slot_columns(flat(hidden_light), me, devices).T
    down_grad = [
        jnp.dot(hidden_slots, flat(part), preferred_element_type=F32)
        for part in own_half_first(grad_out, half_place)
    ]
    mix_slots = slot_columns(flat(light_mix), me, devices).T
    out_grad = [
        jnp.dot(mix_slots, flat(part), preferred_element_type=F32)
        for part in own_half_first(middle_low, half_place)
    ]
    first_sum = scatter_sum(
        jnp.concatenate(
            [
                slot_block(gate_up_grad, devices),
                slot_block(down_grad, devices),
                slot_block(out_grad, devices),
                slot_vectors((ffn_gain_grad, route_ffn_grad), me, devices),
            ],
            axis=2,
        )
    )
    block = width // devices
    block_ff = light_down.shape[0] // devices
    cuts = [0]
    for rows in (
        block * light_gate_up.shape[1] // 2 // LANES,
        block_ff * width // 2 // LANES,
        block * width // 2 // LANES,
        block,
    ):
        cuts.append(cuts[-1] + rows)
    light_gate_up_grad = unslot(first_sum[cuts[0] : cuts[1]], light_gate_up.shape[1] // 2)
    light_down_grad = unslot(first_sum[cuts[1] : cuts[2]], width // 2)
    light_out_grad = unslot(first_sum[cuts[2] : cuts[3]], width // 2)
    ffn_gain_grad = first_sum[cuts[3] : cuts[4], 0]
    route_ffn_grad = first_sum[cuts[3] : cuts[4], 1]

    group = min(4, devices)
    low_place, high_place = me % group, me // group
    groups = devices // group
    unit = ffn_heavy // devices
    gate_up_parts = heavy_gate_up.reshape(width, 2, groups, group, unit)
    gate_up_mine = lax.dynamic_index_in_dim(gate_up_parts, low_place, 3, False)
    down_mine = lax.dynamic_index_in_dim(
        heavy_down.reshape(groups, group, unit, width), low_place, 1, False
    )
    x_all = flat(ffn_all)
    up_all = flat(ffn_low_all)
    hidden_mine, gate_mine, up_mine = geglu(
        x_all,
        gate_up_mine.reshape(width, -1),
        down_mine.reshape(-1, width),
        up_all,
    )
    hidden_block = lax.dynamic_slice_in_dim(hidden_mine, high_place * unit, unit, 1)
    heavy_down_half = [
        jnp.dot(hidden_block.T, part, preferred_element_type=F32)
        for part in own_half_first(up_all, half_place)
    ]
    heavy_down_grad = heavy_down_half[0] + swap(heavy_down_half[1].astype(BF16), "dp", 1).astype(F32)
    x_group = lax.dynamic_slice_in_dim(x_all, high_place * group * block, group * block, 1)
    x_group = x_group.reshape(-1, group, block)
    x_group = jnp.take(x_group, jnp.arange(group) ^ low_place, axis=1).reshape(-1, group * block)
    gate_half, up_half = (
        jnp.dot(x_group.T, part, preferred_element_type=F32) for part in (gate_mine, up_mine)
    )
    kept = jnp.where(half_place == 0, gate_half, up_half)
    sent = jnp.where(half_place == 0, up_half, gate_half)
    kept = (kept + swap(sent.astype(BF16), "dp", 1).astype(F32)).reshape(group, block, groups, unit)
    pieces = [kept[0]]
    for place in range(1, group):
        pieces.append(swap(kept[place].astype(BF16), "seq", place).astype(F32))
    pieces = jnp.take(jnp.stack(pieces, axis=2), jnp.arange(group) ^ low_place, axis=2)
    heavy_gate_up_grad = pieces.reshape(block, ffn_heavy)

    mix_grad = matmul_t(middle_low, light_out).astype(BF16)
    mix_grad = mix_grad.reshape(row_count, seg_span, light_heads, DL)
    val_grad = jnp.einsum("rhqk,rqhd->rkhd", probs_low, mix_grad, preferred_element_type=F32)
    prob_grad = jnp.einsum("rqhd,rkhd->rhqk", mix_grad, val_ext, preferred_element_type=F32)
    delta = jnp.sum(probs_light * prob_grad, axis=-1, keepdims=True)
    score_grad = (probs_light * (prob_grad - delta)).astype(BF16)
    query_grad = jnp.einsum("rhqk,rkhd->rqhd", score_grad, key_ext, preferred_element_type=F32)
    key_grad = jnp.einsum("rhqk,rqhd->rkhd", score_grad, query_low, preferred_element_type=F32)
    query_grad = (query_grad * light_scale).reshape(row_count, seg_span, width).astype(BF16)
    kv_grad = jnp.concatenate(
        [
            (key_grad * light_scale).reshape(row_count, extent, width),
            val_grad.reshape(row_count, extent, width),
        ],
        axis=-1,
    ).astype(BF16)
    normed_grad_ext = matmul_t(kv_grad, light_qkv[:, width:])
    normed_grad = matmul_t(query_grad, light_qkv[:, :width])
    normed_grad = normed_grad + normed_grad_ext[:, RADIUS : RADIUS + seg_span]
    from_right = shifted(normed_grad_ext[:, :RADIUS].astype(BF16), "seq", -1)
    from_left = shifted(normed_grad_ext[:, seg_span + RADIUS :].astype(BF16), "seq", 1)
    normed_grad = normed_grad.at[:, :RADIUS].add(from_left.astype(F32))
    normed_grad = normed_grad.at[:, seg_span - RADIUS :].add(from_right.astype(F32))

    hq_all = matmul(query_all, heavy_q).astype(BF16)
    do2_all = matmul_t(proj_all, heavy_out).astype(BF16)
    mix_all, dhq_all, dhk_all, dhv_all = heavy_both(
        hq_all, keys_all, vals_all, query_seg, key_seg, do2_all
    )
    dhkv_all = jnp.concatenate([dhk_all, dhv_all], axis=-1)
    mine = lambda v: lax.dynamic_slice_in_dim(flat(v), me * block, block, 1).T
    heavy_grads = [
        own_half_first(jnp.dot(mine(left), flat(right), preferred_element_type=F32), half_place)
        for left, right in ((query_all, dhq_all), (key_all, dhkv_all), (mix_all, proj_all))
    ]
    heavy_kept = jnp.concatenate([pair[0] for pair in heavy_grads], axis=-1)
    heavy_sent = jnp.concatenate([pair[1] for pair in heavy_grads], axis=-1)
    heavy_sum = heavy_kept + swap(heavy_sent.astype(BF16), "dp", 1).astype(F32)
    heavy_half = heavy_width // 2
    heavy_q_grad = heavy_sum[:, :heavy_half]
    heavy_kv_grad = heavy_sum[:, heavy_half : 3 * heavy_half]
    heavy_out_grad = heavy_sum[:, 3 * heavy_half :]
    query_logit_grad = query_gate_grad * query_gate * (1.0 - query_gate)
    route_query_grad = jnp.sum(query_logit_grad[..., None] * query_normed, axis=(0, 1))
    query_rows_grad = (
        matmul_t(dhq_all[:, :routed_own], heavy_q) + query_logit_grad[..., None] * route_query_full
    )
    key_rows_grad = matmul_t(dhkv_all[:, :routed_own], heavy_kv)
    normed_grad = (
        normed_grad
        + place_rows(query_rows_grad, own_query, seg_span)
        + place_rows(key_rows_grad, own_key, seg_span)
    )
    attn_gain_grad = jnp.sum(normed_grad * hidden * factor_one, axis=(0, 1))
    hidden_norm_grad = norm_back(hidden, factor_one, attn_gain, normed_grad)
    grad_tokens = (middle_grad + hidden_norm_grad).astype(BF16)

    own_slots = slot_columns(flat(normed_low), me, devices).T
    ext_slots = slot_columns(flat(normed_ext_low), me, devices).T
    qkv_grad = jnp.concatenate(
        [
            jnp.dot(own_slots, flat(query_grad), preferred_element_type=F32),
            jnp.dot(ext_slots, flat(kv_grad), preferred_element_type=F32),
        ],
        axis=-1,
    )
    second_sum = scatter_sum(
        jnp.concatenate(
            [
                slot_block(own_half_first(qkv_grad, half_place), devices),
                slot_vectors((attn_gain_grad, route_query_grad), me, devices),
            ],
            axis=2,
        )
    )
    qkv_cols = light_qkv.shape[1] // 2
    qkv_rows = block * qkv_cols // LANES
    light_qkv_grad = unslot(second_sum[:qkv_rows], qkv_cols)
    attn_gain_grad = second_sum[qkv_rows:, 0]
    route_query_grad = second_sum[qkv_rows:, 1]
    return (
        outputs,
        grad_tokens,
        attn_gain_grad,
        light_qkv_grad,
        light_out_grad,
        heavy_q_grad,
        heavy_kv_grad,
        heavy_out_grad,
        route_query_grad,
        ffn_gain_grad,
        light_gate_up_grad,
        light_down_grad,
        heavy_gate_up_grad,
        heavy_down_grad,
        route_ffn_grad,
        rms_stats,
    )


VMEM = pl.BlockSpec(memory_space=pltpu.VMEM)
SMEM = pl.BlockSpec(memory_space=pltpu.SMEM)
ANY = pl.BlockSpec(memory_space=pl.ANY)
HBM = pl.BlockSpec(memory_space=pltpu.HBM)
GELU_RATE = math.sqrt(2.0 / math.pi)
GELU_CUBE = 0.044715
MIB = 1024 * 1024
CUTS = 4


def shape(dims, dtype):
    return jax.ShapeDtypeStruct(dims, dtype)


def call(kernel, outs, ins, smem=0, scratch=(), micros=1, mib=16, after=(), hbm=0):
    used = len(ins)

    def body(*refs):
        kernel(*refs[:used], *refs[used + len(after) :])

    return pl.pallas_call(
        body,
        out_shape=outs,
        in_specs=[HBM] * hbm + [SMEM] * smem + [VMEM] * (used - smem - hbm) + [ANY] * len(after),
        out_specs=[VMEM] * len(outs),
        scratch_shapes=list(scratch),
        compiler_params=pltpu.CompilerParams(vmem_limit_bytes=mib * MIB),
        cost_estimate=cost(micros),
    )(*ins, *after)


def cost(micros):
    return pl.CostEstimate(flops=int(micros * 10**9), bytes_accessed=10**6, transcendentals=0)


def dot(left, right):
    return jnp.dot(left, right, preferred_element_type=F32)


def dot_t(left, right):
    return lax.dot_general(left, right, (((1,), (1,)), ((), ())), preferred_element_type=F32)


def t_dot(left, right):
    return lax.dot_general(left, right, (((0,), (0,)), ((), ())), preferred_element_type=F32)


def row_factor(value):
    return lax.rsqrt(jnp.mean(value * value, axis=-1, keepdims=True) + EPSILON)


def as_column(row):
    count = row.shape[1]
    down = lax.broadcasted_iota(jnp.int32, (count, count), 0)
    along = lax.broadcasted_iota(jnp.int32, (count, count), 1)
    return jnp.sum(jnp.where(down == along, row, 0.0), axis=1, keepdims=True)


def head_window(head, size):
    first = head * size // LANES * LANES
    lanes = (head * size + size - 1) // LANES * LANES + LANES - first
    place = lax.broadcasted_iota(jnp.int32, (1, lanes), 1) + first
    return first, lanes, (place >= head * size) & (place < head * size + size)


def slot_owners(me, bits):
    owners = []
    for p in range(1 << len(bits)):
        flips = sum(bit for k, bit in enumerate(bits) if p >> (len(bits) - 1 - k) & 1)
        owners.append(flips ^ me)
    return owners


def slot_select(width, bits, me):
    block = width >> len(bits)
    along = lax.broadcasted_iota(jnp.int32, (block, width), 1)
    inside = lax.broadcasted_iota(jnp.int32, (block, width), 0)
    rows = [(along == inside + owner * block).astype(F32) for owner in slot_owners(me, bits)]
    return jnp.concatenate(rows, axis=0).astype(BF16)


def two_gelu(value):
    square = value * value
    bend = jnp.tanh(GELU_RATE * value * (1.0 + GELU_CUBE * square))
    half = 0.5 * (1.0 + bend)
    slope = half + 0.5 * value * (1.0 - bend * bend) * GELU_RATE * (1.0 + 3.0 * GELU_CUBE * square)
    return value * half, slope


def first_kernel(
    routed, route_in, segs_in, tokens_in, gain_in, ffn_gain_in, route_q_in, route_f_in,
    keys, upper, lower, table,
    route, seg_at, segs, tokens, gain, ffn_gain, route_q, route_f, normed, picked, sems,
):
    copies = [
        pltpu.make_async_copy(source, target, sems.at[k])
        for k, (source, target) in enumerate(
            (
                (tokens_in, tokens),
                (gain_in, gain),
                (route_in, route),
                (segs_in, seg_at),
                (segs_in, segs),
                (ffn_gain_in, ffn_gain),
                (route_q_in, route_q),
                (route_f_in, route_f),
            )
        )
    ]
    for copy in copies:
        copy.start()
    for copy in copies:
        copy.wait()
    rows, span, width = tokens.shape
    me = lax.axis_index("seq")
    for k, vector in enumerate((gain, ffn_gain, route_q, route_f)):
        table[k : k + 1, :] = vector[...].astype(F32).reshape(1, width)
    hidden = tokens[...].reshape(rows * span, width).astype(F32)
    normed[...] = hidden * row_factor(hidden) * table[0:1, :]
    for r in range(rows):
        for k in range(routed):
            place = route[r, me * routed + k] - me * span
            at = pl.ds(r * routed + k, 1)
            picked[at, :width] = normed[pl.ds(r * span + place, 1), :]
            picked[at, width:] = jnp.full((1, LANES), (seg_at[r, place] + 2).astype(F32))
    keys[...] = picked[...].astype(BF16).reshape(keys.shape)
    marks = (segs[...] + 2).astype(F32)
    for out, start in ((upper, span - RADIUS), (lower, 0)):
        out[:, :RADIUS, :] = tokens[:, start : start + RADIUS, :]
        out[:, RADIUS:, :] = jnp.zeros((rows, 16, width), BF16)
        for r in range(rows):
            out[r, RADIUS:, :span] = jnp.broadcast_to(marks[r : r + 1], (16, span)).astype(BF16)


def light_kernel(
    before, tokens, after, segs, table, w_qkv, w_out,
    normed, query, keyval, probs, mix, attn, seg_row, mix_t,
):
    rows, span, width = tokens.shape
    extent = span + 2 * RADIUS
    own_all = rows * span
    heads = width // DL
    places = []
    for r in range(rows):
        places.append((tokens, r, span, r * span, r * extent + RADIUS))
    for r in range(rows):
        rim = own_all + 2 * r * RADIUS
        places.append((before, r, RADIUS, rim, r * extent))
        places.append((after, r, RADIUS, rim + RADIUS, r * extent + RADIUS + span))
    for part, r, size, at, _ in places:
        value = part[r, :size, :].astype(F32)
        normed[at : at + size, :] = (value * row_factor(value) * table[0:1, :]).astype(BF16)
    made = dot(normed[...], w_qkv[:, width:]).astype(BF16)
    for _, _, size, at, to in places:
        keyval[to : to + size, :] = made[at : at + size]
    query[...] = dot(normed[:own_all, :], w_qkv[:, :width]).astype(BF16)
    down = lax.broadcasted_iota(jnp.int32, (extent, span), 0)
    along = lax.broadcasted_iota(jnp.int32, (extent, span), 1)
    near = jnp.abs(along - down + RADIUS) <= RADIUS
    for r in range(rows):
        marks = (segs[r : r + 1, :] + 2).astype(F32)
        seg_row[:, :span] = before[r, RADIUS : RADIUS + 8, :span].astype(F32)
        seg_row[:, span : 2 * span] = jnp.broadcast_to(marks, (8, span))
        seg_row[:, 2 * span :] = after[r, RADIUS : RADIUS + 8, :span].astype(F32)
        columns = [as_column(seg_row[0:1, c * span : (c + 1) * span]) for c in range(3)]
        key_marks = jnp.concatenate([columns[0][span - RADIUS :], columns[1], columns[2][:RADIUS]], axis=0)
        allowed = near & (key_marks == marks)
        key_rows = slice(r * extent, (r + 1) * extent)
        val_t = keyval[key_rows, width:].T
        for h in range(heads):
            first, lanes, mask = head_window(h, DL)
            window = slice(first, first + lanes)
            q_head = jnp.where(mask, query[r * span : (r + 1) * span, window], 0)
            scores = dot_t(keyval[key_rows, window], q_head)
            scores = jnp.where(allowed, scores * (1.0 / math.sqrt(DL)), NEG_FILL)
            numer = jnp.exp(scores - jnp.max(scores, axis=0, keepdims=True))
            share = (numer / jnp.sum(numer, axis=0, keepdims=True)).astype(BF16)
            probs[r * heads + h] = share
            mix_t[h * DL : (h + 1) * DL, :] = dot(val_t[h * DL : (h + 1) * DL, :], share)
        mix[r * span : (r + 1) * span, :] = mix_t[...].T.astype(BF16)
    attn[...] = dot(mix[...], w_out[...])


def stat_row(value):
    total = jnp.sum(jnp.sum(value, axis=0, keepdims=True), axis=1, keepdims=True)
    return jnp.broadcast_to(total, (1, LANES))


def valid_column(segs):
    rows = segs.shape[0]
    parts = [as_column((segs[r : r + 1, :] >= 0).astype(F32)) for r in range(rows)]
    return jnp.concatenate(parts, axis=0)


def router(rows, weights):
    return jax.nn.sigmoid(jnp.sum(rows[...] * weights, axis=-1, keepdims=True))


def gathered(refs, row, lanes):
    value = jnp.concatenate([ref[:, row, :, lanes] for ref in refs], axis=0)
    return value.reshape(-1, value.shape[-1])


def middle_kernel(routed, parts, q_route, f_route, seg_at, tokens, segs, *refs):
    keys, refs = refs[:parts], refs[parts:]
    attn, upstream, table, w_q, w_kv, w_out = refs[:6]
    middle, normed_two, keyval, payload, q_rows, f_rows, f_up, proj, f_marks, stats = refs[6:16]
    full, marks, placed = refs[16:]
    rows, span, width = tokens.shape
    me = lax.axis_index("seq")
    hidden = tokens[...].reshape(rows * span, width).astype(F32)
    full[...] = hidden * row_factor(hidden) * table[0:1, :]
    for r in range(rows):
        for k in range(routed):
            at = pl.ds(r * routed + k, 1)
            place = q_route[r, me * routed + k] - me * span
            q_rows[at, :] = full[pl.ds(r * span + place, 1), :]
            marks[at, :] = jnp.full((1, LANES), (seg_at[r, place] + 2).astype(F32))
            place = f_route[r, k] - me * span
            f_marks[at, :] = jnp.full((1, LANES), (seg_at[r, place] + 2).astype(F32))
    q_low = q_rows[...].astype(BF16)
    payload[:, :, 2 * width : 3 * width] = q_low.reshape(rows, routed, width)
    payload[:, :, 3 * width :] = marks[...].astype(BF16).reshape(rows, routed, LANES)
    key_low = jnp.concatenate([gathered(keys, r, slice(0, width)) for r in range(rows)], axis=0)
    keyval[...] = dot(key_low, w_kv[...]).astype(BF16).reshape(keyval.shape)
    query = dot(q_low, w_q[...]).astype(BF16)
    heads = width // DH
    lane = lax.broadcasted_iota(jnp.int32, (1, width), 1)
    masks = [(lane >= h * DH) & (lane < (h + 1) * DH) for h in range(heads)]
    mixed = []
    for r in range(rows):
        mine = query[r * routed : (r + 1) * routed]
        wide = jnp.concatenate([jnp.where(m, mine, 0) for m in masks], axis=0)
        scores = dot_t(wide, keyval[r, :, :width]) * (1.0 / math.sqrt(DH))
        key_marks = gathered(keys, r, slice(width, width + LANES)).astype(F32).T[0:1, :]
        query_marks = jnp.concatenate([marks[r * routed : (r + 1) * routed, 0:1]] * heads, axis=0)
        scores = jnp.where(query_marks == key_marks, scores, NEG_FILL)
        peak = jnp.maximum(jnp.max(scores, axis=-1, keepdims=True), 0.0)
        numer = jnp.exp(scores - peak)
        share = numer / (jnp.exp(-peak) + jnp.sum(numer, axis=-1, keepdims=True))
        part = dot(share.astype(BF16), keyval[r, :, width:])
        total = jnp.zeros((routed, width), F32)
        for h in range(heads):
            total = total + jnp.where(masks[h], part[h * routed : (h + 1) * routed], 0.0)
        mixed.append(total)
    mixed = jnp.concatenate(mixed, axis=0).astype(BF16)
    proj[...] = dot(mixed, w_out[...])
    placed[...] = router(q_rows, table[2:3, :]) * proj[...]
    light = attn[...]
    middle[...] = hidden + light
    for r in range(rows):
        for k in range(routed):
            place = q_route[r, me * routed + k] - me * span
            at = pl.ds(r * span + place, 1)
            middle[at, :] = middle[at, :] + placed[pl.ds(r * routed + k, 1), :]
    valid = valid_column(segs)
    stats[...] = jnp.zeros(stats.shape, F32)
    stats[0:1, :] = stat_row(valid * hidden * hidden)
    stats[1:2, :] = stat_row(valid * light * light)
    stats[2:3, :] = stat_row(jnp.where(marks[:, 0:1] >= 2.0, placed[...] * placed[...], 0.0))
    stats[5:6, :] = stat_row(valid)
    mid = middle[...]
    full[...] = mid * row_factor(mid) * table[1:2, :]
    normed_two[...] = full[...].astype(BF16)
    for r in range(rows):
        for k in range(routed):
            place = f_route[r, k] - me * span
            f_rows[pl.ds(r * routed + k, 1), :] = full[pl.ds(r * span + place, 1), :]
    full[...] = upstream[...].reshape(rows * span, width).astype(F32)
    for r in range(rows):
        for k in range(routed):
            place = f_route[r, k] - me * span
            f_up[pl.ds(r * routed + k, 1), :] = full[pl.ds(r * span + place, 1), :]
    f_low = (router(f_rows, table[3:4, :]) * f_up[...]).astype(BF16)
    payload[:, :, :width] = f_rows[...].astype(BF16).reshape(rows, routed, width)
    payload[:, :, width : 2 * width] = f_low.reshape(rows, routed, width)


def glu_parts(inputs, back_in, gate_w, up_w, down_w):
    act, slope = two_gelu(dot(inputs, gate_w))
    lift = dot(inputs, up_w)
    back = dot_t(back_in, down_w)
    hidden = (act * lift).astype(BF16)
    return hidden, (back * lift * slope).astype(BF16), (back * act).astype(BF16)


def three_parts(value):
    high = value.astype(BF16).astype(F32)
    middle = (value - high).astype(BF16).astype(F32)
    return high, middle, value - high - middle


def light_ffn_kernel(normed_two, upstream, w_gate_up, w_down, z_light, d_light, hidden_out, grad_gate, grad_up):
    width = normed_two.shape[1]
    inner = w_down.shape[0]
    back_in = upstream[...].reshape(-1, width)
    unit = 256
    for at in range(0, inner, unit):
        part = slice(at, at + unit)
        gate_w, up_w = w_gate_up[:, part], w_gate_up[:, inner + at : inner + at + unit]
        hidden, d_gate, d_up = glu_parts(normed_two[...], back_in, gate_w, up_w, w_down[part, :])
        hidden_out[:, part] = hidden
        grad_gate[:, part] = d_gate
        grad_up[:, part] = d_up
    z_light[...] = dot(hidden_out[...], w_down[...])
    d_light[...] = dot_t(grad_gate[...], w_gate_up[:, :inner]) + dot_t(grad_up[...], w_gate_up[:, inner:])


def pass_share(step_refs, share_refs, me, group):
    gate, up, down = step_refs
    gate_out, up_out, down_out = share_refs
    unit = gate_out.shape[2]
    at = pl.ds(pl.multiple_of(lax.rem(me, group) * unit, unit), unit)
    gate_out[0] = gate[:, at]
    up_out[0] = up[:, at]
    down_out[0] = down[at, :]


def heavy_steps(step, sums_in, h_gate, h_up, h_down, f_rows, f_up, table, z_heavy, d_heavy):
    @pl.when(step == 0)
    def _():
        for total, value in zip((z_heavy, d_heavy), sums_in):
            total[...] = value

    f_gate = router(f_rows, table[3:4, :])
    f_low = (f_gate * f_up[...]).astype(BF16)
    f_in = f_rows[...].astype(BF16)
    hidden, d_gate, d_up = glu_parts(f_in, f_low, h_gate[...], h_up[...], h_down[...])
    z_heavy[...] += dot(hidden, h_down[...])
    d_heavy[...] += dot_t(d_gate, h_gate[...]) + dot_t(d_up, h_up[...])
    return f_gate


def ffn_first_kernel(
    group, h_gate, h_up, h_down, f_rows, f_up, table, z_heavy, d_heavy, gate_out, up_out, down_out
):
    zero = jnp.zeros(z_heavy.shape, F32)
    heavy_steps(pl.program_id(0), (zero, zero), h_gate, h_up, h_down, f_rows, f_up, table, z_heavy, d_heavy)
    pass_share((h_gate, h_up, h_down), (gate_out, up_out, down_out), lax.axis_index("seq"), group)


def ffn_last_kernel(
    routed, group, q_route, f_route, h_gate, h_up, h_down, z_in, d_in, upstream, middle, z_light, d_light_in,
    q_rows, f_rows, f_up, proj, f_marks, table, stats, segs,
    outputs, dmid, dmid_low, payload, vectors, gate_out, up_out, down_out,
    z_heavy, d_heavy, placed, full, d_light,
):
    step = pl.program_id(0)
    width = middle.shape[1]
    rows, span = segs.shape
    me = lax.axis_index("seq")
    f_gate = heavy_steps(
        step, (z_in[...], d_in[...]), h_gate, h_up, h_down, f_rows, f_up, table, z_heavy, d_heavy
    )
    pass_share((h_gate, h_up, h_down), (gate_out, up_out, down_out), me, group)

    @pl.when(step == pl.num_programs(0) - 1)
    def _():
        mid = middle[...]
        d_light[...] = d_light_in[...]
        placed[...] = f_gate * z_heavy[...]
        full[...] = mid + z_light[...]
        logit = jnp.sum(f_up[...] * z_heavy[...], axis=-1, keepdims=True) * f_gate * (1.0 - f_gate)
        d_heavy[...] += logit * table[3:4, :]
        for r in range(rows):
            for k in range(routed):
                place = f_route[r, k] - me * span
                at, source = pl.ds(r * span + place, 1), pl.ds(r * routed + k, 1)
                full[at, :] = full[at, :] + placed[source, :]
                d_light[at, :] = d_light[at, :] + d_heavy[source, :]
        outputs[...] = full[...].astype(BF16).reshape(outputs.shape)
        factor = row_factor(mid)
        d_norm = d_light[...]
        vectors[...] = jnp.zeros(vectors.shape, F32)
        vectors[0:1, :] = jnp.sum(d_norm * mid * factor, axis=0, keepdims=True)
        vectors[1:2, :] = jnp.sum(logit * f_rows[...], axis=0, keepdims=True)
        weighted = d_norm * table[1:2, :]
        inner = jnp.mean(weighted * mid, axis=-1, keepdims=True)
        total = upstream[...].reshape(rows * span, width).astype(F32) + factor * weighted - mid * (factor * factor * factor) * inner
        dmid[...] = total
        dmid_low[...] = total.astype(BF16)
        sums = stats[...]
        place = lax.broadcasted_iota(jnp.int32, sums.shape, 0)
        lane = lax.broadcasted_iota(jnp.int32, sums.shape, 1)
        light_sum = stat_row(valid_column(segs) * z_light[...] * z_light[...])
        heavy_sum = stat_row(jnp.where(f_marks[:, 0:1] >= 2.0, placed[...] * placed[...], 0.0))
        sums = jnp.where(place == 3, light_sum, jnp.where(place == 4, heavy_sum, sums))
        lanes = jnp.zeros(sums.shape, F32)
        for k, part in enumerate(three_parts(sums)):
            lanes = lanes + jnp.where(lane == place + 8 * k, part, 0.0)
        lanes = jnp.sum(lanes, axis=0, keepdims=True)
        full[...] = total
        for r in range(rows):
            for k in range(routed):
                place = q_route[r, me * routed + k] - me * span
                placed[pl.ds(r * routed + k, 1), :] = full[pl.ds(r * span + place, 1), :]
        q_gate = router(q_rows, table[2:3, :])
        logit = jnp.sum(placed[...] * proj[...], axis=-1, keepdims=True) * q_gate * (1.0 - q_gate)
        payload[:, :, :width] = (q_gate * placed[...]).astype(BF16).reshape(rows, routed, width)
        lane = lax.broadcasted_iota(jnp.int32, (rows * routed, LANES), 1)
        extra = jnp.broadcast_to(lanes, (rows * routed, LANES))
        for k, part in enumerate(three_parts(logit)):
            extra = jnp.where(lane == 24 + k, part, extra)
        payload[:, :, width:] = extra.astype(BF16).reshape(rows, routed, LANES)


def halves_of(value, place):
    half = value.shape[-1] // 2
    first, second = value[..., :half], value[..., half:]
    return jnp.where(place == 0, first, second), jnp.where(place == 0, second, first)


def store_slots(outs, place, base, grads):
    each = outs[0].shape[0]
    block = grads.shape[0] // (each * len(outs))
    low = grads.astype(BF16)
    for c in range(grads.shape[1] // LANES):
        for p in range(each * len(outs)):
            part = low[p * block : (p + 1) * block, c * LANES : (c + 1) * LANES]
            outs[p // each][p % each, place, pl.ds(base + c * block, block), :] = part
    return base + grads.shape[1] // LANES * block


def slot_vector_block(select, vectors):
    table = jnp.concatenate([vectors, jnp.zeros((LANES - vectors.shape[0], vectors.shape[1]), F32)], axis=0)
    return dot_t(select, table.astype(BF16))


def loop_slots(outs, base, left, right, lanes, half_of):
    block = left.shape[0] // (outs[0].shape[0] * len(outs))

    def chunk(i, carry):
        grads = dot(left[...], right[:, pl.ds(pl.multiple_of(i * lanes, lanes), lanes)])
        half, at = half_of(i)
        store_slots(outs, half, pl.multiple_of(base + at * (block * lanes // LANES), 16), grads)
        return carry

    lax.fori_loop(0, right.shape[1] // lanes, chunk, 0)


def first_grads_kernel(bits, normed_two, grad_gate, grad_up, hidden, upstream, *refs):
    outs, (inputs_t, hidden_t, back_in) = refs[:-3], refs[-3:]
    width = normed_two.shape[1]
    me = lax.axis_index("seq")
    place = lax.axis_index("dp")
    inputs_t[...] = dot_t(slot_select(width, bits, me), normed_two[...]).astype(BF16)
    loop_slots(outs, 0, inputs_t, grad_gate, 256, lambda i: (place, i))
    loop_slots(outs, 0, inputs_t, grad_up, 256, lambda i: (1 - place, i))
    hidden_t[...] = dot_t(slot_select(hidden.shape[1], bits, me), hidden[...]).astype(BF16)
    back_in[...] = upstream[...].reshape(-1, width)
    base = grad_gate.shape[1] // LANES * (width >> len(bits))
    loop_slots(outs, base, hidden_t, back_in, width // 2, lambda i: (i ^ place, 0))


def light_back_kernel(
    bits, dmid_low, query, keyval, probs, normed, mix, vectors, table, w_qkv, w_out,
    dnorm, to_right, to_left, *refs,
):
    outs, (dq, dkv, d_row, dq_t, select, inputs_t) = refs[:-6], refs[-6:]
    rows, rim, width = to_right.shape
    span = dmid_low.shape[0] // rows
    extent = span + 2 * rim
    own_all = rows * span
    heads = width // DL
    scale = 1.0 / math.sqrt(DL)
    place = lax.axis_index("dp")
    mix_grad = dot_t(dmid_low[...], w_out[...]).astype(BF16)
    for r in range(rows):
        key_rows = slice(r * extent, (r + 1) * extent)
        own_rows = slice(r * span, (r + 1) * span)
        key_t = keyval[key_rows, :width].T
        d_row[...] = jnp.zeros(d_row.shape, F32)
        for h in range(heads):
            first, lanes, mask = head_window(h, DL)
            window = slice(first, first + lanes)
            v_window = slice(width + first, width + first + lanes)
            q_head = jnp.where(mask, query[own_rows, window], 0)
            g_head = jnp.where(mask, mix_grad[own_rows, window], 0)
            share = probs[r * heads + h]
            full_share = share.astype(F32)
            prob_grad = dot_t(keyval[key_rows, v_window], g_head)
            delta = jnp.sum(full_share * prob_grad, axis=0, keepdims=True)
            score_grad = (full_share * (prob_grad - delta)).astype(BF16)
            d_row[:, window] += dot(score_grad, q_head)
            d_row[:, v_window] += dot(share, g_head)
            dq_t[h * DL : (h + 1) * DL, :] = dot(key_t[h * DL : (h + 1) * DL, :], score_grad)
        dq[own_rows, :] = (dq_t[...].T * scale).astype(BF16)
        rim_at = own_all + 2 * r * rim
        for size, at, to in ((span, rim, r * span), (rim, 0, rim_at), (rim, rim + span, rim_at + rim)):
            dkv[to : to + size, :width] = (d_row[at : at + size, :width] * scale).astype(BF16)
            dkv[to : to + size, width:] = d_row[at : at + size, width:].astype(BF16)
    d_rim = dot_t(dkv[own_all:, :], w_qkv[:, width:])
    dnorm[...] = dot_t(dq[...], w_qkv[:, :width]) + dot_t(dkv[:own_all, :], w_qkv[:, width:])
    gain_grad = jnp.sum(dnorm[...] * normed[:own_all, :].astype(F32), axis=0, keepdims=True)
    gain_grad = gain_grad + jnp.sum(d_rim * normed[own_all:, :].astype(F32), axis=0, keepdims=True)
    gain_grad = gain_grad / table[0:1, :]
    for r in range(rows):
        to_left[r] = d_rim[2 * r * rim : (2 * r + 1) * rim].astype(BF16)
        to_right[r] = d_rim[(2 * r + 1) * rim : (2 * r + 2) * rim].astype(BF16)
    half = width // 2
    select[...] = slot_select(width, bits, lax.axis_index("seq"))
    inputs_t[...] = dot_t(select[...], normed[...]).astype(BF16)
    base = store_slots(outs, place, 0, dot(inputs_t[:, :own_all], dq[...]))
    grads = dot(inputs_t[...], dkv[:, :width])
    base = store_slots(outs, place, base, grads[:, :half])
    base_two = store_slots(outs, 1 - place, 0, grads[:, half:])
    store_slots(outs, 1 - place, base_two, dot(inputs_t[...], dkv[:, width:]))
    grads = dot(dot_t(select[...], mix[...]).astype(BF16), dmid_low[...])
    base_two = store_slots(outs, place, base, grads[:, :half])
    store_slots(outs, 1 - place, base, grads[:, half:])
    line = lax.broadcasted_iota(jnp.int32, (8, width), 0)
    block = slot_vector_block(select[...], jnp.where(line == 2, gain_grad, vectors[...]))
    for which in range(2):
        store_slots(outs, which, base_two, block)


def heavy_ffn_kernel(parts, *refs):
    blocks, weights, (kept, sent) = refs[:parts], refs[parts:-2], refs[-2:]
    halves = [weights[k : k + 3] for k in range(0, len(weights), 3)]
    each, width, unit = halves[0][0].shape
    devices = lax.axis_size("seq")
    group = devices // (each * len(halves))
    me = lax.axis_index("seq")
    place = lax.axis_index("dp")
    low_place = lax.rem(me, group)
    high_place = lax.div(me, group)
    rows = range(blocks[0].shape[1])
    inputs = jnp.concatenate([gathered(blocks, r, slice(0, width)) for r in rows], axis=0)
    back_in = jnp.concatenate([gathered(blocks, r, slice(width, 2 * width)) for r in rows], axis=0)
    block = width // devices
    along = lax.broadcasted_iota(jnp.int32, (block, width), 1)
    inside = lax.broadcasted_iota(jnp.int32, (block, width), 0)
    picks = []
    for j in range(group):
        owner = high_place * group + (low_place ^ j)
        picks.append((along == inside + owner * block).astype(F32))
    picked = dot_t(jnp.concatenate(picks, axis=0).astype(BF16), inputs).astype(BF16)
    count = group * block

    def share(at, z, half):
        gate_w, up_w, down_w = (ref[at] for ref in halves[half])
        hidden, d_gate, d_up = glu_parts(inputs, back_in, gate_w, up_w, down_w)
        lanes = pl.ds(pl.multiple_of(z * unit, unit), unit)
        kept[:count, lanes] = dot(picked, jnp.where(place == 0, d_gate, d_up))
        sent[:count, lanes] = dot(picked, jnp.where(place == 0, d_up, d_gate)).astype(BF16)

        @pl.when(z == high_place)
        def _():
            hidden_t = hidden.T
            for out, part in zip((kept, sent), halves_of(back_in, place)):
                grad = dot(hidden_t, part).astype(out.dtype)
                size = grad.shape[1]
                out[count:, :size] = grad[: unit // 2]
                out[count:, size : 2 * size] = grad[unit // 2 :]
                out[count:, 2 * size :] = jnp.zeros((unit // 2, out.shape[1] - 2 * size), out.dtype)

    for half in range(len(halves)):

        def one(at, carry, half=half):
            share(at, half * each + at, half)
            return carry

        lax.fori_loop(0, each, one, 0)


def heavy_row_kernel(routed, counts, *refs):
    lists = []
    for count in counts:
        lists.append(refs[:count])
        refs = refs[count:]
    routed_parts, proj_parts, key_parts = lists
    keyval, table, w_q, w_kv, w_out, grads, parts, sums, sent, mix_t, dq_t, dkv = refs
    width = w_q.shape[0]
    scale = 1.0 / math.sqrt(DH)
    me = lax.axis_index("seq")
    r = lax.rem(me, 2)
    block = width // lax.axis_size("seq")
    along = lax.broadcasted_iota(jnp.int32, (block, width), 1)
    inside = lax.broadcasted_iota(jnp.int32, (block, width), 0)
    own = [(along == inside + at * block).astype(F32) for at in (me, me ^ 1)]
    own = jnp.concatenate(own, axis=0).astype(BF16)
    in_q = gathered(routed_parts, r, slice(2 * width, 3 * width))
    in_k = gathered(key_parts, r, slice(0, width))
    q_marks = gathered(routed_parts, r, slice(3 * width, 3 * width + LANES)).astype(F32).T[0:1, :]
    k_marks = gathered(key_parts, r, slice(width, width + LANES)).astype(F32)[:, 0:1]
    allowed = k_marks == q_marks
    grad_in = gathered(proj_parts, r, slice(0, width))
    extra = gathered(proj_parts, r, slice(width, width + LANES)).astype(F32)
    sums[...] = jnp.broadcast_to(
        sum(jnp.sum(ref[:, 0, 0:1, width:].astype(F32), axis=0) for ref in proj_parts), sums.shape
    )
    query = dot(in_q, w_q[...]).astype(BF16)
    mix_grad = dot_t(grad_in, w_out[...]).astype(BF16)
    key_t = keyval[r, :, :width].T
    val_t = keyval[r, :, width:].T
    lane = lax.broadcasted_iota(jnp.int32, (1, LANES), 1)
    for first in range(0, width, LANES):
        window = slice(first, first + LANES)
        v_window = slice(width + first, width + first + LANES)
        keys_w, vals_w = keyval[r, :, window], keyval[r, :, v_window]
        dk, dv = None, None
        for h in range(first // DH, (first + LANES) // DH):
            mask = (lane + first >= h * DH) & (lane + first < (h + 1) * DH)
            q_head = jnp.where(mask, query[:, window], 0)
            g_head = jnp.where(mask, mix_grad[:, window], 0)
            scores = jnp.where(allowed, dot_t(keys_w, q_head) * scale, NEG_FILL)
            peak = jnp.maximum(jnp.max(scores, axis=0, keepdims=True), 0.0)
            numer = jnp.exp(scores - peak)
            share = numer / (jnp.exp(-peak) + jnp.sum(numer, axis=0, keepdims=True))
            share_low = share.astype(BF16)
            prob_grad = dot_t(vals_w, g_head)
            delta = jnp.sum(share * prob_grad, axis=0, keepdims=True)
            score_grad = (share * (prob_grad - delta)).astype(BF16)
            at = slice(h * DH, (h + 1) * DH)
            mix_t[at, :] = dot(val_t[at, :], share_low).astype(BF16)
            dq_t[at, :] = dot(key_t[at, :], score_grad)
            part_k, part_v = dot(score_grad, q_head), dot(share_low, g_head)
            dk, dv = (part_k, part_v) if dk is None else (dk + part_k, dv + part_v)
        dkv[:, window] = (dk * scale).astype(BF16)
        dkv[:, v_window] = dv.astype(BF16)
    dq = (dq_t[...].T * scale).astype(BF16)
    in_q_t = dot_t(own, in_q)
    logits = jnp.sum(jnp.where((lane >= 24) & (lane < 27), extra, 0.0), axis=1, keepdims=True)
    logit_row = jnp.sum(extra.T[24:27, :], axis=0, keepdims=True)
    at = 0
    for grad in (
        dot(in_q_t.astype(BF16), dq),
        dot(dot_t(own, in_k).astype(BF16), dkv[...]),
        dot(dot(own, mix_t[...]).astype(BF16), grad_in),
        jnp.broadcast_to(jnp.sum(in_q_t * logit_row, axis=1, keepdims=True), (2 * block, LANES)),
    ):
        lanes = slice(at, at + grad.shape[1])
        grads[:, lanes] = grad[:block]
        sent[:block, lanes] = grad[block:].astype(BF16)
        at += grad.shape[1]
    half = dq.shape[0] // 2
    ours = lambda v: jnp.concatenate([v[:routed], v[half : half + routed]], axis=0)
    q_part = dot_t(ours(dq), w_q[...]) + ours(logits) * table[2:3, :]
    k_part = dot_t(ours(dkv), w_kv[...])
    for k, part in enumerate((q_part, k_part)):
        parts[k] = part[:routed]
        sent[block:, k * width : (k + 1) * width] = part[routed:].astype(BF16)
    sent[block:, 2 * width :] = jnp.zeros((routed, sent.shape[1] - 2 * width), BF16)


def heavy_last_kernel(
    routed, q_route, k_route, grads_in, parts_in, sums_in, got, dnorm, from_left, from_right, dmid, tokens, table,
    w_q, w_kv, grad_tokens, kept, sent, total, parts,
):
    rows, span, width = tokens.shape
    me = lax.axis_index("seq")
    place = lax.axis_index("dp")
    block = width // lax.axis_size("seq")
    grads = grads_in[...] + got[:block, :].astype(F32)
    for k in range(2):
        parts[lax.rem(me, 2), k] = parts_in[k]
        parts[1 - lax.rem(me, 2), k] = got[block:, k * width : (k + 1) * width].astype(F32)
    for r in range(rows):
        at = r * span
        total[at : at + span, :] = dnorm[at : at + span, :]
        total[at : at + RADIUS, :] += from_left[r].astype(F32)
        total[at + span - RADIUS : at + span, :] += from_right[r].astype(F32)
        for k in range(routed):
            for which, route in enumerate((q_route, k_route)):
                spot = route[r, me * routed + k] - me * span
                row = pl.ds(at + spot, 1)
                total[row, :] = total[row, :] + parts[r, which, k : k + 1, :]
    hidden = tokens[...].reshape(rows * span, width).astype(F32)
    factor = row_factor(hidden)
    weighted = total[...] * table[0:1, :]
    inner = jnp.mean(weighted * hidden, axis=-1, keepdims=True)
    d_hidden = dmid[...] + factor * weighted - hidden * (factor * factor * factor) * inner
    grad_tokens[...] = d_hidden.astype(BF16).reshape(grad_tokens.shape)
    along = lax.broadcasted_iota(jnp.int32, (block, width), 1)
    inside = lax.broadcasted_iota(jnp.int32, (block, width), 0)
    own_full = (along == inside + me * block).astype(F32)
    own = own_full.astype(BF16)
    own_gain = jnp.sum(own_full * table[0:1, :], axis=1, keepdims=True)
    own_route = jnp.sum(own_full * table[2:3, :], axis=1, keepdims=True)
    route_grad = grads[:, 4 * width : 4 * width + 1]
    gain_grad = jnp.sum(dot(own, w_q[...]) * grads[:, :width], axis=1, keepdims=True)
    gain_grad = gain_grad + jnp.sum(dot(own, w_kv[...]) * grads[:, width : 3 * width], axis=1, keepdims=True)
    gain_grad = (gain_grad + own_route * route_grad) / own_gain
    lane = lax.broadcasted_iota(jnp.int32, (block, LANES), 1)
    sums = sums_in[...]
    sums = sums + pltpu.roll(sums, LANES - 8, 1) + pltpu.roll(sums, LANES - 16, 1)
    sums = jnp.where(lane[:8] < 8, sums, 0.0)
    vectors = jnp.where(lane == 0, gain_grad, jnp.where(lane == 1, route_grad, 0.0))
    own_sums = pltpu.roll(sums, 8, 1)[0:1, :]
    sent_sums = jnp.zeros((1, LANES), F32)
    for k, part in enumerate(three_parts(sums)):
        sent_sums = sent_sums + pltpu.roll(part, 8 + 8 * k, 1)[0:1, :]
    at = 0
    for grad in (grads[:, :width], grads[:, width : 3 * width], grads[:, 3 * width : 4 * width]):
        mine, other = halves_of(grad, place)
        size = mine.shape[1]
        kept[:, at : at + size] = mine
        sent[:, at : at + size] = other.astype(BF16)
        at += size
    kept[:, at:] = vectors + own_sums
    sent[:, at:] = (vectors + sent_sums).astype(BF16)


def mix_kernel(plans, count, *refs):
    ins, outs = refs[:count], refs[count:]
    for out, parts in zip(outs, plans):
        for target, sources in parts:
            values = [ins[k][index] for k, index in sources]
            if len(values) > 1:
                values = [sum(v.astype(F32) for v in values)]
            out[target] = values[0].astype(out.dtype)


def finish_light_kernel(kept, received, *outs):
    total = kept[0, 0].astype(F32) + received[0, 0].astype(F32)
    base = 0
    for ref in outs:
        block = ref.shape[0]
        for c in range(ref.shape[1] // LANES):
            ref[:, c * LANES : (c + 1) * LANES] = total[base : base + block]
            base += block


def finish_heavy_kernel(heavy_kept, heavy_got, q_out, kv_out, out_out, vectors, stats):
    total = heavy_kept[...] + heavy_got[...].astype(F32)
    at = 0
    for ref in (q_out, kv_out, out_out, vectors):
        ref[...] = total[:, at : at + ref.shape[1]]
        at += ref.shape[1]
    sums = total[:8, at - LANES :]
    stats[...] = sums + pltpu.roll(sums, LANES - 8, 1) + pltpu.roll(sums, LANES - 16, 1)


def finish_ffn_kernel(groups, *refs):
    pieces, gate_up_out = refs[:-1], refs[-1]
    group = len(pieces)
    low_place = lax.rem(lax.axis_index("seq"), group)
    unit = pieces[0].shape[1] // groups
    for j, piece in enumerate(pieces):
        for z in range(groups):
            at = pl.multiple_of((z * group + (low_place ^ j)) * unit, unit)
            gate_up_out[:, pl.ds(at, unit)] = piece[:, z * unit : (z + 1) * unit].astype(F32)


def blend(ins, outs, after=(), micros=1, mib=6):
    kernel = functools.partial(mix_kernel, [parts for _, _, parts in outs], len(ins))
    return call(kernel, [shape(dims, dtype) for dims, dtype, _ in outs], ins, mib=mib, after=after, micros=micros)


ALL = slice(None)


def joined(ins, first, cuts):
    blocks = [(first + k, b) for k, part in enumerate(ins) for b in range(part.shape[0])]
    each = len(blocks) // cuts
    dims = (each, *ins[0].shape[1:])
    outs = []
    for c in range(cuts):
        outs.append((dims, ins[0].dtype, [(k, [source]) for k, source in enumerate(blocks[c * each : (c + 1) * each])]))
    return outs


def pair_part(target, pair, index):
    return (target, [(2 * pair, index), (2 * pair + 1, index)])


def side_by_side(rows):
    half = rows // 2
    dims = (4, 2, half, LANES)
    low, high = (ALL, ALL, slice(0, half)), (ALL, ALL, slice(half, rows))
    place = lambda k: slice(2 * k, 2 * k + 2)
    ways = [((0, 1), low), ((2, 3), low), ((0, 2), high), ((1, 3), high)]
    return [(dims, BF16, [pair_part(place(k), p, index) for k, p in enumerate(pairs)]) for pairs, index in ways]


def crossed(rows):
    dims = (2, 2, rows // 2, LANES)
    sides = (slice(0, 2), slice(2, 4))
    return [(dims, BF16, [pair_part(ALL, pair, side)]) for pair in (0, 1) for side in sides]


def halved(rows, first):
    half = rows // 2
    places = ((ALL, ALL, slice(0, half)), (ALL, ALL, slice(half, rows)))
    outs = []
    for way in (slice(0, 1), slice(1, 2)):
        parts = [pair_part(place, first + k, (ALL, way)) for k, place in enumerate(places)]
        outs.append(((2, 1, rows, LANES), BF16, parts))
    return outs


def last_half(rows, pair):
    return [((1, 1, rows, LANES), BF16, [pair_part(ALL, pair, way)]) for way in (slice(0, 1), slice(1, 2))]


def skip_operand(kernel, place):
    return lambda *refs: kernel(*refs[:place], *refs[place + 1 :])


def local_kernels(
    tokens,
    segments,
    query_route,
    kv_route,
    ffn_route,
    grad_out,
    attn_gain,
    light_qkv,
    light_out,
    heavy_q,
    heavy_kv,
    heavy_out,
    route_query,
    ffn_gain,
    light_gate_up,
    light_down,
    heavy_gate_up,
    heavy_down,
    route_ffn,
):
    rows, span, width = tokens.shape
    devices = lax.axis_size("seq")
    routed = query_route.shape[1] // devices
    own, count = rows * span, rows * routed
    per_row = devices * routed
    extent = span + 2 * RADIUS
    block = width // devices
    light_heads = width // DL
    ffn_light, ffn_heavy = light_down.shape[0], heavy_down.shape[0]
    marked = width + LANES

    rim = shape((rows, RADIUS + 16, width), BF16)
    keys, upper, lower, table = call(
        functools.partial(first_kernel, routed),
        [shape((rows, routed, marked), BF16), rim, rim, shape((4, width), F32)],
        [kv_route, segments, tokens, attn_gain, ffn_gain, route_query, route_ffn],
        hbm=7,
        scratch=[
            pltpu.SMEM(kv_route.shape, jnp.int32),
            pltpu.SMEM(segments.shape, jnp.int32),
            pltpu.VMEM(segments.shape, jnp.int32),
            pltpu.VMEM(tokens.shape, BF16),
            pltpu.VMEM((width,), F32),
            pltpu.VMEM((width,), F32),
            pltpu.VMEM((width,), BF16),
            pltpu.VMEM((width,), BF16),
            pltpu.VMEM((own, width), F32),
            pltpu.VMEM((count, marked), F32),
            pltpu.SemaphoreType.DMA((8,)),
        ],
        mib=58,
    )
    bits = (1, 2, 4, 8)
    keys = keys[None]
    keys_got = [swap(keys, "seq", flip) for flip in (8, 4, 12)]
    before = shifted(upper, "seq", 1)
    after = shifted(lower, "seq", -1)
    (keys_four,) = blend([keys, *keys_got], joined([keys, *keys_got], 0, 1), mib=4)
    keys_four_got = swap(keys_four, "seq", 2)
    last = keys_four

    normed, query, keyval, probs, mix, attn = call(
        light_kernel,
        [
            shape((rows * extent, width), BF16),
            shape((own, width), BF16),
            shape((rows * extent, 2 * width), BF16),
            shape((rows * light_heads, extent, span), BF16),
            shape((own, width), BF16),
            shape((own, width), F32),
        ],
        [before, tokens, after, segments, table, light_qkv, light_out],
        scratch=[pltpu.VMEM((8, 3 * span), F32), pltpu.VMEM((width, span), F32)],
        micros=6,
        mib=14,
        after=[last],
    )
    held = [keys_four, keys_four_got]
    (keys_eight,) = blend(held, joined(held, 0, 1), [attn], mib=4)
    key_parts = [keys_eight, swap(keys_eight, "seq", 1)]

    small = shape((count, width), F32)
    middle, normed_two, keyval_all, payload, q_rows, f_rows, f_up, proj, f_marks, stats = call(
        functools.partial(middle_kernel, routed, len(key_parts)),
        [
            shape((own, width), F32),
            shape((own, width), BF16),
            shape((rows, per_row, 2 * width), BF16),
            shape((rows, routed, 3 * width + LANES), BF16),
            small,
            small,
            small,
            small,
            shape((count, LANES), F32),
            shape((8, LANES), F32),
        ],
        [
            query_route, ffn_route, segments, tokens, segments, *key_parts, attn, grad_out,
            table, heavy_q, heavy_kv, heavy_out,
        ],
        smem=3,
        scratch=[
            pltpu.VMEM((own, width), F32),
            pltpu.VMEM((count, LANES), F32),
            pltpu.VMEM((count, width), F32),
        ],
        micros=4,
        mib=8,
    )
    payload = payload[None]
    payload_got = [swap(payload, "seq", flip) for flip in (8, 4, 12)]

    share = shape((own, ffn_light), BF16)
    z_light, d_light, hidden, grad_gate, grad_up = call(
        light_ffn_kernel,
        [shape((own, width), F32), shape((own, width), F32), share, share, share],
        [normed_two, grad_out, light_gate_up, light_down],
        micros=6,
        mib=9,
    )
    half_rows = (width // 2) // LANES
    slot_rows = block * ffn_light // LANES + ffn_light // devices * half_rows
    slots = [shape((devices // (2 * CUTS), 2, slot_rows, LANES), BF16)] * (2 * CUTS)
    slots = call(
        functools.partial(first_grads_kernel, bits),
        slots,
        [normed_two, grad_gate, grad_up, hidden, grad_out],
        scratch=[
            pltpu.VMEM((width, own), BF16),
            pltpu.VMEM((ffn_light, own), BF16),
            pltpu.VMEM((own, width), BF16),
        ],
        micros=4,
        mib=9,
    )
    core = len(slots) // 2
    first_core = list(zip(slots[:core], [swap(part, "seq", 1) for part in slots[core:]]))
    held = [payload, *payload_got]
    (routed_four,) = blend(held, joined(held, 0, 1), [slots[0]], mib=4)
    routed_four_got = swap(routed_four, "seq", 2)

    steps = 4
    group = min(4, devices)
    groups = devices // group
    unit = ffn_heavy // devices
    heavy_unit = ffn_heavy // steps
    whole = lambda *dims: pl.BlockSpec(dims, lambda j: (0,) * len(dims))

    def streamed(first):
        columns = lambda at: pl.BlockSpec((width, heavy_unit), lambda j: (0, at + first + j))
        return [columns(0), columns(steps), pl.BlockSpec((heavy_unit, width), lambda j: (first + j, 0))]

    half = steps // 2
    share_dims = [(half, width, unit), (half, width, unit), (half, unit, width)]
    share_shapes = [shape(dims, BF16) for dims in share_dims]
    share_specs = [pl.BlockSpec((1, *dims[1:]), lambda j: (j, 0, 0)) for dims in share_dims]
    z_heavy, d_heavy, *shares_one = pl.pallas_call(
        skip_operand(functools.partial(ffn_first_kernel, group), 6),
        grid=(half,),
        out_shape=[small, small, *share_shapes],
        in_specs=streamed(0) + [whole(count, width)] * 2 + [whole(4, width), ANY],
        out_specs=[whole(count, width)] * 2 + share_specs,
        compiler_params=pltpu.CompilerParams(vmem_limit_bytes=12 * MIB),
        cost_estimate=cost(6),
    )(heavy_gate_up, heavy_gate_up, heavy_down, f_rows, f_up, table, routed_four)
    rows_one = slots[0].shape[2]
    part = rows_one // 2
    low, high = slice(0, part), slice(part, rows_one)
    one, two = slice(0, 1), slice(1, 2)
    span_of = lambda k: slice(2 * k, 2 * k + 2)
    ins = [v for pair in first_core for v in pair]
    left_keep, left_sent, right_keep, right_sent = blend(ins, side_by_side(rows_one), [z_heavy])
    first_pairs = [left_keep, swap(left_sent, "seq", 2), right_keep, swap(right_sent, "seq", 4)]
    outputs, dmid, dmid_low, proj_payload, vectors, *shares_two = pl.pallas_call(
        skip_operand(functools.partial(ffn_last_kernel, routed, group), 19),
        grid=(half,),
        out_shape=[
            shape((rows, span, width), BF16),
            shape((own, width), F32),
            shape((own, width), BF16),
            shape((rows, routed, marked), BF16),
            shape((8, width), F32),
            *share_shapes,
        ],
        in_specs=[SMEM, SMEM]
        + streamed(half)
        + [whole(count, width)] * 2
        + [whole(rows, span, width)]
        + [whole(own, width)] * 3
        + [whole(count, width)] * 4
        + [whole(count, LANES), whole(4, width), whole(8, LANES), whole(rows, span), ANY],
        out_specs=[
            whole(rows, span, width),
            whole(own, width),
            whole(own, width),
            whole(rows, routed, marked),
            whole(8, width),
            *share_specs,
        ],
        scratch_shapes=[pltpu.VMEM((count, width), F32)] * 3 + [pltpu.VMEM((own, width), F32)] * 2,
        compiler_params=pltpu.CompilerParams(vmem_limit_bytes=16 * MIB),
        cost_estimate=cost(7),
    )(
        query_route, ffn_route, heavy_gate_up, heavy_gate_up, heavy_down, z_heavy, d_heavy, grad_out, middle,
        z_light, d_light, q_rows, f_rows, f_up, proj, f_marks, table, stats, segments, left_keep,
    )
    proj_payload = proj_payload[None]
    proj_got = [swap(proj_payload, "seq", flip) for flip in (8, 4, 12)]

    slot_rows = block * 3 * half_rows + block * half_rows + block
    slots = [shape((devices // (2 * CUTS), 2, slot_rows, LANES), BF16)] * (2 * CUTS)
    rim = shape((rows, RADIUS, width), BF16)
    dnorm, to_right, to_left, *slots = call(
        functools.partial(light_back_kernel, bits),
        [shape((own, width), F32), rim, rim, *slots],
        [dmid_low, query, keyval, probs, normed, mix, vectors, table, light_qkv, light_out],
        scratch=[
            pltpu.VMEM((own, width), BF16),
            pltpu.VMEM((rows * extent, 2 * width), BF16),
            pltpu.VMEM((extent, 2 * width), F32),
            pltpu.VMEM((width, span), F32),
            pltpu.VMEM((width, width), BF16),
            pltpu.VMEM((width, rows * extent), BF16),
        ],
        micros=3,
        mib=12,
    )
    from_left = shifted(to_right, "seq", 1)
    from_right = shifted(to_left, "seq", -1)
    second_core = list(zip(slots[:core], [swap(part, "seq", 1) for part in slots[core:]]))

    held_proj, held_routed = [proj_payload, *proj_got], [routed_four, routed_four_got]
    left_keep, left_sent, right_keep, right_sent, proj_four, *routed_eight = blend(
        first_pairs + held_proj + held_routed,
        crossed(rows_one) + joined(held_proj, 4, 1) + joined(held_routed, 4 + len(held_proj), 2),
        [dnorm],
    )
    first_pairs = [left_keep, swap(left_sent, "seq", 4), right_keep, swap(right_sent, "seq", 2)]
    proj_four_got = swap(proj_four, "seq", 2)
    routed_parts = routed_eight + [swap(piece, "seq", 1) for piece in routed_eight]

    heavy_rows = group * block + unit // 2
    ffn_kept, ffn_sent = call(
        functools.partial(heavy_ffn_kernel, len(routed_parts)),
        [shape((heavy_rows, groups * unit), F32), shape((heavy_rows, groups * unit), BF16)],
        [*routed_parts, *shares_one, *shares_two],
        micros=7,
        mib=11,
        after=[left_keep],
    )
    ffn_got = swap(ffn_sent, "dp", 1)

    rows_two = slots[0].shape[2]
    ins = [v for pair in second_core for v in pair]
    held = [proj_four, proj_four_got]
    left_keep, left_sent, right_keep, right_sent, *proj_eight = blend(
        ins + held, side_by_side(rows_two) + joined(held, len(ins), 2), [ffn_kept]
    )
    second_pairs = [left_keep, swap(left_sent, "seq", 2), right_keep, swap(right_sent, "seq", 4)]
    proj_parts = proj_eight + [swap(piece, "seq", 1) for piece in proj_eight]

    gathers = (routed_parts, proj_parts, key_parts)
    grad_lanes = 4 * width + LANES
    heavy_grads, heavy_parts, sums, pair_sent = call(
        functools.partial(heavy_row_kernel, routed, [len(parts) for parts in gathers]),
        [
            shape((block, grad_lanes), F32),
            shape((2, routed, width), F32),
            shape((8, LANES), F32),
            shape((block + routed, grad_lanes), BF16),
        ],
        [*sum(gathers, []), keyval_all, table, heavy_q, heavy_kv, heavy_out],
        scratch=[
            pltpu.VMEM((width, per_row), BF16),
            pltpu.VMEM((width, per_row), F32),
            pltpu.VMEM((per_row, 2 * width), BF16),
        ],
        micros=9,
        mib=8,
        after=[left_keep],
    )
    pair_got = swap(pair_sent, "seq", 1)
    below = slice(group * block, heavy_rows)
    down_lanes = [slice(0, width // 2), slice(width // 2, width)]
    rows_of = lambda j: slice(j * block, (j + 1) * block)
    ins = second_pairs + [ffn_kept, ffn_got] + first_pairs
    left_keep, left_sent, right_keep, right_sent, first_keep, first_sent, heavy_down_grad, *pieces = blend(
        ins,
        crossed(rows_two)
        + halved(rows_one, 3)
        + [
            (
                (unit, width // 2),
                F32,
                [pair_part(slice(k * unit // 2, (k + 1) * unit // 2), 2, (below, down_lanes[k])) for k in (0, 1)],
            ),
        ]
        + [
            ((block, groups * unit), F32 if j == 0 else BF16, [pair_part(ALL, 2, rows_of(j))])
            for j in range(group)
        ],
        [sums],
    )
    second_pairs = [left_keep, swap(left_sent, "seq", 4), right_keep, swap(right_sent, "seq", 2)]
    first_pair = [first_keep, swap(first_sent, "dp", 1)]
    pieces = [pieces[0]] + [swap(pieces[j], "seq", j) for j in range(1, group)]
    grad_tokens, heavy_kept, heavy_sent = call(
        functools.partial(heavy_last_kernel, routed),
        [
            shape((rows, span, width), BF16),
            shape((block, 2 * width + LANES), F32),
            shape((block, 2 * width + LANES), BF16),
        ],
        [
            query_route, kv_route, heavy_grads, heavy_parts, sums, pair_got, dnorm, from_left, from_right,
            dmid, tokens, table, heavy_q, heavy_kv,
        ],
        smem=2,
        scratch=[pltpu.VMEM((own, width), F32), pltpu.VMEM((rows, 2, routed, width), F32)],
        micros=2,
        mib=7,
        after=[left_keep],
    )
    heavy_got = swap(heavy_sent, "dp", 1)
    second_keep, second_sent, first_keep, first_sent = blend(
        second_pairs + first_pair, halved(rows_two, 0) + last_half(rows_one, 2), [heavy_kept]
    )
    first_pair = [first_keep, swap(first_sent, "seq", 8)]
    second_pair = [second_keep, swap(second_sent, "dp", 1)]
    second_keep, second_sent = blend(second_pair, last_half(rows_two, 0))
    second_pair = [second_keep, swap(second_sent, "seq", 8)]
    (heavy_gate_up_grad,) = call(
        functools.partial(finish_ffn_kernel, groups),
        [shape((block, ffn_heavy), F32)],
        pieces,
        micros=0.5,
        mib=4,
        after=[second_keep],
    )
    heavy_q_grad, heavy_kv_grad, heavy_out_grad, heavy_vectors, stats = call(
        finish_heavy_kernel,
        [
            shape((block, width // 2), F32),
            shape((block, width), F32),
            shape((block, width // 2), F32),
            shape((block, LANES), F32),
            shape((8, LANES), F32),
        ],
        [heavy_kept, heavy_got],
        mib=4,
        after=[heavy_gate_up_grad],
    )
    light_gate_up_grad, light_down_grad = call(
        finish_light_kernel,
        [shape((block, ffn_light), F32), shape((ffn_light // devices, width // 2), F32)],
        first_pair,
        mib=4,
        after=[heavy_vectors],
    )
    light_qkv_grad, light_out_grad, light_vectors = call(
        finish_light_kernel,
        [
            shape((block, 3 * width // 2), F32),
            shape((block, width // 2), F32),
            shape((block, LANES), F32),
        ],
        second_pair,
        mib=4,
        after=[light_down_grad],
    )
    sums = stats[0, 8:14]
    return (
        outputs,
        grad_tokens,
        light_vectors[:, 2] + heavy_vectors[:, 0],
        light_qkv_grad,
        light_out_grad,
        heavy_q_grad,
        heavy_kv_grad,
        heavy_out_grad,
        heavy_vectors[:, 1],
        light_vectors[:, 0],
        light_gate_up_grad,
        light_down_grad,
        heavy_gate_up_grad,
        heavy_down_grad,
        light_vectors[:, 1],
        jnp.sqrt(sums[:5] / (sums[5] * width)),
    )


def local(tokens, segments, query_route, *others):
    block = tokens.shape[2] // lax.axis_size("seq")
    fits = query_route.shape[1] <= 256 and block % 16 == 0 and tokens.shape[0] == 2
    return (local_kernels if fits else local_wide)(tokens, segments, query_route, *others)


def solution(mesh):
    placed = (
        P("dp", "seq", None),
        P("dp", "seq"),
        P("dp", None),
        P("dp", None),
        P("dp", "seq"),
        P("dp", "seq", None),
    ) + (P(),) * 13
    matrix = P("seq", "dp")
    vector = P("seq")
    return jax.shard_map(
        local,
        mesh=mesh,
        in_specs=placed,
        out_specs=(
            P("dp", "seq", None),
            P("dp", "seq", None),
            vector,
            matrix,
            matrix,
            matrix,
            matrix,
            matrix,
            vector,
            vector,
            matrix,
            matrix,
            matrix,
            matrix,
            vector,
            P(),
        ),
        check_vma=False,
    )
```

```python
import functools
import math

import jax
import jax.numpy as jnp
from jax import lax
from jax.experimental import pallas as pl
from jax.experimental.pallas import tpu as pltpu
from jax.sharding import PartitionSpec as P

DL = 96
DH = 64
RADIUS = 64
LANES = 128


PRECISE = lax.Precision.HIGHEST
EPSILON = 1e-06
NEG_FILL = -1e30
F32 = jnp.float32
BF16 = jnp.bfloat16


def swap(value, axis, bit):
    return lax.ppermute(value, axis, [(i, i ^ bit) for i in range(lax.axis_size(axis))])


def shifted(block, axis, distance):
    devices = range(lax.axis_size(axis))
    route = [(i - distance, i) for i in devices if i - distance in devices]
    return lax.ppermute(block, axis, route)


def gather_blocks(block):
    held = block[None]
    bit = lax.axis_size("seq") // 2
    while bit:
        held = jnp.concatenate([held, swap(held, "seq", bit)], axis=0)
        bit //= 2
    return held


def add_halves(value, dim, axis, bit, out_type=BF16):
    half = value.shape[dim] // 2
    keep = lax.slice_in_dim(value, 0, half, axis=dim)
    sent = lax.slice_in_dim(value, half, 2 * half, axis=dim)
    return (keep.astype(F32) + swap(sent, axis, bit).astype(F32)).astype(out_type)


def scatter_sum(slots):
    devices = lax.axis_size("seq")
    rows = slots.shape[2]
    slots = add_halves(slots, 0, "seq", 1)
    left, right = slots[:, :, : rows // 2], slots[:, :, rows // 2 :]
    left = add_halves(left, 0, "seq", 2)
    right = add_halves(right, 1, "dp", 1)
    left = add_halves(left, 1, "dp", 1)
    right = add_halves(right, 0, "seq", 2)
    both = jnp.concatenate([left, right], axis=2)
    bit = 4
    while bit < devices:
        both = add_halves(both, 0, "seq", bit, BF16 if 2 * bit < devices else F32)
        bit *= 2
    return both[0, 0]


def slot_places(me, devices):
    bits = devices.bit_length() - 1
    places = [int(format(p, f"0{bits}b")[::-1], 2) for p in range(devices)]
    return jnp.array(places, jnp.int32) ^ me


def slot_columns(value, me, devices):
    width = value.shape[-1]
    block = width // devices
    order = (slot_places(me, devices)[:, None] * block + jnp.arange(block)[None, :]).reshape(-1)
    onehot = (jnp.arange(width)[:, None] == order[None, :]).astype(BF16)
    return jnp.dot(value, onehot, preferred_element_type=F32).astype(BF16)


def own_half_first(value, place):
    half = value.shape[-1] // 2
    first, second = value[..., :half], value[..., half:]
    return (jnp.where(place == 0, first, second), jnp.where(place == 0, second, first))


def slot_block(grad_halves, devices):
    stacked = jnp.stack(grad_halves)
    _, total, cols = stacked.shape
    parts = stacked.reshape(2, devices, total // devices, cols // LANES, LANES)
    return parts.transpose(1, 0, 3, 2, 4).reshape(devices, 2, -1, LANES).astype(BF16)


def unslot(rows, cols):
    return rows.reshape(cols // LANES, -1, LANES).transpose(1, 0, 2).reshape(-1, cols)


def slot_vectors(vectors, me, devices):
    block = vectors[0].shape[0] // devices
    table = jnp.stack(vectors, axis=-1).reshape(devices, block, len(vectors))
    table = jnp.take(table, slot_places(me, devices), axis=0)
    table = jnp.pad(table, ((0, 0), (0, 0), (0, LANES - len(vectors))))
    return jnp.broadcast_to(table[:, None], (devices, 2, block, LANES)).astype(BF16)


def split_parts(value):
    high = lax.reduce_precision(value, 8, 7)
    middle = lax.reduce_precision(value - high, 8, 7)
    return (high, middle, value - high - middle)


def rms_factor(hidden):
    return lax.rsqrt(jnp.mean(hidden * hidden, axis=-1, keepdims=True) + EPSILON)


def norm_back(hidden, factor, gain_vec, upstream):
    weighted = upstream * gain_vec
    inner_mean = jnp.mean(weighted * hidden, axis=-1, keepdims=True)
    return factor * weighted - hidden * (factor * factor * factor) * inner_mean


def pick_rows(source, positions):
    return jnp.take_along_axis(source, positions[..., None], axis=1)


def place_rows(values, positions, extent):
    onehot = (positions[..., None] == jnp.arange(extent)[None, None, :]).astype(F32)
    return jnp.einsum("rqs,rqd->rsd", onehot, values, precision=PRECISE)


def matmul(left, right):
    return jnp.einsum("...d,de->...e", left, right, preferred_element_type=F32)


def matmul_t(left, right):
    return jnp.einsum("...e,de->...d", left, right, preferred_element_type=F32)


def outer(left, right):
    return jnp.einsum("rsd,rse->de", left, right, preferred_element_type=F32)


def glu_value(gate_part, up_part):
    return jax.nn.gelu(gate_part, approximate=True) * up_part


def geglu(inputs, gate_up, down, upstream_low):
    width = down.shape[0]
    both = matmul(inputs, gate_up)
    gate_part, up_part = both[..., :width], both[..., width:]
    hidden, pull_back = jax.vjp(glu_value, gate_part, up_part)
    gate_grad, up_grad = pull_back(matmul_t(upstream_low, down))
    return (hidden.astype(BF16), gate_grad.astype(BF16), up_grad.astype(BF16))


def routed_probs(query_heads, key_heads, query_seg, key_seg):
    scores = jnp.einsum("rqd,rkd->rqk", query_heads, key_heads, preferred_element_type=F32)
    scores = scores / math.sqrt(DH)
    allowed = query_seg[:, :, None] == key_seg[:, None, :]
    scores = jnp.where(allowed, scores, NEG_FILL)
    peak = jnp.maximum(jnp.max(scores, axis=-1, keepdims=True), 0.0)
    numer = jnp.exp(scores - peak)
    return numer / (jnp.exp(-peak) + jnp.sum(numer, axis=-1, keepdims=True))


def heavy_forward(query, keys, vals, query_seg, key_seg):
    def head(parts):
        query_h, key_h, val_h = parts
        probs = routed_probs(query_h, key_h, query_seg, key_seg).astype(BF16)
        return jnp.einsum("rqk,rkd->rqd", probs, val_h, preferred_element_type=F32).astype(BF16)

    return join_heads(jax.vmap(head)((split_heads(query), split_heads(keys), split_heads(vals))))


def heavy_both(query, keys, vals, query_seg, key_seg, mix_grad):
    def head(parts, query_seg=query_seg, key_seg=key_seg):
        query_h, key_h, val_h, grad_h = parts
        probs = routed_probs(query_h, key_h, query_seg, key_seg)
        probs_low = probs.astype(BF16)
        mix = jnp.einsum("rqk,rkd->rqd", probs_low, val_h, preferred_element_type=F32)
        prob_grad = jnp.einsum("rqd,rkd->rqk", grad_h, val_h, preferred_element_type=F32)
        delta = jnp.sum(probs * prob_grad, axis=-1, keepdims=True)
        score_grad = (probs * (prob_grad - delta)).astype(BF16)
        dquery = jnp.einsum("rqk,rkd->rqd", score_grad, key_h, preferred_element_type=F32)
        dkey = jnp.einsum("rqk,rqd->rkd", score_grad, query_h, preferred_element_type=F32)
        dval = jnp.einsum("rqk,rqd->rkd", probs_low, grad_h, preferred_element_type=F32)
        scale = 1.0 / math.sqrt(DH)
        return (mix.astype(BF16), (dquery * scale).astype(BF16), (dkey * scale).astype(BF16), dval.astype(BF16))

    heads = tuple(split_heads(v) for v in (query, keys, vals, mix_grad))
    if query.shape[1] <= 512:
        return tuple(join_heads(v) for v in jax.vmap(head)(heads))
    count, rows = heads[0].shape[:2]
    place = jnp.tile(jnp.arange(rows), count)
    parts = tuple(v.reshape(count * rows, 1, *v.shape[2:]) for v in heads)
    done = lax.map(lambda p: head(p[0], query_seg[p[1]][None], key_seg[p[1]][None]), (parts, place))
    return tuple(join_heads(v.reshape(count, rows, *v.shape[2:])) for v in done)


def split_heads(value):
    rows, tokens, width = value.shape
    return value.reshape(rows, tokens, width // DH, DH).transpose(2, 0, 1, 3)


def join_heads(value):
    heads, rows, tokens, width = value.shape
    return value.transpose(1, 2, 0, 3).reshape(rows, tokens, heads * width)


def tokens_of(blocks):
    devices, rows, count, width = blocks.shape
    return blocks.transpose(1, 0, 2, 3).reshape(rows, devices * count, width)


def with_segment(rows, segs):
    marks = jnp.broadcast_to((segs + 2).astype(BF16)[..., None], segs.shape + (LANES,))
    return jnp.concatenate([rows, marks], axis=-1)


def local_wide(
    tokens,
    segments,
    query_route,
    kv_route,
    ffn_route,
    grad_out,
    attn_gain,
    light_qkv,
    light_out,
    heavy_q,
    heavy_kv,
    heavy_out,
    route_query,
    ffn_gain,
    light_gate_up,
    light_down,
    heavy_gate_up,
    heavy_down,
    route_ffn,
):
    row_count, seg_span, width = tokens.shape
    light_heads = width // DL
    ffn_heavy = heavy_down.shape[0]
    devices = lax.axis_size("seq")
    me = lax.axis_index("seq")
    half_place = lax.axis_index("dp")
    anchor = me * seg_span
    routed_own = query_route.shape[1] // devices
    own_query = lax.dynamic_slice_in_dim(query_route, me * routed_own, routed_own, 1) - anchor
    own_key = lax.dynamic_slice_in_dim(kv_route, me * routed_own, routed_own, 1) - anchor
    own_ffn = ffn_route - anchor

    marked = with_segment(tokens, segments)
    before = shifted(marked[:, seg_span - RADIUS :], "seq", 1)
    after = shifted(marked[:, :RADIUS], "seq", -1)
    hidden = tokens.astype(F32)
    factor_one = rms_factor(hidden)
    normed = hidden * factor_one * attn_gain
    normed_low = normed.astype(BF16)
    key_rows = pick_rows(normed_low, own_key)
    key_payload = with_segment(key_rows, jnp.take_along_axis(segments, own_key, axis=1))
    key_blocks = tokens_of(gather_blocks(key_payload))
    key_all, key_seg = key_blocks[..., :width], key_blocks[..., width]

    extended = jnp.concatenate([before, marked, after], axis=1)
    seg_ext = extended[..., width]
    hidden_ext = extended[..., :width].astype(F32)
    factor_ext = rms_factor(hidden_ext)
    normed_ext_low = (hidden_ext * factor_ext * attn_gain).astype(BF16)
    extent = seg_span + 2 * RADIUS
    query_low = matmul(normed_low, light_qkv[:, :width]).astype(BF16)
    query_low = query_low.reshape(row_count, seg_span, light_heads, DL)
    kv_ext = matmul(normed_ext_low, light_qkv[:, width:]).astype(BF16)
    key_ext = kv_ext[..., :width].reshape(row_count, extent, light_heads, DL)
    val_ext = kv_ext[..., width:].reshape(row_count, extent, light_heads, DL)
    offset = jnp.arange(seg_span)[:, None] - jnp.arange(extent)[None, :] + RADIUS
    seg_own = seg_ext[:, RADIUS : RADIUS + seg_span]
    allowed = (jnp.abs(offset) <= RADIUS)[None] & (seg_own[:, :, None] == seg_ext[:, None, :])
    light_scale = 1.0 / math.sqrt(DL)
    scores = jnp.einsum("rqhd,rkhd->rhqk", query_low, key_ext, preferred_element_type=F32)
    scores = jnp.where(allowed[:, None], scores * light_scale, NEG_FILL)
    numerators = jnp.exp(scores - jnp.max(scores, axis=-1, keepdims=True))
    probs_light = numerators / jnp.sum(numerators, axis=-1, keepdims=True)
    probs_low = probs_light.astype(BF16)
    light_mix = jnp.einsum("rhqk,rkhd->rqhd", probs_low, val_ext, preferred_element_type=F32)
    light_mix = light_mix.reshape(row_count, seg_span, width).astype(BF16)
    light_attn = matmul(light_mix, light_out)

    query_rows = pick_rows(normed_low, own_query)
    query_seg_own = (jnp.take_along_axis(segments, own_query, axis=1) + 2).astype(BF16)
    heavy_query = matmul(query_rows, heavy_q).astype(BF16)
    keyval_all = matmul(key_all, heavy_kv).astype(BF16)
    heavy_width = heavy_q.shape[1]
    keys_all, vals_all = keyval_all[..., :heavy_width], keyval_all[..., heavy_width:]
    heavy_mix = heavy_forward(heavy_query, keys_all, vals_all, query_seg_own, key_seg)
    heavy_proj = matmul(heavy_mix, heavy_out)
    query_normed = pick_rows(normed, own_query)
    route_query_full = route_query.astype(F32)
    query_gate = jax.nn.sigmoid(jnp.sum(query_normed * route_query_full, axis=-1))
    heavy_attn = place_rows(query_gate[..., None] * heavy_proj, own_query, seg_span)

    middle = hidden + light_attn + heavy_attn
    factor_two = rms_factor(middle)
    normed_two = middle * factor_two * ffn_gain
    low_two = normed_two.astype(BF16)
    upstream = grad_out.astype(F32)
    ffn_normed = pick_rows(normed_two, own_ffn)
    ffn_rows = ffn_normed.astype(BF16)
    route_ffn_full = route_ffn.astype(F32)
    ffn_gate = jax.nn.sigmoid(jnp.sum(ffn_normed * route_ffn_full, axis=-1))
    ffn_upstream = pick_rows(upstream, own_ffn)
    ffn_low = (ffn_upstream * ffn_gate[..., None]).astype(BF16)
    routed_payload = with_segment(
        jnp.concatenate([ffn_rows, ffn_low, query_rows], axis=-1),
        jnp.take_along_axis(segments, own_query, axis=1),
    )
    routed_blocks = tokens_of(gather_blocks(routed_payload))
    ffn_all = routed_blocks[..., :width]
    ffn_low_all = routed_blocks[..., width : 2 * width]
    query_all = routed_blocks[..., 2 * width : 3 * width]
    query_seg = routed_blocks[..., 3 * width]

    hidden_light, gate_grad, up_grad = geglu(low_two, light_gate_up, light_down, grad_out)
    light_ff = matmul(hidden_light, light_down)
    light_both = jnp.concatenate([gate_grad, up_grad], axis=-1)
    normed_two_grad = matmul_t(light_both, light_gate_up)
    hidden_heavy, gate_grad_h, up_grad_h = geglu(ffn_rows, heavy_gate_up, heavy_down, ffn_low)
    heavy_ffn_proj = matmul(hidden_heavy, heavy_down)
    heavy_ff = place_rows(ffn_gate[..., None] * heavy_ffn_proj, own_ffn, seg_span)
    outputs = (middle + light_ff + heavy_ff).astype(BF16)
    ffn_gate_grad = jnp.sum(ffn_upstream * heavy_ffn_proj, axis=-1)
    ffn_logit_grad = ffn_gate_grad * ffn_gate * (1.0 - ffn_gate)
    route_ffn_grad = jnp.sum(ffn_logit_grad[..., None] * ffn_normed, axis=(0, 1))
    ffn_rows_grad = matmul_t(jnp.concatenate([gate_grad_h, up_grad_h], axis=-1), heavy_gate_up)
    ffn_rows_grad = ffn_rows_grad + ffn_logit_grad[..., None] * route_ffn_full
    normed_two_grad = normed_two_grad + place_rows(ffn_rows_grad, own_ffn, seg_span)
    ffn_gain_grad = jnp.sum(normed_two_grad * middle * factor_two, axis=(0, 1))
    middle_grad = upstream + norm_back(middle, factor_two, ffn_gain, normed_two_grad)
    middle_low = middle_grad.astype(BF16)

    valid_rows = (segments >= 0).astype(F32)[..., None]
    sums = jnp.stack(
        [
            jnp.sum(valid_rows * branch * branch)
            for branch in (hidden, light_attn, heavy_attn, light_ff, heavy_ff)
        ]
        + [jnp.sum(valid_rows)]
    )
    heavy_upstream = pick_rows(middle_grad, own_query)
    query_gate_grad = jnp.sum(heavy_upstream * heavy_proj, axis=-1)
    proj_low = (heavy_upstream * query_gate[..., None]).astype(BF16)
    sum_lanes = jnp.pad(jnp.concatenate(split_parts(sums)), (0, LANES - 18)).astype(BF16)
    sum_lanes = jnp.broadcast_to(sum_lanes, proj_low.shape[:2] + (LANES,))
    proj_blocks = gather_blocks(jnp.concatenate([proj_low, sum_lanes], axis=-1))
    sums_all = jnp.sum(proj_blocks[:, 0, 0, width : width + 18].astype(F32), axis=0)
    sums_all = jnp.sum(sums_all.reshape(3, 6), axis=0)
    sums_all = sums_all + swap(sums_all, "dp", 1)
    rms_stats = jnp.sqrt(sums_all[:5] / (sums_all[5] * width))
    proj_all = tokens_of(proj_blocks)[..., :width]

    flat = lambda v: v.reshape(-1, v.shape[-1])
    gate_up_grad = [
        jnp.dot(slot_columns(flat(low_two), me, devices).T, flat(part), preferred_element_type=F32)
        for part in own_half_first(light_both, half_place)
    ]
    hidden_slots = slot_columns(flat(hidden_light), me, devices).T
    down_grad = [
        jnp.dot(hidden_slots, flat(part), preferred_element_type=F32)
        for part in own_half_first(grad_out, half_place)
    ]
    mix_slots = slot_columns(flat(light_mix), me, devices).T
    out_grad = [
        jnp.dot(mix_slots, flat(part), preferred_element_type=F32)
        for part in own_half_first(middle_low, half_place)
    ]
    first_sum = scatter_sum(
        jnp.concatenate(
            [
                slot_block(gate_up_grad, devices),
                slot_block(down_grad, devices),
                slot_block(out_grad, devices),
                slot_vectors((ffn_gain_grad, route_ffn_grad), me, devices),
            ],
            axis=2,
        )
    )
    block = width // devices
    block_ff = light_down.shape[0] // devices
    cuts = [0]
    for rows in (
        block * light_gate_up.shape[1] // 2 // LANES,
        block_ff * width // 2 // LANES,
        block * width // 2 // LANES,
        block,
    ):
        cuts.append(cuts[-1] + rows)
    light_gate_up_grad = unslot(first_sum[cuts[0] : cuts[1]], light_gate_up.shape[1] // 2)
    light_down_grad = unslot(first_sum[cuts[1] : cuts[2]], width // 2)
    light_out_grad = unslot(first_sum[cuts[2] : cuts[3]], width // 2)
    ffn_gain_grad = first_sum[cuts[3] : cuts[4], 0]
    route_ffn_grad = first_sum[cuts[3] : cuts[4], 1]

    group = min(4, devices)
    low_place, high_place = me % group, me // group
    groups = devices // group
    unit = ffn_heavy // devices
    gate_up_parts = heavy_gate_up.reshape(width, 2, groups, group, unit)
    gate_up_mine = lax.dynamic_index_in_dim(gate_up_parts, low_place, 3, False)
    down_mine = lax.dynamic_index_in_dim(
        heavy_down.reshape(groups, group, unit, width), low_place, 1, False
    )
    x_all = flat(ffn_all)
    up_all = flat(ffn_low_all)
    hidden_mine, gate_mine, up_mine = geglu(
        x_all,
        gate_up_mine.reshape(width, -1),
        down_mine.reshape(-1, width),
        up_all,
    )
    hidden_block = lax.dynamic_slice_in_dim(hidden_mine, high_place * unit, unit, 1)
    heavy_down_half = [
        jnp.dot(hidden_block.T, part, preferred_element_type=F32)
        for part in own_half_first(up_all, half_place)
    ]
    heavy_down_grad = heavy_down_half[0] + swap(heavy_down_half[1].astype(BF16), "dp", 1).astype(F32)
    x_group = lax.dynamic_slice_in_dim(x_all, high_place * group * block, group * block, 1)
    x_group = x_group.reshape(-1, group, block)
    x_group = jnp.take(x_group, jnp.arange(group) ^ low_place, axis=1).reshape(-1, group * block)
    gate_half, up_half = (
        jnp.dot(x_group.T, part, preferred_element_type=F32) for part in (gate_mine, up_mine)
    )
    kept = jnp.where(half_place == 0, gate_half, up_half)
    sent = jnp.where(half_place == 0, up_half, gate_half)
    kept = (kept + swap(sent.astype(BF16), "dp", 1).astype(F32)).reshape(group, block, groups, unit)
    pieces = [kept[0]]
    for place in range(1, group):
        pieces.append(swap(kept[place].astype(BF16), "seq", place).astype(F32))
    pieces = jnp.take(jnp.stack(pieces, axis=2), jnp.arange(group) ^ low_place, axis=2)
    heavy_gate_up_grad = pieces.reshape(block, ffn_heavy)

    mix_grad = matmul_t(middle_low, light_out).astype(BF16)
    mix_grad = mix_grad.reshape(row_count, seg_span, light_heads, DL)
    val_grad = jnp.einsum("rhqk,rqhd->rkhd", probs_low, mix_grad, preferred_element_type=F32)
    prob_grad = jnp.einsum("rqhd,rkhd->rhqk", mix_grad, val_ext, preferred_element_type=F32)
    delta = jnp.sum(probs_light * prob_grad, axis=-1, keepdims=True)
    score_grad = (probs_light * (prob_grad - delta)).astype(BF16)
    query_grad = jnp.einsum("rhqk,rkhd->rqhd", score_grad, key_ext, preferred_element_type=F32)
    key_grad = jnp.einsum("rhqk,rqhd->rkhd", score_grad, query_low, preferred_element_type=F32)
    query_grad = (query_grad * light_scale).reshape(row_count, seg_span, width).astype(BF16)
    kv_grad = jnp.concatenate(
        [
            (key_grad * light_scale).reshape(row_count, extent, width),
            val_grad.reshape(row_count, extent, width),
        ],
        axis=-1,
    ).astype(BF16)
    normed_grad_ext = matmul_t(kv_grad, light_qkv[:, width:])
    normed_grad = matmul_t(query_grad, light_qkv[:, :width])
    normed_grad = normed_grad + normed_grad_ext[:, RADIUS : RADIUS + seg_span]
    from_right = shifted(normed_grad_ext[:, :RADIUS].astype(BF16), "seq", -1)
    from_left = shifted(normed_grad_ext[:, seg_span + RADIUS :].astype(BF16), "seq", 1)
    normed_grad = normed_grad.at[:, :RADIUS].add(from_left.astype(F32))
    normed_grad = normed_grad.at[:, seg_span - RADIUS :].add(from_right.astype(F32))

    hq_all = matmul(query_all, heavy_q).astype(BF16)
    do2_all = matmul_t(proj_all, heavy_out).astype(BF16)
    mix_all, dhq_all, dhk_all, dhv_all = heavy_both(
        hq_all, keys_all, vals_all, query_seg, key_seg, do2_all
    )
    dhkv_all = jnp.concatenate([dhk_all, dhv_all], axis=-1)
    mine = lambda v: lax.dynamic_slice_in_dim(flat(v), me * block, block, 1).T
    heavy_grads = [
        own_half_first(jnp.dot(mine(left), flat(right), preferred_element_type=F32), half_place)
        for left, right in ((query_all, dhq_all), (key_all, dhkv_all), (mix_all, proj_all))
    ]
    heavy_kept = jnp.concatenate([pair[0] for pair in heavy_grads], axis=-1)
    heavy_sent = jnp.concatenate([pair[1] for pair in heavy_grads], axis=-1)
    heavy_sum = heavy_kept + swap(heavy_sent.astype(BF16), "dp", 1).astype(F32)
    heavy_half = heavy_width // 2
    heavy_q_grad = heavy_sum[:, :heavy_half]
    heavy_kv_grad = heavy_sum[:, heavy_half : 3 * heavy_half]
    heavy_out_grad = heavy_sum[:, 3 * heavy_half :]
    query_logit_grad = query_gate_grad * query_gate * (1.0 - query_gate)
    route_query_grad = jnp.sum(query_logit_grad[..., None] * query_normed, axis=(0, 1))
    query_rows_grad = (
        matmul_t(dhq_all[:, :routed_own], heavy_q) + query_logit_grad[..., None] * route_query_full
    )
    key_rows_grad = matmul_t(dhkv_all[:, :routed_own], heavy_kv)
    normed_grad = (
        normed_grad
        + place_rows(query_rows_grad, own_query, seg_span)
        + place_rows(key_rows_grad, own_key, seg_span)
    )
    attn_gain_grad = jnp.sum(normed_grad * hidden * factor_one, axis=(0, 1))
    hidden_norm_grad = norm_back(hidden, factor_one, attn_gain, normed_grad)
    grad_tokens = (middle_grad + hidden_norm_grad).astype(BF16)

    own_slots = slot_columns(flat(normed_low), me, devices).T
    ext_slots = slot_columns(flat(normed_ext_low), me, devices).T
    qkv_grad = jnp.concatenate(
        [
            jnp.dot(own_slots, flat(query_grad), preferred_element_type=F32),
            jnp.dot(ext_slots, flat(kv_grad), preferred_element_type=F32),
        ],
        axis=-1,
    )
    second_sum = scatter_sum(
        jnp.concatenate(
            [
                slot_block(own_half_first(qkv_grad, half_place), devices),
                slot_vectors((attn_gain_grad, route_query_grad), me, devices),
            ],
            axis=2,
        )
    )
    qkv_cols = light_qkv.shape[1] // 2
    qkv_rows = block * qkv_cols // LANES
    light_qkv_grad = unslot(second_sum[:qkv_rows], qkv_cols)
    attn_gain_grad = second_sum[qkv_rows:, 0]
    route_query_grad = second_sum[qkv_rows:, 1]
    return (
        outputs,
        grad_tokens,
        attn_gain_grad,
        light_qkv_grad,
        light_out_grad,
        heavy_q_grad,
        heavy_kv_grad,
        heavy_out_grad,
        route_query_grad,
        ffn_gain_grad,
        light_gate_up_grad,
        light_down_grad,
        heavy_gate_up_grad,
        heavy_down_grad,
        route_ffn_grad,
        rms_stats,
    )


VMEM = pl.BlockSpec(memory_space=pltpu.VMEM)
SMEM = pl.BlockSpec(memory_space=pltpu.SMEM)
ANY = pl.BlockSpec(memory_space=pl.ANY)
HBM = pl.BlockSpec(memory_space=pltpu.HBM)
GELU_RATE = math.sqrt(2.0 / math.pi)
GELU_CUBE = 0.044715
MIB = 1024 * 1024
FIRST_CUTS = 4
SECOND_CUTS = 2


def shape(dims, dtype):
    return jax.ShapeDtypeStruct(dims, dtype)


def call(kernel, outs, ins, smem=0, scratch=(), micros=1, mib=16, after=(), hbm=0):
    used = len(ins)

    def body(*refs):
        kernel(*refs[:used], *refs[used + len(after) :])

    return pl.pallas_call(
        body,
        out_shape=outs,
        in_specs=[HBM] * hbm + [SMEM] * smem + [VMEM] * (used - smem - hbm) + [ANY] * len(after),
        out_specs=[VMEM] * len(outs),
        scratch_shapes=list(scratch),
        compiler_params=pltpu.CompilerParams(vmem_limit_bytes=mib * MIB),
        cost_estimate=cost(micros),
    )(*ins, *after)


def cost(micros):
    return pl.CostEstimate(flops=int(micros * 10**9), bytes_accessed=10**6, transcendentals=0)


def dot(left, right):
    return jnp.dot(left, right, preferred_element_type=F32)


def dot_t(left, right):
    return lax.dot_general(left, right, (((1,), (1,)), ((), ())), preferred_element_type=F32)


def t_dot(left, right):
    return lax.dot_general(left, right, (((0,), (0,)), ((), ())), preferred_element_type=F32)


def row_factor(value):
    return lax.rsqrt(jnp.mean(value * value, axis=-1, keepdims=True) + EPSILON)


def as_column(row):
    count = row.shape[1]
    down = lax.broadcasted_iota(jnp.int32, (count, count), 0)
    along = lax.broadcasted_iota(jnp.int32, (count, count), 1)
    return jnp.sum(jnp.where(down == along, row, 0.0), axis=1, keepdims=True)


def head_window(head, size):
    first = head * size // LANES * LANES
    lanes = (head * size + size - 1) // LANES * LANES + LANES - first
    place = lax.broadcasted_iota(jnp.int32, (1, lanes), 1) + first
    return first, lanes, (place >= head * size) & (place < head * size + size)


def slot_owners(me, bits):
    owners = []
    for p in range(1 << len(bits)):
        flips = sum(bit for k, bit in enumerate(bits) if p >> (len(bits) - 1 - k) & 1)
        owners.append(flips ^ me)
    return owners


def slot_select(width, bits, me):
    block = width >> len(bits)
    along = lax.broadcasted_iota(jnp.int32, (block, width), 1)
    inside = lax.broadcasted_iota(jnp.int32, (block, width), 0)
    rows = [(along == inside + owner * block).astype(F32) for owner in slot_owners(me, bits)]
    return jnp.concatenate(rows, axis=0).astype(BF16)


def two_gelu(value):
    square = value * value
    bend = jnp.tanh(GELU_RATE * value * (1.0 + GELU_CUBE * square))
    half = 0.5 * (1.0 + bend)
    slope = half + 0.5 * value * (1.0 - bend * bend) * GELU_RATE * (1.0 + 3.0 * GELU_CUBE * square)
    return value * half, slope


def first_kernel(
    routed, route_in, segs_in, tokens_in, gain_in, ffn_gain_in, route_q_in, route_f_in,
    keys, upper, lower, table,
    route, seg_at, segs, tokens, gain, ffn_gain, route_q, route_f, normed, picked, sems,
):
    copies = [
        pltpu.make_async_copy(source, target, sems.at[k])
        for k, (source, target) in enumerate(
            (
                (tokens_in, tokens),
                (gain_in, gain),
                (route_in, route),
                (segs_in, seg_at),
                (segs_in, segs),
                (ffn_gain_in, ffn_gain),
                (route_q_in, route_q),
                (route_f_in, route_f),
            )
        )
    ]
    for copy in copies:
        copy.start()
    for copy in copies:
        copy.wait()
    rows, span, width = tokens.shape
    me = lax.axis_index("seq")
    for k, vector in enumerate((gain, ffn_gain, route_q, route_f)):
        table[k : k + 1, :] = vector[...].astype(F32).reshape(1, width)
    hidden = tokens[...].reshape(rows * span, width).astype(F32)
    normed[...] = hidden * row_factor(hidden) * table[0:1, :]
    for r in range(rows):
        for k in range(routed):
            place = route[r, me * routed + k] - me * span
            at = pl.ds(r * routed + k, 1)
            picked[at, :width] = normed[pl.ds(r * span + place, 1), :]
            picked[at, width:] = jnp.full((1, LANES), (seg_at[r, place] + 2).astype(F32))
    keys[...] = picked[...].astype(BF16).reshape(keys.shape)
    marks = (segs[...] + 2).astype(F32)
    for out, start in ((upper, span - RADIUS), (lower, 0)):
        out[:, :RADIUS, :] = tokens[:, start : start + RADIUS, :]
        out[:, RADIUS:, :] = jnp.zeros((rows, 16, width), BF16)
        for r in range(rows):
            out[r, RADIUS:, :span] = jnp.broadcast_to(marks[r : r + 1], (16, span)).astype(BF16)


def light_kernel(
    before, tokens, after, segs, table, w_qkv, w_out,
    normed, query, keyval, probs, mix, attn, seg_row, mix_t,
):
    rows, span, width = tokens.shape
    extent = span + 2 * RADIUS
    own_all = rows * span
    heads = width // DL
    places = []
    for r in range(rows):
        places.append((tokens, r, span, r * span, r * extent + RADIUS))
    for r in range(rows):
        rim = own_all + 2 * r * RADIUS
        places.append((before, r, RADIUS, rim, r * extent))
        places.append((after, r, RADIUS, rim + RADIUS, r * extent + RADIUS + span))
    for part, r, size, at, _ in places:
        value = part[r, :size, :].astype(F32)
        normed[at : at + size, :] = (value * row_factor(value) * table[0:1, :]).astype(BF16)
    made = dot(normed[...], w_qkv[:, width:]).astype(BF16)
    for _, _, size, at, to in places:
        keyval[to : to + size, :] = made[at : at + size]
    query[...] = dot(normed[:own_all, :], w_qkv[:, :width]).astype(BF16)
    down = lax.broadcasted_iota(jnp.int32, (extent, span), 0)
    along = lax.broadcasted_iota(jnp.int32, (extent, span), 1)
    near = jnp.abs(along - down + RADIUS) <= RADIUS
    for r in range(rows):
        marks = (segs[r : r + 1, :] + 2).astype(F32)
        seg_row[:, :span] = before[r, RADIUS : RADIUS + 8, :span].astype(F32)
        seg_row[:, span : 2 * span] = jnp.broadcast_to(marks, (8, span))
        seg_row[:, 2 * span :] = after[r, RADIUS : RADIUS + 8, :span].astype(F32)
        columns = [as_column(seg_row[0:1, c * span : (c + 1) * span]) for c in range(3)]
        key_marks = jnp.concatenate([columns[0][span - RADIUS :], columns[1], columns[2][:RADIUS]], axis=0)
        allowed = near & (key_marks == marks)
        key_rows = slice(r * extent, (r + 1) * extent)
        val_t = keyval[key_rows, width:].T
        for h in range(heads):
            first, lanes, mask = head_window(h, DL)
            window = slice(first, first + lanes)
            q_head = jnp.where(mask, query[r * span : (r + 1) * span, window], 0)
            scores = dot_t(keyval[key_rows, window], q_head)
            scores = jnp.where(allowed, scores * (1.0 / math.sqrt(DL)), NEG_FILL)
            numer = jnp.exp(scores - jnp.max(scores, axis=0, keepdims=True))
            share = (numer / jnp.sum(numer, axis=0, keepdims=True)).astype(BF16)
            probs[r * heads + h] = share
            mix_t[h * DL : (h + 1) * DL, :] = dot(val_t[h * DL : (h + 1) * DL, :], share)
        mix[r * span : (r + 1) * span, :] = mix_t[...].T.astype(BF16)
    attn[...] = dot(mix[...], w_out[...])


def stat_row(value):
    total = jnp.sum(jnp.sum(value, axis=0, keepdims=True), axis=1, keepdims=True)
    return jnp.broadcast_to(total, (1, LANES))


def valid_column(segs):
    rows = segs.shape[0]
    parts = [as_column((segs[r : r + 1, :] >= 0).astype(F32)) for r in range(rows)]
    return jnp.concatenate(parts, axis=0)


def router(rows, weights):
    return jax.nn.sigmoid(jnp.sum(rows[...] * weights, axis=-1, keepdims=True))


def gathered(refs, row, lanes):
    value = jnp.concatenate([ref[:, row, :, lanes] for ref in refs], axis=0)
    return value.reshape(-1, value.shape[-1])


def middle_kernel(routed, parts, q_route, f_route, seg_at, tokens, segs, *refs):
    keys, refs = refs[:parts], refs[parts:]
    attn, upstream, table, w_q, w_kv, w_out = refs[:6]
    middle, normed_two, keyval, payload, q_rows, f_rows, f_up, proj, f_marks, stats = refs[6:16]
    full, marks, placed = refs[16:]
    rows, span, width = tokens.shape
    me = lax.axis_index("seq")
    hidden = tokens[...].reshape(rows * span, width).astype(F32)
    full[...] = hidden * row_factor(hidden) * table[0:1, :]
    for r in range(rows):
        for k in range(routed):
            at = pl.ds(r * routed + k, 1)
            place = q_route[r, me * routed + k] - me * span
            q_rows[at, :] = full[pl.ds(r * span + place, 1), :]
            marks[at, :] = jnp.full((1, LANES), (seg_at[r, place] + 2).astype(F32))
            place = f_route[r, k] - me * span
            f_marks[at, :] = jnp.full((1, LANES), (seg_at[r, place] + 2).astype(F32))
    q_low = q_rows[...].astype(BF16)
    payload[:, :, 2 * width : 3 * width] = q_low.reshape(rows, routed, width)
    payload[:, :, 3 * width :] = marks[...].astype(BF16).reshape(rows, routed, LANES)
    key_low = jnp.concatenate([gathered(keys, r, slice(0, width)) for r in range(rows)], axis=0)
    keyval[...] = dot(key_low, w_kv[...]).astype(BF16).reshape(keyval.shape)
    query = dot(q_low, w_q[...]).astype(BF16)
    heads = width // DH
    lane = lax.broadcasted_iota(jnp.int32, (1, width), 1)
    masks = [(lane >= h * DH) & (lane < (h + 1) * DH) for h in range(heads)]
    mixed = []
    for r in range(rows):
        mine = query[r * routed : (r + 1) * routed]
        wide = jnp.concatenate([jnp.where(m, mine, 0) for m in masks], axis=0)
        scores = dot_t(wide, keyval[r, :, :width]) * (1.0 / math.sqrt(DH))
        key_marks = gathered(keys, r, slice(width, width + LANES)).astype(F32).T[0:1, :]
        query_marks = jnp.concatenate([marks[r * routed : (r + 1) * routed, 0:1]] * heads, axis=0)
        scores = jnp.where(query_marks == key_marks, scores, NEG_FILL)
        peak = jnp.maximum(jnp.max(scores, axis=-1, keepdims=True), 0.0)
        numer = jnp.exp(scores - peak)
        share = numer / (jnp.exp(-peak) + jnp.sum(numer, axis=-1, keepdims=True))
        part = dot(share.astype(BF16), keyval[r, :, width:])
        total = jnp.zeros((routed, width), F32)
        for h in range(heads):
            total = total + jnp.where(masks[h], part[h * routed : (h + 1) * routed], 0.0)
        mixed.append(total)
    mixed = jnp.concatenate(mixed, axis=0).astype(BF16)
    proj[...] = dot(mixed, w_out[...])
    placed[...] = router(q_rows, table[2:3, :]) * proj[...]
    light = attn[...]
    middle[...] = hidden + light
    for r in range(rows):
        for k in range(routed):
            place = q_route[r, me * routed + k] - me * span
            at = pl.ds(r * span + place, 1)
            middle[at, :] = middle[at, :] + placed[pl.ds(r * routed + k, 1), :]
    valid = valid_column(segs)
    stats[...] = jnp.zeros(stats.shape, F32)
    stats[0:1, :] = stat_row(valid * hidden * hidden)
    stats[1:2, :] = stat_row(valid * light * light)
    stats[2:3, :] = stat_row(jnp.where(marks[:, 0:1] >= 2.0, placed[...] * placed[...], 0.0))
    stats[5:6, :] = stat_row(valid)
    mid = middle[...]
    full[...] = mid * row_factor(mid) * table[1:2, :]
    normed_two[...] = full[...].astype(BF16)
    for r in range(rows):
        for k in range(routed):
            place = f_route[r, k] - me * span
            f_rows[pl.ds(r * routed + k, 1), :] = full[pl.ds(r * span + place, 1), :]
    full[...] = upstream[...].reshape(rows * span, width).astype(F32)
    for r in range(rows):
        for k in range(routed):
            place = f_route[r, k] - me * span
            f_up[pl.ds(r * routed + k, 1), :] = full[pl.ds(r * span + place, 1), :]
    f_low = (router(f_rows, table[3:4, :]) * f_up[...]).astype(BF16)
    payload[:, :, :width] = f_rows[...].astype(BF16).reshape(rows, routed, width)
    payload[:, :, width : 2 * width] = f_low.reshape(rows, routed, width)


def glu_parts(inputs, back_in, gate_w, up_w, down_w):
    act, slope = two_gelu(dot(inputs, gate_w))
    lift = dot(inputs, up_w)
    back = dot_t(back_in, down_w)
    hidden = (act * lift).astype(BF16)
    return hidden, (back * lift * slope).astype(BF16), (back * act).astype(BF16)


def three_parts(value):
    high = value.astype(BF16).astype(F32)
    middle = (value - high).astype(BF16).astype(F32)
    return high, middle, value - high - middle


def light_ffn_kernel(normed_two, upstream, w_gate_up, w_down, z_light, d_light, hidden_out, grad_gate, grad_up):
    width = normed_two.shape[1]
    inner = w_down.shape[0]
    back_in = upstream[...].reshape(-1, width)
    unit = 256
    for at in range(0, inner, unit):
        part = slice(at, at + unit)
        gate_w, up_w = w_gate_up[:, part], w_gate_up[:, inner + at : inner + at + unit]
        hidden, d_gate, d_up = glu_parts(normed_two[...], back_in, gate_w, up_w, w_down[part, :])
        hidden_out[:, part] = hidden
        grad_gate[:, part] = d_gate
        grad_up[:, part] = d_up
    z_light[...] = dot(hidden_out[...], w_down[...])
    d_light[...] = dot_t(grad_gate[...], w_gate_up[:, :inner]) + dot_t(grad_up[...], w_gate_up[:, inner:])


def pass_share(step_refs, share_refs, me, group):
    gate, up, down = step_refs
    gate_out, up_out, down_out = share_refs
    unit = gate_out.shape[2]
    at = pl.ds(pl.multiple_of(lax.rem(me, group) * unit, unit), unit)
    gate_out[0] = gate[:, at]
    up_out[0] = up[:, at]
    down_out[0] = down[at, :]


def heavy_steps(step, sums_in, h_gate, h_up, h_down, f_rows, f_up, table, z_heavy, d_heavy):
    @pl.when(step == 0)
    def _():
        for total, value in zip((z_heavy, d_heavy), sums_in):
            total[...] = value

    f_gate = router(f_rows, table[3:4, :])
    f_low = (f_gate * f_up[...]).astype(BF16)
    f_in = f_rows[...].astype(BF16)
    hidden, d_gate, d_up = glu_parts(f_in, f_low, h_gate[...], h_up[...], h_down[...])
    z_heavy[...] += dot(hidden, h_down[...])
    d_heavy[...] += dot_t(d_gate, h_gate[...]) + dot_t(d_up, h_up[...])
    return f_gate


def ffn_first_kernel(
    group, h_gate, h_up, h_down, f_rows, f_up, table, z_heavy, d_heavy, gate_out, up_out, down_out
):
    zero = jnp.zeros(z_heavy.shape, F32)
    heavy_steps(pl.program_id(0), (zero, zero), h_gate, h_up, h_down, f_rows, f_up, table, z_heavy, d_heavy)
    pass_share((h_gate, h_up, h_down), (gate_out, up_out, down_out), lax.axis_index("seq"), group)


def ffn_last_kernel(
    routed, group, q_route, f_route, h_gate, h_up, h_down, z_in, d_in, upstream, middle, z_light, d_light_in,
    q_rows, f_rows, f_up, proj, f_marks, table, stats, segs,
    outputs, dmid, dmid_low, payload, vectors, gate_out, up_out, down_out,
    z_heavy, d_heavy, placed, full, d_light,
):
    step = pl.program_id(0)
    width = middle.shape[1]
    rows, span = segs.shape
    me = lax.axis_index("seq")
    f_gate = heavy_steps(
        step, (z_in[...], d_in[...]), h_gate, h_up, h_down, f_rows, f_up, table, z_heavy, d_heavy
    )
    pass_share((h_gate, h_up, h_down), (gate_out, up_out, down_out), me, group)

    @pl.when(step == pl.num_programs(0) - 1)
    def _():
        mid = middle[...]
        d_light[...] = d_light_in[...]
        placed[...] = f_gate * z_heavy[...]
        full[...] = mid + z_light[...]
        logit = jnp.sum(f_up[...] * z_heavy[...], axis=-1, keepdims=True) * f_gate * (1.0 - f_gate)
        d_heavy[...] += logit * table[3:4, :]
        for r in range(rows):
            for k in range(routed):
                place = f_route[r, k] - me * span
                at, source = pl.ds(r * span + place, 1), pl.ds(r * routed + k, 1)
                full[at, :] = full[at, :] + placed[source, :]
                d_light[at, :] = d_light[at, :] + d_heavy[source, :]
        outputs[...] = full[...].astype(BF16).reshape(outputs.shape)
        factor = row_factor(mid)
        d_norm = d_light[...]
        vectors[...] = jnp.zeros(vectors.shape, F32)
        vectors[0:1, :] = jnp.sum(d_norm * mid * factor, axis=0, keepdims=True)
        vectors[1:2, :] = jnp.sum(logit * f_rows[...], axis=0, keepdims=True)
        weighted = d_norm * table[1:2, :]
        inner = jnp.mean(weighted * mid, axis=-1, keepdims=True)
        total = upstream[...].reshape(rows * span, width).astype(F32) + factor * weighted - mid * (factor * factor * factor) * inner
        dmid[...] = total
        dmid_low[...] = total.astype(BF16)
        sums = stats[...]
        place = lax.broadcasted_iota(jnp.int32, sums.shape, 0)
        lane = lax.broadcasted_iota(jnp.int32, sums.shape, 1)
        light_sum = stat_row(valid_column(segs) * z_light[...] * z_light[...])
        heavy_sum = stat_row(jnp.where(f_marks[:, 0:1] >= 2.0, placed[...] * placed[...], 0.0))
        sums = jnp.where(place == 3, light_sum, jnp.where(place == 4, heavy_sum, sums))
        lanes = jnp.zeros(sums.shape, F32)
        for k, part in enumerate(three_parts(sums)):
            lanes = lanes + jnp.where(lane == place + 8 * k, part, 0.0)
        lanes = jnp.sum(lanes, axis=0, keepdims=True)
        full[...] = total
        for r in range(rows):
            for k in range(routed):
                place = q_route[r, me * routed + k] - me * span
                placed[pl.ds(r * routed + k, 1), :] = full[pl.ds(r * span + place, 1), :]
        q_gate = router(q_rows, table[2:3, :])
        logit = jnp.sum(placed[...] * proj[...], axis=-1, keepdims=True) * q_gate * (1.0 - q_gate)
        payload[:, :, :width] = (q_gate * placed[...]).astype(BF16).reshape(rows, routed, width)
        lane = lax.broadcasted_iota(jnp.int32, (rows * routed, LANES), 1)
        extra = jnp.broadcast_to(lanes, (rows * routed, LANES))
        for k, part in enumerate(three_parts(logit)):
            extra = jnp.where(lane == 24 + k, part, extra)
        payload[:, :, width:] = extra.astype(BF16).reshape(rows, routed, LANES)


def halves_of(value, place):
    half = value.shape[-1] // 2
    first, second = value[..., :half], value[..., half:]
    return jnp.where(place == 0, first, second), jnp.where(place == 0, second, first)


def store_slots(outs, place, base, grads):
    each = outs[0].shape[0]
    block = grads.shape[0] // (each * len(outs))
    low = grads.astype(BF16)
    for c in range(grads.shape[1] // LANES):
        for p in range(each * len(outs)):
            part = low[p * block : (p + 1) * block, c * LANES : (c + 1) * LANES]
            outs[p // each][p % each, place, pl.ds(base + c * block, block), :] = part
    return base + grads.shape[1] // LANES * block


def slot_vector_block(select, vectors):
    table = jnp.concatenate([vectors, jnp.zeros((LANES - vectors.shape[0], vectors.shape[1]), F32)], axis=0)
    return dot_t(select, table.astype(BF16))


def loop_slots(outs, base, left, right, lanes, half_of):
    block = left.shape[0] // (outs[0].shape[0] * len(outs))

    def chunk(i, carry):
        grads = dot(left[...], right[:, pl.ds(pl.multiple_of(i * lanes, lanes), lanes)])
        half, at = half_of(i)
        store_slots(outs, half, pl.multiple_of(base + at * (block * lanes // LANES), 16), grads)
        return carry

    lax.fori_loop(0, right.shape[1] // lanes, chunk, 0)


def first_grads_kernel(bits, normed_two, grad_gate, grad_up, hidden, upstream, *refs):
    outs, (inputs_t, hidden_t, back_in) = refs[:-3], refs[-3:]
    width = normed_two.shape[1]
    me = lax.axis_index("seq")
    place = lax.axis_index("dp")
    inputs_t[...] = dot_t(slot_select(width, bits, me), normed_two[...]).astype(BF16)
    loop_slots(outs, 0, inputs_t, grad_gate, 256, lambda i: (place, i))
    loop_slots(outs, 0, inputs_t, grad_up, 256, lambda i: (1 - place, i))
    hidden_t[...] = dot_t(slot_select(hidden.shape[1], bits, me), hidden[...]).astype(BF16)
    back_in[...] = upstream[...].reshape(-1, width)
    base = grad_gate.shape[1] // LANES * (width >> len(bits))
    loop_slots(outs, base, hidden_t, back_in, width // 2, lambda i: (i ^ place, 0))


def light_back_kernel(
    bits, dmid_low, query, keyval, probs, normed, mix, vectors, table, w_qkv, w_out,
    dnorm, to_right, to_left, *refs,
):
    outs, (dq, dkv, d_row, dq_t, select, inputs_t) = refs[:-6], refs[-6:]
    rows, rim, width = to_right.shape
    span = dmid_low.shape[0] // rows
    extent = span + 2 * rim
    own_all = rows * span
    heads = width // DL
    scale = 1.0 / math.sqrt(DL)
    place = lax.axis_index("dp")
    mix_grad = dot_t(dmid_low[...], w_out[...]).astype(BF16)
    for r in range(rows):
        key_rows = slice(r * extent, (r + 1) * extent)
        own_rows = slice(r * span, (r + 1) * span)
        key_t = keyval[key_rows, :width].T
        d_row[...] = jnp.zeros(d_row.shape, F32)
        for h in range(heads):
            first, lanes, mask = head_window(h, DL)
            window = slice(first, first + lanes)
            v_window = slice(width + first, width + first + lanes)
            q_head = jnp.where(mask, query[own_rows, window], 0)
            g_head = jnp.where(mask, mix_grad[own_rows, window], 0)
            share = probs[r * heads + h]
            full_share = share.astype(F32)
            prob_grad = dot_t(keyval[key_rows, v_window], g_head)
            delta = jnp.sum(full_share * prob_grad, axis=0, keepdims=True)
            score_grad = (full_share * (prob_grad - delta)).astype(BF16)
            d_row[:, window] += dot(score_grad, q_head)
            d_row[:, v_window] += dot(share, g_head)
            dq_t[h * DL : (h + 1) * DL, :] = dot(key_t[h * DL : (h + 1) * DL, :], score_grad)
        dq[own_rows, :] = (dq_t[...].T * scale).astype(BF16)
        rim_at = own_all + 2 * r * rim
        for size, at, to in ((span, rim, r * span), (rim, 0, rim_at), (rim, rim + span, rim_at + rim)):
            dkv[to : to + size, :width] = (d_row[at : at + size, :width] * scale).astype(BF16)
            dkv[to : to + size, width:] = d_row[at : at + size, width:].astype(BF16)
    d_rim = dot_t(dkv[own_all:, :], w_qkv[:, width:])
    dnorm[...] = dot_t(dq[...], w_qkv[:, :width]) + dot_t(dkv[:own_all, :], w_qkv[:, width:])
    gain_grad = jnp.sum(dnorm[...] * normed[:own_all, :].astype(F32), axis=0, keepdims=True)
    gain_grad = gain_grad + jnp.sum(d_rim * normed[own_all:, :].astype(F32), axis=0, keepdims=True)
    gain_grad = gain_grad / table[0:1, :]
    for r in range(rows):
        to_left[r] = d_rim[2 * r * rim : (2 * r + 1) * rim].astype(BF16)
        to_right[r] = d_rim[(2 * r + 1) * rim : (2 * r + 2) * rim].astype(BF16)
    half = width // 2
    select[...] = slot_select(width, bits, lax.axis_index("seq"))
    inputs_t[...] = dot_t(select[...], normed[...]).astype(BF16)
    base = store_slots(outs, place, 0, dot(inputs_t[:, :own_all], dq[...]))
    grads = dot(inputs_t[...], dkv[:, :width])
    base = store_slots(outs, place, base, grads[:, :half])
    base_two = store_slots(outs, 1 - place, 0, grads[:, half:])
    store_slots(outs, 1 - place, base_two, dot(inputs_t[...], dkv[:, width:]))
    grads = dot(dot_t(select[...], mix[...]).astype(BF16), dmid_low[...])
    base_two = store_slots(outs, place, base, grads[:, :half])
    store_slots(outs, 1 - place, base, grads[:, half:])
    line = lax.broadcasted_iota(jnp.int32, (8, width), 0)
    block = slot_vector_block(select[...], jnp.where(line == 2, gain_grad, vectors[...]))
    for which in range(2):
        store_slots(outs, which, base_two, block)


def heavy_ffn_kernel(parts, *refs):
    blocks, weights, (kept, sent) = refs[:parts], refs[parts:-2], refs[-2:]
    halves = [weights[k : k + 3] for k in range(0, len(weights), 3)]
    each, width, unit = halves[0][0].shape
    devices = lax.axis_size("seq")
    group = devices // (each * len(halves))
    me = lax.axis_index("seq")
    place = lax.axis_index("dp")
    low_place = lax.rem(me, group)
    high_place = lax.div(me, group)
    rows = range(blocks[0].shape[1])
    inputs = jnp.concatenate([gathered(blocks, r, slice(0, width)) for r in rows], axis=0)
    back_in = jnp.concatenate([gathered(blocks, r, slice(width, 2 * width)) for r in rows], axis=0)
    block = width // devices
    along = lax.broadcasted_iota(jnp.int32, (block, width), 1)
    inside = lax.broadcasted_iota(jnp.int32, (block, width), 0)
    picks = []
    for j in range(group):
        owner = high_place * group + (low_place ^ j)
        picks.append((along == inside + owner * block).astype(F32))
    picked = dot_t(jnp.concatenate(picks, axis=0).astype(BF16), inputs).astype(BF16)
    count = group * block

    def share(at, z, half):
        gate_w, up_w, down_w = (ref[at] for ref in halves[half])
        hidden, d_gate, d_up = glu_parts(inputs, back_in, gate_w, up_w, down_w)
        lanes = pl.ds(pl.multiple_of(z * unit, unit), unit)
        kept[:count, lanes] = dot(picked, jnp.where(place == 0, d_gate, d_up))
        sent[:count, lanes] = dot(picked, jnp.where(place == 0, d_up, d_gate)).astype(BF16)

        @pl.when(z == high_place)
        def _():
            hidden_t = hidden.T
            for out, part in zip((kept, sent), halves_of(back_in, place)):
                grad = dot(hidden_t, part).astype(out.dtype)
                size = grad.shape[1]
                out[count:, :size] = grad[: unit // 2]
                out[count:, size : 2 * size] = grad[unit // 2 :]
                out[count:, 2 * size :] = jnp.zeros((unit // 2, out.shape[1] - 2 * size), out.dtype)

    for half in range(len(halves)):

        def one(at, carry, half=half):
            share(at, half * each + at, half)
            return carry

        lax.fori_loop(0, each, one, 0)


def heavy_row_kernel(routed, counts, *refs):
    lists = []
    for count in counts:
        lists.append(refs[:count])
        refs = refs[count:]
    routed_parts, proj_parts, key_parts = lists
    keyval, table, w_q, w_kv, w_out, grads, parts, sums, sent, mix_t, dq_t, dkv = refs
    width = w_q.shape[0]
    scale = 1.0 / math.sqrt(DH)
    me = lax.axis_index("seq")
    r = lax.rem(me, 2)
    block = width // lax.axis_size("seq")
    along = lax.broadcasted_iota(jnp.int32, (block, width), 1)
    inside = lax.broadcasted_iota(jnp.int32, (block, width), 0)
    own = [(along == inside + at * block).astype(F32) for at in (me, me ^ 1)]
    own = jnp.concatenate(own, axis=0).astype(BF16)
    in_q = gathered(routed_parts, r, slice(2 * width, 3 * width))
    in_k = gathered(key_parts, r, slice(0, width))
    q_marks = gathered(routed_parts, r, slice(3 * width, 3 * width + LANES)).astype(F32).T[0:1, :]
    k_marks = gathered(key_parts, r, slice(width, width + LANES)).astype(F32)[:, 0:1]
    allowed = k_marks == q_marks
    grad_in = gathered(proj_parts, r, slice(0, width))
    extra = gathered(proj_parts, r, slice(width, width + LANES)).astype(F32)
    sums[...] = jnp.broadcast_to(
        sum(jnp.sum(ref[:, 0, 0:1, width:].astype(F32), axis=0) for ref in proj_parts), sums.shape
    )
    query = dot(in_q, w_q[...]).astype(BF16)
    mix_grad = dot_t(grad_in, w_out[...]).astype(BF16)
    key_t = keyval[r, :, :width].T
    val_t = keyval[r, :, width:].T
    lane = lax.broadcasted_iota(jnp.int32, (1, LANES), 1)
    for first in range(0, width, LANES):
        window = slice(first, first + LANES)
        v_window = slice(width + first, width + first + LANES)
        keys_w, vals_w = keyval[r, :, window], keyval[r, :, v_window]
        dk, dv = None, None
        for h in range(first // DH, (first + LANES) // DH):
            mask = (lane + first >= h * DH) & (lane + first < (h + 1) * DH)
            q_head = jnp.where(mask, query[:, window], 0)
            g_head = jnp.where(mask, mix_grad[:, window], 0)
            scores = jnp.where(allowed, dot_t(keys_w, q_head) * scale, NEG_FILL)
            peak = jnp.maximum(jnp.max(scores, axis=0, keepdims=True), 0.0)
            numer = jnp.exp(scores - peak)
            share = numer / (jnp.exp(-peak) + jnp.sum(numer, axis=0, keepdims=True))
            share_low = share.astype(BF16)
            prob_grad = dot_t(vals_w, g_head)
            delta = jnp.sum(share * prob_grad, axis=0, keepdims=True)
            score_grad = (share * (prob_grad - delta)).astype(BF16)
            at = slice(h * DH, (h + 1) * DH)
            mix_t[at, :] = dot(val_t[at, :], share_low).astype(BF16)
            dq_t[at, :] = dot(key_t[at, :], score_grad)
            part_k, part_v = dot(score_grad, q_head), dot(share_low, g_head)
            dk, dv = (part_k, part_v) if dk is None else (dk + part_k, dv + part_v)
        dkv[:, window] = (dk * scale).astype(BF16)
        dkv[:, v_window] = dv.astype(BF16)
    dq = (dq_t[...].T * scale).astype(BF16)
    in_q_t = dot_t(own, in_q)
    logits = jnp.sum(jnp.where((lane >= 24) & (lane < 27), extra, 0.0), axis=1, keepdims=True)
    logit_row = jnp.sum(extra.T[24:27, :], axis=0, keepdims=True)
    at = 0
    for grad in (
        dot(in_q_t.astype(BF16), dq),
        dot(dot_t(own, in_k).astype(BF16), dkv[...]),
        dot(dot(own, mix_t[...]).astype(BF16), grad_in),
        jnp.broadcast_to(jnp.sum(in_q_t * logit_row, axis=1, keepdims=True), (2 * block, LANES)),
    ):
        lanes = slice(at, at + grad.shape[1])
        grads[:, lanes] = grad[:block]
        sent[:block, lanes] = grad[block:].astype(BF16)
        at += grad.shape[1]
    half = dq.shape[0] // 2
    ours = lambda v: jnp.concatenate([v[:routed], v[half : half + routed]], axis=0)
    q_part = dot_t(ours(dq), w_q[...]) + ours(logits) * table[2:3, :]
    k_part = dot_t(ours(dkv), w_kv[...])
    for k, part in enumerate((q_part, k_part)):
        parts[k] = part[:routed]
        sent[block:, k * width : (k + 1) * width] = part[routed:].astype(BF16)
    sent[block:, 2 * width :] = jnp.zeros((routed, sent.shape[1] - 2 * width), BF16)


def heavy_last_kernel(
    routed, q_route, k_route, grads_in, parts_in, sums_in, got, dnorm, from_left, from_right, dmid, tokens, table,
    w_q, w_kv, grad_tokens, kept, sent, total, parts,
):
    rows, span, width = tokens.shape
    me = lax.axis_index("seq")
    place = lax.axis_index("dp")
    block = width // lax.axis_size("seq")
    grads = grads_in[...] + got[:block, :].astype(F32)
    for k in range(2):
        parts[lax.rem(me, 2), k] = parts_in[k]
        parts[1 - lax.rem(me, 2), k] = got[block:, k * width : (k + 1) * width].astype(F32)
    for r in range(rows):
        at = r * span
        total[at : at + span, :] = dnorm[at : at + span, :]
        total[at : at + RADIUS, :] += from_left[r].astype(F32)
        total[at + span - RADIUS : at + span, :] += from_right[r].astype(F32)
        for k in range(routed):
            for which, route in enumerate((q_route, k_route)):
                spot = route[r, me * routed + k] - me * span
                row = pl.ds(at + spot, 1)
                total[row, :] = total[row, :] + parts[r, which, k : k + 1, :]
    hidden = tokens[...].reshape(rows * span, width).astype(F32)
    factor = row_factor(hidden)
    weighted = total[...] * table[0:1, :]
    inner = jnp.mean(weighted * hidden, axis=-1, keepdims=True)
    d_hidden = dmid[...] + factor * weighted - hidden * (factor * factor * factor) * inner
    grad_tokens[...] = d_hidden.astype(BF16).reshape(grad_tokens.shape)
    along = lax.broadcasted_iota(jnp.int32, (block, width), 1)
    inside = lax.broadcasted_iota(jnp.int32, (block, width), 0)
    own_full = (along == inside + me * block).astype(F32)
    own = own_full.astype(BF16)
    own_gain = jnp.sum(own_full * table[0:1, :], axis=1, keepdims=True)
    own_route = jnp.sum(own_full * table[2:3, :], axis=1, keepdims=True)
    route_grad = grads[:, 4 * width : 4 * width + 1]
    gain_grad = jnp.sum(dot(own, w_q[...]) * grads[:, :width], axis=1, keepdims=True)
    gain_grad = gain_grad + jnp.sum(dot(own, w_kv[...]) * grads[:, width : 3 * width], axis=1, keepdims=True)
    gain_grad = (gain_grad + own_route * route_grad) / own_gain
    lane = lax.broadcasted_iota(jnp.int32, (block, LANES), 1)
    sums = sums_in[...]
    sums = sums + pltpu.roll(sums, LANES - 8, 1) + pltpu.roll(sums, LANES - 16, 1)
    sums = jnp.where(lane[:8] < 8, sums, 0.0)
    vectors = jnp.where(lane == 0, gain_grad, jnp.where(lane == 1, route_grad, 0.0))
    own_sums = pltpu.roll(sums, 8, 1)[0:1, :]
    sent_sums = jnp.zeros((1, LANES), F32)
    for k, part in enumerate(three_parts(sums)):
        sent_sums = sent_sums + pltpu.roll(part, 8 + 8 * k, 1)[0:1, :]
    at = 0
    for grad in (grads[:, :width], grads[:, width : 3 * width], grads[:, 3 * width : 4 * width]):
        mine, other = halves_of(grad, place)
        size = mine.shape[1]
        kept[:, at : at + size] = mine
        sent[:, at : at + size] = other.astype(BF16)
        at += size
    kept[:, at:] = vectors + own_sums
    sent[:, at:] = (vectors + sent_sums).astype(BF16)


def mix_kernel(plans, count, *refs):
    ins, outs = refs[:count], refs[count:]
    for out, parts in zip(outs, plans):
        for target, sources in parts:
            dims = out.at[target].shape
            values = [ins[k][index].reshape(dims) for k, index in sources]
            if len(values) > 1:
                values = [sum(v.astype(F32) for v in values)]
            out[target] = values[0].astype(out.dtype)


def finish_light_kernel(kept, received, *outs):
    total = kept[0, 0].astype(F32) + received[0, 0].astype(F32)
    base = 0
    for ref in outs:
        block = ref.shape[0]
        for c in range(ref.shape[1] // LANES):
            ref[:, c * LANES : (c + 1) * LANES] = total[base : base + block]
            base += block


def finish_heavy_kernel(heavy_kept, heavy_got, q_out, kv_out, out_out, vectors, stats):
    total = heavy_kept[...] + heavy_got[...].astype(F32)
    at = 0
    for ref in (q_out, kv_out, out_out, vectors):
        ref[...] = total[:, at : at + ref.shape[1]]
        at += ref.shape[1]
    sums = total[:8, at - LANES :]
    stats[...] = sums + pltpu.roll(sums, LANES - 8, 1) + pltpu.roll(sums, LANES - 16, 1)


def finish_ffn_kernel(groups, *refs):
    pieces, gate_up_out = refs[:-1], refs[-1]
    group = len(pieces)
    low_place = lax.rem(lax.axis_index("seq"), group)
    unit = pieces[0].shape[1] // groups
    for j, piece in enumerate(pieces):
        for z in range(groups):
            at = pl.multiple_of((z * group + (low_place ^ j)) * unit, unit)
            gate_up_out[:, pl.ds(at, unit)] = piece[:, z * unit : (z + 1) * unit].astype(F32)


def blend(ins, outs, after=(), micros=1, mib=6):
    kernel = functools.partial(mix_kernel, [parts for _, _, parts in outs], len(ins))
    return call(kernel, [shape(dims, dtype) for dims, dtype, _ in outs], ins, mib=mib, after=after, micros=micros)


ALL = slice(None)


def joined(ins, first, cuts):
    blocks = [(first + k, b) for k, part in enumerate(ins) for b in range(part.shape[0])]
    each = len(blocks) // cuts
    dims = (each, *ins[0].shape[1:])
    outs = []
    for c in range(cuts):
        outs.append((dims, ins[0].dtype, [(k, [source]) for k, source in enumerate(blocks[c * each : (c + 1) * each])]))
    return outs


def pair_part(target, pair, index):
    return (target, [(2 * pair, index), (2 * pair + 1, index)])


def side_by_side(rows, cuts):
    half = rows // 2
    dims = (4, 2, half, LANES)
    each = 8 // cuts
    ways = [((0, 2), slice(0, half)), ((4, 6), slice(0, half)), ((0, 4), slice(half, rows)), ((2, 6), slice(half, rows))]
    outs = []
    for starts, part in ways:
        parts = []
        for k, start in enumerate(starts):
            inside = slice(start % each, start % each + 2)
            parts.append(pair_part(slice(2 * k, 2 * k + 2), start // each, (inside, ALL, part)))
        outs.append((dims, BF16, parts))
    return outs


def crossed(rows):
    dims = (2, 2, rows // 2, LANES)
    sides = (slice(0, 2), slice(2, 4))
    return [(dims, BF16, [pair_part(ALL, pair, side)]) for pair in (0, 1) for side in sides]


def halved(rows, first):
    half = rows // 2
    places = ((ALL, ALL, slice(0, half)), (ALL, ALL, slice(half, rows)))
    outs = []
    for way in (slice(0, 1), slice(1, 2)):
        parts = [pair_part(place, first + k, (ALL, way)) for k, place in enumerate(places)]
        outs.append(((2, 1, rows, LANES), BF16, parts))
    return outs


def last_half(rows, pair):
    return [((1, 1, rows, LANES), BF16, [pair_part(ALL, pair, way)]) for way in (slice(0, 1), slice(1, 2))]


def flat_halved(rows, keep, got, base):
    half = rows // 2
    ways = []
    for way in (0, 1):
        parts = []
        for slot in (0, 1):
            at = base + (2 * slot + way) * half
            sources = [(keep, (slot, way)), (got, slice(at, at + half))]
            parts.append(((slot, 0, slice(half, rows)), sources))
        ways.append(parts)
    return ways


def lanes_of(c):
    return slice(c * LANES, (c + 1) * LANES)


def skip_operand(kernel, place):
    return lambda *refs: kernel(*refs[:place], *refs[place + 1 :])


def local_kernels(
    tokens,
    segments,
    query_route,
    kv_route,
    ffn_route,
    grad_out,
    attn_gain,
    light_qkv,
    light_out,
    heavy_q,
    heavy_kv,
    heavy_out,
    route_query,
    ffn_gain,
    light_gate_up,
    light_down,
    heavy_gate_up,
    heavy_down,
    route_ffn,
):
    rows, span, width = tokens.shape
    devices = lax.axis_size("seq")
    routed = query_route.shape[1] // devices
    own, count = rows * span, rows * routed
    per_row = devices * routed
    extent = span + 2 * RADIUS
    block = width // devices
    light_heads = width // DL
    ffn_light, ffn_heavy = light_down.shape[0], heavy_down.shape[0]
    marked = width + LANES

    rim = shape((rows, RADIUS + 16, width), BF16)
    keys, upper, lower, table = call(
        functools.partial(first_kernel, routed),
        [shape((rows, routed, marked), BF16), rim, rim, shape((4, width), F32)],
        [kv_route, segments, tokens, attn_gain, ffn_gain, route_query, route_ffn],
        hbm=7,
        scratch=[
            pltpu.SMEM(kv_route.shape, jnp.int32),
            pltpu.SMEM(segments.shape, jnp.int32),
            pltpu.VMEM(segments.shape, jnp.int32),
            pltpu.VMEM(tokens.shape, BF16),
            pltpu.VMEM((width,), F32),
            pltpu.VMEM((width,), F32),
            pltpu.VMEM((width,), BF16),
            pltpu.VMEM((width,), BF16),
            pltpu.VMEM((own, width), F32),
            pltpu.VMEM((count, marked), F32),
            pltpu.SemaphoreType.DMA((8,)),
        ],
        mib=58,
    )
    bits = (1, 2, 4, 8)
    keys = keys[None]
    keys_got = [swap(keys, "seq", flip) for flip in (8, 4, 12)]
    before = shifted(upper, "seq", 1)
    after = shifted(lower, "seq", -1)
    (keys_four,) = blend([keys, *keys_got], joined([keys, *keys_got], 0, 1), mib=4)
    keys_four_got = swap(keys_four, "seq", 2)
    last = keys_four

    normed, query, keyval, probs, mix, attn = call(
        light_kernel,
        [
            shape((rows * extent, width), BF16),
            shape((own, width), BF16),
            shape((rows * extent, 2 * width), BF16),
            shape((rows * light_heads, extent, span), BF16),
            shape((own, width), BF16),
            shape((own, width), F32),
        ],
        [before, tokens, after, segments, table, light_qkv, light_out],
        scratch=[pltpu.VMEM((8, 3 * span), F32), pltpu.VMEM((width, span), F32)],
        micros=6,
        mib=14,
        after=[last],
    )
    held = [keys_four, keys_four_got]
    (keys_eight,) = blend(held, joined(held, 0, 1), [attn], mib=4)
    key_parts = [keys_eight, swap(keys_eight, "seq", 1)]

    small = shape((count, width), F32)
    middle, normed_two, keyval_all, payload, q_rows, f_rows, f_up, proj, f_marks, stats = call(
        functools.partial(middle_kernel, routed, len(key_parts)),
        [
            shape((own, width), F32),
            shape((own, width), BF16),
            shape((rows, per_row, 2 * width), BF16),
            shape((rows, routed, 3 * width + LANES), BF16),
            small,
            small,
            small,
            small,
            shape((count, LANES), F32),
            shape((8, LANES), F32),
        ],
        [
            query_route, ffn_route, segments, tokens, segments, *key_parts, attn, grad_out,
            table, heavy_q, heavy_kv, heavy_out,
        ],
        smem=3,
        scratch=[
            pltpu.VMEM((own, width), F32),
            pltpu.VMEM((count, LANES), F32),
            pltpu.VMEM((count, width), F32),
        ],
        micros=4,
        mib=8,
    )
    payload = payload[None]
    payload_got = [swap(payload, "seq", flip) for flip in (8, 4, 12)]

    share = shape((own, ffn_light), BF16)
    z_light, d_light, hidden, grad_gate, grad_up = call(
        light_ffn_kernel,
        [shape((own, width), F32), shape((own, width), F32), share, share, share],
        [normed_two, grad_out, light_gate_up, light_down],
        micros=6,
        mib=9,
    )
    half_rows = (width // 2) // LANES
    slot_rows = block * ffn_light // LANES + ffn_light // devices * half_rows
    slots = [shape((devices // (2 * FIRST_CUTS), 2, slot_rows, LANES), BF16)] * (2 * FIRST_CUTS)
    slots = call(
        functools.partial(first_grads_kernel, bits),
        slots,
        [normed_two, grad_gate, grad_up, hidden, grad_out],
        scratch=[
            pltpu.VMEM((width, own), BF16),
            pltpu.VMEM((ffn_light, own), BF16),
            pltpu.VMEM((own, width), BF16),
        ],
        micros=4,
        mib=9,
    )
    core = len(slots) // 2
    first_core = list(zip(slots[:core], [swap(part, "seq", 1) for part in slots[core:]]))
    held = [payload, *payload_got]
    (routed_four,) = blend(held, joined(held, 0, 1), [slots[0]], mib=4)
    routed_four_got = swap(routed_four, "seq", 2)

    steps = 4
    group = min(4, devices)
    groups = devices // group
    unit = ffn_heavy // devices
    heavy_unit = ffn_heavy // steps
    whole = lambda *dims: pl.BlockSpec(dims, lambda j: (0,) * len(dims))

    def streamed(first):
        columns = lambda at: pl.BlockSpec((width, heavy_unit), lambda j: (0, at + first + j))
        return [columns(0), columns(steps), pl.BlockSpec((heavy_unit, width), lambda j: (first + j, 0))]

    half = steps // 2
    share_dims = [(half, width, unit), (half, width, unit), (half, unit, width)]
    share_shapes = [shape(dims, BF16) for dims in share_dims]
    share_specs = [pl.BlockSpec((1, *dims[1:]), lambda j: (j, 0, 0)) for dims in share_dims]
    z_heavy, d_heavy, *shares_one = pl.pallas_call(
        skip_operand(functools.partial(ffn_first_kernel, group), 6),
        grid=(half,),
        out_shape=[small, small, *share_shapes],
        in_specs=streamed(0) + [whole(count, width)] * 2 + [whole(4, width), ANY],
        out_specs=[whole(count, width)] * 2 + share_specs,
        compiler_params=pltpu.CompilerParams(vmem_limit_bytes=12 * MIB),
        cost_estimate=cost(6),
    )(heavy_gate_up, heavy_gate_up, heavy_down, f_rows, f_up, table, routed_four)
    rows_one = slots[0].shape[2]
    part = rows_one // 2
    low, high = slice(0, part), slice(part, rows_one)
    one, two = slice(0, 1), slice(1, 2)
    span_of = lambda k: slice(2 * k, 2 * k + 2)
    ins = [v for pair in first_core for v in pair]
    each = 8 // FIRST_CUTS
    halves = [
        (
            (8, 1, rows_one, LANES),
            BF16,
            [pair_part(slice(k * each, (k + 1) * each), k, (ALL, way)) for k in range(FIRST_CUTS)],
        )
        for way in (slice(0, 1), slice(1, 2))
    ]
    left_keep, left_sent = blend(ins, halves, [z_heavy])
    first_pairs = [left_keep, swap(left_sent, "dp", 1)]
    outputs, dmid, dmid_low, proj_payload, vectors, *shares_two = pl.pallas_call(
        skip_operand(functools.partial(ffn_last_kernel, routed, group), 19),
        grid=(half,),
        out_shape=[
            shape((rows, span, width), BF16),
            shape((own, width), F32),
            shape((own, width), BF16),
            shape((rows, routed, marked), BF16),
            shape((8, width), F32),
            *share_shapes,
        ],
        in_specs=[SMEM, SMEM]
        + streamed(half)
        + [whole(count, width)] * 2
        + [whole(rows, span, width)]
        + [whole(own, width)] * 3
        + [whole(count, width)] * 4
        + [whole(count, LANES), whole(4, width), whole(8, LANES), whole(rows, span), ANY],
        out_specs=[
            whole(rows, span, width),
            whole(own, width),
            whole(own, width),
            whole(rows, routed, marked),
            whole(8, width),
            *share_specs,
        ],
        scratch_shapes=[pltpu.VMEM((count, width), F32)] * 3 + [pltpu.VMEM((own, width), F32)] * 2,
        compiler_params=pltpu.CompilerParams(vmem_limit_bytes=16 * MIB),
        cost_estimate=cost(7),
    )(
        query_route, ffn_route, heavy_gate_up, heavy_gate_up, heavy_down, z_heavy, d_heavy, grad_out, middle,
        z_light, d_light, q_rows, f_rows, f_up, proj, f_marks, table, stats, segments, left_keep,
    )
    proj_payload = proj_payload[None]
    proj_got = [swap(proj_payload, "seq", flip) for flip in (8, 4, 12)]

    slot_rows = block * 3 * half_rows + block * half_rows + block
    slots = [shape((devices // (2 * SECOND_CUTS), 2, slot_rows, LANES), BF16)] * (2 * SECOND_CUTS)
    rim = shape((rows, RADIUS, width), BF16)
    dnorm, to_right, to_left, *slots = call(
        functools.partial(light_back_kernel, bits),
        [shape((own, width), F32), rim, rim, *slots],
        [dmid_low, query, keyval, probs, normed, mix, vectors, table, light_qkv, light_out],
        scratch=[
            pltpu.VMEM((own, width), BF16),
            pltpu.VMEM((rows * extent, 2 * width), BF16),
            pltpu.VMEM((extent, 2 * width), F32),
            pltpu.VMEM((width, span), F32),
            pltpu.VMEM((width, width), BF16),
            pltpu.VMEM((width, rows * extent), BF16),
        ],
        micros=3,
        mib=12,
    )
    from_left = shifted(to_right, "seq", 1)
    from_right = shifted(to_left, "seq", -1)
    core = len(slots) // 2
    second_core = list(zip(slots[:core], [swap(part, "seq", 1) for part in slots[core:]]))

    held_proj, held_routed = [proj_payload, *proj_got], [routed_four, routed_four_got]
    side = (4, 1, rows_one, LANES)
    sides = [
        (side, BF16, [pair_part(slice(2 * k, 2 * k + 2), 0, slice(4 * k + at, 4 * k + at + 2)) for k in (0, 1)])
        for at in (0, 2)
    ]
    first_keep, first_sent, proj_four, *routed_eight = blend(
        first_pairs + held_proj + held_routed,
        sides + joined(held_proj, 2, 1) + joined(held_routed, 6, 1),
        [dnorm],
    )
    first_pairs = [first_keep, swap(first_sent, "seq", 4)]
    held_proj = [proj_four, swap(proj_four, "seq", 2)]
    routed_parts = routed_eight + [swap(piece, "seq", 1) for piece in routed_eight]

    heavy_rows = group * block + unit // 2
    ffn_kept, ffn_sent = call(
        functools.partial(heavy_ffn_kernel, len(routed_parts)),
        [shape((heavy_rows, groups * unit), F32), shape((heavy_rows, groups * unit), BF16)],
        [*routed_parts, *shares_one, *shares_two],
        micros=7,
        mib=11,
        after=[left_keep],
    )
    ffn_got = swap(ffn_sent, "dp", 1)

    rows_two = slots[0].shape[2]
    ins = [v for pair in second_core for v in pair]
    left_keep, left_sent, right_keep, right_sent = blend(
        ins, side_by_side(rows_two, SECOND_CUTS), [ffn_kept], micros=1
    )
    (proj_eight,) = blend(held_proj, joined(held_proj, 0, 1), [left_keep])
    proj_parts = [proj_eight, swap(proj_eight, "seq", 1)]
    second_pairs = [left_keep, swap(left_sent, "seq", 2), right_keep, swap(right_sent, "seq", 4)]

    gathers = (routed_parts, proj_parts, key_parts)
    grad_lanes = 4 * width + LANES
    heavy_grads, heavy_parts, sums, pair_sent = call(
        functools.partial(heavy_row_kernel, routed, [len(parts) for parts in gathers]),
        [
            shape((block, grad_lanes), F32),
            shape((2, routed, width), F32),
            shape((8, LANES), F32),
            shape((block + routed, grad_lanes), BF16),
        ],
        [*sum(gathers, []), keyval_all, table, heavy_q, heavy_kv, heavy_out],
        scratch=[
            pltpu.VMEM((width, per_row), BF16),
            pltpu.VMEM((width, per_row), F32),
            pltpu.VMEM((per_row, 2 * width), BF16),
        ],
        micros=9,
        mib=8,
        after=[proj_eight],
    )
    pair_got = swap(pair_sent, "seq", 1)
    first_keep, first_sent = blend(
        first_pairs,
        [((2, 1, rows_one, LANES), BF16, [pair_part(ALL, 0, slice(at, at + 2))]) for at in (0, 2)],
        [sums],
    )
    first_pairs = [first_keep, swap(first_sent, "seq", 2)]
    from_left, from_right = blend(
        [from_left, from_right], [(from_left.shape, BF16, [(ALL, [(k, ALL)])]) for k in (0, 1)], [first_keep]
    )
    below = slice(group * block, heavy_rows)
    down_lanes = [slice(0, width // 2), slice(width // 2, width)]
    rows_of = lambda j: slice(j * block, (j + 1) * block)
    kept_side, sent_side, kept_other, sent_other = crossed(rows_two)
    sent_rows = 2 * rows_two
    parts = [(slice(0, sent_rows), sent_other[2][0][1])]
    for c in range(groups * unit // LANES):
        at = sent_rows + c * block
        parts.append(pair_part(slice(at, at + block), 2, (rows_of(2), lanes_of(c))))
    merged = ((sent_rows + groups * unit // LANES * block, LANES), BF16, parts)
    downs = [pair_part(slice(k * unit // 2, (k + 1) * unit // 2), 2, (below, down_lanes[k])) for k in (0, 1)]
    left_keep, left_sent, right_keep, x_sent, heavy_down_grad, *pieces = blend(
        second_pairs + [ffn_kept, ffn_got],
        [kept_side, sent_side, kept_other, merged, ((unit, width // 2), F32, downs)]
        + [
            ((block, groups * unit), F32 if j == 0 else BF16, [pair_part(ALL, 2, rows_of(j))])
            for j in (0, 1, 3)
        ],
        [from_left],
    )
    second_pairs = [left_keep, swap(left_sent, "seq", 4), right_keep, swap(x_sent, "seq", 2)]
    pieces = [pieces[0], swap(pieces[1], "seq", 1), None, swap(pieces[2], "seq", 3)]
    grad_tokens, heavy_kept, heavy_sent = call(
        functools.partial(heavy_last_kernel, routed),
        [
            shape((rows, span, width), BF16),
            shape((block, 2 * width + LANES), F32),
            shape((block, 2 * width + LANES), BF16),
        ],
        [
            query_route, kv_route, heavy_grads, heavy_parts, sums, pair_got, dnorm, from_left, from_right,
            dmid, tokens, table, heavy_q, heavy_kv,
        ],
        smem=2,
        scratch=[pltpu.VMEM((own, width), F32), pltpu.VMEM((rows, 2, routed, width), F32)],
        micros=2,
        mib=7,
        after=[left_keep],
    )
    ways = flat_halved(rows_two, 2, 3, 0)
    for way in (0, 1):
        index = (ALL, slice(way, way + 1))
        ways[way].insert(0, ((ALL, ALL, slice(0, rows_two // 2)), [(0, index), (1, index)]))
    sent_parts = []
    for (slot, _, place), sources in ways[1][1:]:
        sent_parts.append((slice(slot * rows_two + place.start, slot * rows_two + place.stop), sources))
    for slot in (0, 1):
        at = slot * rows_two
        sources = [(0, (slot, 1)), (1, (slot, 1))]
        sent_parts.append((slice(at, at + rows_two // 2), sources))
    piece_parts = []
    for c in range(groups * unit // LANES):
        at = sent_rows + c * block
        piece_parts.append(((ALL, lanes_of(c)), [(3, slice(at, at + block))]))
    second_keep, y_sent, pieces[2], first_keep, first_sent = blend(
        second_pairs + first_pairs,
        [
            ((2, 1, rows_two, LANES), BF16, ways[0]),
            ((2 * rows_two, LANES), BF16, sent_parts),
        ]
        + [((block, groups * unit), BF16, piece_parts)]
        + [((1, 1, rows_one, LANES), BF16, [pair_part(ALL, 2, slice(slot, slot + 1))]) for slot in (0, 1)],
        [heavy_kept],
    )
    y_got = swap(y_sent, "dp", 1)
    first_pair = [first_keep, swap(first_sent, "seq", 8)]
    second_keep, second_sent, heavy_sent = blend(
        [second_keep, y_got, heavy_sent],
        [
            ((1, 1, rows_two, LANES), BF16, [(ALL, [(0, slot), (1, slice(slot * rows_two, (slot + 1) * rows_two))])])
            for slot in (0, 1)
        ]
        + [(heavy_sent.shape, BF16, [(ALL, [(2, ALL)])])],
    )
    heavy_got = swap(heavy_sent, "dp", 1)
    second_pair = [second_keep, swap(second_sent, "seq", 8)]
    light_gate_up_grad, light_down_grad = call(
        finish_light_kernel,
        [shape((block, ffn_light), F32), shape((ffn_light // devices, width // 2), F32)],
        first_pair,
        mib=4,
        after=[second_keep],
    )
    (heavy_gate_up_grad,) = call(
        functools.partial(finish_ffn_kernel, groups),
        [shape((block, ffn_heavy), F32)],
        pieces,
        micros=0.5,
        mib=4,
        after=[light_down_grad],
    )
    heavy_q_grad, heavy_kv_grad, heavy_out_grad, heavy_vectors, stats = call(
        finish_heavy_kernel,
        [
            shape((block, width // 2), F32),
            shape((block, width), F32),
            shape((block, width // 2), F32),
            shape((block, LANES), F32),
            shape((8, LANES), F32),
        ],
        [heavy_kept, heavy_got],
        mib=4,
        after=[heavy_gate_up_grad],
    )
    light_qkv_grad, light_out_grad, light_vectors = call(
        finish_light_kernel,
        [
            shape((block, 3 * width // 2), F32),
            shape((block, width // 2), F32),
            shape((block, LANES), F32),
        ],
        second_pair,
        mib=4,
        after=[heavy_vectors],
    )
    sums = stats[0, 8:14]
    return (
        outputs,
        grad_tokens,
        light_vectors[:, 2] + heavy_vectors[:, 0],
        light_qkv_grad,
        light_out_grad,
        heavy_q_grad,
        heavy_kv_grad,
        heavy_out_grad,
        heavy_vectors[:, 1],
        light_vectors[:, 0],
        light_gate_up_grad,
        light_down_grad,
        heavy_gate_up_grad,
        heavy_down_grad,
        light_vectors[:, 1],
        jnp.sqrt(sums[:5] / (sums[5] * width)),
    )


def local(tokens, segments, query_route, *others):
    block = tokens.shape[2] // lax.axis_size("seq")
    fits = query_route.shape[1] <= 256 and block % 16 == 0 and tokens.shape[0] == 2
    return (local_kernels if fits else local_wide)(tokens, segments, query_route, *others)


def solution(mesh):
    placed = (
        P("dp", "seq", None),
        P("dp", "seq"),
        P("dp", None),
        P("dp", None),
        P("dp", "seq"),
        P("dp", "seq", None),
    ) + (P(),) * 13
    matrix = P("seq", "dp")
    vector = P("seq")
    return jax.shard_map(
        local,
        mesh=mesh,
        in_specs=placed,
        out_specs=(
            P("dp", "seq", None),
            P("dp", "seq", None),
            vector,
            matrix,
            matrix,
            matrix,
            matrix,
            matrix,
            vector,
            vector,
            matrix,
            matrix,
            matrix,
            matrix,
            vector,
            P(),
        ),
        check_vma=False,
    )
```

```python
import functools
import math

import jax
import jax.numpy as jnp
from jax import lax
from jax.experimental import pallas as pl
from jax.experimental.pallas import tpu as pltpu
from jax.sharding import PartitionSpec as P

DL = 96
DH = 64
RADIUS = 64
LANES = 128


PRECISE = lax.Precision.HIGHEST
EPSILON = 1e-06
NEG_FILL = -1e30
F32 = jnp.float32
BF16 = jnp.bfloat16


def swap(value, axis, bit):
    return lax.ppermute(value, axis, [(i, i ^ bit) for i in range(lax.axis_size(axis))])


def shifted(block, axis, distance):
    devices = range(lax.axis_size(axis))
    route = [(i - distance, i) for i in devices if i - distance in devices]
    return lax.ppermute(block, axis, route)


def gather_blocks(block):
    held = block[None]
    bit = lax.axis_size("seq") // 2
    while bit:
        held = jnp.concatenate([held, swap(held, "seq", bit)], axis=0)
        bit //= 2
    return held


def add_halves(value, dim, axis, bit, out_type=BF16):
    half = value.shape[dim] // 2
    keep = lax.slice_in_dim(value, 0, half, axis=dim)
    sent = lax.slice_in_dim(value, half, 2 * half, axis=dim)
    return (keep.astype(F32) + swap(sent, axis, bit).astype(F32)).astype(out_type)


def scatter_sum(slots):
    devices = lax.axis_size("seq")
    rows = slots.shape[2]
    slots = add_halves(slots, 0, "seq", 1)
    left, right = slots[:, :, : rows // 2], slots[:, :, rows // 2 :]
    left = add_halves(left, 0, "seq", 2)
    right = add_halves(right, 1, "dp", 1)
    left = add_halves(left, 1, "dp", 1)
    right = add_halves(right, 0, "seq", 2)
    both = jnp.concatenate([left, right], axis=2)
    bit = 4
    while bit < devices:
        both = add_halves(both, 0, "seq", bit, BF16 if 2 * bit < devices else F32)
        bit *= 2
    return both[0, 0]


def slot_places(me, devices):
    bits = devices.bit_length() - 1
    places = [int(format(p, f"0{bits}b")[::-1], 2) for p in range(devices)]
    return jnp.array(places, jnp.int32) ^ me


def slot_columns(value, me, devices):
    width = value.shape[-1]
    block = width // devices
    order = (slot_places(me, devices)[:, None] * block + jnp.arange(block)[None, :]).reshape(-1)
    onehot = (jnp.arange(width)[:, None] == order[None, :]).astype(BF16)
    return jnp.dot(value, onehot, preferred_element_type=F32).astype(BF16)


def own_half_first(value, place):
    half = value.shape[-1] // 2
    first, second = value[..., :half], value[..., half:]
    return (jnp.where(place == 0, first, second), jnp.where(place == 0, second, first))


def slot_block(grad_halves, devices):
    stacked = jnp.stack(grad_halves)
    _, total, cols = stacked.shape
    parts = stacked.reshape(2, devices, total // devices, cols // LANES, LANES)
    return parts.transpose(1, 0, 3, 2, 4).reshape(devices, 2, -1, LANES).astype(BF16)


def unslot(rows, cols):
    return rows.reshape(cols // LANES, -1, LANES).transpose(1, 0, 2).reshape(-1, cols)


def slot_vectors(vectors, me, devices):
    block = vectors[0].shape[0] // devices
    table = jnp.stack(vectors, axis=-1).reshape(devices, block, len(vectors))
    table = jnp.take(table, slot_places(me, devices), axis=0)
    table = jnp.pad(table, ((0, 0), (0, 0), (0, LANES - len(vectors))))
    return jnp.broadcast_to(table[:, None], (devices, 2, block, LANES)).astype(BF16)


def split_parts(value):
    high = lax.reduce_precision(value, 8, 7)
    middle = lax.reduce_precision(value - high, 8, 7)
    return (high, middle, value - high - middle)


def rms_factor(hidden):
    return lax.rsqrt(jnp.mean(hidden * hidden, axis=-1, keepdims=True) + EPSILON)


def norm_back(hidden, factor, gain_vec, upstream):
    weighted = upstream * gain_vec
    inner_mean = jnp.mean(weighted * hidden, axis=-1, keepdims=True)
    return factor * weighted - hidden * (factor * factor * factor) * inner_mean


def pick_rows(source, positions):
    return jnp.take_along_axis(source, positions[..., None], axis=1)


def place_rows(values, positions, extent):
    onehot = (positions[..., None] == jnp.arange(extent)[None, None, :]).astype(F32)
    return jnp.einsum("rqs,rqd->rsd", onehot, values, precision=PRECISE)


def matmul(left, right):
    return jnp.einsum("...d,de->...e", left, right, preferred_element_type=F32)


def matmul_t(left, right):
    return jnp.einsum("...e,de->...d", left, right, preferred_element_type=F32)


def outer(left, right):
    return jnp.einsum("rsd,rse->de", left, right, preferred_element_type=F32)


def glu_value(gate_part, up_part):
    return jax.nn.gelu(gate_part, approximate=True) * up_part


def geglu(inputs, gate_up, down, upstream_low):
    width = down.shape[0]
    both = matmul(inputs, gate_up)
    gate_part, up_part = both[..., :width], both[..., width:]
    hidden, pull_back = jax.vjp(glu_value, gate_part, up_part)
    gate_grad, up_grad = pull_back(matmul_t(upstream_low, down))
    return (hidden.astype(BF16), gate_grad.astype(BF16), up_grad.astype(BF16))


def routed_probs(query_heads, key_heads, query_seg, key_seg):
    scores = jnp.einsum("rqd,rkd->rqk", query_heads, key_heads, preferred_element_type=F32)
    scores = scores / math.sqrt(DH)
    allowed = query_seg[:, :, None] == key_seg[:, None, :]
    scores = jnp.where(allowed, scores, NEG_FILL)
    peak = jnp.maximum(jnp.max(scores, axis=-1, keepdims=True), 0.0)
    numer = jnp.exp(scores - peak)
    return numer / (jnp.exp(-peak) + jnp.sum(numer, axis=-1, keepdims=True))


def heavy_forward(query, keys, vals, query_seg, key_seg):
    def head(parts):
        query_h, key_h, val_h = parts
        probs = routed_probs(query_h, key_h, query_seg, key_seg).astype(BF16)
        return jnp.einsum("rqk,rkd->rqd", probs, val_h, preferred_element_type=F32).astype(BF16)

    return join_heads(jax.vmap(head)((split_heads(query), split_heads(keys), split_heads(vals))))


def heavy_both(query, keys, vals, query_seg, key_seg, mix_grad):
    def head(parts, query_seg=query_seg, key_seg=key_seg):
        query_h, key_h, val_h, grad_h = parts
        probs = routed_probs(query_h, key_h, query_seg, key_seg)
        probs_low = probs.astype(BF16)
        mix = jnp.einsum("rqk,rkd->rqd", probs_low, val_h, preferred_element_type=F32)
        prob_grad = jnp.einsum("rqd,rkd->rqk", grad_h, val_h, preferred_element_type=F32)
        delta = jnp.sum(probs * prob_grad, axis=-1, keepdims=True)
        score_grad = (probs * (prob_grad - delta)).astype(BF16)
        dquery = jnp.einsum("rqk,rkd->rqd", score_grad, key_h, preferred_element_type=F32)
        dkey = jnp.einsum("rqk,rqd->rkd", score_grad, query_h, preferred_element_type=F32)
        dval = jnp.einsum("rqk,rqd->rkd", probs_low, grad_h, preferred_element_type=F32)
        scale = 1.0 / math.sqrt(DH)
        return (mix.astype(BF16), (dquery * scale).astype(BF16), (dkey * scale).astype(BF16), dval.astype(BF16))

    heads = tuple(split_heads(v) for v in (query, keys, vals, mix_grad))
    if query.shape[1] <= 512:
        return tuple(join_heads(v) for v in jax.vmap(head)(heads))
    count, rows = heads[0].shape[:2]
    place = jnp.tile(jnp.arange(rows), count)
    parts = tuple(v.reshape(count * rows, 1, *v.shape[2:]) for v in heads)
    done = lax.map(lambda p: head(p[0], query_seg[p[1]][None], key_seg[p[1]][None]), (parts, place))
    return tuple(join_heads(v.reshape(count, rows, *v.shape[2:])) for v in done)


def split_heads(value):
    rows, tokens, width = value.shape
    return value.reshape(rows, tokens, width // DH, DH).transpose(2, 0, 1, 3)


def join_heads(value):
    heads, rows, tokens, width = value.shape
    return value.transpose(1, 2, 0, 3).reshape(rows, tokens, heads * width)


def tokens_of(blocks):
    devices, rows, count, width = blocks.shape
    return blocks.transpose(1, 0, 2, 3).reshape(rows, devices * count, width)


def with_segment(rows, segs):
    marks = jnp.broadcast_to((segs + 2).astype(BF16)[..., None], segs.shape + (LANES,))
    return jnp.concatenate([rows, marks], axis=-1)


def local_wide(
    tokens,
    segments,
    query_route,
    kv_route,
    ffn_route,
    grad_out,
    attn_gain,
    light_qkv,
    light_out,
    heavy_q,
    heavy_kv,
    heavy_out,
    route_query,
    ffn_gain,
    light_gate_up,
    light_down,
    heavy_gate_up,
    heavy_down,
    route_ffn,
):
    row_count, seg_span, width = tokens.shape
    light_heads = width // DL
    ffn_heavy = heavy_down.shape[0]
    devices = lax.axis_size("seq")
    me = lax.axis_index("seq")
    half_place = lax.axis_index("dp")
    anchor = me * seg_span
    routed_own = query_route.shape[1] // devices
    own_query = lax.dynamic_slice_in_dim(query_route, me * routed_own, routed_own, 1) - anchor
    own_key = lax.dynamic_slice_in_dim(kv_route, me * routed_own, routed_own, 1) - anchor
    own_ffn = ffn_route - anchor

    marked = with_segment(tokens, segments)
    before = shifted(marked[:, seg_span - RADIUS :], "seq", 1)
    after = shifted(marked[:, :RADIUS], "seq", -1)
    hidden = tokens.astype(F32)
    factor_one = rms_factor(hidden)
    normed = hidden * factor_one * attn_gain
    normed_low = normed.astype(BF16)
    key_rows = pick_rows(normed_low, own_key)
    key_payload = with_segment(key_rows, jnp.take_along_axis(segments, own_key, axis=1))
    key_blocks = tokens_of(gather_blocks(key_payload))
    key_all, key_seg = key_blocks[..., :width], key_blocks[..., width]

    extended = jnp.concatenate([before, marked, after], axis=1)
    seg_ext = extended[..., width]
    hidden_ext = extended[..., :width].astype(F32)
    factor_ext = rms_factor(hidden_ext)
    normed_ext_low = (hidden_ext * factor_ext * attn_gain).astype(BF16)
    extent = seg_span + 2 * RADIUS
    query_low = matmul(normed_low, light_qkv[:, :width]).astype(BF16)
    query_low = query_low.reshape(row_count, seg_span, light_heads, DL)
    kv_ext = matmul(normed_ext_low, light_qkv[:, width:]).astype(BF16)
    key_ext = kv_ext[..., :width].reshape(row_count, extent, light_heads, DL)
    val_ext = kv_ext[..., width:].reshape(row_count, extent, light_heads, DL)
    offset = jnp.arange(seg_span)[:, None] - jnp.arange(extent)[None, :] + RADIUS
    seg_own = seg_ext[:, RADIUS : RADIUS + seg_span]
    allowed = (jnp.abs(offset) <= RADIUS)[None] & (seg_own[:, :, None] == seg_ext[:, None, :])
    light_scale = 1.0 / math.sqrt(DL)
    scores = jnp.einsum("rqhd,rkhd->rhqk", query_low, key_ext, preferred_element_type=F32)
    scores = jnp.where(allowed[:, None], scores * light_scale, NEG_FILL)
    numerators = jnp.exp(scores - jnp.max(scores, axis=-1, keepdims=True))
    probs_light = numerators / jnp.sum(numerators, axis=-1, keepdims=True)
    probs_low = probs_light.astype(BF16)
    light_mix = jnp.einsum("rhqk,rkhd->rqhd", probs_low, val_ext, preferred_element_type=F32)
    light_mix = light_mix.reshape(row_count, seg_span, width).astype(BF16)
    light_attn = matmul(light_mix, light_out)

    query_rows = pick_rows(normed_low, own_query)
    query_seg_own = (jnp.take_along_axis(segments, own_query, axis=1) + 2).astype(BF16)
    heavy_query = matmul(query_rows, heavy_q).astype(BF16)
    keyval_all = matmul(key_all, heavy_kv).astype(BF16)
    heavy_width = heavy_q.shape[1]
    keys_all, vals_all = keyval_all[..., :heavy_width], keyval_all[..., heavy_width:]
    heavy_mix = heavy_forward(heavy_query, keys_all, vals_all, query_seg_own, key_seg)
    heavy_proj = matmul(heavy_mix, heavy_out)
    query_normed = pick_rows(normed, own_query)
    route_query_full = route_query.astype(F32)
    query_gate = jax.nn.sigmoid(jnp.sum(query_normed * route_query_full, axis=-1))
    heavy_attn = place_rows(query_gate[..., None] * heavy_proj, own_query, seg_span)

    middle = hidden + light_attn + heavy_attn
    factor_two = rms_factor(middle)
    normed_two = middle * factor_two * ffn_gain
    low_two = normed_two.astype(BF16)
    upstream = grad_out.astype(F32)
    ffn_normed = pick_rows(normed_two, own_ffn)
    ffn_rows = ffn_normed.astype(BF16)
    route_ffn_full = route_ffn.astype(F32)
    ffn_gate = jax.nn.sigmoid(jnp.sum(ffn_normed * route_ffn_full, axis=-1))
    ffn_upstream = pick_rows(upstream, own_ffn)
    ffn_low = (ffn_upstream * ffn_gate[..., None]).astype(BF16)
    routed_payload = with_segment(
        jnp.concatenate([ffn_rows, ffn_low, query_rows], axis=-1),
        jnp.take_along_axis(segments, own_query, axis=1),
    )
    routed_blocks = tokens_of(gather_blocks(routed_payload))
    ffn_all = routed_blocks[..., :width]
    ffn_low_all = routed_blocks[..., width : 2 * width]
    query_all = routed_blocks[..., 2 * width : 3 * width]
    query_seg = routed_blocks[..., 3 * width]

    hidden_light, gate_grad, up_grad = geglu(low_two, light_gate_up, light_down, grad_out)
    light_ff = matmul(hidden_light, light_down)
    light_both = jnp.concatenate([gate_grad, up_grad], axis=-1)
    normed_two_grad = matmul_t(light_both, light_gate_up)
    hidden_heavy, gate_grad_h, up_grad_h = geglu(ffn_rows, heavy_gate_up, heavy_down, ffn_low)
    heavy_ffn_proj = matmul(hidden_heavy, heavy_down)
    heavy_ff = place_rows(ffn_gate[..., None] * heavy_ffn_proj, own_ffn, seg_span)
    outputs = (middle + light_ff + heavy_ff).astype(BF16)
    ffn_gate_grad = jnp.sum(ffn_upstream * heavy_ffn_proj, axis=-1)
    ffn_logit_grad = ffn_gate_grad * ffn_gate * (1.0 - ffn_gate)
    route_ffn_grad = jnp.sum(ffn_logit_grad[..., None] * ffn_normed, axis=(0, 1))
    ffn_rows_grad = matmul_t(jnp.concatenate([gate_grad_h, up_grad_h], axis=-1), heavy_gate_up)
    ffn_rows_grad = ffn_rows_grad + ffn_logit_grad[..., None] * route_ffn_full
    normed_two_grad = normed_two_grad + place_rows(ffn_rows_grad, own_ffn, seg_span)
    ffn_gain_grad = jnp.sum(normed_two_grad * middle * factor_two, axis=(0, 1))
    middle_grad = upstream + norm_back(middle, factor_two, ffn_gain, normed_two_grad)
    middle_low = middle_grad.astype(BF16)

    valid_rows = (segments >= 0).astype(F32)[..., None]
    sums = jnp.stack(
        [
            jnp.sum(valid_rows * branch * branch)
            for branch in (hidden, light_attn, heavy_attn, light_ff, heavy_ff)
        ]
        + [jnp.sum(valid_rows)]
    )
    heavy_upstream = pick_rows(middle_grad, own_query)
    query_gate_grad = jnp.sum(heavy_upstream * heavy_proj, axis=-1)
    proj_low = (heavy_upstream * query_gate[..., None]).astype(BF16)
    sum_lanes = jnp.pad(jnp.concatenate(split_parts(sums)), (0, LANES - 18)).astype(BF16)
    sum_lanes = jnp.broadcast_to(sum_lanes, proj_low.shape[:2] + (LANES,))
    proj_blocks = gather_blocks(jnp.concatenate([proj_low, sum_lanes], axis=-1))
    sums_all = jnp.sum(proj_blocks[:, 0, 0, width : width + 18].astype(F32), axis=0)
    sums_all = jnp.sum(sums_all.reshape(3, 6), axis=0)
    sums_all = sums_all + swap(sums_all, "dp", 1)
    rms_stats = jnp.sqrt(sums_all[:5] / (sums_all[5] * width))
    proj_all = tokens_of(proj_blocks)[..., :width]

    flat = lambda v: v.reshape(-1, v.shape[-1])
    gate_up_grad = [
        jnp.dot(slot_columns(flat(low_two), me, devices).T, flat(part), preferred_element_type=F32)
        for part in own_half_first(light_both, half_place)
    ]
    hidden_slots = slot_columns(flat(hidden_light), me, devices).T
    down_grad = [
        jnp.dot(hidden_slots, flat(part), preferred_element_type=F32)
        for part in own_half_first(grad_out, half_place)
    ]
    mix_slots = slot_columns(flat(light_mix), me, devices).T
    out_grad = [
        jnp.dot(mix_slots, flat(part), preferred_element_type=F32)
        for part in own_half_first(middle_low, half_place)
    ]
    first_sum = scatter_sum(
        jnp.concatenate(
            [
                slot_block(gate_up_grad, devices),
                slot_block(down_grad, devices),
                slot_block(out_grad, devices),
                slot_vectors((ffn_gain_grad, route_ffn_grad), me, devices),
            ],
            axis=2,
        )
    )
    block = width // devices
    block_ff = light_down.shape[0] // devices
    cuts = [0]
    for rows in (
        block * light_gate_up.shape[1] // 2 // LANES,
        block_ff * width // 2 // LANES,
        block * width // 2 // LANES,
        block,
    ):
        cuts.append(cuts[-1] + rows)
    light_gate_up_grad = unslot(first_sum[cuts[0] : cuts[1]], light_gate_up.shape[1] // 2)
    light_down_grad = unslot(first_sum[cuts[1] : cuts[2]], width // 2)
    light_out_grad = unslot(first_sum[cuts[2] : cuts[3]], width // 2)
    ffn_gain_grad = first_sum[cuts[3] : cuts[4], 0]
    route_ffn_grad = first_sum[cuts[3] : cuts[4], 1]

    group = min(4, devices)
    low_place, high_place = me % group, me // group
    groups = devices // group
    unit = ffn_heavy // devices
    gate_up_parts = heavy_gate_up.reshape(width, 2, groups, group, unit)
    gate_up_mine = lax.dynamic_index_in_dim(gate_up_parts, low_place, 3, False)
    down_mine = lax.dynamic_index_in_dim(
        heavy_down.reshape(groups, group, unit, width), low_place, 1, False
    )
    x_all = flat(ffn_all)
    up_all = flat(ffn_low_all)
    hidden_mine, gate_mine, up_mine = geglu(
        x_all,
        gate_up_mine.reshape(width, -1),
        down_mine.reshape(-1, width),
        up_all,
    )
    hidden_block = lax.dynamic_slice_in_dim(hidden_mine, high_place * unit, unit, 1)
    heavy_down_half = [
        jnp.dot(hidden_block.T, part, preferred_element_type=F32)
        for part in own_half_first(up_all, half_place)
    ]
    heavy_down_grad = heavy_down_half[0] + swap(heavy_down_half[1].astype(BF16), "dp", 1).astype(F32)
    x_group = lax.dynamic_slice_in_dim(x_all, high_place * group * block, group * block, 1)
    x_group = x_group.reshape(-1, group, block)
    x_group = jnp.take(x_group, jnp.arange(group) ^ low_place, axis=1).reshape(-1, group * block)
    gate_half, up_half = (
        jnp.dot(x_group.T, part, preferred_element_type=F32) for part in (gate_mine, up_mine)
    )
    kept = jnp.where(half_place == 0, gate_half, up_half)
    sent = jnp.where(half_place == 0, up_half, gate_half)
    kept = (kept + swap(sent.astype(BF16), "dp", 1).astype(F32)).reshape(group, block, groups, unit)
    pieces = [kept[0]]
    for place in range(1, group):
        pieces.append(swap(kept[place].astype(BF16), "seq", place).astype(F32))
    pieces = jnp.take(jnp.stack(pieces, axis=2), jnp.arange(group) ^ low_place, axis=2)
    heavy_gate_up_grad = pieces.reshape(block, ffn_heavy)

    mix_grad = matmul_t(middle_low, light_out).astype(BF16)
    mix_grad = mix_grad.reshape(row_count, seg_span, light_heads, DL)
    val_grad = jnp.einsum("rhqk,rqhd->rkhd", probs_low, mix_grad, preferred_element_type=F32)
    prob_grad = jnp.einsum("rqhd,rkhd->rhqk", mix_grad, val_ext, preferred_element_type=F32)
    delta = jnp.sum(probs_light * prob_grad, axis=-1, keepdims=True)
    score_grad = (probs_light * (prob_grad - delta)).astype(BF16)
    query_grad = jnp.einsum("rhqk,rkhd->rqhd", score_grad, key_ext, preferred_element_type=F32)
    key_grad = jnp.einsum("rhqk,rqhd->rkhd", score_grad, query_low, preferred_element_type=F32)
    query_grad = (query_grad * light_scale).reshape(row_count, seg_span, width).astype(BF16)
    kv_grad = jnp.concatenate(
        [
            (key_grad * light_scale).reshape(row_count, extent, width),
            val_grad.reshape(row_count, extent, width),
        ],
        axis=-1,
    ).astype(BF16)
    normed_grad_ext = matmul_t(kv_grad, light_qkv[:, width:])
    normed_grad = matmul_t(query_grad, light_qkv[:, :width])
    normed_grad = normed_grad + normed_grad_ext[:, RADIUS : RADIUS + seg_span]
    from_right = shifted(normed_grad_ext[:, :RADIUS].astype(BF16), "seq", -1)
    from_left = shifted(normed_grad_ext[:, seg_span + RADIUS :].astype(BF16), "seq", 1)
    normed_grad = normed_grad.at[:, :RADIUS].add(from_left.astype(F32))
    normed_grad = normed_grad.at[:, seg_span - RADIUS :].add(from_right.astype(F32))

    hq_all = matmul(query_all, heavy_q).astype(BF16)
    do2_all = matmul_t(proj_all, heavy_out).astype(BF16)
    mix_all, dhq_all, dhk_all, dhv_all = heavy_both(
        hq_all, keys_all, vals_all, query_seg, key_seg, do2_all
    )
    dhkv_all = jnp.concatenate([dhk_all, dhv_all], axis=-1)
    mine = lambda v: lax.dynamic_slice_in_dim(flat(v), me * block, block, 1).T
    heavy_grads = [
        own_half_first(jnp.dot(mine(left), flat(right), preferred_element_type=F32), half_place)
        for left, right in ((query_all, dhq_all), (key_all, dhkv_all), (mix_all, proj_all))
    ]
    heavy_kept = jnp.concatenate([pair[0] for pair in heavy_grads], axis=-1)
    heavy_sent = jnp.concatenate([pair[1] for pair in heavy_grads], axis=-1)
    heavy_sum = heavy_kept + swap(heavy_sent.astype(BF16), "dp", 1).astype(F32)
    heavy_half = heavy_width // 2
    heavy_q_grad = heavy_sum[:, :heavy_half]
    heavy_kv_grad = heavy_sum[:, heavy_half : 3 * heavy_half]
    heavy_out_grad = heavy_sum[:, 3 * heavy_half :]
    query_logit_grad = query_gate_grad * query_gate * (1.0 - query_gate)
    route_query_grad = jnp.sum(query_logit_grad[..., None] * query_normed, axis=(0, 1))
    query_rows_grad = (
        matmul_t(dhq_all[:, :routed_own], heavy_q) + query_logit_grad[..., None] * route_query_full
    )
    key_rows_grad = matmul_t(dhkv_all[:, :routed_own], heavy_kv)
    normed_grad = (
        normed_grad
        + place_rows(query_rows_grad, own_query, seg_span)
        + place_rows(key_rows_grad, own_key, seg_span)
    )
    attn_gain_grad = jnp.sum(normed_grad * hidden * factor_one, axis=(0, 1))
    hidden_norm_grad = norm_back(hidden, factor_one, attn_gain, normed_grad)
    grad_tokens = (middle_grad + hidden_norm_grad).astype(BF16)

    own_slots = slot_columns(flat(normed_low), me, devices).T
    ext_slots = slot_columns(flat(normed_ext_low), me, devices).T
    qkv_grad = jnp.concatenate(
        [
            jnp.dot(own_slots, flat(query_grad), preferred_element_type=F32),
            jnp.dot(ext_slots, flat(kv_grad), preferred_element_type=F32),
        ],
        axis=-1,
    )
    second_sum = scatter_sum(
        jnp.concatenate(
            [
                slot_block(own_half_first(qkv_grad, half_place), devices),
                slot_vectors((attn_gain_grad, route_query_grad), me, devices),
            ],
            axis=2,
        )
    )
    qkv_cols = light_qkv.shape[1] // 2
    qkv_rows = block * qkv_cols // LANES
    light_qkv_grad = unslot(second_sum[:qkv_rows], qkv_cols)
    attn_gain_grad = second_sum[qkv_rows:, 0]
    route_query_grad = second_sum[qkv_rows:, 1]
    return (
        outputs,
        grad_tokens,
        attn_gain_grad,
        light_qkv_grad,
        light_out_grad,
        heavy_q_grad,
        heavy_kv_grad,
        heavy_out_grad,
        route_query_grad,
        ffn_gain_grad,
        light_gate_up_grad,
        light_down_grad,
        heavy_gate_up_grad,
        heavy_down_grad,
        route_ffn_grad,
        rms_stats,
    )


VMEM = pl.BlockSpec(memory_space=pltpu.VMEM)
SMEM = pl.BlockSpec(memory_space=pltpu.SMEM)
ANY = pl.BlockSpec(memory_space=pl.ANY)
HBM = pl.BlockSpec(memory_space=pltpu.HBM)
GELU_RATE = math.sqrt(2.0 / math.pi)
GELU_CUBE = 0.044715
MIB = 1024 * 1024
FIRST_CUTS = 4
SECOND_CUTS = 2


def shape(dims, dtype):
    return jax.ShapeDtypeStruct(dims, dtype)


def call(kernel, outs, ins, smem=0, scratch=(), micros=1, mib=16, after=(), hbm=0):
    used = len(ins)

    def body(*refs):
        kernel(*refs[:used], *refs[used + len(after) :])

    return pl.pallas_call(
        body,
        out_shape=outs,
        in_specs=[HBM] * hbm + [SMEM] * smem + [VMEM] * (used - smem - hbm) + [ANY] * len(after),
        out_specs=[VMEM] * len(outs),
        scratch_shapes=list(scratch),
        compiler_params=pltpu.CompilerParams(vmem_limit_bytes=mib * MIB),
        cost_estimate=cost(micros),
    )(*ins, *after)


def cost(micros):
    return pl.CostEstimate(flops=int(micros * 10**9), bytes_accessed=10**6, transcendentals=0)


def dot(left, right):
    return jnp.dot(left, right, preferred_element_type=F32)


def dot_t(left, right):
    return lax.dot_general(left, right, (((1,), (1,)), ((), ())), preferred_element_type=F32)


def t_dot(left, right):
    return lax.dot_general(left, right, (((0,), (0,)), ((), ())), preferred_element_type=F32)


def row_factor(value):
    return lax.rsqrt(jnp.mean(value * value, axis=-1, keepdims=True) + EPSILON)


def as_column(row):
    count = row.shape[1]
    down = lax.broadcasted_iota(jnp.int32, (count, count), 0)
    along = lax.broadcasted_iota(jnp.int32, (count, count), 1)
    return jnp.sum(jnp.where(down == along, row, 0.0), axis=1, keepdims=True)


def head_window(head, size):
    first = head * size // LANES * LANES
    lanes = (head * size + size - 1) // LANES * LANES + LANES - first
    place = lax.broadcasted_iota(jnp.int32, (1, lanes), 1) + first
    return first, lanes, (place >= head * size) & (place < head * size + size)


def slot_owners(me, bits):
    owners = []
    for p in range(1 << len(bits)):
        flips = sum(bit for k, bit in enumerate(bits) if p >> (len(bits) - 1 - k) & 1)
        owners.append(flips ^ me)
    return owners


def slot_select(width, bits, me):
    block = width >> len(bits)
    along = lax.broadcasted_iota(jnp.int32, (block, width), 1)
    inside = lax.broadcasted_iota(jnp.int32, (block, width), 0)
    rows = [(along == inside + owner * block).astype(F32) for owner in slot_owners(me, bits)]
    return jnp.concatenate(rows, axis=0).astype(BF16)


def two_gelu(value):
    square = value * value
    bend = jnp.tanh(GELU_RATE * value * (1.0 + GELU_CUBE * square))
    half = 0.5 * (1.0 + bend)
    slope = half + 0.5 * value * (1.0 - bend * bend) * GELU_RATE * (1.0 + 3.0 * GELU_CUBE * square)
    return value * half, slope


def first_kernel(
    routed, route_in, segs_in, tokens_in, gain_in, ffn_gain_in, route_q_in, route_f_in,
    keys, upper, lower, table,
    route, seg_at, segs, tokens, gain, ffn_gain, route_q, route_f, normed, picked, sems,
):
    copies = [
        pltpu.make_async_copy(source, target, sems.at[k])
        for k, (source, target) in enumerate(
            (
                (tokens_in, tokens),
                (gain_in, gain),
                (route_in, route),
                (segs_in, seg_at),
                (segs_in, segs),
                (ffn_gain_in, ffn_gain),
                (route_q_in, route_q),
                (route_f_in, route_f),
            )
        )
    ]
    for copy in copies:
        copy.start()
    for copy in copies:
        copy.wait()
    rows, span, width = tokens.shape
    me = lax.axis_index("seq")
    for k, vector in enumerate((gain, ffn_gain, route_q, route_f)):
        table[k : k + 1, :] = vector[...].astype(F32).reshape(1, width)
    hidden = tokens[...].reshape(rows * span, width).astype(F32)
    normed[...] = hidden * row_factor(hidden) * table[0:1, :]
    for r in range(rows):
        for k in range(routed):
            place = route[r, me * routed + k] - me * span
            at = pl.ds(r * routed + k, 1)
            picked[at, :width] = normed[pl.ds(r * span + place, 1), :]
            picked[at, width:] = jnp.full((1, LANES), (seg_at[r, place] + 2).astype(F32))
    keys[...] = picked[...].astype(BF16).reshape(keys.shape)
    marks = (segs[...] + 2).astype(F32)
    for out, start in ((upper, span - RADIUS), (lower, 0)):
        out[:, :RADIUS, :] = tokens[:, start : start + RADIUS, :]
        out[:, RADIUS:, :] = jnp.zeros((rows, 16, width), BF16)
        for r in range(rows):
            out[r, RADIUS:, :span] = jnp.broadcast_to(marks[r : r + 1], (16, span)).astype(BF16)


def light_kernel(
    before, tokens, after, segs, table, w_qkv, w_out,
    normed, query, keyval, probs, mix, attn, seg_row, mix_t,
):
    rows, span, width = tokens.shape
    extent = span + 2 * RADIUS
    own_all = rows * span
    heads = width // DL
    places = []
    for r in range(rows):
        places.append((tokens, r, span, r * span, r * extent + RADIUS))
    for r in range(rows):
        rim = own_all + 2 * r * RADIUS
        places.append((before, r, RADIUS, rim, r * extent))
        places.append((after, r, RADIUS, rim + RADIUS, r * extent + RADIUS + span))
    for part, r, size, at, _ in places:
        value = part[r, :size, :].astype(F32)
        normed[at : at + size, :] = (value * row_factor(value) * table[0:1, :]).astype(BF16)
    made = dot(normed[...], w_qkv[:, width:]).astype(BF16)
    for _, _, size, at, to in places:
        keyval[to : to + size, :] = made[at : at + size]
    query[...] = dot(normed[:own_all, :], w_qkv[:, :width]).astype(BF16)
    down = lax.broadcasted_iota(jnp.int32, (extent, span), 0)
    along = lax.broadcasted_iota(jnp.int32, (extent, span), 1)
    near = jnp.abs(along - down + RADIUS) <= RADIUS
    for r in range(rows):
        marks = (segs[r : r + 1, :] + 2).astype(F32)
        seg_row[:, :span] = before[r, RADIUS:, :span].astype(F32)[:8]
        seg_row[:, span : 2 * span] = jnp.broadcast_to(marks, (8, span))
        seg_row[:, 2 * span :] = after[r, RADIUS:, :span].astype(F32)[:8]
        columns = [as_column(seg_row[0:1, c * span : (c + 1) * span]) for c in range(3)]
        key_marks = jnp.concatenate([columns[0][span - RADIUS :], columns[1], columns[2][:RADIUS]], axis=0)
        allowed = near & (key_marks == marks)
        key_rows = slice(r * extent, (r + 1) * extent)
        val_t = keyval[key_rows, width:].T
        for h in range(heads):
            first, lanes, mask = head_window(h, DL)
            window = slice(first, first + lanes)
            q_head = jnp.where(mask, query[r * span : (r + 1) * span, window], 0)
            scores = dot_t(keyval[key_rows, window], q_head)
            scores = jnp.where(allowed, scores * (1.0 / math.sqrt(DL)), NEG_FILL)
            numer = jnp.exp(scores - jnp.max(scores, axis=0, keepdims=True))
            share = (numer / jnp.sum(numer, axis=0, keepdims=True)).astype(BF16)
            probs[r * heads + h] = share
            mix_t[h * DL : (h + 1) * DL, :] = dot(val_t[h * DL : (h + 1) * DL, :], share)
        mix[r * span : (r + 1) * span, :] = mix_t[...].T.astype(BF16)
    attn[...] = dot(mix[...], w_out[...])


def stat_row(value):
    total = jnp.sum(jnp.sum(value, axis=0, keepdims=True), axis=1, keepdims=True)
    return jnp.broadcast_to(total, (1, LANES))


def valid_column(segs):
    rows = segs.shape[0]
    parts = [as_column((segs[r : r + 1, :] >= 0).astype(F32)) for r in range(rows)]
    return jnp.concatenate(parts, axis=0)


def router(rows, weights):
    return jax.nn.sigmoid(jnp.sum(rows[...] * weights, axis=-1, keepdims=True))


def gathered(refs, row, lanes):
    value = jnp.concatenate([ref[:, row, :, lanes] for ref in refs], axis=0)
    return value.reshape(-1, value.shape[-1])


def middle_kernel(routed, parts, q_route, f_route, seg_at, tokens, segs, *refs):
    keys, refs = refs[:parts], refs[parts:]
    attn, upstream, table, w_q, w_kv, w_out = refs[:6]
    middle, normed_two, keyval, payload, q_rows, f_rows, f_up, proj, f_marks, stats = refs[6:16]
    full, marks, placed = refs[16:]
    rows, span, width = tokens.shape
    me = lax.axis_index("seq")
    hidden = tokens[...].reshape(rows * span, width).astype(F32)
    full[...] = hidden * row_factor(hidden) * table[0:1, :]
    for r in range(rows):
        for k in range(routed):
            at = pl.ds(r * routed + k, 1)
            place = q_route[r, me * routed + k] - me * span
            q_rows[at, :] = full[pl.ds(r * span + place, 1), :]
            marks[at, :] = jnp.full((1, LANES), (seg_at[r, place] + 2).astype(F32))
            place = f_route[r, k] - me * span
            f_marks[at, :] = jnp.full((1, LANES), (seg_at[r, place] + 2).astype(F32))
    q_low = q_rows[...].astype(BF16)
    payload[:, :, 2 * width : 3 * width] = q_low.reshape(rows, routed, width)
    payload[:, :, 3 * width :] = marks[...].astype(BF16).reshape(rows, routed, LANES)
    key_low = jnp.concatenate([gathered(keys, r, slice(0, width)) for r in range(rows)], axis=0)
    keyval[...] = dot(key_low, w_kv[...]).astype(BF16).reshape(keyval.shape)
    query = dot(q_low, w_q[...]).astype(BF16)
    heads = width // DH
    lane = lax.broadcasted_iota(jnp.int32, (1, width), 1)
    masks = [(lane >= h * DH) & (lane < (h + 1) * DH) for h in range(heads)]
    mixed = []
    for r in range(rows):
        mine = query[r * routed : (r + 1) * routed]
        wide = jnp.concatenate([jnp.where(m, mine, 0) for m in masks], axis=0)
        scores = dot_t(wide, keyval[r, :, :width]) * (1.0 / math.sqrt(DH))
        key_marks = gathered(keys, r, slice(width, width + LANES)).astype(F32).T[0:1, :]
        query_marks = jnp.concatenate([marks[r * routed : (r + 1) * routed, 0:1]] * heads, axis=0)
        scores = jnp.where(query_marks == key_marks, scores, NEG_FILL)
        peak = jnp.maximum(jnp.max(scores, axis=-1, keepdims=True), 0.0)
        numer = jnp.exp(scores - peak)
        share = numer / (jnp.exp(-peak) + jnp.sum(numer, axis=-1, keepdims=True))
        part = dot(share.astype(BF16), keyval[r, :, width:])
        total = jnp.zeros((routed, width), F32)
        for h in range(heads):
            total = total + jnp.where(masks[h], part[h * routed : (h + 1) * routed], 0.0)
        mixed.append(total)
    mixed = jnp.concatenate(mixed, axis=0).astype(BF16)
    proj[...] = dot(mixed, w_out[...])
    placed[...] = router(q_rows, table[2:3, :]) * proj[...]
    light = attn[...]
    middle[...] = hidden + light
    for r in range(rows):
        for k in range(routed):
            place = q_route[r, me * routed + k] - me * span
            at = pl.ds(r * span + place, 1)
            middle[at, :] = middle[at, :] + placed[pl.ds(r * routed + k, 1), :]
    valid = valid_column(segs)
    stats[...] = jnp.zeros(stats.shape, F32)
    stats[0:1, :] = stat_row(valid * hidden * hidden)
    stats[1:2, :] = stat_row(valid * light * light)
    stats[2:3, :] = stat_row(jnp.where(marks[:, 0:1] >= 2.0, placed[...] * placed[...], 0.0))
    stats[5:6, :] = stat_row(valid)
    mid = middle[...]
    full[...] = mid * row_factor(mid) * table[1:2, :]
    normed_two[...] = full[...].astype(BF16)
    for r in range(rows):
        for k in range(routed):
            place = f_route[r, k] - me * span
            f_rows[pl.ds(r * routed + k, 1), :] = full[pl.ds(r * span + place, 1), :]
    full[...] = upstream[...].reshape(rows * span, width).astype(F32)
    for r in range(rows):
        for k in range(routed):
            place = f_route[r, k] - me * span
            f_up[pl.ds(r * routed + k, 1), :] = full[pl.ds(r * span + place, 1), :]
    f_low = (router(f_rows, table[3:4, :]) * f_up[...]).astype(BF16)
    payload[:, :, :width] = f_rows[...].astype(BF16).reshape(rows, routed, width)
    payload[:, :, width : 2 * width] = f_low.reshape(rows, routed, width)


def glu_parts(inputs, back_in, gate_w, up_w, down_w):
    act, slope = two_gelu(dot(inputs, gate_w))
    lift = dot(inputs, up_w)
    back = dot_t(back_in, down_w)
    hidden = (act * lift).astype(BF16)
    return hidden, (back * lift * slope).astype(BF16), (back * act).astype(BF16)


def three_parts(value):
    high = value.astype(BF16).astype(F32)
    middle = (value - high).astype(BF16).astype(F32)
    return high, middle, value - high - middle


def light_ffn_kernel(normed_two, upstream, w_gate_up, w_down, z_light, d_light, hidden_out, grad_gate, grad_up):
    width = normed_two.shape[1]
    inner = w_down.shape[0]
    back_in = upstream[...].reshape(-1, width)
    unit = 256
    for at in range(0, inner, unit):
        part = slice(at, at + unit)
        gate_w, up_w = w_gate_up[:, part], w_gate_up[:, inner + at : inner + at + unit]
        hidden, d_gate, d_up = glu_parts(normed_two[...], back_in, gate_w, up_w, w_down[part, :])
        hidden_out[:, part] = hidden
        grad_gate[:, part] = d_gate
        grad_up[:, part] = d_up
    z_light[...] = dot(hidden_out[...], w_down[...])
    d_light[...] = dot_t(grad_gate[...], w_gate_up[:, :inner]) + dot_t(grad_up[...], w_gate_up[:, inner:])


def pass_share(step_refs, share_refs, me, group):
    gate, up, down = step_refs
    gate_out, up_out, down_out = share_refs
    unit = gate_out.shape[2]
    at = pl.ds(pl.multiple_of(lax.rem(me, group) * unit, unit), unit)
    gate_out[0] = gate[:, at]
    up_out[0] = up[:, at]
    down_out[0] = down[at, :]


def heavy_steps(step, sums_in, h_gate, h_up, h_down, f_rows, f_up, table, z_heavy, d_heavy):
    @pl.when(step == 0)
    def _():
        for total, value in zip((z_heavy, d_heavy), sums_in):
            total[...] = value

    f_gate = router(f_rows, table[3:4, :])
    f_low = (f_gate * f_up[...]).astype(BF16)
    f_in = f_rows[...].astype(BF16)
    hidden, d_gate, d_up = glu_parts(f_in, f_low, h_gate[...], h_up[...], h_down[...])
    z_heavy[...] += dot(hidden, h_down[...])
    d_heavy[...] += dot_t(d_gate, h_gate[...]) + dot_t(d_up, h_up[...])
    return f_gate


def ffn_first_kernel(
    group, h_gate, h_up, h_down, f_rows, f_up, table, z_heavy, d_heavy, gate_out, up_out, down_out
):
    zero = jnp.zeros(z_heavy.shape, F32)
    heavy_steps(pl.program_id(0), (zero, zero), h_gate, h_up, h_down, f_rows, f_up, table, z_heavy, d_heavy)
    pass_share((h_gate, h_up, h_down), (gate_out, up_out, down_out), lax.axis_index("seq"), group)


def ffn_last_kernel(
    routed, group, q_route, f_route, h_gate, h_up, h_down, z_in, d_in, upstream, middle, z_light, d_light_in,
    q_rows, f_rows, f_up, proj, f_marks, table, stats, segs,
    outputs, dmid, dmid_low, payload, vectors, gate_out, up_out, down_out,
    z_heavy, d_heavy, placed, full, d_light,
):
    step = pl.program_id(0)
    width = middle.shape[1]
    rows, span = segs.shape
    me = lax.axis_index("seq")
    f_gate = heavy_steps(
        step, (z_in[...], d_in[...]), h_gate, h_up, h_down, f_rows, f_up, table, z_heavy, d_heavy
    )
    pass_share((h_gate, h_up, h_down), (gate_out, up_out, down_out), me, group)

    @pl.when(step == pl.num_programs(0) - 1)
    def _():
        mid = middle[...]
        d_light[...] = d_light_in[...]
        placed[...] = f_gate * z_heavy[...]
        full[...] = mid + z_light[...]
        logit = jnp.sum(f_up[...] * z_heavy[...], axis=-1, keepdims=True) * f_gate * (1.0 - f_gate)
        d_heavy[...] += logit * table[3:4, :]
        for r in range(rows):
            for k in range(routed):
                place = f_route[r, k] - me * span
                at, source = pl.ds(r * span + place, 1), pl.ds(r * routed + k, 1)
                full[at, :] = full[at, :] + placed[source, :]
                d_light[at, :] = d_light[at, :] + d_heavy[source, :]
        outputs[...] = full[...].astype(BF16).reshape(outputs.shape)
        factor = row_factor(mid)
        d_norm = d_light[...]
        vectors[...] = jnp.zeros(vectors.shape, F32)
        vectors[0:1, :] = jnp.sum(d_norm * mid * factor, axis=0, keepdims=True)
        vectors[1:2, :] = jnp.sum(logit * f_rows[...], axis=0, keepdims=True)
        weighted = d_norm * table[1:2, :]
        inner = jnp.mean(weighted * mid, axis=-1, keepdims=True)
        total = upstream[...].reshape(rows * span, width).astype(F32) + factor * weighted - mid * (factor * factor * factor) * inner
        dmid[...] = total
        dmid_low[...] = total.astype(BF16)
        sums = stats[...]
        place = lax.broadcasted_iota(jnp.int32, sums.shape, 0)
        lane = lax.broadcasted_iota(jnp.int32, sums.shape, 1)
        light_sum = stat_row(valid_column(segs) * z_light[...] * z_light[...])
        heavy_sum = stat_row(jnp.where(f_marks[:, 0:1] >= 2.0, placed[...] * placed[...], 0.0))
        sums = jnp.where(place == 3, light_sum, jnp.where(place == 4, heavy_sum, sums))
        lanes = jnp.zeros(sums.shape, F32)
        for k, part in enumerate(three_parts(sums)):
            lanes = lanes + jnp.where(lane == place + 8 * k, part, 0.0)
        lanes = jnp.sum(lanes, axis=0, keepdims=True)
        full[...] = total
        for r in range(rows):
            for k in range(routed):
                place = q_route[r, me * routed + k] - me * span
                placed[pl.ds(r * routed + k, 1), :] = full[pl.ds(r * span + place, 1), :]
        q_gate = router(q_rows, table[2:3, :])
        logit = jnp.sum(placed[...] * proj[...], axis=-1, keepdims=True) * q_gate * (1.0 - q_gate)
        payload[:, :, :width] = (q_gate * placed[...]).astype(BF16).reshape(rows, routed, width)
        lane = lax.broadcasted_iota(jnp.int32, (rows * routed, LANES), 1)
        extra = jnp.broadcast_to(lanes, (rows * routed, LANES))
        for k, part in enumerate(three_parts(logit)):
            extra = jnp.where(lane == 24 + k, part, extra)
        payload[:, :, width:] = extra.astype(BF16).reshape(rows, routed, LANES)


def halves_of(value, place):
    half = value.shape[-1] // 2
    first, second = value[..., :half], value[..., half:]
    return jnp.where(place == 0, first, second), jnp.where(place == 0, second, first)


def store_slots(outs, place, base, grads):
    each = outs[0].shape[0]
    block = grads.shape[0] // (each * len(outs))
    low = grads.astype(BF16)
    for c in range(grads.shape[1] // LANES):
        for p in range(each * len(outs)):
            part = low[p * block : (p + 1) * block, c * LANES : (c + 1) * LANES]
            outs[p // each][p % each, place, pl.ds(base + c * block, block), :] = part
    return base + grads.shape[1] // LANES * block


def slot_vector_block(select, vectors):
    table = jnp.concatenate([vectors, jnp.zeros((LANES - vectors.shape[0], vectors.shape[1]), F32)], axis=0)
    return dot_t(select, table.astype(BF16))


def loop_slots(outs, base, left, right, lanes, half_of):
    block = left.shape[0] // (outs[0].shape[0] * len(outs))

    def chunk(i, carry):
        grads = dot(left[...], right[:, pl.ds(pl.multiple_of(i * lanes, lanes), lanes)])
        half, at = half_of(i)
        store_slots(outs, half, pl.multiple_of(base + at * (block * lanes // LANES), 16), grads)
        return carry

    lax.fori_loop(0, right.shape[1] // lanes, chunk, 0)


def first_grads_kernel(bits, normed_two, grad_gate, grad_up, hidden, upstream, *refs):
    outs, (inputs_t, hidden_t, back_in) = refs[:-3], refs[-3:]
    width = normed_two.shape[1]
    me = lax.axis_index("seq")
    place = lax.axis_index("dp")
    inputs_t[...] = dot_t(slot_select(width, bits, me), normed_two[...]).astype(BF16)
    loop_slots(outs, 0, inputs_t, grad_gate, 256, lambda i: (place, i))
    loop_slots(outs, 0, inputs_t, grad_up, 256, lambda i: (1 - place, i))
    hidden_t[...] = dot_t(slot_select(hidden.shape[1], bits, me), hidden[...]).astype(BF16)
    back_in[...] = upstream[...].reshape(-1, width)
    base = grad_gate.shape[1] // LANES * (width >> len(bits))
    loop_slots(outs, base, hidden_t, back_in, width // 2, lambda i: (i ^ place, 0))


def light_back_kernel(
    bits, dmid_low, query, keyval, probs, normed, mix, vectors, table, w_qkv, w_out,
    dnorm, to_right, to_left, *refs,
):
    outs, (dq, dkv, d_row, dq_t, select, inputs_t) = refs[:-6], refs[-6:]
    rows, rim, width = to_right.shape
    span = dmid_low.shape[0] // rows
    extent = span + 2 * rim
    own_all = rows * span
    heads = width // DL
    scale = 1.0 / math.sqrt(DL)
    place = lax.axis_index("dp")
    mix_grad = dot_t(dmid_low[...], w_out[...]).astype(BF16)
    for r in range(rows):
        key_rows = slice(r * extent, (r + 1) * extent)
        own_rows = slice(r * span, (r + 1) * span)
        key_t = keyval[key_rows, :width].T
        d_row[...] = jnp.zeros(d_row.shape, F32)
        for h in range(heads):
            first, lanes, mask = head_window(h, DL)
            window = slice(first, first + lanes)
            v_window = slice(width + first, width + first + lanes)
            q_head = jnp.where(mask, query[own_rows, window], 0)
            g_head = jnp.where(mask, mix_grad[own_rows, window], 0)
            share = probs[r * heads + h]
            full_share = share.astype(F32)
            prob_grad = dot_t(keyval[key_rows, v_window], g_head)
            delta = jnp.sum(full_share * prob_grad, axis=0, keepdims=True)
            score_grad = (full_share * (prob_grad - delta)).astype(BF16)
            d_row[:, window] += dot(score_grad, q_head)
            d_row[:, v_window] += dot(share, g_head)
            dq_t[h * DL : (h + 1) * DL, :] = dot(key_t[h * DL : (h + 1) * DL, :], score_grad)
        dq[own_rows, :] = (dq_t[...].T * scale).astype(BF16)
        rim_at = own_all + 2 * r * rim
        for size, at, to in ((span, rim, r * span), (rim, 0, rim_at), (rim, rim + span, rim_at + rim)):
            dkv[to : to + size, :width] = (d_row[at : at + size, :width] * scale).astype(BF16)
            dkv[to : to + size, width:] = d_row[at : at + size, width:].astype(BF16)
    d_rim = dot_t(dkv[own_all:, :], w_qkv[:, width:])
    dnorm[...] = dot_t(dq[...], w_qkv[:, :width]) + dot_t(dkv[:own_all, :], w_qkv[:, width:])
    gain_grad = jnp.sum(dnorm[...] * normed[:own_all, :].astype(F32), axis=0, keepdims=True)
    gain_grad = gain_grad + jnp.sum(d_rim * normed[own_all:, :].astype(F32), axis=0, keepdims=True)
    gain_grad = gain_grad / table[0:1, :]
    for r in range(rows):
        to_left[r] = d_rim[2 * r * rim : (2 * r + 1) * rim].astype(BF16)
        to_right[r] = d_rim[(2 * r + 1) * rim : (2 * r + 2) * rim].astype(BF16)
    half = width // 2
    select[...] = slot_select(width, bits, lax.axis_index("seq"))
    inputs_t[...] = dot_t(select[...], normed[...]).astype(BF16)
    base = store_slots(outs, place, 0, dot(inputs_t[:, :own_all], dq[...]))
    grads = dot(inputs_t[...], dkv[:, :width])
    base = store_slots(outs, place, base, grads[:, :half])
    base_two = store_slots(outs, 1 - place, 0, grads[:, half:])
    store_slots(outs, 1 - place, base_two, dot(inputs_t[...], dkv[:, width:]))
    grads = dot(dot_t(select[...], mix[...]).astype(BF16), dmid_low[...])
    base_two = store_slots(outs, place, base, grads[:, :half])
    store_slots(outs, 1 - place, base, grads[:, half:])
    line = lax.broadcasted_iota(jnp.int32, (8, width), 0)
    block = slot_vector_block(select[...], jnp.where(line == 2, gain_grad, vectors[...]))
    for which in range(2):
        base = store_slots(outs, which, base_two, block)
    for out in outs:
        out[:, :, base:, :] = jnp.zeros((out.shape[0], 2, out.shape[2] - base, LANES), BF16)


def heavy_ffn_kernel(parts, *refs):
    blocks, weights, (kept, sent) = refs[:parts], refs[parts:-2], refs[-2:]
    halves = [weights[k : k + 3] for k in range(0, len(weights), 3)]
    each, width, unit = halves[0][0].shape
    devices = lax.axis_size("seq")
    group = devices // (each * len(halves))
    me = lax.axis_index("seq")
    place = lax.axis_index("dp")
    low_place = lax.rem(me, group)
    high_place = lax.div(me, group)
    rows = range(blocks[0].shape[1])
    inputs = jnp.concatenate([gathered(blocks, r, slice(0, width)) for r in rows], axis=0)
    back_in = jnp.concatenate([gathered(blocks, r, slice(width, 2 * width)) for r in rows], axis=0)
    block = width // devices
    along = lax.broadcasted_iota(jnp.int32, (block, width), 1)
    inside = lax.broadcasted_iota(jnp.int32, (block, width), 0)
    picks = []
    for j in range(group):
        owner = high_place * group + (low_place ^ j)
        picks.append((along == inside + owner * block).astype(F32))
    picked = dot_t(jnp.concatenate(picks, axis=0).astype(BF16), inputs).astype(BF16)
    count = group * block

    def share(at, z, half):
        gate_w, up_w, down_w = (ref[at] for ref in halves[half])
        hidden, d_gate, d_up = glu_parts(inputs, back_in, gate_w, up_w, down_w)
        lanes = pl.ds(pl.multiple_of(z * unit, unit), unit)
        kept[:count, lanes] = dot(picked, jnp.where(place == 0, d_gate, d_up))
        sent[:count, lanes] = dot(picked, jnp.where(place == 0, d_up, d_gate)).astype(BF16)

        @pl.when(z == high_place)
        def _():
            hidden_t = hidden.T
            for out, part in zip((kept, sent), halves_of(back_in, place)):
                grad = dot(hidden_t, part).astype(out.dtype)
                size = grad.shape[1]
                out[count:, :size] = grad[: unit // 2]
                out[count:, size : 2 * size] = grad[unit // 2 :]
                out[count:, 2 * size :] = jnp.zeros((unit // 2, out.shape[1] - 2 * size), out.dtype)

    for half in range(len(halves)):

        def one(at, carry, half=half):
            share(at, half * each + at, half)
            return carry

        lax.fori_loop(0, each, one, 0)


def heavy_row_kernel(routed, counts, *refs):
    lists = []
    for count in counts:
        lists.append(refs[:count])
        refs = refs[count:]
    routed_parts, proj_parts, key_parts = lists
    keyval, table, w_q, w_kv, w_out, grads, parts, sums, sent, mix_t, dq_t, dkv = refs
    width = w_q.shape[0]
    scale = 1.0 / math.sqrt(DH)
    me = lax.axis_index("seq")
    r = lax.rem(me, 2)
    block = width // lax.axis_size("seq")
    along = lax.broadcasted_iota(jnp.int32, (block, width), 1)
    inside = lax.broadcasted_iota(jnp.int32, (block, width), 0)
    own = [(along == inside + at * block).astype(F32) for at in (me, me ^ 1)]
    own = jnp.concatenate(own, axis=0).astype(BF16)
    in_q = gathered(routed_parts, r, slice(2 * width, 3 * width))
    in_k = gathered(key_parts, r, slice(0, width))
    q_marks = gathered(routed_parts, r, slice(3 * width, 3 * width + LANES)).astype(F32).T[0:1, :]
    k_marks = gathered(key_parts, r, slice(width, width + LANES)).astype(F32)[:, 0:1]
    allowed = k_marks == q_marks
    grad_in = gathered(proj_parts, r, slice(0, width))
    extra = gathered(proj_parts, r, slice(width, width + LANES)).astype(F32)
    sums[...] = jnp.broadcast_to(
        sum(jnp.sum(ref[:, 0, :, width:].astype(F32), axis=0) for ref in proj_parts)[0:1], sums.shape
    )
    query = dot(in_q, w_q[...]).astype(BF16)
    mix_grad = dot_t(grad_in, w_out[...]).astype(BF16)
    key_t = keyval[r, :, :width].T
    val_t = keyval[r, :, width:].T
    lane = lax.broadcasted_iota(jnp.int32, (1, LANES), 1)
    for first in range(0, width, LANES):
        window = slice(first, first + LANES)
        v_window = slice(width + first, width + first + LANES)
        keys_w, vals_w = keyval[r, :, window], keyval[r, :, v_window]
        dk, dv = None, None
        for h in range(first // DH, (first + LANES) // DH):
            mask = (lane + first >= h * DH) & (lane + first < (h + 1) * DH)
            q_head = jnp.where(mask, query[:, window], 0)
            g_head = jnp.where(mask, mix_grad[:, window], 0)
            scores = jnp.where(allowed, dot_t(keys_w, q_head) * scale, NEG_FILL)
            peak = jnp.maximum(jnp.max(scores, axis=0, keepdims=True), 0.0)
            numer = jnp.exp(scores - peak)
            share = numer / (jnp.exp(-peak) + jnp.sum(numer, axis=0, keepdims=True))
            share_low = share.astype(BF16)
            prob_grad = dot_t(vals_w, g_head)
            delta = jnp.sum(share * prob_grad, axis=0, keepdims=True)
            score_grad = (share * (prob_grad - delta)).astype(BF16)
            at = slice(h * DH, (h + 1) * DH)
            mix_t[at, :] = dot(val_t[at, :], share_low).astype(BF16)
            dq_t[at, :] = dot(key_t[at, :], score_grad)
            part_k, part_v = dot(score_grad, q_head), dot(share_low, g_head)
            dk, dv = (part_k, part_v) if dk is None else (dk + part_k, dv + part_v)
        dkv[:, window] = (dk * scale).astype(BF16)
        dkv[:, v_window] = dv.astype(BF16)
    dq = (dq_t[...].T * scale).astype(BF16)
    in_q_t = dot_t(own, in_q)
    logits = jnp.sum(jnp.where((lane >= 24) & (lane < 27), extra, 0.0), axis=1, keepdims=True)
    logit_row = jnp.sum(extra.T[24:27, :], axis=0, keepdims=True)
    at = 0
    for grad in (
        dot(in_q_t.astype(BF16), dq),
        dot(dot_t(own, in_k).astype(BF16), dkv[...]),
        dot(dot(own, mix_t[...]).astype(BF16), grad_in),
        jnp.broadcast_to(jnp.sum(in_q_t * logit_row, axis=1, keepdims=True), (2 * block, LANES)),
    ):
        lanes = slice(at, at + grad.shape[1])
        grads[:, lanes] = grad[:block]
        sent[:block, lanes] = grad[block:].astype(BF16)
        at += grad.shape[1]
    half = dq.shape[0] // 2
    ours = lambda v: jnp.concatenate([v[:routed], v[half : half + routed]], axis=0)
    q_part = dot_t(ours(dq), w_q[...]) + ours(logits) * table[2:3, :]
    k_part = dot_t(ours(dkv), w_kv[...])
    for k, part in enumerate((q_part, k_part)):
        parts[k] = part[:routed]
        sent[block:, k * width : (k + 1) * width] = part[routed:].astype(BF16)
    sent[block:, 2 * width :] = jnp.zeros((routed, sent.shape[1] - 2 * width), BF16)


def heavy_last_kernel(
    routed, q_route, k_route, grads_in, parts_in, sums_in, got, dnorm, from_left, from_right, dmid, tokens, table,
    w_q, w_kv, grad_tokens, kept, sent, total, parts,
):
    rows, span, width = tokens.shape
    me = lax.axis_index("seq")
    place = lax.axis_index("dp")
    block = width // lax.axis_size("seq")
    grads = grads_in[...] + got[:block, :].astype(F32)
    for k in range(2):
        parts[lax.rem(me, 2), k] = parts_in[k]
        parts[1 - lax.rem(me, 2), k] = got[block:, k * width : (k + 1) * width].astype(F32)
    for r in range(rows):
        at = r * span
        total[at : at + span, :] = dnorm[at : at + span, :]
        total[at : at + RADIUS, :] += from_left[r].astype(F32)
        total[at + span - RADIUS : at + span, :] += from_right[r].astype(F32)
        for k in range(routed):
            for which, route in enumerate((q_route, k_route)):
                spot = route[r, me * routed + k] - me * span
                row = pl.ds(at + spot, 1)
                total[row, :] = total[row, :] + parts[r, which, k : k + 1, :]
    hidden = tokens[...].reshape(rows * span, width).astype(F32)
    factor = row_factor(hidden)
    weighted = total[...] * table[0:1, :]
    inner = jnp.mean(weighted * hidden, axis=-1, keepdims=True)
    d_hidden = dmid[...] + factor * weighted - hidden * (factor * factor * factor) * inner
    grad_tokens[...] = d_hidden.astype(BF16).reshape(grad_tokens.shape)
    along = lax.broadcasted_iota(jnp.int32, (block, width), 1)
    inside = lax.broadcasted_iota(jnp.int32, (block, width), 0)
    own_full = (along == inside + me * block).astype(F32)
    own = own_full.astype(BF16)
    own_gain = jnp.sum(own_full * table[0:1, :], axis=1, keepdims=True)
    own_route = jnp.sum(own_full * table[2:3, :], axis=1, keepdims=True)
    route_grad = grads[:, 4 * width : 4 * width + 1]
    gain_grad = jnp.sum(dot(own, w_q[...]) * grads[:, :width], axis=1, keepdims=True)
    gain_grad = gain_grad + jnp.sum(dot(own, w_kv[...]) * grads[:, width : 3 * width], axis=1, keepdims=True)
    gain_grad = (gain_grad + own_route * route_grad) / own_gain
    lane = lax.broadcasted_iota(jnp.int32, (block, LANES), 1)
    sums = sums_in[...]
    sums = sums + pltpu.roll(sums, LANES - 8, 1) + pltpu.roll(sums, LANES - 16, 1)
    sums = jnp.where(lane[:8] < 8, sums, 0.0)
    vectors = jnp.where(lane == 0, gain_grad, jnp.where(lane == 1, route_grad, 0.0))
    own_sums = pltpu.roll(sums, 8, 1)[0:1, :]
    sent_sums = jnp.zeros((1, LANES), F32)
    for k, part in enumerate(three_parts(sums)):
        sent_sums = sent_sums + pltpu.roll(part, 8 + 8 * k, 1)[0:1, :]
    at = 0
    for grad in (grads[:, :width], grads[:, width : 3 * width], grads[:, 3 * width : 4 * width]):
        mine, other = halves_of(grad, place)
        size = mine.shape[1]
        kept[:, at : at + size] = mine
        sent[:, at : at + size] = other.astype(BF16)
        at += size
    kept[:, at:] = vectors + own_sums
    sent[:, at:] = (vectors + sent_sums).astype(BF16)


def mix_kernel(plans, count, *refs):
    ins, outs = refs[:count], refs[count:]
    for out, parts in zip(outs, plans):
        for target, sources in parts:
            dims = out.at[target].shape
            values = [ins[k][index].reshape(dims) for k, index in sources]
            if len(values) > 1:
                values = [sum(v.astype(F32) for v in values)]
            out[target] = values[0].astype(out.dtype)


def finish_light_kernel(kept, received, *outs):
    total = kept[0, 0].astype(F32) + received[0, 0].astype(F32)
    base = 0
    for ref in outs:
        block = ref.shape[0]
        for c in range(ref.shape[1] // LANES):
            ref[:, c * LANES : (c + 1) * LANES] = total[base : base + block]
            base += block


def finish_heavy_kernel(heavy_kept, heavy_got, q_out, kv_out, out_out, vectors, stats):
    total = heavy_kept[...] + heavy_got[...].astype(F32)
    at = 0
    for ref in (q_out, kv_out, out_out, vectors):
        ref[...] = total[:, at : at + ref.shape[1]]
        at += ref.shape[1]
    sums = total[:8, at - LANES :]
    stats[...] = sums + pltpu.roll(sums, LANES - 8, 1) + pltpu.roll(sums, LANES - 16, 1)


def finish_ffn_kernel(groups, *refs):
    pieces, gate_up_out = refs[:-1], refs[-1]
    group = len(pieces)
    low_place = lax.rem(lax.axis_index("seq"), group)
    unit = pieces[0].shape[1] // groups
    for j, piece in enumerate(pieces):
        for z in range(groups):
            at = pl.multiple_of((z * group + (low_place ^ j)) * unit, unit)
            gate_up_out[:, pl.ds(at, unit)] = piece[:, z * unit : (z + 1) * unit].astype(F32)


def blend(ins, outs, after=(), micros=1, mib=6):
    kernel = functools.partial(mix_kernel, [parts for _, _, parts in outs], len(ins))
    return call(kernel, [shape(dims, dtype) for dims, dtype, _ in outs], ins, mib=mib, after=after, micros=micros)


ALL = slice(None)


def joined(ins, first, cuts):
    blocks = [(first + k, b) for k, part in enumerate(ins) for b in range(part.shape[0])]
    each = len(blocks) // cuts
    dims = (each, *ins[0].shape[1:])
    outs = []
    for c in range(cuts):
        outs.append((dims, ins[0].dtype, [(k, [source]) for k, source in enumerate(blocks[c * each : (c + 1) * each])]))
    return outs


def pair_part(target, pair, index):
    return (target, [(2 * pair, index), (2 * pair + 1, index)])


def side_by_side(rows, cuts):
    half = rows // 2
    dims = (4, 2, half, LANES)
    each = 8 // cuts
    ways = [((0, 2), slice(0, half)), ((4, 6), slice(0, half)), ((0, 4), slice(half, rows)), ((2, 6), slice(half, rows))]
    outs = []
    for starts, part in ways:
        parts = []
        for k, start in enumerate(starts):
            inside = slice(start % each, start % each + 2)
            parts.append(pair_part(slice(2 * k, 2 * k + 2), start // each, (inside, ALL, part)))
        outs.append((dims, BF16, parts))
    return outs


def crossed(rows):
    dims = (2, 2, rows // 2, LANES)
    sides = (slice(0, 2), slice(2, 4))
    return [(dims, BF16, [pair_part(ALL, pair, side)]) for pair in (0, 1) for side in sides]


def halved(rows, first):
    half = rows // 2
    places = ((ALL, ALL, slice(0, half)), (ALL, ALL, slice(half, rows)))
    outs = []
    for way in (slice(0, 1), slice(1, 2)):
        parts = [pair_part(place, first + k, (ALL, way)) for k, place in enumerate(places)]
        outs.append(((2, 1, rows, LANES), BF16, parts))
    return outs


def last_half(rows, pair):
    return [((1, 1, rows, LANES), BF16, [pair_part(ALL, pair, way)]) for way in (slice(0, 1), slice(1, 2))]


def flat_halved(rows, keep, got, base):
    half = rows // 2
    ways = []
    for way in (0, 1):
        parts = []
        for slot in (0, 1):
            at = base + (2 * slot + way) * half
            sources = [(keep, (slot, way)), (got, slice(at, at + half))]
            parts.append(((slot, 0, slice(half, rows)), sources))
        ways.append(parts)
    return ways


def lanes_of(c):
    return slice(c * LANES, (c + 1) * LANES)


def skip_operand(kernel, place):
    return lambda *refs: kernel(*refs[:place], *refs[place + 1 :])


def local_kernels(
    tokens,
    segments,
    query_route,
    kv_route,
    ffn_route,
    grad_out,
    attn_gain,
    light_qkv,
    light_out,
    heavy_q,
    heavy_kv,
    heavy_out,
    route_query,
    ffn_gain,
    light_gate_up,
    light_down,
    heavy_gate_up,
    heavy_down,
    route_ffn,
):
    rows, span, width = tokens.shape
    devices = lax.axis_size("seq")
    routed = query_route.shape[1] // devices
    own, count = rows * span, rows * routed
    per_row = devices * routed
    extent = span + 2 * RADIUS
    block = width // devices
    light_heads = width // DL
    ffn_light, ffn_heavy = light_down.shape[0], heavy_down.shape[0]
    marked = width + LANES

    rim = shape((rows, RADIUS + 16, width), BF16)
    keys, upper, lower, table = call(
        functools.partial(first_kernel, routed),
        [shape((rows, routed, marked), BF16), rim, rim, shape((4, width), F32)],
        [kv_route, segments, tokens, attn_gain, ffn_gain, route_query, route_ffn],
        hbm=7,
        scratch=[
            pltpu.SMEM(kv_route.shape, jnp.int32),
            pltpu.SMEM(segments.shape, jnp.int32),
            pltpu.VMEM(segments.shape, jnp.int32),
            pltpu.VMEM(tokens.shape, BF16),
            pltpu.VMEM((width,), F32),
            pltpu.VMEM((width,), F32),
            pltpu.VMEM((width,), BF16),
            pltpu.VMEM((width,), BF16),
            pltpu.VMEM((own, width), F32),
            pltpu.VMEM((count, marked), F32),
            pltpu.SemaphoreType.DMA((8,)),
        ],
        mib=58,
    )
    bits = (1, 2, 4, 8)
    keys = keys[None]
    keys_got = [swap(keys, "seq", flip) for flip in (8, 4, 12)]
    before = shifted(upper, "seq", 1)
    after = shifted(lower, "seq", -1)
    (keys_four,) = blend([keys, *keys_got], joined([keys, *keys_got], 0, 1), mib=4)
    keys_four_got = swap(keys_four, "seq", 2)
    last = keys_four

    normed, query, keyval, probs, mix, attn = call(
        light_kernel,
        [
            shape((rows * extent, width), BF16),
            shape((own, width), BF16),
            shape((rows * extent, 2 * width), BF16),
            shape((rows * light_heads, extent, span), BF16),
            shape((own, width), BF16),
            shape((own, width), F32),
        ],
        [before, tokens, after, segments, table, light_qkv, light_out],
        scratch=[pltpu.VMEM((8, 3 * span), F32), pltpu.VMEM((width, span), F32)],
        micros=6,
        mib=14,
        after=[last],
    )
    held = [keys_four, keys_four_got]
    (keys_eight,) = blend(held, joined(held, 0, 1), [attn], mib=4)
    key_parts = [keys_eight, swap(keys_eight, "seq", 1)]

    small = shape((count, width), F32)
    middle, normed_two, keyval_all, payload, q_rows, f_rows, f_up, proj, f_marks, stats = call(
        functools.partial(middle_kernel, routed, len(key_parts)),
        [
            shape((own, width), F32),
            shape((own, width), BF16),
            shape((rows, per_row, 2 * width), BF16),
            shape((rows, routed, 3 * width + LANES), BF16),
            small,
            small,
            small,
            small,
            shape((count, LANES), F32),
            shape((8, LANES), F32),
        ],
        [
            query_route, ffn_route, segments, tokens, segments, *key_parts, attn, grad_out,
            table, heavy_q, heavy_kv, heavy_out,
        ],
        smem=3,
        scratch=[
            pltpu.VMEM((own, width), F32),
            pltpu.VMEM((count, LANES), F32),
            pltpu.VMEM((count, width), F32),
        ],
        micros=4,
        mib=8,
    )
    payload = payload[None]
    payload_got = [swap(payload, "seq", flip) for flip in (8, 4, 12)]

    share = shape((own, ffn_light), BF16)
    z_light, d_light, hidden, grad_gate, grad_up = call(
        light_ffn_kernel,
        [shape((own, width), F32), shape((own, width), F32), share, share, share],
        [normed_two, grad_out, light_gate_up, light_down],
        micros=6,
        mib=9,
    )
    half_rows = (width // 2) // LANES
    slot_rows = block * ffn_light // LANES + ffn_light // devices * half_rows
    slots = [shape((devices // (2 * FIRST_CUTS), 2, slot_rows, LANES), BF16)] * (2 * FIRST_CUTS)
    slots = call(
        functools.partial(first_grads_kernel, bits),
        slots,
        [normed_two, grad_gate, grad_up, hidden, grad_out],
        scratch=[
            pltpu.VMEM((width, own), BF16),
            pltpu.VMEM((ffn_light, own), BF16),
            pltpu.VMEM((own, width), BF16),
        ],
        micros=4,
        mib=9,
    )
    core = len(slots) // 2
    first_core = list(zip(slots[:core], [swap(part, "seq", 1) for part in slots[core:]]))
    held = [payload, *payload_got]
    (routed_four,) = blend(held, joined(held, 0, 1), [slots[0]], mib=4)
    routed_four_got = swap(routed_four, "seq", 2)

    steps = 4
    group = min(4, devices)
    groups = devices // group
    unit = ffn_heavy // devices
    heavy_unit = ffn_heavy // steps
    whole = lambda *dims: pl.BlockSpec(dims, lambda j: (0,) * len(dims))

    def streamed(first):
        columns = lambda at: pl.BlockSpec((width, heavy_unit), lambda j: (0, at + first + j))
        return [columns(0), columns(steps), pl.BlockSpec((heavy_unit, width), lambda j: (first + j, 0))]

    half = steps // 2
    share_dims = [(half, width, unit), (half, width, unit), (half, unit, width)]
    share_shapes = [shape(dims, BF16) for dims in share_dims]
    share_specs = [pl.BlockSpec((1, *dims[1:]), lambda j: (j, 0, 0)) for dims in share_dims]
    z_heavy, d_heavy, *shares_one = pl.pallas_call(
        skip_operand(functools.partial(ffn_first_kernel, group), 6),
        grid=(half,),
        out_shape=[small, small, *share_shapes],
        in_specs=streamed(0) + [whole(count, width)] * 2 + [whole(4, width), ANY],
        out_specs=[whole(count, width)] * 2 + share_specs,
        compiler_params=pltpu.CompilerParams(vmem_limit_bytes=12 * MIB),
        cost_estimate=cost(6),
    )(heavy_gate_up, heavy_gate_up, heavy_down, f_rows, f_up, table, routed_four)
    rows_one = slots[0].shape[2]
    ins = [v for pair in first_core for v in pair]
    each = 8 // FIRST_CUTS
    halves = [
        (
            (8, 1, rows_one, LANES),
            BF16,
            [pair_part(slice(k * each, (k + 1) * each), k, (ALL, way)) for k in range(FIRST_CUTS)],
        )
        for way in (slice(0, 1), slice(1, 2))
    ]
    left_keep, left_sent = blend(ins, halves, [z_heavy])
    first_pairs = [left_keep, swap(left_sent, "dp", 1)]
    outputs, dmid, dmid_low, proj_payload, vectors, *shares_two = pl.pallas_call(
        skip_operand(functools.partial(ffn_last_kernel, routed, group), 19),
        grid=(half,),
        out_shape=[
            shape((rows, span, width), BF16),
            shape((own, width), F32),
            shape((own, width), BF16),
            shape((rows, routed, marked), BF16),
            shape((8, width), F32),
            *share_shapes,
        ],
        in_specs=[SMEM, SMEM]
        + streamed(half)
        + [whole(count, width)] * 2
        + [whole(rows, span, width)]
        + [whole(own, width)] * 3
        + [whole(count, width)] * 4
        + [whole(count, LANES), whole(4, width), whole(8, LANES), whole(rows, span), ANY],
        out_specs=[
            whole(rows, span, width),
            whole(own, width),
            whole(own, width),
            whole(rows, routed, marked),
            whole(8, width),
            *share_specs,
        ],
        scratch_shapes=[pltpu.VMEM((count, width), F32)] * 3 + [pltpu.VMEM((own, width), F32)] * 2,
        compiler_params=pltpu.CompilerParams(vmem_limit_bytes=16 * MIB),
        cost_estimate=cost(7),
    )(
        query_route, ffn_route, heavy_gate_up, heavy_gate_up, heavy_down, z_heavy, d_heavy, grad_out, middle,
        z_light, d_light, q_rows, f_rows, f_up, proj, f_marks, table, stats, segments, left_keep,
    )
    proj_payload = proj_payload[None]
    proj_got = [swap(proj_payload, "seq", flip) for flip in (8, 4, 12)]

    slot_rows = block * 3 * half_rows + block * half_rows + block + 16
    slots = [shape((devices // (2 * SECOND_CUTS), 2, slot_rows, LANES), BF16)] * (2 * SECOND_CUTS)
    rim = shape((rows, RADIUS, width), BF16)
    dnorm, to_right, to_left, *slots = call(
        functools.partial(light_back_kernel, bits),
        [shape((own, width), F32), rim, rim, *slots],
        [dmid_low, query, keyval, probs, normed, mix, vectors, table, light_qkv, light_out],
        scratch=[
            pltpu.VMEM((own, width), BF16),
            pltpu.VMEM((rows * extent, 2 * width), BF16),
            pltpu.VMEM((extent, 2 * width), F32),
            pltpu.VMEM((width, span), F32),
            pltpu.VMEM((width, width), BF16),
            pltpu.VMEM((width, rows * extent), BF16),
        ],
        micros=3,
        mib=12,
    )
    from_left = shifted(to_right, "seq", 1)
    from_right = shifted(to_left, "seq", -1)
    core = len(slots) // 2
    second_core = list(zip(slots[:core], [swap(part, "seq", 1) for part in slots[core:]]))

    held_proj, held_routed = [proj_payload, *proj_got], [routed_four, routed_four_got]
    side = (4, 1, rows_one, LANES)
    sides = [
        (side, BF16, [pair_part(slice(2 * k, 2 * k + 2), 0, slice(4 * k + at, 4 * k + at + 2)) for k in (0, 1)])
        for at in (0, 2)
    ]
    first_keep, first_sent, proj_four, *routed_eight = blend(
        first_pairs + held_proj + held_routed,
        sides + joined(held_proj, 2, 1) + joined(held_routed, 6, 1),
        [dnorm],
    )
    first_pairs = [first_keep, swap(first_sent, "seq", 4)]
    held_proj = [proj_four, swap(proj_four, "seq", 2)]
    routed_parts = routed_eight + [swap(piece, "seq", 1) for piece in routed_eight]

    heavy_rows = group * block + unit // 2
    ffn_kept, ffn_sent = call(
        functools.partial(heavy_ffn_kernel, len(routed_parts)),
        [shape((heavy_rows, groups * unit), F32), shape((heavy_rows, groups * unit), BF16)],
        [*routed_parts, *shares_one, *shares_two],
        micros=7,
        mib=11,
        after=[left_keep],
    )
    ffn_got = swap(ffn_sent, "dp", 1)

    rows_two = slots[0].shape[2]
    ins = [v for pair in second_core for v in pair]
    left_keep, left_sent, right_keep, right_sent = blend(
        ins, side_by_side(rows_two, SECOND_CUTS), [ffn_kept], micros=1
    )
    (proj_eight,) = blend(held_proj, joined(held_proj, 0, 1), [left_keep])
    proj_parts = [proj_eight, swap(proj_eight, "seq", 1)]
    second_pairs = [left_keep, swap(left_sent, "seq", 2), right_keep, swap(right_sent, "seq", 4)]

    gathers = (routed_parts, proj_parts, key_parts)
    grad_lanes = 4 * width + LANES
    heavy_grads, heavy_parts, sums, pair_sent = call(
        functools.partial(heavy_row_kernel, routed, [len(parts) for parts in gathers]),
        [
            shape((block, grad_lanes), F32),
            shape((2, routed, width), F32),
            shape((8, LANES), F32),
            shape((block + routed, grad_lanes), BF16),
        ],
        [*sum(gathers, []), keyval_all, table, heavy_q, heavy_kv, heavy_out],
        scratch=[
            pltpu.VMEM((width, per_row), BF16),
            pltpu.VMEM((width, per_row), F32),
            pltpu.VMEM((per_row, 2 * width), BF16),
        ],
        micros=9,
        mib=8,
        after=[proj_eight],
    )
    pair_got = swap(pair_sent, "seq", 1)
    first_keep, first_sent = blend(
        first_pairs,
        [((2, 1, rows_one, LANES), BF16, [pair_part(ALL, 0, slice(at, at + 2))]) for at in (0, 2)],
        [sums],
    )
    first_pairs = [first_keep, swap(first_sent, "seq", 2)]
    from_left, from_right = blend(
        [from_left, from_right], [(from_left.shape, BF16, [(ALL, [(k, ALL)])]) for k in (0, 1)], [first_keep]
    )
    below = slice(group * block, heavy_rows)
    down_lanes = [slice(0, width // 2), slice(width // 2, width)]
    rows_of = lambda j: slice(j * block, (j + 1) * block)
    kept_side, sent_side, kept_other, sent_other = crossed(rows_two)
    sent_rows = 2 * rows_two
    parts = [(slice(0, sent_rows), sent_other[2][0][1])]
    for c in range(groups * unit // LANES):
        at = sent_rows + c * block
        parts.append(pair_part(slice(at, at + block), 2, (rows_of(2), lanes_of(c))))
    merged = ((sent_rows + groups * unit // LANES * block, LANES), BF16, parts)
    downs = [pair_part(slice(k * unit // 2, (k + 1) * unit // 2), 2, (below, down_lanes[k])) for k in (0, 1)]
    left_keep, left_sent, right_keep, x_sent, heavy_down_grad, *pieces = blend(
        second_pairs + [ffn_kept, ffn_got],
        [kept_side, sent_side, kept_other, merged, ((unit, width // 2), F32, downs)]
        + [
            ((block, groups * unit), F32 if j == 0 else BF16, [pair_part(ALL, 2, rows_of(j))])
            for j in (0, 1, 3)
        ],
        [from_left],
    )
    second_pairs = [left_keep, swap(left_sent, "seq", 4), right_keep, swap(x_sent, "seq", 2)]
    pieces = [pieces[0], swap(pieces[1], "seq", 1), None, swap(pieces[2], "seq", 3)]
    grad_tokens, heavy_kept, heavy_sent = call(
        functools.partial(heavy_last_kernel, routed),
        [
            shape((rows, span, width), BF16),
            shape((block, 2 * width + LANES), F32),
            shape((block, 2 * width + LANES), BF16),
        ],
        [
            query_route, kv_route, heavy_grads, heavy_parts, sums, pair_got, dnorm, from_left, from_right,
            dmid, tokens, table, heavy_q, heavy_kv,
        ],
        smem=2,
        scratch=[pltpu.VMEM((own, width), F32), pltpu.VMEM((rows, 2, routed, width), F32)],
        micros=2,
        mib=7,
        after=[left_keep],
    )
    ways = flat_halved(rows_two, 2, 3, 0)
    for way in (0, 1):
        index = (ALL, slice(way, way + 1))
        ways[way].insert(0, ((ALL, ALL, slice(0, rows_two // 2)), [(0, index), (1, index)]))
    sent_parts = []
    for (slot, _, place), sources in ways[1][1:]:
        sent_parts.append((slice(slot * rows_two + place.start, slot * rows_two + place.stop), sources))
    for slot in (0, 1):
        at = slot * rows_two
        sources = [(0, (slot, 1)), (1, (slot, 1))]
        sent_parts.append((slice(at, at + rows_two // 2), sources))
    piece_parts = []
    for c in range(groups * unit // LANES):
        at = sent_rows + c * block
        piece_parts.append(((ALL, lanes_of(c)), [(3, slice(at, at + block))]))
    second_keep, y_sent, pieces[2] = blend(
        second_pairs,
        [
            ((2, 1, rows_two, LANES), BF16, ways[0]),
            ((2 * rows_two, LANES), BF16, sent_parts),
        ]
        + [((block, groups * unit), BF16, piece_parts)],
        [heavy_kept],
    )
    y_got = swap(y_sent, "dp", 1)
    first_keep, first_sent = blend(first_pairs, last_half(rows_one, 0), [second_keep])
    first_pair = [first_keep, swap(first_sent, "seq", 8)]
    (heavy_gate_up_grad,) = call(
        functools.partial(finish_ffn_kernel, groups),
        [shape((block, ffn_heavy), F32)],
        pieces,
        micros=0.5,
        mib=4,
        after=[first_keep],
    )
    second_keep, second_sent, heavy_sent = blend(
        [second_keep, y_got, heavy_sent],
        [
            ((1, 1, rows_two, LANES), BF16, [(ALL, [(0, slot), (1, slice(slot * rows_two, (slot + 1) * rows_two))])])
            for slot in (0, 1)
        ]
        + [(heavy_sent.shape, BF16, [(ALL, [(2, ALL)])])],
        [heavy_gate_up_grad],
    )
    heavy_got = swap(heavy_sent, "dp", 1)
    second_pair = [second_keep, swap(second_sent, "seq", 8)]
    light_gate_up_grad, light_down_grad = call(
        finish_light_kernel,
        [shape((block, ffn_light), F32), shape((ffn_light // devices, width // 2), F32)],
        first_pair,
        mib=4,
        after=[second_keep],
    )
    heavy_q_grad, heavy_kv_grad, heavy_out_grad, heavy_vectors, stats = call(
        finish_heavy_kernel,
        [
            shape((block, width // 2), F32),
            shape((block, width), F32),
            shape((block, width // 2), F32),
            shape((block, LANES), F32),
            shape((8, LANES), F32),
        ],
        [heavy_kept, heavy_got],
        mib=4,
        after=[light_down_grad],
    )
    light_qkv_grad, light_out_grad, light_vectors = call(
        finish_light_kernel,
        [
            shape((block, 3 * width // 2), F32),
            shape((block, width // 2), F32),
            shape((block, LANES), F32),
        ],
        second_pair,
        mib=4,
        after=[heavy_vectors],
    )
    sums = stats[0, 8:14]
    return (
        outputs,
        grad_tokens,
        light_vectors[:, 2] + heavy_vectors[:, 0],
        light_qkv_grad,
        light_out_grad,
        heavy_q_grad,
        heavy_kv_grad,
        heavy_out_grad,
        heavy_vectors[:, 1],
        light_vectors[:, 0],
        light_gate_up_grad,
        light_down_grad,
        heavy_gate_up_grad,
        heavy_down_grad,
        light_vectors[:, 1],
        jnp.sqrt(sums[:5] / (sums[5] * width)),
    )


def local(tokens, segments, query_route, *others):
    block = tokens.shape[2] // lax.axis_size("seq")
    fits = query_route.shape[1] <= 256 and block % 16 == 0 and tokens.shape[0] == 2
    return (local_kernels if fits else local_wide)(tokens, segments, query_route, *others)


def solution(mesh):
    placed = (
        P("dp", "seq", None),
        P("dp", "seq"),
        P("dp", None),
        P("dp", None),
        P("dp", "seq"),
        P("dp", "seq", None),
    ) + (P(),) * 13
    matrix = P("seq", "dp")
    vector = P("seq")
    return jax.shard_map(
        local,
        mesh=mesh,
        in_specs=placed,
        out_specs=(
            P("dp", "seq", None),
            P("dp", "seq", None),
            vector,
            matrix,
            matrix,
            matrix,
            matrix,
            matrix,
            vector,
            vector,
            matrix,
            matrix,
            matrix,
            matrix,
            vector,
            P(),
        ),
        check_vma=False,
    )
```

```python
import functools
import math

import jax
import jax.numpy as jnp
from jax import lax
from jax.experimental import pallas as pl
from jax.experimental.pallas import tpu as pltpu
from jax.sharding import PartitionSpec as P

DL = 96
DH = 64
RADIUS = 64
LANES = 128


PRECISE = lax.Precision.HIGHEST
EPSILON = 1e-06
NEG_FILL = -1e30
F32 = jnp.float32
BF16 = jnp.bfloat16


def swap(value, axis, bit):
    return lax.ppermute(value, axis, [(i, i ^ bit) for i in range(lax.axis_size(axis))])


def shifted(block, axis, distance):
    devices = range(lax.axis_size(axis))
    route = [(i - distance, i) for i in devices if i - distance in devices]
    return lax.ppermute(block, axis, route)


def gather_blocks(block):
    held = block[None]
    bit = lax.axis_size("seq") // 2
    while bit:
        held = jnp.concatenate([held, swap(held, "seq", bit)], axis=0)
        bit //= 2
    return held


def add_halves(value, dim, axis, bit, out_type=BF16):
    half = value.shape[dim] // 2
    keep = lax.slice_in_dim(value, 0, half, axis=dim)
    sent = lax.slice_in_dim(value, half, 2 * half, axis=dim)
    return (keep.astype(F32) + swap(sent, axis, bit).astype(F32)).astype(out_type)


def scatter_sum(slots):
    devices = lax.axis_size("seq")
    rows = slots.shape[2]
    slots = add_halves(slots, 0, "seq", 1)
    left, right = slots[:, :, : rows // 2], slots[:, :, rows // 2 :]
    left = add_halves(left, 0, "seq", 2)
    right = add_halves(right, 1, "dp", 1)
    left = add_halves(left, 1, "dp", 1)
    right = add_halves(right, 0, "seq", 2)
    both = jnp.concatenate([left, right], axis=2)
    bit = 4
    while bit < devices:
        both = add_halves(both, 0, "seq", bit, BF16 if 2 * bit < devices else F32)
        bit *= 2
    return both[0, 0]


def slot_places(me, devices):
    bits = devices.bit_length() - 1
    places = [int(format(p, f"0{bits}b")[::-1], 2) for p in range(devices)]
    return jnp.array(places, jnp.int32) ^ me


def slot_columns(value, me, devices):
    width = value.shape[-1]
    block = width // devices
    order = (slot_places(me, devices)[:, None] * block + jnp.arange(block)[None, :]).reshape(-1)
    onehot = (jnp.arange(width)[:, None] == order[None, :]).astype(BF16)
    return jnp.dot(value, onehot, preferred_element_type=F32).astype(BF16)


def own_half_first(value, place):
    half = value.shape[-1] // 2
    first, second = value[..., :half], value[..., half:]
    return (jnp.where(place == 0, first, second), jnp.where(place == 0, second, first))


def slot_block(grad_halves, devices):
    stacked = jnp.stack(grad_halves)
    _, total, cols = stacked.shape
    parts = stacked.reshape(2, devices, total // devices, cols // LANES, LANES)
    return parts.transpose(1, 0, 3, 2, 4).reshape(devices, 2, -1, LANES).astype(BF16)


def unslot(rows, cols):
    return rows.reshape(cols // LANES, -1, LANES).transpose(1, 0, 2).reshape(-1, cols)


def slot_vectors(vectors, me, devices):
    block = vectors[0].shape[0] // devices
    table = jnp.stack(vectors, axis=-1).reshape(devices, block, len(vectors))
    table = jnp.take(table, slot_places(me, devices), axis=0)
    table = jnp.pad(table, ((0, 0), (0, 0), (0, LANES - len(vectors))))
    return jnp.broadcast_to(table[:, None], (devices, 2, block, LANES)).astype(BF16)


def split_parts(value):
    high = lax.reduce_precision(value, 8, 7)
    middle = lax.reduce_precision(value - high, 8, 7)
    return (high, middle, value - high - middle)


def rms_factor(hidden):
    return lax.rsqrt(jnp.mean(hidden * hidden, axis=-1, keepdims=True) + EPSILON)


def norm_back(hidden, factor, gain_vec, upstream):
    weighted = upstream * gain_vec
    inner_mean = jnp.mean(weighted * hidden, axis=-1, keepdims=True)
    return factor * weighted - hidden * (factor * factor * factor) * inner_mean


def pick_rows(source, positions):
    return jnp.take_along_axis(source, positions[..., None], axis=1)


def place_rows(values, positions, extent):
    onehot = (positions[..., None] == jnp.arange(extent)[None, None, :]).astype(F32)
    return jnp.einsum("rqs,rqd->rsd", onehot, values, precision=PRECISE)


def matmul(left, right):
    return jnp.einsum("...d,de->...e", left, right, preferred_element_type=F32)


def matmul_t(left, right):
    return jnp.einsum("...e,de->...d", left, right, preferred_element_type=F32)


def outer(left, right):
    return jnp.einsum("rsd,rse->de", left, right, preferred_element_type=F32)


def glu_value(gate_part, up_part):
    return jax.nn.gelu(gate_part, approximate=True) * up_part


def geglu(inputs, gate_up, down, upstream_low):
    width = down.shape[0]
    both = matmul(inputs, gate_up)
    gate_part, up_part = both[..., :width], both[..., width:]
    hidden, pull_back = jax.vjp(glu_value, gate_part, up_part)
    gate_grad, up_grad = pull_back(matmul_t(upstream_low, down))
    return (hidden.astype(BF16), gate_grad.astype(BF16), up_grad.astype(BF16))


def routed_probs(query_heads, key_heads, query_seg, key_seg):
    scores = jnp.einsum("rqd,rkd->rqk", query_heads, key_heads, preferred_element_type=F32)
    scores = scores / math.sqrt(DH)
    allowed = query_seg[:, :, None] == key_seg[:, None, :]
    scores = jnp.where(allowed, scores, NEG_FILL)
    peak = jnp.maximum(jnp.max(scores, axis=-1, keepdims=True), 0.0)
    numer = jnp.exp(scores - peak)
    return numer / (jnp.exp(-peak) + jnp.sum(numer, axis=-1, keepdims=True))


def heavy_forward(query, keys, vals, query_seg, key_seg):
    def head(parts):
        query_h, key_h, val_h = parts
        probs = routed_probs(query_h, key_h, query_seg, key_seg).astype(BF16)
        return jnp.einsum("rqk,rkd->rqd", probs, val_h, preferred_element_type=F32).astype(BF16)

    return join_heads(jax.vmap(head)((split_heads(query), split_heads(keys), split_heads(vals))))


def heavy_both(query, keys, vals, query_seg, key_seg, mix_grad):
    def head(parts, query_seg=query_seg, key_seg=key_seg):
        query_h, key_h, val_h, grad_h = parts
        probs = routed_probs(query_h, key_h, query_seg, key_seg)
        probs_low = probs.astype(BF16)
        mix = jnp.einsum("rqk,rkd->rqd", probs_low, val_h, preferred_element_type=F32)
        prob_grad = jnp.einsum("rqd,rkd->rqk", grad_h, val_h, preferred_element_type=F32)
        delta = jnp.sum(probs * prob_grad, axis=-1, keepdims=True)
        score_grad = (probs * (prob_grad - delta)).astype(BF16)
        dquery = jnp.einsum("rqk,rkd->rqd", score_grad, key_h, preferred_element_type=F32)
        dkey = jnp.einsum("rqk,rqd->rkd", score_grad, query_h, preferred_element_type=F32)
        dval = jnp.einsum("rqk,rqd->rkd", probs_low, grad_h, preferred_element_type=F32)
        scale = 1.0 / math.sqrt(DH)
        return (mix.astype(BF16), (dquery * scale).astype(BF16), (dkey * scale).astype(BF16), dval.astype(BF16))

    heads = tuple(split_heads(v) for v in (query, keys, vals, mix_grad))
    if query.shape[1] <= 512:
        return tuple(join_heads(v) for v in jax.vmap(head)(heads))
    count, rows = heads[0].shape[:2]
    place = jnp.tile(jnp.arange(rows), count)
    parts = tuple(v.reshape(count * rows, 1, *v.shape[2:]) for v in heads)
    done = lax.map(lambda p: head(p[0], query_seg[p[1]][None], key_seg[p[1]][None]), (parts, place))
    return tuple(join_heads(v.reshape(count, rows, *v.shape[2:])) for v in done)


def split_heads(value):
    rows, tokens, width = value.shape
    return value.reshape(rows, tokens, width // DH, DH).transpose(2, 0, 1, 3)


def join_heads(value):
    heads, rows, tokens, width = value.shape
    return value.transpose(1, 2, 0, 3).reshape(rows, tokens, heads * width)


def tokens_of(blocks):
    devices, rows, count, width = blocks.shape
    return blocks.transpose(1, 0, 2, 3).reshape(rows, devices * count, width)


def with_segment(rows, segs):
    marks = jnp.broadcast_to((segs + 2).astype(BF16)[..., None], segs.shape + (LANES,))
    return jnp.concatenate([rows, marks], axis=-1)


def local_wide(
    tokens,
    segments,
    query_route,
    kv_route,
    ffn_route,
    grad_out,
    attn_gain,
    light_qkv,
    light_out,
    heavy_q,
    heavy_kv,
    heavy_out,
    route_query,
    ffn_gain,
    light_gate_up,
    light_down,
    heavy_gate_up,
    heavy_down,
    route_ffn,
):
    row_count, seg_span, width = tokens.shape
    light_heads = width // DL
    ffn_heavy = heavy_down.shape[0]
    devices = lax.axis_size("seq")
    me = lax.axis_index("seq")
    half_place = lax.axis_index("dp")
    anchor = me * seg_span
    routed_own = query_route.shape[1] // devices
    own_query = lax.dynamic_slice_in_dim(query_route, me * routed_own, routed_own, 1) - anchor
    own_key = lax.dynamic_slice_in_dim(kv_route, me * routed_own, routed_own, 1) - anchor
    own_ffn = ffn_route - anchor

    marked = with_segment(tokens, segments)
    before = shifted(marked[:, seg_span - RADIUS :], "seq", 1)
    after = shifted(marked[:, :RADIUS], "seq", -1)
    hidden = tokens.astype(F32)
    factor_one = rms_factor(hidden)
    normed = hidden * factor_one * attn_gain
    normed_low = normed.astype(BF16)
    key_rows = pick_rows(normed_low, own_key)
    key_payload = with_segment(key_rows, jnp.take_along_axis(segments, own_key, axis=1))
    key_blocks = tokens_of(gather_blocks(key_payload))
    key_all, key_seg = key_blocks[..., :width], key_blocks[..., width]

    extended = jnp.concatenate([before, marked, after], axis=1)
    seg_ext = extended[..., width]
    hidden_ext = extended[..., :width].astype(F32)
    factor_ext = rms_factor(hidden_ext)
    normed_ext_low = (hidden_ext * factor_ext * attn_gain).astype(BF16)
    extent = seg_span + 2 * RADIUS
    query_low = matmul(normed_low, light_qkv[:, :width]).astype(BF16)
    query_low = query_low.reshape(row_count, seg_span, light_heads, DL)
    kv_ext = matmul(normed_ext_low, light_qkv[:, width:]).astype(BF16)
    key_ext = kv_ext[..., :width].reshape(row_count, extent, light_heads, DL)
    val_ext = kv_ext[..., width:].reshape(row_count, extent, light_heads, DL)
    offset = jnp.arange(seg_span)[:, None] - jnp.arange(extent)[None, :] + RADIUS
    seg_own = seg_ext[:, RADIUS : RADIUS + seg_span]
    allowed = (jnp.abs(offset) <= RADIUS)[None] & (seg_own[:, :, None] == seg_ext[:, None, :])
    light_scale = 1.0 / math.sqrt(DL)
    scores = jnp.einsum("rqhd,rkhd->rhqk", query_low, key_ext, preferred_element_type=F32)
    scores = jnp.where(allowed[:, None], scores * light_scale, NEG_FILL)
    numerators = jnp.exp(scores - jnp.max(scores, axis=-1, keepdims=True))
    probs_light = numerators / jnp.sum(numerators, axis=-1, keepdims=True)
    probs_low = probs_light.astype(BF16)
    light_mix = jnp.einsum("rhqk,rkhd->rqhd", probs_low, val_ext, preferred_element_type=F32)
    light_mix = light_mix.reshape(row_count, seg_span, width).astype(BF16)
    light_attn = matmul(light_mix, light_out)

    query_rows = pick_rows(normed_low, own_query)
    query_seg_own = (jnp.take_along_axis(segments, own_query, axis=1) + 2).astype(BF16)
    heavy_query = matmul(query_rows, heavy_q).astype(BF16)
    keyval_all = matmul(key_all, heavy_kv).astype(BF16)
    heavy_width = heavy_q.shape[1]
    keys_all, vals_all = keyval_all[..., :heavy_width], keyval_all[..., heavy_width:]
    heavy_mix = heavy_forward(heavy_query, keys_all, vals_all, query_seg_own, key_seg)
    heavy_proj = matmul(heavy_mix, heavy_out)
    query_normed = pick_rows(normed, own_query)
    route_query_full = route_query.astype(F32)
    query_gate = jax.nn.sigmoid(jnp.sum(query_normed * route_query_full, axis=-1))
    heavy_attn = place_rows(query_gate[..., None] * heavy_proj, own_query, seg_span)

    middle = hidden + light_attn + heavy_attn
    factor_two = rms_factor(middle)
    normed_two = middle * factor_two * ffn_gain
    low_two = normed_two.astype(BF16)
    upstream = grad_out.astype(F32)
    ffn_normed = pick_rows(normed_two, own_ffn)
    ffn_rows = ffn_normed.astype(BF16)
    route_ffn_full = route_ffn.astype(F32)
    ffn_gate = jax.nn.sigmoid(jnp.sum(ffn_normed * route_ffn_full, axis=-1))
    ffn_upstream = pick_rows(upstream, own_ffn)
    ffn_low = (ffn_upstream * ffn_gate[..., None]).astype(BF16)
    routed_payload = with_segment(
        jnp.concatenate([ffn_rows, ffn_low, query_rows], axis=-1),
        jnp.take_along_axis(segments, own_query, axis=1),
    )
    routed_blocks = tokens_of(gather_blocks(routed_payload))
    ffn_all = routed_blocks[..., :width]
    ffn_low_all = routed_blocks[..., width : 2 * width]
    query_all = routed_blocks[..., 2 * width : 3 * width]
    query_seg = routed_blocks[..., 3 * width]

    hidden_light, gate_grad, up_grad = geglu(low_two, light_gate_up, light_down, grad_out)
    light_ff = matmul(hidden_light, light_down)
    light_both = jnp.concatenate([gate_grad, up_grad], axis=-1)
    normed_two_grad = matmul_t(light_both, light_gate_up)
    hidden_heavy, gate_grad_h, up_grad_h = geglu(ffn_rows, heavy_gate_up, heavy_down, ffn_low)
    heavy_ffn_proj = matmul(hidden_heavy, heavy_down)
    heavy_ff = place_rows(ffn_gate[..., None] * heavy_ffn_proj, own_ffn, seg_span)
    outputs = (middle + light_ff + heavy_ff).astype(BF16)
    ffn_gate_grad = jnp.sum(ffn_upstream * heavy_ffn_proj, axis=-1)
    ffn_logit_grad = ffn_gate_grad * ffn_gate * (1.0 - ffn_gate)
    route_ffn_grad = jnp.sum(ffn_logit_grad[..., None] * ffn_normed, axis=(0, 1))
    ffn_rows_grad = matmul_t(jnp.concatenate([gate_grad_h, up_grad_h], axis=-1), heavy_gate_up)
    ffn_rows_grad = ffn_rows_grad + ffn_logit_grad[..., None] * route_ffn_full
    normed_two_grad = normed_two_grad + place_rows(ffn_rows_grad, own_ffn, seg_span)
    ffn_gain_grad = jnp.sum(normed_two_grad * middle * factor_two, axis=(0, 1))
    middle_grad = upstream + norm_back(middle, factor_two, ffn_gain, normed_two_grad)
    middle_low = middle_grad.astype(BF16)

    valid_rows = (segments >= 0).astype(F32)[..., None]
    sums = jnp.stack(
        [
            jnp.sum(valid_rows * branch * branch)
            for branch in (hidden, light_attn, heavy_attn, light_ff, heavy_ff)
        ]
        + [jnp.sum(valid_rows)]
    )
    heavy_upstream = pick_rows(middle_grad, own_query)
    query_gate_grad = jnp.sum(heavy_upstream * heavy_proj, axis=-1)
    proj_low = (heavy_upstream * query_gate[..., None]).astype(BF16)
    sum_lanes = jnp.pad(jnp.concatenate(split_parts(sums)), (0, LANES - 18)).astype(BF16)
    sum_lanes = jnp.broadcast_to(sum_lanes, proj_low.shape[:2] + (LANES,))
    proj_blocks = gather_blocks(jnp.concatenate([proj_low, sum_lanes], axis=-1))
    sums_all = jnp.sum(proj_blocks[:, 0, 0, width : width + 18].astype(F32), axis=0)
    sums_all = jnp.sum(sums_all.reshape(3, 6), axis=0)
    sums_all = sums_all + swap(sums_all, "dp", 1)
    rms_stats = jnp.sqrt(sums_all[:5] / (sums_all[5] * width))
    proj_all = tokens_of(proj_blocks)[..., :width]

    flat = lambda v: v.reshape(-1, v.shape[-1])
    gate_up_grad = [
        jnp.dot(slot_columns(flat(low_two), me, devices).T, flat(part), preferred_element_type=F32)
        for part in own_half_first(light_both, half_place)
    ]
    hidden_slots = slot_columns(flat(hidden_light), me, devices).T
    down_grad = [
        jnp.dot(hidden_slots, flat(part), preferred_element_type=F32)
        for part in own_half_first(grad_out, half_place)
    ]
    mix_slots = slot_columns(flat(light_mix), me, devices).T
    out_grad = [
        jnp.dot(mix_slots, flat(part), preferred_element_type=F32)
        for part in own_half_first(middle_low, half_place)
    ]
    first_sum = scatter_sum(
        jnp.concatenate(
            [
                slot_block(gate_up_grad, devices),
                slot_block(down_grad, devices),
                slot_block(out_grad, devices),
                slot_vectors((ffn_gain_grad, route_ffn_grad), me, devices),
            ],
            axis=2,
        )
    )
    block = width // devices
    block_ff = light_down.shape[0] // devices
    cuts = [0]
    for rows in (
        block * light_gate_up.shape[1] // 2 // LANES,
        block_ff * width // 2 // LANES,
        block * width // 2 // LANES,
        block,
    ):
        cuts.append(cuts[-1] + rows)
    light_gate_up_grad = unslot(first_sum[cuts[0] : cuts[1]], light_gate_up.shape[1] // 2)
    light_down_grad = unslot(first_sum[cuts[1] : cuts[2]], width // 2)
    light_out_grad = unslot(first_sum[cuts[2] : cuts[3]], width // 2)
    ffn_gain_grad = first_sum[cuts[3] : cuts[4], 0]
    route_ffn_grad = first_sum[cuts[3] : cuts[4], 1]

    group = min(4, devices)
    low_place, high_place = me % group, me // group
    groups = devices // group
    unit = ffn_heavy // devices
    gate_up_parts = heavy_gate_up.reshape(width, 2, groups, group, unit)
    gate_up_mine = lax.dynamic_index_in_dim(gate_up_parts, low_place, 3, False)
    down_mine = lax.dynamic_index_in_dim(
        heavy_down.reshape(groups, group, unit, width), low_place, 1, False
    )
    x_all = flat(ffn_all)
    up_all = flat(ffn_low_all)
    hidden_mine, gate_mine, up_mine = geglu(
        x_all,
        gate_up_mine.reshape(width, -1),
        down_mine.reshape(-1, width),
        up_all,
    )
    hidden_block = lax.dynamic_slice_in_dim(hidden_mine, high_place * unit, unit, 1)
    heavy_down_half = [
        jnp.dot(hidden_block.T, part, preferred_element_type=F32)
        for part in own_half_first(up_all, half_place)
    ]
    heavy_down_grad = heavy_down_half[0] + swap(heavy_down_half[1].astype(BF16), "dp", 1).astype(F32)
    x_group = lax.dynamic_slice_in_dim(x_all, high_place * group * block, group * block, 1)
    x_group = x_group.reshape(-1, group, block)
    x_group = jnp.take(x_group, jnp.arange(group) ^ low_place, axis=1).reshape(-1, group * block)
    gate_half, up_half = (
        jnp.dot(x_group.T, part, preferred_element_type=F32) for part in (gate_mine, up_mine)
    )
    kept = jnp.where(half_place == 0, gate_half, up_half)
    sent = jnp.where(half_place == 0, up_half, gate_half)
    kept = (kept + swap(sent.astype(BF16), "dp", 1).astype(F32)).reshape(group, block, groups, unit)
    pieces = [kept[0]]
    for place in range(1, group):
        pieces.append(swap(kept[place].astype(BF16), "seq", place).astype(F32))
    pieces = jnp.take(jnp.stack(pieces, axis=2), jnp.arange(group) ^ low_place, axis=2)
    heavy_gate_up_grad = pieces.reshape(block, ffn_heavy)

    mix_grad = matmul_t(middle_low, light_out).astype(BF16)
    mix_grad = mix_grad.reshape(row_count, seg_span, light_heads, DL)
    val_grad = jnp.einsum("rhqk,rqhd->rkhd", probs_low, mix_grad, preferred_element_type=F32)
    prob_grad = jnp.einsum("rqhd,rkhd->rhqk", mix_grad, val_ext, preferred_element_type=F32)
    delta = jnp.sum(probs_light * prob_grad, axis=-1, keepdims=True)
    score_grad = (probs_light * (prob_grad - delta)).astype(BF16)
    query_grad = jnp.einsum("rhqk,rkhd->rqhd", score_grad, key_ext, preferred_element_type=F32)
    key_grad = jnp.einsum("rhqk,rqhd->rkhd", score_grad, query_low, preferred_element_type=F32)
    query_grad = (query_grad * light_scale).reshape(row_count, seg_span, width).astype(BF16)
    kv_grad = jnp.concatenate(
        [
            (key_grad * light_scale).reshape(row_count, extent, width),
            val_grad.reshape(row_count, extent, width),
        ],
        axis=-1,
    ).astype(BF16)
    normed_grad_ext = matmul_t(kv_grad, light_qkv[:, width:])
    normed_grad = matmul_t(query_grad, light_qkv[:, :width])
    normed_grad = normed_grad + normed_grad_ext[:, RADIUS : RADIUS + seg_span]
    from_right = shifted(normed_grad_ext[:, :RADIUS].astype(BF16), "seq", -1)
    from_left = shifted(normed_grad_ext[:, seg_span + RADIUS :].astype(BF16), "seq", 1)
    normed_grad = normed_grad.at[:, :RADIUS].add(from_left.astype(F32))
    normed_grad = normed_grad.at[:, seg_span - RADIUS :].add(from_right.astype(F32))

    hq_all = matmul(query_all, heavy_q).astype(BF16)
    do2_all = matmul_t(proj_all, heavy_out).astype(BF16)
    mix_all, dhq_all, dhk_all, dhv_all = heavy_both(
        hq_all, keys_all, vals_all, query_seg, key_seg, do2_all
    )
    dhkv_all = jnp.concatenate([dhk_all, dhv_all], axis=-1)
    mine = lambda v: lax.dynamic_slice_in_dim(flat(v), me * block, block, 1).T
    heavy_grads = [
        own_half_first(jnp.dot(mine(left), flat(right), preferred_element_type=F32), half_place)
        for left, right in ((query_all, dhq_all), (key_all, dhkv_all), (mix_all, proj_all))
    ]
    heavy_kept = jnp.concatenate([pair[0] for pair in heavy_grads], axis=-1)
    heavy_sent = jnp.concatenate([pair[1] for pair in heavy_grads], axis=-1)
    heavy_sum = heavy_kept + swap(heavy_sent.astype(BF16), "dp", 1).astype(F32)
    heavy_half = heavy_width // 2
    heavy_q_grad = heavy_sum[:, :heavy_half]
    heavy_kv_grad = heavy_sum[:, heavy_half : 3 * heavy_half]
    heavy_out_grad = heavy_sum[:, 3 * heavy_half :]
    query_logit_grad = query_gate_grad * query_gate * (1.0 - query_gate)
    route_query_grad = jnp.sum(query_logit_grad[..., None] * query_normed, axis=(0, 1))
    query_rows_grad = (
        matmul_t(dhq_all[:, :routed_own], heavy_q) + query_logit_grad[..., None] * route_query_full
    )
    key_rows_grad = matmul_t(dhkv_all[:, :routed_own], heavy_kv)
    normed_grad = (
        normed_grad
        + place_rows(query_rows_grad, own_query, seg_span)
        + place_rows(key_rows_grad, own_key, seg_span)
    )
    attn_gain_grad = jnp.sum(normed_grad * hidden * factor_one, axis=(0, 1))
    hidden_norm_grad = norm_back(hidden, factor_one, attn_gain, normed_grad)
    grad_tokens = (middle_grad + hidden_norm_grad).astype(BF16)

    own_slots = slot_columns(flat(normed_low), me, devices).T
    ext_slots = slot_columns(flat(normed_ext_low), me, devices).T
    qkv_grad = jnp.concatenate(
        [
            jnp.dot(own_slots, flat(query_grad), preferred_element_type=F32),
            jnp.dot(ext_slots, flat(kv_grad), preferred_element_type=F32),
        ],
        axis=-1,
    )
    second_sum = scatter_sum(
        jnp.concatenate(
            [
                slot_block(own_half_first(qkv_grad, half_place), devices),
                slot_vectors((attn_gain_grad, route_query_grad), me, devices),
            ],
            axis=2,
        )
    )
    qkv_cols = light_qkv.shape[1] // 2
    qkv_rows = block * qkv_cols // LANES
    light_qkv_grad = unslot(second_sum[:qkv_rows], qkv_cols)
    attn_gain_grad = second_sum[qkv_rows:, 0]
    route_query_grad = second_sum[qkv_rows:, 1]
    return (
        outputs,
        grad_tokens,
        attn_gain_grad,
        light_qkv_grad,
        light_out_grad,
        heavy_q_grad,
        heavy_kv_grad,
        heavy_out_grad,
        route_query_grad,
        ffn_gain_grad,
        light_gate_up_grad,
        light_down_grad,
        heavy_gate_up_grad,
        heavy_down_grad,
        route_ffn_grad,
        rms_stats,
    )


VMEM = pl.BlockSpec(memory_space=pltpu.VMEM)
SMEM = pl.BlockSpec(memory_space=pltpu.SMEM)
ANY = pl.BlockSpec(memory_space=pl.ANY)
HBM = pl.BlockSpec(memory_space=pltpu.HBM)
GELU_RATE = math.sqrt(2.0 / math.pi)
GELU_CUBE = 0.044715
MIB = 1024 * 1024
FIRST_CUTS = 4
SECOND_CUTS = 2


def shape(dims, dtype):
    return jax.ShapeDtypeStruct(dims, dtype)


def call(kernel, outs, ins, smem=0, scratch=(), micros=1, mib=16, after=(), hbm=0):
    used = len(ins)

    def body(*refs):
        kernel(*refs[:used], *refs[used + len(after) :])

    return pl.pallas_call(
        body,
        out_shape=outs,
        in_specs=[HBM] * hbm + [SMEM] * smem + [VMEM] * (used - smem - hbm) + [ANY] * len(after),
        out_specs=[VMEM] * len(outs),
        scratch_shapes=list(scratch),
        compiler_params=pltpu.CompilerParams(vmem_limit_bytes=mib * MIB),
        cost_estimate=cost(micros),
    )(*ins, *after)


def cost(micros):
    return pl.CostEstimate(flops=int(micros * 10**9), bytes_accessed=10**6, transcendentals=0)


def dot(left, right):
    return jnp.dot(left, right, preferred_element_type=F32)


def dot_t(left, right):
    return lax.dot_general(left, right, (((1,), (1,)), ((), ())), preferred_element_type=F32)


def t_dot(left, right):
    return lax.dot_general(left, right, (((0,), (0,)), ((), ())), preferred_element_type=F32)


def row_factor(value):
    return lax.rsqrt(jnp.mean(value * value, axis=-1, keepdims=True) + EPSILON)


def as_column(row):
    count = row.shape[1]
    down = lax.broadcasted_iota(jnp.int32, (count, count), 0)
    along = lax.broadcasted_iota(jnp.int32, (count, count), 1)
    return jnp.sum(jnp.where(down == along, row, 0.0), axis=1, keepdims=True)


def head_window(head, size):
    first = head * size // LANES * LANES
    lanes = (head * size + size - 1) // LANES * LANES + LANES - first
    place = lax.broadcasted_iota(jnp.int32, (1, lanes), 1) + first
    return first, lanes, (place >= head * size) & (place < head * size + size)


def slot_owners(me, bits):
    owners = []
    for p in range(1 << len(bits)):
        flips = sum(bit for k, bit in enumerate(bits) if p >> (len(bits) - 1 - k) & 1)
        owners.append(flips ^ me)
    return owners


def slot_select(width, bits, me):
    block = width >> len(bits)
    along = lax.broadcasted_iota(jnp.int32, (block, width), 1)
    inside = lax.broadcasted_iota(jnp.int32, (block, width), 0)
    rows = [(along == inside + owner * block).astype(F32) for owner in slot_owners(me, bits)]
    return jnp.concatenate(rows, axis=0).astype(BF16)


def two_gelu(value):
    square = value * value
    bend = jnp.tanh(GELU_RATE * value * (1.0 + GELU_CUBE * square))
    half = 0.5 * (1.0 + bend)
    slope = half + 0.5 * value * (1.0 - bend * bend) * GELU_RATE * (1.0 + 3.0 * GELU_CUBE * square)
    return value * half, slope


def first_kernel(
    routed, route_in, segs_in, tokens_in, gain_in, ffn_gain_in, route_q_in, route_f_in,
    keys, upper, lower, table,
    route, seg_at, segs, tokens, gain, ffn_gain, route_q, route_f, normed, picked, sems,
):
    copies = [
        pltpu.make_async_copy(source, target, sems.at[k])
        for k, (source, target) in enumerate(
            (
                (tokens_in, tokens),
                (gain_in, gain),
                (route_in, route),
                (segs_in, seg_at),
                (segs_in, segs),
                (ffn_gain_in, ffn_gain),
                (route_q_in, route_q),
                (route_f_in, route_f),
            )
        )
    ]
    for copy in copies:
        copy.start()
    for copy in copies:
        copy.wait()
    rows, span, width = tokens.shape
    me = lax.axis_index("seq")
    for k, vector in enumerate((gain, ffn_gain, route_q, route_f)):
        table[k : k + 1, :] = vector[...].astype(F32).reshape(1, width)
    hidden = tokens[...].reshape(rows * span, width).astype(F32)
    normed[...] = hidden * row_factor(hidden) * table[0:1, :]
    for r in range(rows):
        for k in range(routed):
            place = route[r, me * routed + k] - me * span
            at = pl.ds(r * routed + k, 1)
            picked[at, :width] = normed[pl.ds(r * span + place, 1), :]
            picked[at, width:] = jnp.full((1, LANES), (seg_at[r, place] + 2).astype(F32))
    keys[...] = picked[...].astype(BF16).reshape(keys.shape)
    marks = (segs[...] + 2).astype(F32)
    for out, start in ((upper, span - RADIUS), (lower, 0)):
        out[:, :RADIUS, :] = tokens[:, start : start + RADIUS, :]
        out[:, RADIUS:, :] = jnp.zeros((rows, 16, width), BF16)
        for r in range(rows):
            out[r, RADIUS:, :span] = jnp.broadcast_to(marks[r : r + 1], (16, span)).astype(BF16)


def light_kernel(
    before, tokens, after, segs, table, w_qkv, w_out,
    normed, query, keyval, probs, mix, attn, seg_row, mix_t,
):
    rows, span, width = tokens.shape
    extent = span + 2 * RADIUS
    own_all = rows * span
    heads = width // DL
    places = []
    for r in range(rows):
        places.append((tokens, r, span, r * span, r * extent + RADIUS))
    for r in range(rows):
        rim = own_all + 2 * r * RADIUS
        places.append((before, r, RADIUS, rim, r * extent))
        places.append((after, r, RADIUS, rim + RADIUS, r * extent + RADIUS + span))
    for part, r, size, at, _ in places:
        value = part[r, :size, :].astype(F32)
        normed[at : at + size, :] = (value * row_factor(value) * table[0:1, :]).astype(BF16)
    made = dot(normed[...], w_qkv[:, width:]).astype(BF16)
    for _, _, size, at, to in places:
        keyval[to : to + size, :] = made[at : at + size]
    query[...] = dot(normed[:own_all, :], w_qkv[:, :width]).astype(BF16)
    down = lax.broadcasted_iota(jnp.int32, (extent, span), 0)
    along = lax.broadcasted_iota(jnp.int32, (extent, span), 1)
    near = jnp.abs(along - down + RADIUS) <= RADIUS
    for r in range(rows):
        marks = (segs[r : r + 1, :] + 2).astype(F32)
        seg_row[:, :span] = before[r, RADIUS:, :span].astype(F32)[:8]
        seg_row[:, span : 2 * span] = jnp.broadcast_to(marks, (8, span))
        seg_row[:, 2 * span :] = after[r, RADIUS:, :span].astype(F32)[:8]
        columns = [as_column(seg_row[0:1, c * span : (c + 1) * span]) for c in range(3)]
        key_marks = jnp.concatenate([columns[0][span - RADIUS :], columns[1], columns[2][:RADIUS]], axis=0)
        allowed = near & (key_marks == marks)
        key_rows = slice(r * extent, (r + 1) * extent)
        val_t = keyval[key_rows, width:].T
        for h in range(heads):
            first, lanes, mask = head_window(h, DL)
            window = slice(first, first + lanes)
            q_head = jnp.where(mask, query[r * span : (r + 1) * span, window], 0)
            scores = dot_t(keyval[key_rows, window], q_head)
            scores = jnp.where(allowed, scores * (1.0 / math.sqrt(DL)), NEG_FILL)
            numer = jnp.exp(scores - jnp.max(scores, axis=0, keepdims=True))
            share = (numer / jnp.sum(numer, axis=0, keepdims=True)).astype(BF16)
            probs[r * heads + h] = share
            mix_t[h * DL : (h + 1) * DL, :] = dot(val_t[h * DL : (h + 1) * DL, :], share)
        mix[r * span : (r + 1) * span, :] = mix_t[...].T.astype(BF16)
    attn[...] = dot(mix[...], w_out[...])


def stat_row(value):
    total = jnp.sum(jnp.sum(value, axis=0, keepdims=True), axis=1, keepdims=True)
    return jnp.broadcast_to(total, (1, LANES))


def valid_column(segs):
    rows = segs.shape[0]
    parts = [as_column((segs[r : r + 1, :] >= 0).astype(F32)) for r in range(rows)]
    return jnp.concatenate(parts, axis=0)


def router(rows, weights):
    return jax.nn.sigmoid(jnp.sum(rows[...] * weights, axis=-1, keepdims=True))


def gathered(refs, row, lanes):
    value = jnp.concatenate([ref[:, row, :, lanes] for ref in refs], axis=0)
    return value.reshape(-1, value.shape[-1])


def middle_kernel(routed, parts, q_route, f_route, seg_at, tokens, segs, *refs):
    keys, refs = refs[:parts], refs[parts:]
    attn, upstream, table, w_q, w_kv, w_out = refs[:6]
    middle, normed_two, keyval, payload, q_rows, f_rows, f_up, proj, f_marks, stats = refs[6:16]
    full, marks, placed = refs[16:]
    rows, span, width = tokens.shape
    me = lax.axis_index("seq")
    hidden = tokens[...].reshape(rows * span, width).astype(F32)
    full[...] = hidden * row_factor(hidden) * table[0:1, :]
    for r in range(rows):
        for k in range(routed):
            at = pl.ds(r * routed + k, 1)
            place = q_route[r, me * routed + k] - me * span
            q_rows[at, :] = full[pl.ds(r * span + place, 1), :]
            marks[at, :] = jnp.full((1, LANES), (seg_at[r, place] + 2).astype(F32))
            place = f_route[r, k] - me * span
            f_marks[at, :] = jnp.full((1, LANES), (seg_at[r, place] + 2).astype(F32))
    q_low = q_rows[...].astype(BF16)
    payload[:, :, 2 * width : 3 * width] = q_low.reshape(rows, routed, width)
    payload[:, :, 3 * width :] = marks[...].astype(BF16).reshape(rows, routed, LANES)
    key_low = jnp.concatenate([gathered(keys, r, slice(0, width)) for r in range(rows)], axis=0)
    keyval[...] = dot(key_low, w_kv[...]).astype(BF16).reshape(keyval.shape)
    query = dot(q_low, w_q[...]).astype(BF16)
    heads = width // DH
    lane = lax.broadcasted_iota(jnp.int32, (1, width), 1)
    masks = [(lane >= h * DH) & (lane < (h + 1) * DH) for h in range(heads)]
    mixed = []
    for r in range(rows):
        mine = query[r * routed : (r + 1) * routed]
        wide = jnp.concatenate([jnp.where(m, mine, 0) for m in masks], axis=0)
        scores = dot_t(wide, keyval[r, :, :width]) * (1.0 / math.sqrt(DH))
        key_marks = gathered(keys, r, slice(width, width + LANES)).astype(F32).T[0:1, :]
        query_marks = jnp.concatenate([marks[r * routed : (r + 1) * routed, 0:1]] * heads, axis=0)
        scores = jnp.where(query_marks == key_marks, scores, NEG_FILL)
        peak = jnp.maximum(jnp.max(scores, axis=-1, keepdims=True), 0.0)
        numer = jnp.exp(scores - peak)
        share = numer / (jnp.exp(-peak) + jnp.sum(numer, axis=-1, keepdims=True))
        part = dot(share.astype(BF16), keyval[r, :, width:])
        total = jnp.zeros((routed, width), F32)
        for h in range(heads):
            total = total + jnp.where(masks[h], part[h * routed : (h + 1) * routed], 0.0)
        mixed.append(total)
    mixed = jnp.concatenate(mixed, axis=0).astype(BF16)
    proj[...] = dot(mixed, w_out[...])
    placed[...] = router(q_rows, table[2:3, :]) * proj[...]
    light = attn[...]
    middle[...] = hidden + light
    for r in range(rows):
        for k in range(routed):
            place = q_route[r, me * routed + k] - me * span
            at = pl.ds(r * span + place, 1)
            middle[at, :] = middle[at, :] + placed[pl.ds(r * routed + k, 1), :]
    valid = valid_column(segs)
    stats[...] = jnp.zeros(stats.shape, F32)
    stats[0:1, :] = stat_row(valid * hidden * hidden)
    stats[1:2, :] = stat_row(valid * light * light)
    stats[2:3, :] = stat_row(jnp.where(marks[:, 0:1] >= 2.0, placed[...] * placed[...], 0.0))
    stats[5:6, :] = stat_row(valid)
    mid = middle[...]
    full[...] = mid * row_factor(mid) * table[1:2, :]
    normed_two[...] = full[...].astype(BF16)
    for r in range(rows):
        for k in range(routed):
            place = f_route[r, k] - me * span
            f_rows[pl.ds(r * routed + k, 1), :] = full[pl.ds(r * span + place, 1), :]
    full[...] = upstream[...].reshape(rows * span, width).astype(F32)
    for r in range(rows):
        for k in range(routed):
            place = f_route[r, k] - me * span
            f_up[pl.ds(r * routed + k, 1), :] = full[pl.ds(r * span + place, 1), :]
    f_low = (router(f_rows, table[3:4, :]) * f_up[...]).astype(BF16)
    payload[:, :, :width] = f_rows[...].astype(BF16).reshape(rows, routed, width)
    payload[:, :, width : 2 * width] = f_low.reshape(rows, routed, width)


def glu_parts(inputs, back_in, gate_w, up_w, down_w):
    act, slope = two_gelu(dot(inputs, gate_w))
    lift = dot(inputs, up_w)
    back = dot_t(back_in, down_w)
    hidden = (act * lift).astype(BF16)
    return hidden, (back * lift * slope).astype(BF16), (back * act).astype(BF16)


def three_parts(value):
    high = value.astype(BF16).astype(F32)
    middle = (value - high).astype(BF16).astype(F32)
    return high, middle, value - high - middle


def light_ffn_kernel(normed_two, upstream, w_gate_up, w_down, z_light, d_light, hidden_out, grad_gate, grad_up):
    width = normed_two.shape[1]
    inner = w_down.shape[0]
    back_in = upstream[...].reshape(-1, width)
    unit = 256
    for at in range(0, inner, unit):
        part = slice(at, at + unit)
        gate_w, up_w = w_gate_up[:, part], w_gate_up[:, inner + at : inner + at + unit]
        hidden, d_gate, d_up = glu_parts(normed_two[...], back_in, gate_w, up_w, w_down[part, :])
        hidden_out[:, part] = hidden
        grad_gate[:, part] = d_gate
        grad_up[:, part] = d_up
    z_light[...] = dot(hidden_out[...], w_down[...])
    d_light[...] = dot_t(grad_gate[...], w_gate_up[:, :inner]) + dot_t(grad_up[...], w_gate_up[:, inner:])


def pass_share(step_refs, share_refs, me, group):
    gate, up, down = step_refs
    gate_out, up_out, down_out = share_refs
    unit = gate_out.shape[2]
    at = pl.ds(pl.multiple_of(lax.rem(me, group) * unit, unit), unit)
    gate_out[0] = gate[:, at]
    up_out[0] = up[:, at]
    down_out[0] = down[at, :]


def heavy_steps(step, sums_in, h_gate, h_up, h_down, f_rows, f_up, table, z_heavy, d_heavy):
    @pl.when(step == 0)
    def _():
        for total, value in zip((z_heavy, d_heavy), sums_in):
            total[...] = value

    f_gate = router(f_rows, table[3:4, :])
    f_low = (f_gate * f_up[...]).astype(BF16)
    f_in = f_rows[...].astype(BF16)
    hidden, d_gate, d_up = glu_parts(f_in, f_low, h_gate[...], h_up[...], h_down[...])
    z_heavy[...] += dot(hidden, h_down[...])
    d_heavy[...] += dot_t(d_gate, h_gate[...]) + dot_t(d_up, h_up[...])
    return f_gate


def ffn_first_kernel(
    group, h_gate, h_up, h_down, f_rows, f_up, table, z_heavy, d_heavy, gate_out, up_out, down_out
):
    zero = jnp.zeros(z_heavy.shape, F32)
    heavy_steps(pl.program_id(0), (zero, zero), h_gate, h_up, h_down, f_rows, f_up, table, z_heavy, d_heavy)
    pass_share((h_gate, h_up, h_down), (gate_out, up_out, down_out), lax.axis_index("seq"), group)


def ffn_last_kernel(
    routed, group, q_route, f_route, h_gate, h_up, h_down, z_in, d_in, upstream, middle, z_light, d_light_in,
    q_rows, f_rows, f_up, proj, f_marks, table, stats, segs,
    outputs, dmid, dmid_low, payload, vectors, gate_out, up_out, down_out,
    z_heavy, d_heavy, placed, full, d_light,
):
    step = pl.program_id(0)
    width = middle.shape[1]
    rows, span = segs.shape
    me = lax.axis_index("seq")
    f_gate = heavy_steps(
        step, (z_in[...], d_in[...]), h_gate, h_up, h_down, f_rows, f_up, table, z_heavy, d_heavy
    )
    pass_share((h_gate, h_up, h_down), (gate_out, up_out, down_out), me, group)

    @pl.when(step == pl.num_programs(0) - 1)
    def _():
        mid = middle[...]
        d_light[...] = d_light_in[...]
        placed[...] = f_gate * z_heavy[...]
        full[...] = mid + z_light[...]
        logit = jnp.sum(f_up[...] * z_heavy[...], axis=-1, keepdims=True) * f_gate * (1.0 - f_gate)
        d_heavy[...] += logit * table[3:4, :]
        for r in range(rows):
            for k in range(routed):
                place = f_route[r, k] - me * span
                at, source = pl.ds(r * span + place, 1), pl.ds(r * routed + k, 1)
                full[at, :] = full[at, :] + placed[source, :]
                d_light[at, :] = d_light[at, :] + d_heavy[source, :]
        outputs[...] = full[...].astype(BF16).reshape(outputs.shape)
        factor = row_factor(mid)
        d_norm = d_light[...]
        vectors[...] = jnp.zeros(vectors.shape, F32)
        vectors[0:1, :] = jnp.sum(d_norm * mid * factor, axis=0, keepdims=True)
        vectors[1:2, :] = jnp.sum(logit * f_rows[...], axis=0, keepdims=True)
        weighted = d_norm * table[1:2, :]
        inner = jnp.mean(weighted * mid, axis=-1, keepdims=True)
        total = upstream[...].reshape(rows * span, width).astype(F32) + factor * weighted - mid * (factor * factor * factor) * inner
        dmid[...] = total
        dmid_low[...] = total.astype(BF16)
        sums = stats[...]
        place = lax.broadcasted_iota(jnp.int32, sums.shape, 0)
        lane = lax.broadcasted_iota(jnp.int32, sums.shape, 1)
        light_sum = stat_row(valid_column(segs) * z_light[...] * z_light[...])
        heavy_sum = stat_row(jnp.where(f_marks[:, 0:1] >= 2.0, placed[...] * placed[...], 0.0))
        sums = jnp.where(place == 3, light_sum, jnp.where(place == 4, heavy_sum, sums))
        lanes = jnp.zeros(sums.shape, F32)
        for k, part in enumerate(three_parts(sums)):
            lanes = lanes + jnp.where(lane == place + 8 * k, part, 0.0)
        lanes = jnp.sum(lanes, axis=0, keepdims=True)
        full[...] = total
        for r in range(rows):
            for k in range(routed):
                place = q_route[r, me * routed + k] - me * span
                placed[pl.ds(r * routed + k, 1), :] = full[pl.ds(r * span + place, 1), :]
        q_gate = router(q_rows, table[2:3, :])
        logit = jnp.sum(placed[...] * proj[...], axis=-1, keepdims=True) * q_gate * (1.0 - q_gate)
        payload[:, :, :width] = (q_gate * placed[...]).astype(BF16).reshape(rows, routed, width)
        lane = lax.broadcasted_iota(jnp.int32, (rows * routed, LANES), 1)
        extra = jnp.broadcast_to(lanes, (rows * routed, LANES))
        for k, part in enumerate(three_parts(logit)):
            extra = jnp.where(lane == 24 + k, part, extra)
        payload[:, :, width:] = extra.astype(BF16).reshape(rows, routed, LANES)


def halves_of(value, place):
    half = value.shape[-1] // 2
    first, second = value[..., :half], value[..., half:]
    return jnp.where(place == 0, first, second), jnp.where(place == 0, second, first)


def store_slots(outs, place, base, grads):
    each = outs[0].shape[0]
    block = grads.shape[0] // (each * len(outs))
    low = grads.astype(BF16)
    for c in range(grads.shape[1] // LANES):
        for p in range(each * len(outs)):
            part = low[p * block : (p + 1) * block, c * LANES : (c + 1) * LANES]
            outs[p // each][p % each, place, pl.ds(base + c * block, block), :] = part
    return base + grads.shape[1] // LANES * block


def store_vectors(outs, base, select, vectors):
    width = vectors.shape[1]
    count = outs[0].shape[0] * len(outs)
    table = jnp.concatenate([vectors, jnp.zeros((16 - vectors.shape[0], width), F32)], axis=0)
    table = dot_t(table.astype(BF16), select)
    each = outs[0].shape[0]
    for p in range(count):
        part = pltpu.roll(table, (width - p * (width // count)) % width, 1)[:, :LANES].astype(BF16)
        for half in range(2):
            outs[p // each][p % each, half, base : base + 16, :] = part


def loop_slots(outs, base, left, right, lanes, half_of):
    block = left.shape[0] // (outs[0].shape[0] * len(outs))

    def chunk(i, carry):
        grads = dot(left[...], right[:, pl.ds(pl.multiple_of(i * lanes, lanes), lanes)])
        half, at = half_of(i)
        store_slots(outs, half, pl.multiple_of(base + at * (block * lanes // LANES), 16), grads)
        return carry

    lax.fori_loop(0, right.shape[1] // lanes, chunk, 0)


def first_grads_kernel(bits, normed_two, grad_gate, grad_up, hidden, upstream, *refs):
    outs, (inputs_t, hidden_t, back_in) = refs[:-3], refs[-3:]
    width = normed_two.shape[1]
    me = lax.axis_index("seq")
    place = lax.axis_index("dp")
    inputs_t[...] = dot_t(slot_select(width, bits, me), normed_two[...]).astype(BF16)
    loop_slots(outs, 0, inputs_t, grad_gate, 256, lambda i: (place, i))
    loop_slots(outs, 0, inputs_t, grad_up, 256, lambda i: (1 - place, i))
    hidden_t[...] = dot_t(slot_select(hidden.shape[1], bits, me), hidden[...]).astype(BF16)
    back_in[...] = upstream[...].reshape(-1, width)
    base = grad_gate.shape[1] // LANES * (width >> len(bits))
    loop_slots(outs, base, hidden_t, back_in, width // 2, lambda i: (i ^ place, 0))


def light_back_kernel(
    bits, dmid_low, query, keyval, probs, normed, mix, vectors, table, w_qkv, w_out,
    dnorm, to_right, to_left, *refs,
):
    outs, (dq, dkv, d_row, dq_t, select, inputs_t) = refs[:-6], refs[-6:]
    rows, rim, width = to_right.shape
    span = dmid_low.shape[0] // rows
    extent = span + 2 * rim
    own_all = rows * span
    heads = width // DL
    scale = 1.0 / math.sqrt(DL)
    place = lax.axis_index("dp")
    mix_grad = dot_t(dmid_low[...], w_out[...]).astype(BF16)
    for r in range(rows):
        key_rows = slice(r * extent, (r + 1) * extent)
        own_rows = slice(r * span, (r + 1) * span)
        key_t = keyval[key_rows, :width].T
        d_row[...] = jnp.zeros(d_row.shape, F32)
        for h in range(heads):
            first, lanes, mask = head_window(h, DL)
            window = slice(first, first + lanes)
            v_window = slice(width + first, width + first + lanes)
            q_head = jnp.where(mask, query[own_rows, window], 0)
            g_head = jnp.where(mask, mix_grad[own_rows, window], 0)
            share = probs[r * heads + h]
            full_share = share.astype(F32)
            prob_grad = dot_t(keyval[key_rows, v_window], g_head)
            delta = jnp.sum(full_share * prob_grad, axis=0, keepdims=True)
            score_grad = (full_share * (prob_grad - delta)).astype(BF16)
            d_row[:, window] += dot(score_grad, q_head)
            d_row[:, v_window] += dot(share, g_head)
            dq_t[h * DL : (h + 1) * DL, :] = dot(key_t[h * DL : (h + 1) * DL, :], score_grad)
        dq[own_rows, :] = (dq_t[...].T * scale).astype(BF16)
        rim_at = own_all + 2 * r * rim
        for size, at, to in ((span, rim, r * span), (rim, 0, rim_at), (rim, rim + span, rim_at + rim)):
            dkv[to : to + size, :width] = (d_row[at : at + size, :width] * scale).astype(BF16)
            dkv[to : to + size, width:] = d_row[at : at + size, width:].astype(BF16)
    d_rim = dot_t(dkv[own_all:, :], w_qkv[:, width:])
    dnorm[...] = dot_t(dq[...], w_qkv[:, :width]) + dot_t(dkv[:own_all, :], w_qkv[:, width:])
    gain_grad = jnp.sum(dnorm[...] * normed[:own_all, :].astype(F32), axis=0, keepdims=True)
    gain_grad = gain_grad + jnp.sum(d_rim * normed[own_all:, :].astype(F32), axis=0, keepdims=True)
    gain_grad = gain_grad / table[0:1, :]
    for r in range(rows):
        to_left[r] = d_rim[2 * r * rim : (2 * r + 1) * rim].astype(BF16)
        to_right[r] = d_rim[(2 * r + 1) * rim : (2 * r + 2) * rim].astype(BF16)
    half = width // 2
    select[...] = slot_select(width, bits, lax.axis_index("seq"))
    inputs_t[...] = dot_t(select[...], normed[...]).astype(BF16)
    base = store_slots(outs, place, 0, dot(inputs_t[:, :own_all], dq[...]))
    grads = dot(inputs_t[...], dkv[:, :width])
    base = store_slots(outs, place, base, grads[:, :half])
    base_two = store_slots(outs, 1 - place, 0, grads[:, half:])
    store_slots(outs, 1 - place, base_two, dot(inputs_t[...], dkv[:, width:]))
    grads = dot(dot_t(select[...], mix[...]).astype(BF16), dmid_low[...])
    base_two = store_slots(outs, place, base, grads[:, :half])
    store_slots(outs, 1 - place, base, grads[:, half:])
    line = lax.broadcasted_iota(jnp.int32, (8, width), 0)
    store_vectors(outs, base_two, select[...], jnp.where(line == 2, gain_grad, vectors[...]))
    base = base_two + 16
    for out in outs:
        out[:, :, base:, :] = jnp.zeros((out.shape[0], 2, out.shape[2] - base, LANES), BF16)


def heavy_ffn_kernel(parts, *refs):
    blocks, weights, (kept, sent) = refs[:parts], refs[parts:-2], refs[-2:]
    halves = [weights[k : k + 3] for k in range(0, len(weights), 3)]
    each, width, unit = halves[0][0].shape
    devices = lax.axis_size("seq")
    group = devices // (each * len(halves))
    me = lax.axis_index("seq")
    place = lax.axis_index("dp")
    low_place = lax.rem(me, group)
    high_place = lax.div(me, group)
    rows = range(blocks[0].shape[1])
    inputs = jnp.concatenate([gathered(blocks, r, slice(0, width)) for r in rows], axis=0)
    back_in = jnp.concatenate([gathered(blocks, r, slice(width, 2 * width)) for r in rows], axis=0)
    block = width // devices
    along = lax.broadcasted_iota(jnp.int32, (block, width), 1)
    inside = lax.broadcasted_iota(jnp.int32, (block, width), 0)
    picks = []
    for j in range(group):
        owner = high_place * group + (low_place ^ j)
        picks.append((along == inside + owner * block).astype(F32))
    picked = dot_t(jnp.concatenate(picks, axis=0).astype(BF16), inputs).astype(BF16)
    count = group * block

    def share(at, z, half):
        gate_w, up_w, down_w = (ref[at] for ref in halves[half])
        hidden, d_gate, d_up = glu_parts(inputs, back_in, gate_w, up_w, down_w)
        lanes = pl.ds(pl.multiple_of(z * unit, unit), unit)
        kept[:count, lanes] = dot(picked, jnp.where(place == 0, d_gate, d_up))
        sent[:count, lanes] = dot(picked, jnp.where(place == 0, d_up, d_gate)).astype(BF16)

        @pl.when(z == high_place)
        def _():
            hidden_t = hidden.T
            for out, part in zip((kept, sent), halves_of(back_in, place)):
                grad = dot(hidden_t, part).astype(out.dtype)
                size = grad.shape[1]
                out[count:, :size] = grad[: unit // 2]
                out[count:, size : 2 * size] = grad[unit // 2 :]
                out[count:, 2 * size :] = jnp.zeros((unit // 2, out.shape[1] - 2 * size), out.dtype)

    for half in range(len(halves)):

        def one(at, carry, half=half):
            share(at, half * each + at, half)
            return carry

        lax.fori_loop(0, each, one, 0)


def heavy_row_kernel(routed, counts, *refs):
    lists = []
    for count in counts:
        lists.append(refs[:count])
        refs = refs[count:]
    routed_parts, proj_parts, key_parts = lists
    keyval, table, w_q, w_kv, w_out, grads, parts, sums, sent, mix_t, dq_t, dkv = refs
    width = w_q.shape[0]
    scale = 1.0 / math.sqrt(DH)
    me = lax.axis_index("seq")
    r = lax.rem(me, 2)
    block = width // lax.axis_size("seq")
    along = lax.broadcasted_iota(jnp.int32, (block, width), 1)
    inside = lax.broadcasted_iota(jnp.int32, (block, width), 0)
    own = [(along == inside + at * block).astype(F32) for at in (me, me ^ 1)]
    own = jnp.concatenate(own, axis=0).astype(BF16)
    in_q = gathered(routed_parts, r, slice(2 * width, 3 * width))
    in_k = gathered(key_parts, r, slice(0, width))
    q_marks = gathered(routed_parts, r, slice(3 * width, 3 * width + LANES)).astype(F32).T[0:1, :]
    k_marks = gathered(key_parts, r, slice(width, width + LANES)).astype(F32)[:, 0:1]
    allowed = k_marks == q_marks
    grad_in = gathered(proj_parts, r, slice(0, width))
    extra = gathered(proj_parts, r, slice(width, width + LANES)).astype(F32)
    sums[...] = jnp.broadcast_to(
        sum(jnp.sum(ref[:, 0, :, width:].astype(F32), axis=0) for ref in proj_parts)[0:1], sums.shape
    )
    query = dot(in_q, w_q[...]).astype(BF16)
    mix_grad = dot_t(grad_in, w_out[...]).astype(BF16)
    key_t = keyval[r, :, :width].T
    val_t = keyval[r, :, width:].T
    lane = lax.broadcasted_iota(jnp.int32, (1, LANES), 1)
    for first in range(0, width, LANES):
        window = slice(first, first + LANES)
        v_window = slice(width + first, width + first + LANES)
        keys_w, vals_w = keyval[r, :, window], keyval[r, :, v_window]
        dk, dv = None, None
        for h in range(first // DH, (first + LANES) // DH):
            mask = (lane + first >= h * DH) & (lane + first < (h + 1) * DH)
            q_head = jnp.where(mask, query[:, window], 0)
            g_head = jnp.where(mask, mix_grad[:, window], 0)
            scores = jnp.where(allowed, dot_t(keys_w, q_head) * scale, NEG_FILL)
            peak = jnp.maximum(jnp.max(scores, axis=0, keepdims=True), 0.0)
            numer = jnp.exp(scores - peak)
            share = numer / (jnp.exp(-peak) + jnp.sum(numer, axis=0, keepdims=True))
            share_low = share.astype(BF16)
            prob_grad = dot_t(vals_w, g_head)
            delta = jnp.sum(share * prob_grad, axis=0, keepdims=True)
            score_grad = (share * (prob_grad - delta)).astype(BF16)
            at = slice(h * DH, (h + 1) * DH)
            mix_t[at, :] = dot(val_t[at, :], share_low).astype(BF16)
            dq_t[at, :] = dot(key_t[at, :], score_grad)
            part_k, part_v = dot(score_grad, q_head), dot(share_low, g_head)
            dk, dv = (part_k, part_v) if dk is None else (dk + part_k, dv + part_v)
        dkv[:, window] = (dk * scale).astype(BF16)
        dkv[:, v_window] = dv.astype(BF16)
    dq = (dq_t[...].T * scale).astype(BF16)
    in_q_t = dot_t(own, in_q)
    logits = jnp.sum(jnp.where((lane >= 24) & (lane < 27), extra, 0.0), axis=1, keepdims=True)
    logit_row = jnp.sum(extra.T[24:27, :], axis=0, keepdims=True)
    at = 0
    for grad in (
        dot(in_q_t.astype(BF16), dq),
        dot(dot_t(own, in_k).astype(BF16), dkv[...]),
        dot(dot(own, mix_t[...]).astype(BF16), grad_in),
        jnp.broadcast_to(jnp.sum(in_q_t * logit_row, axis=1, keepdims=True), (2 * block, LANES)),
    ):
        lanes = slice(at, at + grad.shape[1])
        grads[:, lanes] = grad[:block]
        sent[:block, lanes] = grad[block:].astype(BF16)
        at += grad.shape[1]
    half = dq.shape[0] // 2
    ours = lambda v: jnp.concatenate([v[:routed], v[half : half + routed]], axis=0)
    q_part = dot_t(ours(dq), w_q[...]) + ours(logits) * table[2:3, :]
    k_part = dot_t(ours(dkv), w_kv[...])
    for k, part in enumerate((q_part, k_part)):
        parts[k] = part[:routed]
        sent[block:, k * width : (k + 1) * width] = part[routed:].astype(BF16)
    sent[block:, 2 * width :] = jnp.zeros((routed, sent.shape[1] - 2 * width), BF16)


def heavy_last_kernel(
    routed, q_route, k_route, grads_in, parts_in, sums_in, got, dnorm, from_left, from_right, dmid, tokens, table,
    w_q, w_kv, grad_tokens, kept, sent, total, parts,
):
    rows, span, width = tokens.shape
    me = lax.axis_index("seq")
    place = lax.axis_index("dp")
    block = width // lax.axis_size("seq")
    grads = grads_in[...] + got[:block, :].astype(F32)
    for k in range(2):
        parts[lax.rem(me, 2), k] = parts_in[k]
        parts[1 - lax.rem(me, 2), k] = got[block:, k * width : (k + 1) * width].astype(F32)
    for r in range(rows):
        at = r * span
        total[at : at + span, :] = dnorm[at : at + span, :]
        total[at : at + RADIUS, :] += from_left[r].astype(F32)
        total[at + span - RADIUS : at + span, :] += from_right[r].astype(F32)
        for k in range(routed):
            for which, route in enumerate((q_route, k_route)):
                spot = route[r, me * routed + k] - me * span
                row = pl.ds(at + spot, 1)
                total[row, :] = total[row, :] + parts[r, which, k : k + 1, :]
    hidden = tokens[...].reshape(rows * span, width).astype(F32)
    factor = row_factor(hidden)
    weighted = total[...] * table[0:1, :]
    inner = jnp.mean(weighted * hidden, axis=-1, keepdims=True)
    d_hidden = dmid[...] + factor * weighted - hidden * (factor * factor * factor) * inner
    grad_tokens[...] = d_hidden.astype(BF16).reshape(grad_tokens.shape)
    along = lax.broadcasted_iota(jnp.int32, (block, width), 1)
    inside = lax.broadcasted_iota(jnp.int32, (block, width), 0)
    own_full = (along == inside + me * block).astype(F32)
    own = own_full.astype(BF16)
    own_gain = jnp.sum(own_full * table[0:1, :], axis=1, keepdims=True)
    own_route = jnp.sum(own_full * table[2:3, :], axis=1, keepdims=True)
    route_grad = grads[:, 4 * width : 4 * width + 1]
    gain_grad = jnp.sum(dot(own, w_q[...]) * grads[:, :width], axis=1, keepdims=True)
    gain_grad = gain_grad + jnp.sum(dot(own, w_kv[...]) * grads[:, width : 3 * width], axis=1, keepdims=True)
    gain_grad = (gain_grad + own_route * route_grad) / own_gain
    lane = lax.broadcasted_iota(jnp.int32, (block, LANES), 1)
    sums = sums_in[...]
    sums = sums + pltpu.roll(sums, LANES - 8, 1) + pltpu.roll(sums, LANES - 16, 1)
    sums = jnp.where(lane[:8] < 8, sums, 0.0)
    vectors = jnp.where(lane == 0, gain_grad, jnp.where(lane == 1, route_grad, 0.0))
    own_sums = pltpu.roll(sums, 8, 1)[0:1, :]
    sent_sums = jnp.zeros((1, LANES), F32)
    for k, part in enumerate(three_parts(sums)):
        sent_sums = sent_sums + pltpu.roll(part, 8 + 8 * k, 1)[0:1, :]
    at = 0
    for grad in (grads[:, :width], grads[:, width : 3 * width], grads[:, 3 * width : 4 * width]):
        mine, other = halves_of(grad, place)
        size = mine.shape[1]
        kept[:, at : at + size] = mine
        sent[:, at : at + size] = other.astype(BF16)
        at += size
    kept[:, at:] = vectors + own_sums
    sent[:, at:] = (vectors + sent_sums).astype(BF16)


def mix_kernel(plans, count, *refs):
    ins, outs = refs[:count], refs[count:]
    for out, parts in zip(outs, plans):
        for target, sources in parts:
            dims = out.at[target].shape
            values = [ins[k][index].reshape(dims) for k, index in sources]
            if len(values) > 1:
                values = [sum(v.astype(F32) for v in values)]
            out[target] = values[0].astype(out.dtype)


def finish_light_kernel(kept, received, *outs):
    total = kept[0, 0].astype(F32) + received[0, 0].astype(F32)
    base = 0
    for ref in outs:
        block = ref.shape[0]
        for c in range(ref.shape[1] // LANES):
            ref[:, c * LANES : (c + 1) * LANES] = total[base : base + block]
            base += block


def finish_heavy_kernel(heavy_kept, heavy_got, q_out, kv_out, out_out, vectors, stats):
    total = heavy_kept[...] + heavy_got[...].astype(F32)
    at = 0
    for ref in (q_out, kv_out, out_out, vectors):
        ref[...] = total[:, at : at + ref.shape[1]]
        at += ref.shape[1]
    sums = total[:8, at - LANES :]
    stats[...] = sums + pltpu.roll(sums, LANES - 8, 1) + pltpu.roll(sums, LANES - 16, 1)


def finish_ffn_kernel(groups, *refs):
    pieces, gate_up_out = refs[:-1], refs[-1]
    group = len(pieces)
    low_place = lax.rem(lax.axis_index("seq"), group)
    unit = pieces[0].shape[1] // groups
    for j, piece in enumerate(pieces):
        for z in range(groups):
            at = pl.multiple_of((z * group + (low_place ^ j)) * unit, unit)
            gate_up_out[:, pl.ds(at, unit)] = piece[:, z * unit : (z + 1) * unit].astype(F32)


def blend(ins, outs, after=(), micros=1, mib=6):
    kernel = functools.partial(mix_kernel, [parts for _, _, parts in outs], len(ins))
    return call(kernel, [shape(dims, dtype) for dims, dtype, _ in outs], ins, mib=mib, after=after, micros=micros)


ALL = slice(None)


def joined(ins, first, cuts):
    blocks = [(first + k, b) for k, part in enumerate(ins) for b in range(part.shape[0])]
    each = len(blocks) // cuts
    dims = (each, *ins[0].shape[1:])
    outs = []
    for c in range(cuts):
        outs.append((dims, ins[0].dtype, [(k, [source]) for k, source in enumerate(blocks[c * each : (c + 1) * each])]))
    return outs


def pair_part(target, pair, index):
    return (target, [(2 * pair, index), (2 * pair + 1, index)])


def side_by_side(rows, cuts):
    half = rows // 2
    dims = (4, 2, half, LANES)
    each = 8 // cuts
    ways = [((0, 2), slice(0, half)), ((4, 6), slice(0, half)), ((0, 4), slice(half, rows)), ((2, 6), slice(half, rows))]
    outs = []
    for starts, part in ways:
        parts = []
        for k, start in enumerate(starts):
            inside = slice(start % each, start % each + 2)
            parts.append(pair_part(slice(2 * k, 2 * k + 2), start // each, (inside, ALL, part)))
        outs.append((dims, BF16, parts))
    return outs


def crossed(rows):
    dims = (2, 2, rows // 2, LANES)
    sides = (slice(0, 2), slice(2, 4))
    return [(dims, BF16, [pair_part(ALL, pair, side)]) for pair in (0, 1) for side in sides]


def halved(rows, first):
    half = rows // 2
    places = ((ALL, ALL, slice(0, half)), (ALL, ALL, slice(half, rows)))
    outs = []
    for way in (slice(0, 1), slice(1, 2)):
        parts = [pair_part(place, first + k, (ALL, way)) for k, place in enumerate(places)]
        outs.append(((2, 1, rows, LANES), BF16, parts))
    return outs


def last_half(rows, pair):
    return [((1, 1, rows, LANES), BF16, [pair_part(ALL, pair, way)]) for way in (slice(0, 1), slice(1, 2))]


def flat_halved(rows, keep, got, base):
    half = rows // 2
    ways = []
    for way in (0, 1):
        parts = []
        for slot in (0, 1):
            at = base + (2 * slot + way) * half
            sources = [(keep, (slot, way)), (got, slice(at, at + half))]
            parts.append(((slot, 0, slice(half, rows)), sources))
        ways.append(parts)
    return ways


def lanes_of(c):
    return slice(c * LANES, (c + 1) * LANES)


def skip_operand(kernel, place):
    return lambda *refs: kernel(*refs[:place], *refs[place + 1 :])


def local_kernels(
    tokens,
    segments,
    query_route,
    kv_route,
    ffn_route,
    grad_out,
    attn_gain,
    light_qkv,
    light_out,
    heavy_q,
    heavy_kv,
    heavy_out,
    route_query,
    ffn_gain,
    light_gate_up,
    light_down,
    heavy_gate_up,
    heavy_down,
    route_ffn,
):
    rows, span, width = tokens.shape
    devices = lax.axis_size("seq")
    routed = query_route.shape[1] // devices
    own, count = rows * span, rows * routed
    per_row = devices * routed
    extent = span + 2 * RADIUS
    block = width // devices
    light_heads = width // DL
    ffn_light, ffn_heavy = light_down.shape[0], heavy_down.shape[0]
    marked = width + LANES

    rim = shape((rows, RADIUS + 16, width), BF16)
    keys, upper, lower, table = call(
        functools.partial(first_kernel, routed),
        [shape((rows, routed, marked), BF16), rim, rim, shape((4, width), F32)],
        [kv_route, segments, tokens, attn_gain, ffn_gain, route_query, route_ffn],
        hbm=7,
        scratch=[
            pltpu.SMEM(kv_route.shape, jnp.int32),
            pltpu.SMEM(segments.shape, jnp.int32),
            pltpu.VMEM(segments.shape, jnp.int32),
            pltpu.VMEM(tokens.shape, BF16),
            pltpu.VMEM((width,), F32),
            pltpu.VMEM((width,), F32),
            pltpu.VMEM((width,), BF16),
            pltpu.VMEM((width,), BF16),
            pltpu.VMEM((own, width), F32),
            pltpu.VMEM((count, marked), F32),
            pltpu.SemaphoreType.DMA((8,)),
        ],
        mib=58,
    )
    bits = (1, 2, 4, 8)
    keys = keys[None]
    keys_got = [swap(keys, "seq", flip) for flip in (8, 4, 12)]
    before = shifted(upper, "seq", 1)
    after = shifted(lower, "seq", -1)
    (keys_four,) = blend([keys, *keys_got], joined([keys, *keys_got], 0, 1), mib=4)
    keys_four_got = swap(keys_four, "seq", 2)
    last = keys_four

    normed, query, keyval, probs, mix, attn = call(
        light_kernel,
        [
            shape((rows * extent, width), BF16),
            shape((own, width), BF16),
            shape((rows * extent, 2 * width), BF16),
            shape((rows * light_heads, extent, span), BF16),
            shape((own, width), BF16),
            shape((own, width), F32),
        ],
        [before, tokens, after, segments, table, light_qkv, light_out],
        scratch=[pltpu.VMEM((8, 3 * span), F32), pltpu.VMEM((width, span), F32)],
        micros=6,
        mib=14,
        after=[last],
    )
    held = [keys_four, keys_four_got]
    (keys_eight,) = blend(held, joined(held, 0, 1), [attn], mib=4)
    key_parts = [keys_eight, swap(keys_eight, "seq", 1)]

    small = shape((count, width), F32)
    middle, normed_two, keyval_all, payload, q_rows, f_rows, f_up, proj, f_marks, stats = call(
        functools.partial(middle_kernel, routed, len(key_parts)),
        [
            shape((own, width), F32),
            shape((own, width), BF16),
            shape((rows, per_row, 2 * width), BF16),
            shape((rows, routed, 3 * width + LANES), BF16),
            small,
            small,
            small,
            small,
            shape((count, LANES), F32),
            shape((8, LANES), F32),
        ],
        [
            query_route, ffn_route, segments, tokens, segments, *key_parts, attn, grad_out,
            table, heavy_q, heavy_kv, heavy_out,
        ],
        smem=3,
        scratch=[
            pltpu.VMEM((own, width), F32),
            pltpu.VMEM((count, LANES), F32),
            pltpu.VMEM((count, width), F32),
        ],
        micros=4,
        mib=8,
    )
    payload = payload[None]
    payload_got = [swap(payload, "seq", flip) for flip in (8, 4, 12)]

    share = shape((own, ffn_light), BF16)
    z_light, d_light, hidden, grad_gate, grad_up = call(
        light_ffn_kernel,
        [shape((own, width), F32), shape((own, width), F32), share, share, share],
        [normed_two, grad_out, light_gate_up, light_down],
        micros=6,
        mib=9,
    )
    half_rows = (width // 2) // LANES
    slot_rows = block * ffn_light // LANES + ffn_light // devices * half_rows
    slots = [shape((devices // (2 * FIRST_CUTS), 2, slot_rows, LANES), BF16)] * (2 * FIRST_CUTS)
    slots = call(
        functools.partial(first_grads_kernel, bits),
        slots,
        [normed_two, grad_gate, grad_up, hidden, grad_out],
        scratch=[
            pltpu.VMEM((width, own), BF16),
            pltpu.VMEM((ffn_light, own), BF16),
            pltpu.VMEM((own, width), BF16),
        ],
        micros=4,
        mib=9,
    )
    core = len(slots) // 2
    first_core = list(zip(slots[:core], [swap(part, "seq", 1) for part in slots[core:]]))
    held = [payload, *payload_got]
    (routed_four,) = blend(held, joined(held, 0, 1), [slots[0]], mib=4)
    routed_four_got = swap(routed_four, "seq", 2)

    steps = 4
    group = min(4, devices)
    groups = devices // group
    unit = ffn_heavy // devices
    heavy_unit = ffn_heavy // steps
    whole = lambda *dims: pl.BlockSpec(dims, lambda j: (0,) * len(dims))

    def streamed(first):
        columns = lambda at: pl.BlockSpec((width, heavy_unit), lambda j: (0, at + first + j))
        return [columns(0), columns(steps), pl.BlockSpec((heavy_unit, width), lambda j: (first + j, 0))]

    half = steps // 2
    share_dims = [(half, width, unit), (half, width, unit), (half, unit, width)]
    share_shapes = [shape(dims, BF16) for dims in share_dims]
    share_specs = [pl.BlockSpec((1, *dims[1:]), lambda j: (j, 0, 0)) for dims in share_dims]
    z_heavy, d_heavy, *shares_one = pl.pallas_call(
        skip_operand(functools.partial(ffn_first_kernel, group), 6),
        grid=(half,),
        out_shape=[small, small, *share_shapes],
        in_specs=streamed(0) + [whole(count, width)] * 2 + [whole(4, width), ANY],
        out_specs=[whole(count, width)] * 2 + share_specs,
        compiler_params=pltpu.CompilerParams(vmem_limit_bytes=12 * MIB),
        cost_estimate=cost(6),
    )(heavy_gate_up, heavy_gate_up, heavy_down, f_rows, f_up, table, routed_four)
    rows_one = slots[0].shape[2]
    ins = [v for pair in first_core for v in pair]
    each = 8 // FIRST_CUTS
    halves = [
        (
            (8, 1, rows_one, LANES),
            BF16,
            [pair_part(slice(k * each, (k + 1) * each), k, (ALL, way)) for k in range(FIRST_CUTS)],
        )
        for way in (slice(0, 1), slice(1, 2))
    ]
    left_keep, left_sent = blend(ins, halves, [z_heavy])
    first_pairs = [left_keep, swap(left_sent, "dp", 1)]
    outputs, dmid, dmid_low, proj_payload, vectors, *shares_two = pl.pallas_call(
        skip_operand(functools.partial(ffn_last_kernel, routed, group), 19),
        grid=(half,),
        out_shape=[
            shape((rows, span, width), BF16),
            shape((own, width), F32),
            shape((own, width), BF16),
            shape((rows, routed, marked), BF16),
            shape((8, width), F32),
            *share_shapes,
        ],
        in_specs=[SMEM, SMEM]
        + streamed(half)
        + [whole(count, width)] * 2
        + [whole(rows, span, width)]
        + [whole(own, width)] * 3
        + [whole(count, width)] * 4
        + [whole(count, LANES), whole(4, width), whole(8, LANES), whole(rows, span), ANY],
        out_specs=[
            whole(rows, span, width),
            whole(own, width),
            whole(own, width),
            whole(rows, routed, marked),
            whole(8, width),
            *share_specs,
        ],
        scratch_shapes=[pltpu.VMEM((count, width), F32)] * 3 + [pltpu.VMEM((own, width), F32)] * 2,
        compiler_params=pltpu.CompilerParams(vmem_limit_bytes=16 * MIB),
        cost_estimate=cost(7),
    )(
        query_route, ffn_route, heavy_gate_up, heavy_gate_up, heavy_down, z_heavy, d_heavy, grad_out, middle,
        z_light, d_light, q_rows, f_rows, f_up, proj, f_marks, table, stats, segments, left_keep,
    )
    proj_payload = proj_payload[None]
    proj_got = [swap(proj_payload, "seq", flip) for flip in (8, 4, 12)]

    slot_rows = block * 3 * half_rows + block * half_rows + 32
    slots = [shape((devices // (2 * SECOND_CUTS), 2, slot_rows, LANES), BF16)] * (2 * SECOND_CUTS)
    rim = shape((rows, RADIUS, width), BF16)
    dnorm, to_right, to_left, *slots = call(
        functools.partial(light_back_kernel, bits),
        [shape((own, width), F32), rim, rim, *slots],
        [dmid_low, query, keyval, probs, normed, mix, vectors, table, light_qkv, light_out],
        scratch=[
            pltpu.VMEM((own, width), BF16),
            pltpu.VMEM((rows * extent, 2 * width), BF16),
            pltpu.VMEM((extent, 2 * width), F32),
            pltpu.VMEM((width, span), F32),
            pltpu.VMEM((width, width), BF16),
            pltpu.VMEM((width, rows * extent), BF16),
        ],
        micros=3,
        mib=12,
    )
    from_left = shifted(to_right, "seq", 1)
    from_right = shifted(to_left, "seq", -1)
    core = len(slots) // 2
    second_core = list(zip(slots[:core], [swap(part, "seq", 1) for part in slots[core:]]))

    held_proj, held_routed = [proj_payload, *proj_got], [routed_four, routed_four_got]
    side = (4, 1, rows_one, LANES)
    sides = [
        (side, BF16, [pair_part(slice(2 * k, 2 * k + 2), 0, slice(4 * k + at, 4 * k + at + 2)) for k in (0, 1)])
        for at in (0, 2)
    ]
    first_keep, first_sent, proj_four, *routed_eight = blend(
        first_pairs + held_proj + held_routed,
        sides + joined(held_proj, 2, 1) + joined(held_routed, 6, 1),
        [dnorm],
    )
    first_pairs = [first_keep, swap(first_sent, "seq", 4)]
    held_proj = [proj_four, swap(proj_four, "seq", 2)]
    routed_parts = routed_eight + [swap(piece, "seq", 1) for piece in routed_eight]

    heavy_rows = group * block + unit // 2
    ffn_kept, ffn_sent = call(
        functools.partial(heavy_ffn_kernel, len(routed_parts)),
        [shape((heavy_rows, groups * unit), F32), shape((heavy_rows, groups * unit), BF16)],
        [*routed_parts, *shares_one, *shares_two],
        micros=7,
        mib=11,
        after=[left_keep],
    )
    ffn_got = swap(ffn_sent, "dp", 1)

    rows_two = slots[0].shape[2]
    ins = [v for pair in second_core for v in pair]
    left_keep, left_sent, right_keep, right_sent = blend(
        ins, side_by_side(rows_two, SECOND_CUTS), [ffn_kept], micros=1
    )
    (proj_eight,) = blend(held_proj, joined(held_proj, 0, 1), [left_keep])
    proj_parts = [proj_eight, swap(proj_eight, "seq", 1)]
    second_pairs = [left_keep, swap(left_sent, "seq", 2), right_keep, swap(right_sent, "seq", 4)]

    gathers = (routed_parts, proj_parts, key_parts)
    grad_lanes = 4 * width + LANES
    heavy_grads, heavy_parts, sums, pair_sent = call(
        functools.partial(heavy_row_kernel, routed, [len(parts) for parts in gathers]),
        [
            shape((block, grad_lanes), F32),
            shape((2, routed, width), F32),
            shape((8, LANES), F32),
            shape((block + routed, grad_lanes), BF16),
        ],
        [*sum(gathers, []), keyval_all, table, heavy_q, heavy_kv, heavy_out],
        scratch=[
            pltpu.VMEM((width, per_row), BF16),
            pltpu.VMEM((width, per_row), F32),
            pltpu.VMEM((per_row, 2 * width), BF16),
        ],
        micros=9,
        mib=8,
        after=[proj_eight],
    )
    pair_got = swap(pair_sent, "seq", 1)
    first_keep, first_sent = blend(
        first_pairs,
        [((2, 1, rows_one, LANES), BF16, [pair_part(ALL, 0, slice(at, at + 2))]) for at in (0, 2)],
        [sums],
    )
    first_pairs = [first_keep, swap(first_sent, "seq", 2)]
    from_left, from_right = blend(
        [from_left, from_right], [(from_left.shape, BF16, [(ALL, [(k, ALL)])]) for k in (0, 1)], [first_keep]
    )
    below = slice(group * block, heavy_rows)
    down_lanes = [slice(0, width // 2), slice(width // 2, width)]
    rows_of = lambda j: slice(j * block, (j + 1) * block)
    kept_side, sent_side, kept_other, sent_other = crossed(rows_two)
    sent_rows = 2 * rows_two
    parts = [(slice(0, sent_rows), sent_other[2][0][1])]
    for c in range(groups * unit // LANES):
        at = sent_rows + c * block
        parts.append(pair_part(slice(at, at + block), 2, (rows_of(2), lanes_of(c))))
    merged = ((sent_rows + groups * unit // LANES * block, LANES), BF16, parts)
    downs = [pair_part(slice(k * unit // 2, (k + 1) * unit // 2), 2, (below, down_lanes[k])) for k in (0, 1)]
    left_keep, left_sent, right_keep, x_sent, heavy_down_grad, *pieces = blend(
        second_pairs + [ffn_kept, ffn_got],
        [kept_side, sent_side, kept_other, merged, ((unit, width // 2), F32, downs)]
        + [
            ((block, groups * unit), F32 if j == 0 else BF16, [pair_part(ALL, 2, rows_of(j))])
            for j in (0, 1, 3)
        ],
        [from_left],
    )
    second_pairs = [left_keep, swap(left_sent, "seq", 4), right_keep, swap(x_sent, "seq", 2)]
    pieces = [pieces[0], swap(pieces[1], "seq", 1), None, swap(pieces[2], "seq", 3)]
    grad_tokens, heavy_kept, heavy_sent = call(
        functools.partial(heavy_last_kernel, routed),
        [
            shape((rows, span, width), BF16),
            shape((block, 2 * width + LANES), F32),
            shape((block, 2 * width + LANES), BF16),
        ],
        [
            query_route, kv_route, heavy_grads, heavy_parts, sums, pair_got, dnorm, from_left, from_right,
            dmid, tokens, table, heavy_q, heavy_kv,
        ],
        smem=2,
        scratch=[pltpu.VMEM((own, width), F32), pltpu.VMEM((rows, 2, routed, width), F32)],
        micros=2,
        mib=7,
        after=[left_keep],
    )
    ways = flat_halved(rows_two, 2, 3, 0)
    for way in (0, 1):
        index = (ALL, slice(way, way + 1))
        ways[way].insert(0, ((ALL, ALL, slice(0, rows_two // 2)), [(0, index), (1, index)]))
    sent_parts = []
    for (slot, _, place), sources in ways[1][1:]:
        sent_parts.append((slice(slot * rows_two + place.start, slot * rows_two + place.stop), sources))
    for slot in (0, 1):
        at = slot * rows_two
        sources = [(0, (slot, 1)), (1, (slot, 1))]
        sent_parts.append((slice(at, at + rows_two // 2), sources))
    piece_parts = []
    for c in range(groups * unit // LANES):
        at = sent_rows + c * block
        piece_parts.append(((ALL, lanes_of(c)), [(3, slice(at, at + block))]))
    second_keep, y_sent, pieces[2] = blend(
        second_pairs,
        [
            ((2, 1, rows_two, LANES), BF16, ways[0]),
            ((2 * rows_two, LANES), BF16, sent_parts),
        ]
        + [((block, groups * unit), BF16, piece_parts)],
        [heavy_kept],
    )
    y_got = swap(y_sent, "dp", 1)
    first_keep, first_sent = blend(first_pairs, last_half(rows_one, 0), [second_keep])
    first_pair = [first_keep, swap(first_sent, "seq", 8)]
    (heavy_gate_up_grad,) = call(
        functools.partial(finish_ffn_kernel, groups),
        [shape((block, ffn_heavy), F32)],
        pieces,
        micros=0.5,
        mib=4,
        after=[first_keep],
    )
    second_keep, second_sent, heavy_sent = blend(
        [second_keep, y_got, heavy_sent],
        [
            ((1, 1, rows_two, LANES), BF16, [(ALL, [(0, slot), (1, slice(slot * rows_two, (slot + 1) * rows_two))])])
            for slot in (0, 1)
        ]
        + [(heavy_sent.shape, BF16, [(ALL, [(2, ALL)])])],
        [heavy_gate_up_grad],
    )
    heavy_got = swap(heavy_sent, "dp", 1)
    second_pair = [second_keep, swap(second_sent, "seq", 8)]
    light_gate_up_grad, light_down_grad = call(
        finish_light_kernel,
        [shape((block, ffn_light), F32), shape((ffn_light // devices, width // 2), F32)],
        first_pair,
        mib=4,
        after=[second_keep],
    )
    heavy_q_grad, heavy_kv_grad, heavy_out_grad, heavy_vectors, stats = call(
        finish_heavy_kernel,
        [
            shape((block, width // 2), F32),
            shape((block, width), F32),
            shape((block, width // 2), F32),
            shape((block, LANES), F32),
            shape((8, LANES), F32),
        ],
        [heavy_kept, heavy_got],
        mib=4,
        after=[light_down_grad],
    )
    light_qkv_grad, light_out_grad, light_vectors = call(
        finish_light_kernel,
        [
            shape((block, 3 * width // 2), F32),
            shape((block, width // 2), F32),
            shape((16, LANES), F32),
        ],
        second_pair,
        mib=4,
        after=[heavy_vectors],
    )
    sums = stats[0, 8:14]
    return (
        outputs,
        grad_tokens,
        light_vectors[2, :block] + heavy_vectors[:, 0],
        light_qkv_grad,
        light_out_grad,
        heavy_q_grad,
        heavy_kv_grad,
        heavy_out_grad,
        heavy_vectors[:, 1],
        light_vectors[0, :block],
        light_gate_up_grad,
        light_down_grad,
        heavy_gate_up_grad,
        heavy_down_grad,
        light_vectors[1, :block],
        jnp.sqrt(sums[:5] / (sums[5] * width)),
    )


def local(tokens, segments, query_route, *others):
    block = tokens.shape[2] // lax.axis_size("seq")
    fits = query_route.shape[1] <= 256 and block % 16 == 0 and tokens.shape[0] == 2
    return (local_kernels if fits else local_wide)(tokens, segments, query_route, *others)


def solution(mesh):
    placed = (
        P("dp", "seq", None),
        P("dp", "seq"),
        P("dp", None),
        P("dp", None),
        P("dp", "seq"),
        P("dp", "seq", None),
    ) + (P(),) * 13
    matrix = P("seq", "dp")
    vector = P("seq")
    return jax.shard_map(
        local,
        mesh=mesh,
        in_specs=placed,
        out_specs=(
            P("dp", "seq", None),
            P("dp", "seq", None),
            vector,
            matrix,
            matrix,
            matrix,
            matrix,
            matrix,
            vector,
            vector,
            matrix,
            matrix,
            matrix,
            matrix,
            vector,
            P(),
        ),
        check_vma=False,
    )
```
